32 devices in a mesh: gx: 2 (over core), gy: 2 (over x), gz: 8 (over z, y).
Axes of the slice: x: 2, y: 2, z: 4, core: 2. Of those that a mesh axis runs over, the one named last changes fastest.
Arguments:
- a_diag: bfloat16 [8, 12, 64, 4096], P('gx', 'gy', 'gz'), may hold values from -0.75 to 0.75
- a_face: bfloat16 [3, 8, 12, 64, 4096], P(None, 'gx', 'gy', 'gz'), may hold values from -0.75 to 0.75
- prolong: bfloat16 [8, 12, 64, 4096], P('gx', 'gy', 'gz'), may hold values from -0.75 to 0.75
- aggregate: int32 [8, 12, 64], P('gx', 'gy', 'gz'), may hold values from 0 to 23
- pair_slot: int32 [7, 8, 12, 64], P(None, 'gx', 'gy', 'gz'), may hold values from 0 to 6
- row_owner: int32 [768], P(('gx', 'gy', 'gz')), may hold values from 0 to 7, as said below
Outputs:
- coarse: bfloat16 [2, 2, 8, 24, 7, 4096], P('gx', 'gy', 'gz')
The draws below stay inside these ranges and needn't reach their ends.
Inputs may be any that keep to these rules, and one draw needn't show every extreme that they name: `row_owner`: all rows of a device go to owners in its own (gx, gy) column. From each device at most 3 rows go to one owner, and in each column one owner receives exactly 3 rows from every device, so at most 24 rows reach one owner.
All inputs are finite; a program needn't handle non-finite values.
Results may differ from the reference program's by a relative error of at most 0.0049.
Values may be sent and summed in bfloat16 or wider, within the bound.
No kernel may reach another device: no remote copies, remote signals or barrier semaphores. Data moves between devices by JAX's collectives and lax.ppermute only.
A program may use at most 256 MiB of HBM per device.

```python
import jax
import jax.numpy as jnp
from jax import lax

NODES = 64
BLOCK = 4096
SLOTS = 7
BX = 4
BY = 6
BZ = 8
AGG_DEV = 24
NX = 8
NY = 12
NZ = 64
NC = 768
RECV = 24
N_GX = 2
N_GY = 2
N_GZ = 8
DEVICES = 32


def draw_row_owner(key, part):
    capacity = max(2, (AGG_DEV + N_GZ - 1) // N_GZ)
    columns = DEVICES // N_GZ
    key_hot, key_order, key_perm = jax.random.split(key, 3)
    hot = jax.random.randint(key_hot, (columns,), 0, N_GZ)
    hot_dev = jnp.repeat(hot, N_GZ)
    scores = jax.random.randint(key_order, (DEVICES, AGG_DEV), 0, 1 << 20) * AGG_DEV + jnp.arange(AGG_DEV, dtype=jnp.int32)[None, :]
    order = jnp.argsort(scores, axis=1)
    position = jnp.argsort(order, axis=1).astype(jnp.int32)
    others = max(N_GZ - 1, 1)
    perm_scores = jax.random.randint(key_perm, (DEVICES, others), 0, 1 << 20) * others + jnp.arange(others, dtype=jnp.int32)[None, :]
    perm = jnp.argsort(perm_scores, axis=1).astype(jnp.int32)
    group = jnp.clip((position - capacity) // capacity, 0, others - 1)
    offset = jnp.take_along_axis(perm, group, axis=1)
    other = (hot_dev[:, None] + 1 + offset) % N_GZ
    chosen = jnp.where(position < capacity, hot_dev[:, None], other)
    return chosen.reshape(-1).astype(jnp.int32)


def with_ends(drawn, key, smallest, largest):
    longest = drawn.shape.index(max(drawn.shape))
    spots = []
    for shift in (0, 1):
        where = [jax.random.randint(jax.random.fold_in(key, axis), (), 0, length) for axis, length in enumerate(drawn.shape)]
        where[longest] = (where[longest] + shift) % drawn.shape[longest]
        spots.append(tuple(where))
    return drawn.at[spots[0]].set(smallest).at[spots[1]].set(largest)


def steps_of(key, dims, cuts, least, top_value):
    gain, own = 1.0, jax.random.fold_in(key, 6)
    for dim, parts in cuts:
        steps = jnp.exp(jax.random.uniform(jax.random.fold_in(own, dim), (parts,), jnp.float32, least / len(cuts), top_value / len(cuts)))
        gain = gain * jnp.repeat(steps, dims[dim] // parts).reshape([-1 if axis == dim else 1 for axis in range(len(dims))])
    return gain


def bell_draw(stream_key, dims, width, limit, cuts=(), held_as=jnp.bfloat16):
    level = steps_of(stream_key, dims, cuts, -0.22, 0.18) if cuts else 1.0
    drawn = jax.random.normal(stream_key, dims, jnp.float32) * width * level
    return jnp.minimum(jnp.maximum(drawn, -limit), limit).astype(held_as)


def setup_inputs(seed: int = 0) -> dict:
    key_list = jax.random.split(jax.random.key(seed), 7)
    return {
        "a_diag": bell_draw(key_list[0], (NX, NY, NZ, BLOCK), NODES ** -0.5, 0.75, ((0, 2), (1, 2), (2, 8))),
        "a_face": bell_draw(key_list[1], (3, NX, NY, NZ, BLOCK), NODES ** -0.5, 0.75, ((1, 2), (2, 2), (3, 8))),
        "prolong": bell_draw(key_list[2], (NX, NY, NZ, BLOCK), NODES ** -0.5, 0.75, ((0, 2), (1, 2), (2, 8))),
        "aggregate": with_ends(jax.random.randint(key_list[3], (NX, NY, NZ), 0, AGG_DEV), jax.random.fold_in(key_list[3], 1), 0, AGG_DEV - 1).astype(jnp.int32),
        "pair_slot": with_ends(jax.random.randint(key_list[4], (7, NX, NY, NZ), 0, SLOTS), jax.random.fold_in(key_list[4], 1), 0, SLOTS - 1).astype(jnp.int32),
        "row_owner": draw_row_owner(jax.random.fold_in(key_list[6], 71), 0),
    }


def reference(a_diag, a_face, prolong, aggregate, pair_slot, row_owner):
    nodes = NODES
    block = BLOCK
    pad_p = jnp.pad(prolong, ((1, 1), (1, 1), (1, 1), (0, 0)))
    pad_fx = jnp.pad(a_face[0], ((1, 0), (0, 0), (0, 0), (0, 0)))
    jy = jnp.arange(NY, dtype=jnp.int32)
    kz = jnp.arange(NZ, dtype=jnp.int32)

    def mats(x):
        return x.astype(jnp.float32).reshape(NY, NZ, nodes, nodes)

    def forward(a, p):
        return jnp.einsum("yzab,yzbc->yzac", mats(a), mats(p), precision=lax.Precision.HIGHEST)

    def backward(a, p):
        return jnp.einsum("yzba,yzbc->yzac", mats(a), mats(p), precision=lax.Precision.HIGHEST)

    def plane(total, index):
        window = lax.dynamic_slice_in_dim(pad_p, index, 3, 0)
        center = window[1, 1:-1, 1:-1]
        diag_here = lax.dynamic_index_in_dim(a_diag, index, 0, False)
        face_x = lax.dynamic_index_in_dim(a_face[0], index, 0, False)
        face_y = lax.dynamic_index_in_dim(a_face[1], index, 0, False)
        face_z = lax.dynamic_index_in_dim(a_face[2], index, 0, False)
        back_x = lax.dynamic_index_in_dim(pad_fx, index, 0, False)
        back_y = jnp.pad(face_y, ((1, 0), (0, 0), (0, 0)))[:-1]
        back_z = jnp.pad(face_z, ((0, 0), (1, 0), (0, 0)))[:, :-1]
        couple = jnp.stack([
            forward(diag_here, center),
            backward(back_x, window[0, 1:-1, 1:-1]),
            forward(face_x, window[2, 1:-1, 1:-1]),
            backward(back_y, window[1, :-2, 1:-1]),
            forward(face_y, window[1, 2:, 1:-1]),
            backward(back_z, window[1, 1:-1, :-2]),
            forward(face_z, window[1, 1:-1, 2:]),
        ], axis=0).astype(jnp.bfloat16)
        couple = lax.optimization_barrier(couple).astype(jnp.float32)
        terms = jnp.einsum("yzba,fyzbc->fyzac", mats(center), couple, precision=lax.Precision.HIGHEST)
        device = ((index // BX) * N_GY + jy[:, None] // BY) * N_GZ + kz[None, :] // BZ
        rowid = device * AGG_DEV + lax.dynamic_index_in_dim(aggregate, index, 0, False)
        slots = lax.dynamic_index_in_dim(pair_slot, index, 1, False)
        keys = rowid[None] * SLOTS + slots
        total = total + jax.ops.segment_sum(terms.reshape(-1, block), keys.reshape(-1).astype(jnp.int32), NC * SLOTS)
        return total, None

    start = jnp.zeros((NC * SLOTS, block), jnp.float32)
    rows, _ = lax.scan(plane, start, jnp.arange(NX, dtype=jnp.int32))
    columns = N_GX * N_GY
    per_col = N_GZ * AGG_DEV
    rounded = rows.astype(jnp.bfloat16).reshape(columns, per_col, SLOTS, block)
    owners = row_owner.reshape(columns, per_col)
    onehot = (owners[:, :, None] == jnp.arange(N_GZ, dtype=jnp.int32)[None, None, :]).astype(jnp.int32)
    ranks = jnp.cumsum(onehot, axis=1) - 1
    placed = jnp.take_along_axis(ranks, owners[:, :, None], axis=2)[:, :, 0]
    column_ids = jnp.broadcast_to(jnp.arange(columns, dtype=jnp.int32)[:, None], (columns, per_col))
    result = jnp.zeros((columns, N_GZ, RECV, SLOTS, block), jnp.bfloat16)
    result = result.at[column_ids, owners, placed].set(rounded)
    return result.reshape(N_GX, N_GY, N_GZ, RECV, SLOTS, block)
```

```python
import jax
import jax.numpy as jnp
from jax import lax
from jax.sharding import PartitionSpec as P

NODES = 64
SLOTS = 7
AGG_DEV = 24


def with_halo(cells, sides, width):
    for axis, dim in sides:
        count = lax.axis_size(axis)
        ends = count - 1
        head = lax.slice_in_dim(cells, 0, width, axis=dim)
        tail = lax.slice_in_dim(cells, cells.shape[dim] - width, cells.shape[dim], axis=dim)
        cells = jnp.concatenate(
            [
                lax.ppermute(tail, axis, [(i, (i + 1) % count) for i in range(ends)]),
                cells,
                lax.ppermute(head, axis, [((i + 1) % count, i) for i in range(ends)]),
            ],
            axis=dim,
        )
    return cells


def passed_along(block, axis, distance):
    devices = range(lax.axis_size(axis))
    route = [(i - distance, i) for i in devices if i - distance in devices]
    return lax.ppermute(block, axis, route)


def pick_rows(match, source_rows):
    count = match.shape[1]
    source = jnp.sum(match * jnp.arange(count, dtype=jnp.int32)[None, :], axis=1)
    present = jnp.sum(match, axis=1) > 0
    taken = jnp.take(source_rows, source, axis=0)
    return (jnp.where(present[:, None, None], taken, jnp.zeros_like(taken)), present)


def shards(a_diag, a_face, prolong, aggregate, pair_slot, row_owner):
    size_x, size_y, size_z, block = a_diag.shape
    depth = lax.axis_size("gz")
    capacity = max(2, (AGG_DEV + depth - 1) // depth)
    holding = capacity * depth
    padded = with_halo(prolong, (("gx", 0), ("gy", 1), ("gz", 2)), 1)
    rim_x = passed_along(a_face[0, size_x - 1 :], "gx", 1)
    back_x = jnp.concatenate([rim_x, a_face[0, : size_x - 1]], axis=0)
    rim_y = passed_along(a_face[1, :, size_y - 1 :], "gy", 1)
    back_y = jnp.concatenate([rim_y, a_face[1, :, : size_y - 1]], axis=1)
    rim_z = passed_along(a_face[2, :, :, size_z - 1 :], "gz", 1)
    back_z = jnp.concatenate([rim_z, a_face[2, :, :, : size_z - 1]], axis=2)

    def blocks(value):
        return value.reshape(size_x, size_y, size_z, NODES, NODES)

    def forward(left, right):
        return jnp.einsum(
            "xyzab,xyzbc->xyzac", blocks(left), blocks(right), preferred_element_type=jnp.float32
        ).astype(jnp.bfloat16)

    def backward(left, right):
        return jnp.einsum(
            "xyzba,xyzbc->xyzac", blocks(left), blocks(right), preferred_element_type=jnp.float32
        ).astype(jnp.bfloat16)

    center = padded[1:-1, 1:-1, 1:-1]
    pairs = [
        (forward, a_diag, center),
        (backward, back_x, padded[:-2, 1:-1, 1:-1]),
        (forward, a_face[0], padded[2:, 1:-1, 1:-1]),
        (backward, back_y, padded[1:-1, :-2, 1:-1]),
        (forward, a_face[1], padded[1:-1, 2:, 1:-1]),
        (backward, back_z, padded[1:-1, 1:-1, :-2]),
        (forward, a_face[2], padded[1:-1, 1:-1, 2:]),
    ]
    key_ids = jnp.arange(AGG_DEV * SLOTS, dtype=jnp.int32)[:, None]
    summed = jnp.zeros((AGG_DEV * SLOTS, block), jnp.float32)
    for number, (product, left, right) in enumerate(pairs):
        couple = product(left, right)
        term = jnp.einsum(
            "xyzba,xyzbc->xyzac", blocks(center), couple, preferred_element_type=jnp.float32
        ).reshape(-1, block)
        keys = (aggregate * SLOTS + pair_slot[number]).reshape(1, -1)
        select = (key_ids == keys).astype(jnp.float32)
        summed = summed + jnp.dot(
            select, term, precision=lax.Precision.HIGHEST, preferred_element_type=jnp.float32
        )
    rows = summed.reshape(AGG_DEV, SLOTS, block).astype(jnp.bfloat16)
    slots = jnp.arange(holding, dtype=jnp.int32)
    owner_hits = (row_owner[:, None] == jnp.arange(depth, dtype=jnp.int32)[None, :]).astype(jnp.int32)
    rank = jnp.sum((jnp.cumsum(owner_hits, axis=0) - 1) * owner_hits, axis=1)
    place = row_owner * capacity + rank
    match = (place[None, :] == slots[:, None]).astype(jnp.int32)
    outgoing, present = pick_rows(match, rows)
    result = lax.all_to_all(outgoing, "gz", 0, 0, tiled=True)
    if holding != AGG_DEV:
        arrived = lax.all_to_all(present.astype(jnp.int32), "gz", 0, 0, tiled=True)
        target = jnp.cumsum(arrived) - 1
        match = ((arrived[None, :] > 0) & (target[None, :] == slots[:, None])).astype(jnp.int32)
        result, _ = pick_rows(match, result)
    return result.reshape(1, 1, 1, holding, SLOTS, block)


def solution(mesh):
    return jax.shard_map(
        shards,
        mesh=mesh,
        in_specs=(
            P("gx", "gy", "gz", None),
            P(None, "gx", "gy", "gz", None),
            P("gx", "gy", "gz", None),
            P("gx", "gy", "gz"),
            P(None, "gx", "gy", "gz"),
            P(("gx", "gy", "gz")),
        ),
        out_specs=P("gx", "gy", "gz", None, None, None),
        check_vma=False,
    )
```

```python
import functools

import jax
import jax.numpy as jnp
from jax import lax
from jax.experimental import pallas as pl
from jax.experimental.pallas import tpu as pltpu
from jax.sharding import PartitionSpec as P

NODES = 64
SLOTS = 7
AGG_DEV = 24
LANES = 128
HALF = NODES // 2
VMEM_LIMIT = 50 * 1024 * 1024


def passed_along(block, axis, distance):
    devices = range(lax.axis_size(axis))
    route = [(i - distance, i) for i in devices if i - distance in devices]
    return lax.ppermute(block, axis, route)


def pick_rows(match, source_rows):
    count = match.shape[1]
    source = jnp.sum(match * jnp.arange(count, dtype=jnp.int32)[None, :], axis=1)
    present = jnp.sum(match, axis=1) > 0
    taken = jnp.take(source_rows, source, axis=0)
    return (jnp.where(present[:, None, None], taken, jnp.zeros_like(taken)), present)


def low_lanes(rows):
    return lax.broadcasted_iota(jnp.int32, (rows, LANES), 1) < NODES


def swapped(value):
    return pltpu.roll(value, NODES, 1)


def spread(column, stage):
    depth = column.shape[0]
    for k in range(column.shape[1] // LANES):
        stage[depth * k : depth * (k + 1), :] = column[:, LANES * k : LANES * (k + 1)].astype(jnp.float32)


def block_of(stage, z, depth):
    return stage[pl.ds(z, HALF, stride=depth), :]


def stacked_pair(first, second):
    low = low_lanes(HALF)
    even = jnp.where(low, first, swapped(second))
    odd = jnp.where(low, swapped(first), second)
    return jnp.concatenate([even, odd], axis=0).astype(jnp.bfloat16)


def in_order(pair):
    row = lax.broadcasted_iota(jnp.int32, (NODES, NODES), 0)
    col = lax.broadcasted_iota(jnp.int32, (NODES, NODES), 1)
    move = (row == 2 * (col % HALF) + col // HALF).astype(jnp.bfloat16)
    return jnp.dot(move, pair, preferred_element_type=jnp.float32).astype(jnp.bfloat16)


def paired_weights(pair):
    low = low_lanes(NODES)
    zero = jnp.zeros_like(pair)
    first = jnp.where(low, pair, zero)
    second = jnp.where(low, zero, pair)
    left = jnp.concatenate([first, zero, second, zero], axis=0)
    right = jnp.concatenate([zero, first, zero, second], axis=0)
    return jnp.concatenate([left, right], axis=1)


def upright(product):
    return jnp.concatenate([product[:, :LANES], product[:, LANES:]], axis=0).astype(jnp.bfloat16)


def across(left, right):
    return lax.dot_general(left, right, (((0,), (0,)), ((), ())), preferred_element_type=jnp.float32)


def folded(square):
    low = low_lanes(HALF)
    moved = swapped(jnp.where(low, square[HALF : 2 * HALF], square[2 * HALF : 3 * HALF]))
    return (jnp.where(low, square[:HALF], moved), jnp.where(low, moved, square[3 * HALF :]))


def add_to(total, key, value):
    total[key] = total[key] + value


def joined_transposes(left0, right0, left1, right1):
    low = low_lanes(NODES)
    one = across(left0, right0)
    two = across(left1, right1)
    same = jnp.where(low, one[:NODES], two[NODES:])
    other = jnp.where(low, two[:NODES], one[NODES:])
    return (same + swapped(other)).astype(jnp.bfloat16)


def prepare_kernel(p_ref, fx_ref, fy_ref, fz_ref, natural_ref, stacked_ref, shifted_ref, head_x_ref, head_y_ref, head_z_ref,
                   rim_x_ref, rim_y_ref, rim_z_ref, tail_x_ref, tail_y_ref, tail_z_ref, last_z_ref, stage_p, stage_f, first_z, ends_z):
    plane = pl.program_id(0)
    size_y, depth = p_ref.shape[0], p_ref.shape[1]
    pairs = depth // 2

    def tail(blocks, stage, put):
        spread(blocks, stage)
        for z in range(depth):
            put(z, block_of(stage, z, depth).astype(jnp.bfloat16))

    def column(j, carry):
        spread(p_ref[j], stage_p)
        block = [block_of(stage_p, z, depth) for z in range(depth)]
        for p in range(pairs):
            stacked = stacked_pair(block[2 * p], block[2 * p + 1])
            stacked_ref[j, p] = stacked
            natural_ref[j, p] = in_order(stacked)
            shifted_ref[j, p] = stacked_pair(block[(2 * p - 1) % depth], block[2 * p])
        first_z[j] = block[0]
        ends_z[j] = block[depth - 1]
        spread(fz_ref[0, j], stage_f)
        tail_z_ref[j] = block_of(stage_f, depth - 1, depth).astype(jnp.bfloat16)

        @pl.when(plane == pl.num_programs(0) - 1)
        def _():
            spread(fx_ref[0, j], stage_f)
            for p in range(pairs):
                left = [block_of(stage_f, z, depth).astype(jnp.bfloat16) for z in (2 * p, 2 * p + 1)]
                tail_x_ref[j, 2 * p] = left[0]
                tail_x_ref[j, 2 * p + 1] = left[1]
                rim_x_ref[j, p] = joined_transposes(
                    left[0], block[2 * p].astype(jnp.bfloat16), left[1], block[2 * p + 1].astype(jnp.bfloat16))

        return carry

    lax.fori_loop(0, size_y, column, 0)

    spread(fy_ref[0, 0], stage_f)
    block = [block_of(stage_p, z, depth).astype(jnp.bfloat16) for z in range(depth)]
    for p in range(pairs):
        left = [block_of(stage_f, z, depth).astype(jnp.bfloat16) for z in (2 * p, 2 * p + 1)]
        tail_y_ref[0, 2 * p] = left[0]
        tail_y_ref[0, 2 * p + 1] = left[1]
        rim_y_ref[0, p] = joined_transposes(left[0], block[2 * p], left[1], block[2 * p + 1])
    head_y_ref[0] = natural_ref[0]

    @pl.when(plane == 0)
    def _():
        head_x_ref[...] = natural_ref[...]

    for t in range(size_y // 2):
        head_z_ref[t] = in_order(stacked_pair(first_z[2 * t], first_z[2 * t + 1]))
        last_z_ref[t] = stacked_pair(ends_z[2 * t], ends_z[2 * t + 1])
        rim_z_ref[t] = joined_transposes(
            tail_z_ref[2 * t], ends_z[2 * t].astype(jnp.bfloat16),
            tail_z_ref[2 * t + 1], ends_z[2 * t + 1].astype(jnp.bfloat16))


def prepare(prolong, faces, sizes):
    size_x, size_y, depth = sizes
    pairs, block = depth // 2, prolong.shape[-1]
    columns, half = size_x * size_y, size_y // 2
    shape = lambda *dims: jax.ShapeDtypeStruct(dims, jnp.bfloat16)
    by_plane = pl.BlockSpec((size_y, pairs, NODES, LANES), lambda i: (i, 0, 0, 0))
    one_plane = pl.BlockSpec((size_y, pairs, NODES, LANES), lambda i: (0, 0, 0, 0))
    by_column = pl.BlockSpec((1, pairs, NODES, LANES), lambda i: (i, 0, 0, 0))
    by_half = pl.BlockSpec((half, NODES, LANES), lambda i: (i, 0, 0))
    all_pairs = shape(columns, pairs, NODES, LANES)
    return pl.pallas_call(
        prepare_kernel,
        grid=(size_x,),
        in_specs=[
            pl.BlockSpec((size_y, depth, block), lambda i: (i, 0, 0)),
            pl.BlockSpec((1, size_y, depth, block), lambda i: (0, size_x - 1, 0, 0)),
            pl.BlockSpec((1, 1, depth, block), lambda i: (1, i * size_y + size_y - 1, 0, 0)),
            pl.BlockSpec((1, size_y, depth, block), lambda i: (2, i, 0, 0)),
        ],
        out_specs=[
            by_plane, by_plane, by_plane, one_plane, by_column, by_half, one_plane, by_column, by_half,
            pl.BlockSpec((size_y, depth, HALF, LANES), lambda i: (0, 0, 0, 0)),
            pl.BlockSpec((1, depth, HALF, LANES), lambda i: (i, 0, 0, 0)),
            pl.BlockSpec((size_y, HALF, LANES), lambda i: (i, 0, 0)),
            by_half,
        ],
        out_shape=[
            all_pairs, all_pairs, all_pairs,
            shape(size_y, pairs, NODES, LANES), shape(size_x, pairs, NODES, LANES), shape(columns // 2, NODES, LANES),
            shape(size_y, pairs, NODES, LANES), shape(size_x, pairs, NODES, LANES), shape(columns // 2, NODES, LANES),
            shape(size_y, depth, HALF, LANES), shape(size_x, depth, HALF, LANES), shape(columns, HALF, LANES),
            shape(columns // 2, NODES, LANES),
        ],
        scratch_shapes=[
            pltpu.VMEM((depth * HALF, LANES), jnp.float32),
            pltpu.VMEM((depth * HALF, LANES), jnp.float32),
            pltpu.VMEM((size_y, HALF, LANES), jnp.float32),
            pltpu.VMEM((size_y, HALF, LANES), jnp.float32),
        ],
        compiler_params=pltpu.CompilerParams(vmem_limit_bytes=VMEM_LIMIT),
        name="prepare",
    )(prolong, faces, faces, faces)


def interior_kernel(keys, diag_ref, fx_ref, fy_ref, fz_ref, natural_ref, stacked_ref, shifted_ref, out_ref,
                    stages, forward_even, forward_odd, back_even, back_odd):
    plane = pl.program_id(0)
    size_y, depth = diag_ref.shape[0], diag_ref.shape[1]
    pairs = depth // 2
    spare = out_ref.shape[0]
    totals = (forward_even, forward_odd, back_even, back_odd)

    @pl.when(plane == 0)
    def _():
        for total in totals:
            total[...] = jnp.zeros_like(total)

    def column(j, carry):
        here = plane * size_y + j
        below_x = jnp.maximum(here - size_y, 0)
        below_y = jnp.maximum(here - 1, 0)
        row_y = jnp.maximum(j - 1, 0)
        has_x, has_y = plane > 0, j > 0
        for stage, source in zip(range(4), (diag_ref[j], fx_ref[0, j], fy_ref[0, row_y], fz_ref[0, j])):
            spread(source, stages.at[stage])
        for p in range(pairs):
            left = []
            for stage in range(4):
                shift = 1 if stage == 3 else 0
                sides = [block_of(stages.at[stage], (2 * p + side - shift) % depth, depth).astype(jnp.bfloat16) for side in (0, 1)]
                left.append(jnp.concatenate(sides, axis=1))
            product = jnp.dot(
                jnp.concatenate(left, axis=0), paired_weights(natural_ref[j, p]), preferred_element_type=jnp.float32)
            prolongs = (stacked_ref[here, p], stacked_ref[below_x, p], stacked_ref[below_y, p], shifted_ref[j, p])
            for face in range(4):
                couple = upright(product[HALF * face : HALF * (face + 1)])
                square = across(prolongs[face], couple)
                ahead = folded(square)
                for side in (0, 1):
                    z = 2 * p + side
                    if face == 0:
                        key = keys[0, plane, j, z]
                    elif face == 1:
                        key = jnp.where(has_x, keys[2, jnp.maximum(plane - 1, 0), j, z], spare)
                    elif face == 2:
                        key = jnp.where(has_y, keys[4, plane, row_y, z], spare)
                    else:
                        key = keys[6, plane, j, z - 1] if z > 0 else spare
                    add_to(totals[side], key, ahead[side])
                if face == 0:
                    continue
                behind = folded(across(couple, prolongs[face]))
                for side in (0, 1):
                    z = 2 * p + side
                    if face == 1:
                        key = jnp.where(has_x, keys[1, plane, j, z], spare)
                    elif face == 2:
                        key = jnp.where(has_y, keys[3, plane, j, z], spare)
                    else:
                        key = keys[5, plane, j, z] if z > 0 else spare
                    add_to(totals[2 + side], key, behind[side])
        return carry

    lax.fori_loop(0, size_y, column, 0)

    @pl.when(plane == pl.num_programs(0) - 1)
    def _():
        def gather(r, carry):
            for s in range(SLOTS):
                key = r * SLOTS + s
                out_ref[key] = (forward_even[key] + forward_odd[key]) + (back_even[key] + back_odd[key])
            return carry

        lax.fori_loop(0, spare // SLOTS, gather, 0)


def interior(keys, diag, faces, natural, stacked, shifted, sizes):
    size_x, size_y, depth = sizes
    pairs, block = depth // 2, diag.shape[-1]
    columns, rows = size_x * size_y, AGG_DEV * SLOTS
    by_plane = pl.BlockSpec((size_y, pairs, NODES, LANES), lambda i: (i, 0, 0, 0))
    total = pltpu.VMEM((rows + 1, HALF, LANES), jnp.float32)
    return pl.pallas_call(
        interior_kernel,
        grid=(size_x,),
        in_specs=[
            pl.BlockSpec(memory_space=pltpu.SMEM),
            pl.BlockSpec((size_y, depth, block), lambda i: (i, 0, 0)),
            pl.BlockSpec((1, size_y, depth, block), lambda i: (0, jnp.maximum(i - 1, 0), 0, 0)),
            pl.BlockSpec((1, size_y, depth, block), lambda i: (1, i, 0, 0)),
            pl.BlockSpec((1, size_y, depth, block), lambda i: (2, i, 0, 0)),
            by_plane,
            pl.BlockSpec((columns, pairs, NODES, LANES), lambda i: (0, 0, 0, 0)),
            by_plane,
        ],
        out_specs=pl.BlockSpec((rows, HALF, LANES), lambda i: (0, 0, 0)),
        out_shape=jax.ShapeDtypeStruct((rows, HALF, LANES), jnp.float32),
        scratch_shapes=[pltpu.VMEM((4, depth * HALF, LANES), jnp.float32), total, total, total, total],
        compiler_params=pltpu.CompilerParams(vmem_limit_bytes=VMEM_LIMIT),
        cost_estimate=pl.CostEstimate(flops=columns * depth * 14 * NODES**3, bytes_accessed=columns * depth * 6 * block * 2, transcendentals=0),
        name="interior",
    )(keys, diag, faces, faces, faces, natural, stacked, shifted)


def border_kernel(capacity, keys, owners, head_x, head_y, head_z, rim_x, rim_y, rim_z, tail_x, tail_y, tail_z,
                  natural, stacked, first_z, last_z, total_ref, out_ref, ahead_total, back_total, stage, filled):
    size_y, depth = tail_x.shape[0], tail_x.shape[1]
    size_x = tail_y.shape[0]
    pairs = depth // 2
    rows = total_ref.shape[0] // SLOTS
    places = out_ref.shape[0]

    ahead_total[...] = total_ref[...]
    back_total[...] = jnp.zeros_like(back_total)

    def ahead(left0, left1, head, prolong):
        product = jnp.dot(jnp.concatenate([left0, left1], axis=1), paired_weights(head), preferred_element_type=jnp.float32)
        return folded(across(prolong, upright(product)))

    def over_x(j, carry):
        for p in range(pairs):
            sums = ahead(tail_x[j, 2 * p], tail_x[j, 2 * p + 1], head_x[j, p], stacked[(size_x - 1) * size_y + j, p])
            back = folded(across(natural[j, p], rim_x[j, p]))
            for side in (0, 1):
                add_to(ahead_total, keys[2, size_x - 1, j, 2 * p + side], sums[side])
                add_to(back_total, keys[1, 0, j, 2 * p + side], back[side])
        return carry

    def over_y(i, carry):
        for p in range(pairs):
            sums = ahead(tail_y[i, 2 * p], tail_y[i, 2 * p + 1], head_y[i, p], stacked[i * size_y + size_y - 1, p])
            back = folded(across(natural[i * size_y, p], rim_y[i, p]))
            for side in (0, 1):
                add_to(ahead_total, keys[4, i, size_y - 1, 2 * p + side], sums[side])
                add_to(back_total, keys[3, i, 0, 2 * p + side], back[side])
        return carry

    def over_z(i, carry):
        for u in range(size_y // 2):
            t = i * (size_y // 2) + u
            sums = ahead(tail_z[2 * t], tail_z[2 * t + 1], head_z[t], last_z[t])
            back = folded(across(first_z[t], rim_z[t]))
            for side in (0, 1):
                add_to(ahead_total, keys[6, i, 2 * u + side, depth - 1], sums[side])
                add_to(back_total, keys[5, i, 2 * u + side, 0], back[side])
        return carry

    lax.fori_loop(0, size_y, over_x, 0)
    lax.fori_loop(0, size_x, over_y, 0)
    lax.fori_loop(0, size_x, over_z, 0)

    for owner in range(places // capacity):
        filled[owner] = 0
    if places != rows:
        out_ref[...] = jnp.zeros_like(out_ref)

    def emit(r, carry):
        low = low_lanes(HALF // 2)
        owner = owners[r]
        place = owner * capacity + filled[owner]
        filled[owner] = filled[owner] + 1
        for s in range(SLOTS):
            key = r * SLOTS + s
            ahead_total[key] = ahead_total[key] + back_total[key]
            even = ahead_total[key, pl.ds(0, HALF // 2, stride=2), :]
            odd = ahead_total[key, pl.ds(1, HALF // 2, stride=2), :]
            top = jnp.where(low, even, swapped(odd))
            bottom = jnp.where(low, swapped(even), odd)
            stage[pl.ds(s, HALF, stride=8), :] = jnp.concatenate([top, bottom], axis=0)
        for k in range(HALF):
            out_ref[place, :, LANES * k : LANES * (k + 1)] = stage[8 * k : 8 * k + SLOTS, :].astype(jnp.bfloat16)
        return carry

    lax.fori_loop(0, rows, emit, 0)


def border(keys, owners, operands, capacity, places, block):
    rows = AGG_DEV * SLOTS
    smem = pl.BlockSpec(memory_space=pltpu.SMEM)
    total = pltpu.VMEM((rows, HALF, LANES), jnp.float32)
    return pl.pallas_call(
        functools.partial(border_kernel, capacity),
        in_specs=[smem, smem] + [pl.BlockSpec(memory_space=pltpu.VMEM)] * len(operands),
        out_specs=pl.BlockSpec(memory_space=pltpu.VMEM),
        out_shape=jax.ShapeDtypeStruct((places, SLOTS, block), jnp.bfloat16),
        scratch_shapes=[total, total, pltpu.VMEM((8 * HALF, LANES), jnp.float32), pltpu.SMEM((places // capacity,), jnp.int32)],
        compiler_params=pltpu.CompilerParams(vmem_limit_bytes=VMEM_LIMIT),
        name="border",
    )(keys, owners, *operands)


def shards(a_diag, a_face, prolong, aggregate, pair_slot, row_owner):
    size_x, size_y, size_z, block = a_diag.shape
    sizes = (size_x, size_y, size_z)
    columns = size_x * size_y
    depth = lax.axis_size("gz")
    capacity = max(2, (AGG_DEV + depth - 1) // depth)
    holding = capacity * depth
    diag = a_diag.reshape(columns, size_z, block)
    faces = a_face.reshape(3, columns, size_z, block)
    keys = aggregate[None] * SLOTS + pair_slot

    (natural, stacked, shifted, head_x, head_y, head_z, rim_x, rim_y, rim_z, tail_x, tail_y, tail_z, last_z) = prepare(
        prolong.reshape(columns, size_z, block), faces, sizes)
    over_x = passed_along(head_x, "gx", -1)
    over_y = passed_along(head_y, "gy", -1)
    over_z = passed_along(head_z, "gz", -1)
    back_y = passed_along(rim_y, "gy", 1)
    back_z = passed_along(rim_z, "gz", 1)
    back_x = passed_along(rim_x, "gx", 1)
    inner = interior(keys, diag, faces, natural, stacked, shifted, sizes)
    outgoing = border(
        keys, row_owner,
        (over_x, over_y, over_z, back_x, back_y, back_z, tail_x, tail_y, tail_z, natural, stacked, head_z, last_z, inner),
        capacity, holding, block)
    result = lax.all_to_all(outgoing, "gz", 0, 0, tiled=True)
    if holding != AGG_DEV:
        owner_ids = jnp.arange(depth, dtype=jnp.int32)
        counts = jnp.sum((row_owner[:, None] == owner_ids[None, :]).astype(jnp.int32), axis=0)
        arrived_counts = lax.all_to_all(counts, "gz", 0, 0, tiled=True)
        slots = jnp.arange(holding, dtype=jnp.int32)
        arrived = (slots % capacity < jnp.repeat(arrived_counts, capacity)).astype(jnp.int32)
        target = jnp.cumsum(arrived) - 1
        match = ((arrived[None, :] > 0) & (target[None, :] == slots[:, None])).astype(jnp.int32)
        result, _ = pick_rows(match, result)
    return result.reshape(1, 1, 1, holding, SLOTS, block)


def solution(mesh):
    return jax.shard_map(
        shards,
        mesh=mesh,
        in_specs=(
            P("gx", "gy", "gz", None),
            P(None, "gx", "gy", "gz", None),
            P("gx", "gy", "gz", None),
            P("gx", "gy", "gz"),
            P(None, "gx", "gy", "gz"),
            P(("gx", "gy", "gz")),
        ),
        out_specs=P("gx", "gy", "gz", None, None, None),
        check_vma=False,
    )
```

```python
import functools

import jax
import jax.numpy as jnp
from jax import lax
from jax.experimental import pallas as pl
from jax.experimental.pallas import tpu as pltpu
from jax.sharding import PartitionSpec as P

NODES = 64
SLOTS = 7
AGG_DEV = 24
LANES = 128
HALF = NODES // 2
VMEM_LIMIT = 48 * 1024 * 1024
UNROLL = 2


def passed_along(block, axis, distance):
    devices = range(lax.axis_size(axis))
    route = [(i - distance, i) for i in devices if i - distance in devices]
    return lax.ppermute(block, axis, route)


def low_lanes(rows):
    return lax.broadcasted_iota(jnp.int32, (rows, LANES), 1) < NODES


def swapped(value):
    return pltpu.roll(value, NODES, 1)


def spread(column, stage):
    depth = column.shape[0]
    for k in range(column.shape[1] // LANES):
        stage[depth * k : depth * (k + 1), :] = column[:, LANES * k : LANES * (k + 1)].astype(jnp.float32)


def block_of(stage, z, depth):
    return stage[pl.ds(z, HALF, stride=depth), :]


def stacked_pair(first, second):
    low = low_lanes(HALF)
    even = jnp.where(low, first, swapped(second))
    odd = jnp.where(low, swapped(first), second)
    return jnp.concatenate([even, odd], axis=0).astype(jnp.bfloat16)


def in_order(pair):
    row = lax.broadcasted_iota(jnp.int32, (NODES, NODES), 0)
    col = lax.broadcasted_iota(jnp.int32, (NODES, NODES), 1)
    move = (row == 2 * (col % HALF) + col // HALF).astype(jnp.bfloat16)
    return jnp.dot(move, pair, preferred_element_type=jnp.float32).astype(jnp.bfloat16)


def paired_weights(pair):
    low = low_lanes(NODES)
    zero = jnp.zeros_like(pair)
    first = jnp.where(low, pair, zero)
    second = jnp.where(low, zero, pair)
    left = jnp.concatenate([first, zero, second, zero], axis=0)
    right = jnp.concatenate([zero, first, zero, second], axis=0)
    return jnp.concatenate([left, right], axis=1)


def upright(product):
    return jnp.concatenate([product[:, :LANES], product[:, LANES:]], axis=0).astype(jnp.bfloat16)


def across(left, right):
    return lax.dot_general(left, right, (((0,), (0,)), ((), ())), preferred_element_type=jnp.float32)


def folded(square):
    low = low_lanes(HALF)
    moved = swapped(jnp.where(low, square[HALF : 2 * HALF], square[2 * HALF : 3 * HALF]))
    return (jnp.where(low, square[:HALF], moved), jnp.where(low, moved, square[3 * HALF :]))


def add_to(total, key, value):
    total[key] = total[key] + value


def diagonal(square):
    return jnp.where(low_lanes(NODES), square[:NODES], square[NODES:]).astype(jnp.bfloat16)


def prepare_kernel(place_ref, p_ref, fx_ref, fy_ref, fz_ref, natural_ref, stacked_ref, shifted_ref, swap_x_ref, swap_y_ref, head_z_ref, rim_z_ref, last_z_ref,
                   tail_x_ref, tail_y_ref, tail_z_ref, stages, stages_f, ends):
    plane = pl.program_id(0)
    size_y, depth = p_ref.shape[0], p_ref.shape[1]
    pairs = depth // 2

    for j in range(size_y):
        stage = stages.at[j]
        spread(p_ref[j], stage)
        block = [block_of(stage, z, depth) for z in range(depth)]
        for p in range(pairs):
            stacked = stacked_pair(block[2 * p], block[2 * p + 1])
            stacked_ref[j, p] = stacked
            shifted_ref[j, p] = stacked_pair(block[(2 * p - 1) % depth], block[2 * p])
            natural_ref[j, p] = in_order(stacked)
        ends[0, j] = block[0]
        ends[1, j] = block[depth - 1]
        stage_f = stages_f.at[j]
        spread(fz_ref[0, j], stage_f)
        last = block_of(stage_f, depth - 1, depth)
        ends[2, j] = last
        tail_z_ref[j] = last.astype(jnp.bfloat16)

    for t in range(size_y // 2):
        first, last, face = [stacked_pair(ends[kind, 2 * t], ends[kind, 2 * t + 1]) for kind in range(3)]
        head_z_ref[t] = in_order(first)
        last_z_ref[t] = last
        rim_z_ref[t] = diagonal(across(face, last))

    def faces(source, stage, j, tails, rims):
        spread(source, stage)
        block = [block_of(stage, z, depth) for z in range(depth)]
        for z in range(depth):
            tails[z] = block[z].astype(jnp.bfloat16)
        for p in range(pairs):
            rims[p] = diagonal(across(stacked_pair(block[2 * p], block[2 * p + 1]), stacked_ref[j, p]))

    @pl.when(place_ref[1] == 0)
    def _():
        faces(fy_ref[0, 0], stages_f.at[0], size_y - 1, tail_y_ref.at[0], swap_y_ref.at[0])

    @pl.when(place_ref[1] != 0)
    def _():
        swap_y_ref[0] = natural_ref[0]

    @pl.when((place_ref[0] == 0) & (plane == pl.num_programs(0) - 1))
    def _():
        for j in range(size_y):
            faces(fx_ref[0, j], stages_f.at[j], j, tail_x_ref.at[j], swap_x_ref.at[j])

    @pl.when((place_ref[0] != 0) & (plane == 0))
    def _():
        swap_x_ref[...] = natural_ref[...]


def prepare(place, prolong, faces, sizes):
    size_x, size_y, depth = sizes
    pairs, block = depth // 2, prolong.shape[-1]
    columns, half = size_x * size_y, size_y // 2
    shape = lambda *dims: jax.ShapeDtypeStruct(dims, jnp.bfloat16)
    by_half = pl.BlockSpec((half, NODES, LANES), lambda i: (i, 0, 0))
    stage = pltpu.VMEM((size_y, depth * HALF, LANES), jnp.float32)
    return pl.pallas_call(
        prepare_kernel,
        grid=(size_x,),
        in_specs=[
            pl.BlockSpec(memory_space=pltpu.SMEM),
            pl.BlockSpec((size_y, depth, block), lambda i: (i, 0, 0)),
            pl.BlockSpec((1, size_y, depth, block), lambda i: (0, size_x - 1, 0, 0)),
            pl.BlockSpec((1, 1, depth, block), lambda i: (1, i * size_y + size_y - 1, 0, 0)),
            pl.BlockSpec((1, size_y, depth, block), lambda i: (2, i, 0, 0)),
        ],
        out_specs=[
            pl.BlockSpec((size_y, pairs, NODES, LANES), lambda i: (i, 0, 0, 0)),
            pl.BlockSpec((size_y, pairs, NODES, LANES), lambda i: (i, 0, 0, 0)),
            pl.BlockSpec((size_y, pairs, NODES, LANES), lambda i: (i, 0, 0, 0)),
            pl.BlockSpec((size_y, pairs, NODES, LANES), lambda i: (0, 0, 0, 0)),
            pl.BlockSpec((1, pairs, NODES, LANES), lambda i: (i, 0, 0, 0)),
            by_half, by_half, by_half,
            pl.BlockSpec((size_y, depth, HALF, LANES), lambda i: (0, 0, 0, 0)),
            pl.BlockSpec((1, depth, HALF, LANES), lambda i: (i, 0, 0, 0)),
            pl.BlockSpec((size_y, HALF, LANES), lambda i: (i, 0, 0)),
        ],
        out_shape=[
            shape(columns, pairs, NODES, LANES), shape(columns, pairs, NODES, LANES), shape(columns, pairs, NODES, LANES),
            shape(size_y, pairs, NODES, LANES), shape(size_x, pairs, NODES, LANES),
            shape(columns // 2, NODES, LANES), shape(columns // 2, NODES, LANES), shape(columns // 2, NODES, LANES),
            shape(size_y, depth, HALF, LANES), shape(size_x, depth, HALF, LANES), shape(columns, HALF, LANES),
        ],
        scratch_shapes=[
            stage, stage,
            pltpu.VMEM((3, size_y, HALF, LANES), jnp.float32),
        ],
        compiler_params=pltpu.CompilerParams(vmem_limit_bytes=VMEM_LIMIT),
        name="prepare",
    )(place, prolong, faces, faces, faces)


def interior_kernel(keys, diag_ref, fx_ref, fy_ref, fz_ref, natural_ref, stacked_ref, below_ref, shifted_ref, ahead_ref, behind_ref,
                    stages, ahead_even, ahead_odd, behind_even, behind_odd):
    plane = pl.program_id(0)
    size_y, depth = diag_ref.shape[0], diag_ref.shape[1]
    pairs = depth // 2
    spare = ahead_ref.shape[0]
    ahead, behind = (ahead_even, ahead_odd), (behind_even, behind_odd)

    @pl.when(plane == 0)
    def _():
        for total in ahead + behind:
            total[...] = jnp.zeros_like(total)

    def column(j, stage):
        row_y = jnp.maximum(j - 1, 0)
        row_x = jnp.maximum(plane - 1, 0)
        has_x, has_y = plane > 0, j > 0
        for face, source in zip(range(4), (diag_ref[j], fx_ref[0, j], fy_ref[0, row_y], fz_ref[0, j])):
            spread(source, stage.at[face])
        for p in range(pairs):
            left = []
            for face in range(4):
                shift = 1 if face == 3 else 0
                sides = [block_of(stage.at[face], (2 * p + side - shift) % depth, depth).astype(jnp.bfloat16) for side in (0, 1)]
                left.append(jnp.concatenate(sides, axis=1))
            product = jnp.dot(
                jnp.concatenate(left, axis=0), paired_weights(natural_ref[j, p]), preferred_element_type=jnp.float32)
            stacked = (stacked_ref[j, p], below_ref[j, p], stacked_ref[row_y, p], shifted_ref[j, p])
            for face in range(4):
                couple = upright(product[HALF * face : HALF * (face + 1)])
                sums = folded(across(stacked[face], couple))
                for side in (0, 1):
                    z = 2 * p + side
                    if face == 0:
                        add_to(ahead[side], keys[0, plane, j, z], sums[side])
                        continue
                    if face == 1:
                        here, there = keys[2, row_x, j, z], keys[1, plane, j, z]
                        here, there = jnp.where(has_x, here, spare), jnp.where(has_x, there, spare)
                    elif face == 2:
                        here, there = keys[4, plane, row_y, z], keys[3, plane, j, z]
                        here, there = jnp.where(has_y, here, spare), jnp.where(has_y, there, spare)
                    elif z > 0:
                        here, there = keys[6, plane, j, z - 1], keys[5, plane, j, z]
                    else:
                        continue
                    add_to(ahead[side], here, sums[side])
                    add_to(behind[side], there, sums[side])

    def columns(step, carry):
        for u in range(UNROLL):
            column(step * UNROLL + u, stages.at[u])
        return carry

    lax.fori_loop(0, size_y // UNROLL, columns, 0)

    @pl.when(plane == pl.num_programs(0) - 1)
    def _():
        def gather(r, carry):
            for s in range(SLOTS):
                key = r * SLOTS + s
                ahead_ref[key] = ahead_even[key] + ahead_odd[key]
                behind_ref[key] = behind_even[key] + behind_odd[key]
            return carry

        lax.fori_loop(0, spare // SLOTS, gather, 0)


def interior(keys, diag, faces, natural, stacked, shifted, sizes):
    size_x, size_y, depth = sizes
    pairs, block = depth // 2, diag.shape[-1]
    columns, rows = size_x * size_y, AGG_DEV * SLOTS
    total = pltpu.VMEM((rows + 1, HALF, LANES), jnp.float32)
    sums = jax.ShapeDtypeStruct((rows, HALF, LANES), jnp.float32)
    all_rows = pl.BlockSpec((rows, HALF, LANES), lambda i: (0, 0, 0))
    return pl.pallas_call(
        interior_kernel,
        grid=(size_x,),
        in_specs=[
            pl.BlockSpec(memory_space=pltpu.SMEM),
            pl.BlockSpec((size_y, depth, block), lambda i: (i, 0, 0)),
            pl.BlockSpec((1, size_y, depth, block), lambda i: (0, jnp.maximum(i - 1, 0), 0, 0)),
            pl.BlockSpec((1, size_y, depth, block), lambda i: (1, i, 0, 0)),
            pl.BlockSpec((1, size_y, depth, block), lambda i: (2, i, 0, 0)),
            pl.BlockSpec((size_y, pairs, NODES, LANES), lambda i: (i, 0, 0, 0)),
            pl.BlockSpec((size_y, pairs, NODES, LANES), lambda i: (i, 0, 0, 0)),
            pl.BlockSpec((size_y, pairs, NODES, LANES), lambda i: (jnp.maximum(i - 1, 0), 0, 0, 0)),
            pl.BlockSpec((size_y, pairs, NODES, LANES), lambda i: (i, 0, 0, 0)),
        ],
        out_specs=[all_rows, all_rows],
        out_shape=[sums, sums],
        scratch_shapes=[pltpu.VMEM((UNROLL, 4, depth * HALF, LANES), jnp.float32), total, total, total, total],
        compiler_params=pltpu.CompilerParams(vmem_limit_bytes=VMEM_LIMIT),
        cost_estimate=pl.CostEstimate(flops=columns * depth * 14 * NODES**3, bytes_accessed=columns * depth * 6 * block * 2, transcendentals=0),
        name="interior",
    )(keys, diag, faces, faces, faces, natural, stacked, stacked, shifted)


def border_kernel(capacity, keys, owners, place_ref, got_x, got_y, got_z, back_z, tail_x, tail_y, tail_z,
                  natural, stacked, first_z, last_z, ahead_ref, behind_ref, out_ref, extra_ahead, extra_back, wide, filled):
    size_y, depth = tail_x.shape[0], tail_x.shape[1]
    size_x = tail_y.shape[0]
    pairs = depth // 2
    rows = ahead_ref.shape[0] // SLOTS
    places = out_ref.shape[0]
    low = low_lanes(HALF)

    extra_ahead[...] = jnp.zeros_like(extra_ahead)
    extra_back[...] = jnp.zeros_like(extra_back)

    def ahead(left0, left1, head, prolong):
        product = jnp.dot(jnp.concatenate([left0, left1], axis=1), paired_weights(head), preferred_element_type=jnp.float32)
        return folded(across(prolong, upright(product)))

    def back(prolong, rim):
        return folded(across(prolong, rim))

    @pl.when(place_ref[0] == 0)
    def _():
        def over(j, carry):
            for p in range(pairs):
                sums = ahead(tail_x[j, 2 * p], tail_x[j, 2 * p + 1], got_x[j, p],
                             stacked[(size_x - 1) * size_y + j, p])
                for side in (0, 1):
                    add_to(extra_ahead, keys[2, size_x - 1, j, 2 * p + side], sums[side])
            return carry

        lax.fori_loop(0, size_y, over, 0)

    @pl.when(place_ref[0] != 0)
    def _():
        def over(j, carry):
            for p in range(pairs):
                sums = back(natural[j, p], got_x[j, p])
                for side in (0, 1):
                    add_to(extra_back, keys[1, 0, j, 2 * p + side], sums[side])
            return carry

        lax.fori_loop(0, size_y, over, 0)

    @pl.when(place_ref[1] == 0)
    def _():
        def over(i, carry):
            for p in range(pairs):
                sums = ahead(tail_y[i, 2 * p], tail_y[i, 2 * p + 1], got_y[i, p],
                             stacked[i * size_y + size_y - 1, p])
                for side in (0, 1):
                    add_to(extra_ahead, keys[4, i, size_y - 1, 2 * p + side], sums[side])
            return carry

        lax.fori_loop(0, size_x, over, 0)

    @pl.when(place_ref[1] != 0)
    def _():
        def over(i, carry):
            for p in range(pairs):
                sums = back(natural[i * size_y, p], got_y[i, p])
                for side in (0, 1):
                    add_to(extra_back, keys[3, i, 0, 2 * p + side], sums[side])
            return carry

        lax.fori_loop(0, size_x, over, 0)

    def over_z(i, carry):
        for u in range(size_y // 2):
            t = i * (size_y // 2) + u
            sums = ahead(tail_z[2 * t], tail_z[2 * t + 1], got_z[t], last_z[t])
            past = back(first_z[t], back_z[t])
            for side in (0, 1):
                add_to(extra_ahead, keys[6, i, 2 * u + side, depth - 1], sums[side])
                add_to(extra_back, keys[5, i, 2 * u + side, 0], past[side])
        return carry

    lax.fori_loop(0, size_x, over_z, 0)

    for owner in range(places // capacity):
        filled[owner] = 0
    if places != rows:
        out_ref[...] = jnp.zeros_like(out_ref)

    def emit(pair, carry):
        spots = []
        for side in (0, 1):
            owner = owners[2 * pair + side]
            spots.append(owner * capacity + filled[owner])
            filled[owner] = filled[owner] + 1
        for s in range(SLOTS):
            key = [(2 * pair + side) * SLOTS + s for side in (0, 1)]
            one, two = behind_ref[key[0]], behind_ref[key[1]]
            upper = jnp.where(low, one, swapped(two))
            lower = jnp.where(low, swapped(one), two)
            wide[s, :, :NODES] = jnp.concatenate([upper, lower], axis=0).T
            for side in (0, 1):
                extra_ahead[key[side]] = ahead_ref[key[side]] + (extra_ahead[key[side]] + extra_back[key[side]])
                even = extra_ahead[key[side], pl.ds(0, HALF // 2, stride=2), :]
                odd = extra_ahead[key[side], pl.ds(1, HALF // 2, stride=2), :]
                narrow = low[: HALF // 2]
                straight = jnp.concatenate(
                    [jnp.where(narrow, even, swapped(odd)), jnp.where(narrow, swapped(even), odd)], axis=0)
                even = wide[s, pl.ds(NODES * side, HALF, stride=2), :]
                odd = wide[s, pl.ds(NODES * side + 1, HALF, stride=2), :]
                total = straight + jnp.where(low, even, swapped(odd))
                out_ref[spots[side], HALF * s : HALF * (s + 1), :] = total.astype(jnp.bfloat16)
        return carry

    lax.fori_loop(0, rows // 2, emit, 0)


def border(keys, owners, place, operands, capacity, places):
    rows = AGG_DEV * SLOTS
    smem = pl.BlockSpec(memory_space=pltpu.SMEM)
    total = pltpu.VMEM((rows, HALF, LANES), jnp.float32)
    return pl.pallas_call(
        functools.partial(border_kernel, capacity),
        in_specs=[smem, smem, smem] + [pl.BlockSpec(memory_space=pltpu.VMEM)] * len(operands),
        out_specs=pl.BlockSpec(memory_space=pltpu.VMEM),
        out_shape=jax.ShapeDtypeStruct((places, SLOTS * HALF, LANES), jnp.bfloat16),
        scratch_shapes=[total, total, pltpu.VMEM((SLOTS, LANES, LANES), jnp.float32), pltpu.SMEM((places // capacity,), jnp.int32)],
        compiler_params=pltpu.CompilerParams(vmem_limit_bytes=VMEM_LIMIT),
        name="border",
    )(keys, owners, place, *operands)


def layout_kernel(source, rows_ref, out_ref, stage):
    group = pl.program_id(0)
    height = out_ref.shape[1]
    for s in range(SLOTS):
        for r in range(height):
            row = source[group * height + r]
            block = rows_ref[jnp.maximum(row, 0), HALF * s : HALF * (s + 1), :].astype(jnp.float32)
            stage[s, pl.ds(r, HALF, stride=height), :] = jnp.where(row >= 0, block, jnp.zeros_like(block))
        for k in range(HALF):
            out_ref[s, :, LANES * k : LANES * (k + 1)] = stage[s, height * k : height * (k + 1), :].astype(jnp.bfloat16)


def laid_out(source, rows, block):
    places, height = rows.shape[0], 8
    return pl.pallas_call(
        layout_kernel,
        grid=(places // height,),
        in_specs=[pl.BlockSpec(memory_space=pltpu.SMEM), pl.BlockSpec(rows.shape, lambda g: (0, 0, 0))],
        out_specs=pl.BlockSpec((SLOTS, height, block), lambda g: (0, g, 0)),
        out_shape=jax.ShapeDtypeStruct((SLOTS, places, block), jnp.bfloat16),
        scratch_shapes=[pltpu.VMEM((SLOTS, height * HALF, LANES), jnp.float32)],
        compiler_params=pltpu.CompilerParams(vmem_limit_bytes=VMEM_LIMIT),
        name="layout",
    )(source, rows)


def swap(block, axis):
    assert lax.axis_size(axis) == 2
    return lax.ppermute(block, axis, [(0, 1), (1, 0)])


def shards(a_diag, a_face, prolong, aggregate, pair_slot, row_owner):
    size_x, size_y, size_z, block = a_diag.shape
    sizes = (size_x, size_y, size_z)
    columns = size_x * size_y
    depth = lax.axis_size("gz")
    capacity = max(2, (AGG_DEV + depth - 1) // depth)
    holding = capacity * depth
    diag = a_diag.reshape(columns, size_z, block)
    faces = a_face.reshape(3, columns, size_z, block)
    keys = aggregate[None] * SLOTS + pair_slot
    place = jnp.stack([lax.axis_index("gx"), lax.axis_index("gy")]).astype(jnp.int32)

    natural, stacked, shifted, swap_x, swap_y, head_z, rim_z, last_z, tail_x, tail_y, tail_z = prepare(
        place, prolong.reshape(columns, size_z, block), faces, sizes)
    got_z = passed_along(head_z, "gz", -1)
    back_z = passed_along(rim_z, "gz", 1)
    got_y = swap(swap_y, "gy")
    got_x = swap(swap_x, "gx")
    ahead, behind = interior(keys, diag, faces, natural, stacked, shifted, sizes)
    outgoing = border(
        keys, row_owner, place,
        (got_x, got_y, got_z, back_z, tail_x, tail_y, tail_z, natural, stacked, head_z, last_z, ahead, behind), capacity, holding)
    arrived = lax.all_to_all(outgoing, "gz", 0, 0, tiled=True)
    source = jnp.arange(holding, dtype=jnp.int32)
    if holding != AGG_DEV:
        owner_ids = jnp.arange(depth, dtype=jnp.int32)
        counts = jnp.sum((row_owner[:, None] == owner_ids[None, :]).astype(jnp.int32), axis=0)
        arrived_counts = lax.all_to_all(counts, "gz", 0, 0, tiled=True)
        present = source % capacity < jnp.repeat(arrived_counts, capacity)
        target = jnp.cumsum(present.astype(jnp.int32)) - 1
        match = (present[None, :] & (target[None, :] == source[:, None])).astype(jnp.int32)
        source = jnp.sum(match * (source[None, :] + 1), axis=1) - 1
    result = laid_out(source, arrived, block)
    return jnp.transpose(result, (1, 0, 2)).reshape(1, 1, 1, holding, SLOTS, block)


def solution(mesh):
    return jax.shard_map(
        shards,
        mesh=mesh,
        in_specs=(
            P("gx", "gy", "gz", None),
            P(None, "gx", "gy", "gz", None),
            P("gx", "gy", "gz", None),
            P("gx", "gy", "gz"),
            P(None, "gx", "gy", "gz"),
            P(("gx", "gy", "gz")),
        ),
        out_specs=P("gx", "gy", "gz", None, None, None),
        check_vma=False,
    )
```

```python
import functools

import jax
import jax.numpy as jnp
from jax import lax
from jax.experimental import pallas as pl
from jax.experimental.pallas import tpu as pltpu
from jax.sharding import PartitionSpec as P

NODES = 64
SLOTS = 7
AGG_DEV = 24
LANES = 128
HALF = NODES // 2
VMEM_LIMIT = 48 * 1024 * 1024
STEP = 8


def passed_along(block, axis, distance):
    devices = range(lax.axis_size(axis))
    route = [(i - distance, i) for i in devices if i - distance in devices]
    return lax.ppermute(block, axis, route)


def low_lanes(rows):
    return lax.broadcasted_iota(jnp.int32, (rows, LANES), 1) < NODES


def swapped(value):
    return pltpu.roll(value, NODES, 1)


def spread(column, stage):
    depth = column.shape[0]
    for k in range(column.shape[1] // LANES):
        stage[depth * k : depth * (k + 1), :] = column[:, LANES * k : LANES * (k + 1)].astype(jnp.float32)


def block_of(stage, z, depth):
    return stage[pl.ds(z, HALF, stride=depth), :]


def stacked_pair(first, second):
    low = low_lanes(HALF)
    even = jnp.where(low, first, swapped(second))
    odd = jnp.where(low, swapped(first), second)
    return jnp.concatenate([even, odd], axis=0).astype(jnp.bfloat16)


def in_order(pair):
    row = lax.broadcasted_iota(jnp.int32, (NODES, NODES), 0)
    col = lax.broadcasted_iota(jnp.int32, (NODES, NODES), 1)
    move = (row == 2 * (col % HALF) + col // HALF).astype(jnp.bfloat16)
    return jnp.dot(move, pair, preferred_element_type=jnp.float32).astype(jnp.bfloat16)


def paired_weights(pair):
    low = low_lanes(NODES)
    zero = jnp.zeros_like(pair)
    first = jnp.where(low, pair, zero)
    second = jnp.where(low, zero, pair)
    left = jnp.concatenate([first, zero, second, zero], axis=0)
    right = jnp.concatenate([zero, first, zero, second], axis=0)
    return jnp.concatenate([left, right], axis=1)


def upright(product):
    return jnp.concatenate([product[:, :LANES], product[:, LANES:]], axis=0).astype(jnp.bfloat16)


def across(left, right):
    return lax.dot_general(left, right, (((0,), (0,)), ((), ())), preferred_element_type=jnp.float32)


def folded(square):
    low = low_lanes(HALF)
    moved = swapped(jnp.where(low, square[HALF : 2 * HALF], square[2 * HALF : 3 * HALF]))
    return (jnp.where(low, square[:HALF], moved), jnp.where(low, moved, square[3 * HALF :]))


def diagonal(square):
    return jnp.where(low_lanes(NODES), square[:NODES], square[NODES:]).astype(jnp.bfloat16)


def turned_pairs(first, second):
    row = lax.broadcasted_iota(jnp.int32, (LANES, LANES), 0)
    col = lax.broadcasted_iota(jnp.int32, (LANES, LANES), 1)
    return across(jnp.concatenate([first, second], axis=0), (row == col).astype(jnp.bfloat16)).astype(jnp.bfloat16)


def two_pairs(turned, first, second):
    zero = jnp.zeros_like(first)
    couples = jnp.concatenate([jnp.concatenate([first, zero], axis=1), jnp.concatenate([zero, second], axis=1)], axis=0)
    product = jnp.dot(turned, couples, preferred_element_type=jnp.float32)
    return folded(product[:, :LANES]) + folded(product[:, LANES:])


def put(stage, z, term):
    stage[pl.ds(z, HALF, stride=STEP), :] = term


def chosen(keys, rows):
    return (lax.broadcasted_iota(jnp.int32, (rows, keys.shape[1]), 0) == keys).astype(jnp.float32).astype(jnp.bfloat16)


def straightened(first, second):
    low = low_lanes(first.shape[0])
    return jnp.where(low, first, swapped(second)), jnp.where(low, swapped(first), second)


def prepare_kernel(place_ref, p_ref, fx_ref, fy_ref, fz_ref, natural_ref, turned_ref, shifted_ref, swap_x_ref, swap_y_ref, head_z_ref, rim_z_ref,
                   last_z_ref, tail_x_ref, tail_y_ref, tail_z_ref, stages, stages_f, stacks, ends):
    plane = pl.program_id(0)
    size_y, depth = p_ref.shape[0], p_ref.shape[1]
    pairs = depth // 2

    for j in range(size_y):
        stage = stages.at[j]
        spread(p_ref[j], stage)
        block = [block_of(stage, z, depth) for z in range(depth)]
        stacked = [stacked_pair(block[2 * p], block[2 * p + 1]) for p in range(pairs)]
        moved = [stacked_pair(block[(2 * p - 1) % depth], block[2 * p]) for p in range(pairs)]
        for p in range(pairs):
            stacks[j, p] = stacked[p]
            natural_ref[j, p] = in_order(stacked[p])
        for h in range(pairs // 2):
            turned_ref[j, h] = turned_pairs(stacked[2 * h], stacked[2 * h + 1])
            shifted_ref[j, h] = turned_pairs(moved[2 * h], moved[2 * h + 1])
        ends[0, j] = block[0]
        ends[1, j] = block[depth - 1]
        stage_f = stages_f.at[j]
        spread(fz_ref[0, j], stage_f)
        last = block_of(stage_f, depth - 1, depth)
        ends[2, j] = last
        tail_z_ref[j] = last.astype(jnp.bfloat16)

    for t in range(size_y // 2):
        first, last, face = [stacked_pair(ends[kind, 2 * t], ends[kind, 2 * t + 1]) for kind in range(3)]
        head_z_ref[t] = in_order(first)
        last_z_ref[t] = last
        rim_z_ref[t] = diagonal(across(face, last))

    def faces(source, stage, j, tails, rims):
        spread(source, stage)
        block = [block_of(stage, z, depth) for z in range(depth)]
        for z in range(depth):
            tails[z] = block[z].astype(jnp.bfloat16)
        for p in range(pairs):
            rims[p] = diagonal(across(stacked_pair(block[2 * p], block[2 * p + 1]), stacks[j, p]))

    @pl.when(place_ref[1] == 0)
    def _():
        faces(fy_ref[0, 0], stages_f.at[0], size_y - 1, tail_y_ref.at[0], swap_y_ref.at[0])

    @pl.when(place_ref[1] != 0)
    def _():
        swap_y_ref[0] = natural_ref[0]

    @pl.when((place_ref[0] == 0) & (plane == pl.num_programs(0) - 1))
    def _():
        for j in range(size_y):
            faces(fx_ref[0, j], stages_f.at[j], j, tail_x_ref.at[j], swap_x_ref.at[j])

    @pl.when((place_ref[0] != 0) & (plane == 0))
    def _():
        swap_x_ref[...] = natural_ref[...]


def prepare(place, prolong, faces, sizes):
    size_x, size_y, depth = sizes
    pairs, block = depth // 2, prolong.shape[-1]
    columns, half = size_x * size_y, size_y // 2
    shape = lambda *dims: jax.ShapeDtypeStruct(dims, jnp.bfloat16)
    by_half = pl.BlockSpec((half, NODES, LANES), lambda i: (i, 0, 0))
    by_plane = pl.BlockSpec((size_y, pairs // 2, LANES, LANES), lambda i: (i, 0, 0, 0))
    stage = pltpu.VMEM((size_y, depth * HALF, LANES), jnp.float32)
    return pl.pallas_call(
        prepare_kernel,
        grid=(size_x,),
        in_specs=[
            pl.BlockSpec(memory_space=pltpu.SMEM),
            pl.BlockSpec((size_y, depth, block), lambda i: (i, 0, 0)),
            pl.BlockSpec((1, size_y, depth, block), lambda i: (0, size_x - 1, 0, 0)),
            pl.BlockSpec((1, 1, depth, block), lambda i: (1, i * size_y + size_y - 1, 0, 0)),
            pl.BlockSpec((1, size_y, depth, block), lambda i: (2, i, 0, 0)),
        ],
        out_specs=[
            pl.BlockSpec((size_y, pairs, NODES, LANES), lambda i: (i, 0, 0, 0)),
            by_plane, by_plane,
            pl.BlockSpec((size_y, pairs, NODES, LANES), lambda i: (0, 0, 0, 0)),
            pl.BlockSpec((1, pairs, NODES, LANES), lambda i: (i, 0, 0, 0)),
            by_half, by_half, by_half,
            pl.BlockSpec((size_y, depth, HALF, LANES), lambda i: (0, 0, 0, 0)),
            pl.BlockSpec((1, depth, HALF, LANES), lambda i: (i, 0, 0, 0)),
            pl.BlockSpec((size_y, HALF, LANES), lambda i: (i, 0, 0)),
        ],
        out_shape=[
            shape(columns, pairs, NODES, LANES), shape(columns, pairs // 2, LANES, LANES), shape(columns, pairs // 2, LANES, LANES),
            shape(size_y, pairs, NODES, LANES), shape(size_x, pairs, NODES, LANES),
            shape(columns // 2, NODES, LANES), shape(columns // 2, NODES, LANES), shape(columns // 2, NODES, LANES),
            shape(size_y, depth, HALF, LANES), shape(size_x, depth, HALF, LANES), shape(columns, HALF, LANES),
        ],
        scratch_shapes=[
            stage, stage,
            pltpu.VMEM((size_y, pairs, NODES, LANES), jnp.bfloat16),
            pltpu.VMEM((3, size_y, HALF, LANES), jnp.float32),
        ],
        compiler_params=pltpu.CompilerParams(vmem_limit_bytes=VMEM_LIMIT),
        name="prepare",
    )(place, prolong, faces, faces, faces)


def interior_kernel(keys_ref, diag_ref, fx_ref, fy_ref, fz_ref, natural_ref, turned_ref, below_ref, shifted_ref, out_ref,
                    stages, terms, flat, behind, wide):
    plane = pl.program_id(0)
    size_y, depth = diag_ref.shape[0], diag_ref.shape[1]
    pairs = depth // 2
    groups = out_ref.shape[0]
    rows = groups * STEP

    def column(j, stage, term):
        row_y = jnp.maximum(j - 1, 0)
        for face, source in zip(range(4), (diag_ref[j], fx_ref[0, j], fy_ref[0, row_y], fz_ref[0, j])):
            spread(source, stage.at[face])
        couples = []
        for p in range(pairs):
            left = []
            for face in range(4):
                shift = 1 if face == 3 else 0
                sides = [block_of(stage.at[face], (2 * p + side - shift) % depth, depth).astype(jnp.bfloat16) for side in (0, 1)]
                left.append(jnp.concatenate(sides, axis=1))
            product = jnp.dot(
                jnp.concatenate(left, axis=0), paired_weights(natural_ref[j, p]), preferred_element_type=jnp.float32)
            couples.append([upright(product[HALF * face : HALF * (face + 1)]) for face in range(4)])
        for h in range(pairs // 2):
            turned = (turned_ref[j, h], below_ref[j, h], turned_ref[row_y, h], shifted_ref[j, h])
            for face in range(4):
                four = two_pairs(turned[face], couples[2 * h][face], couples[2 * h + 1][face])
                for z in range(4):
                    put(term.at[face], 4 * h + z, four[z])

    def columns(step, carry):
        for u in range(2):
            column(2 * step + u, stages.at[u], terms.at[u])
        for face in range(4):
            for k in range(HALF):
                both = [terms[u, face, STEP * k : STEP * (k + 1), :] for u in range(2)]
                flat[face, plane * (size_y // 2) + step, :, LANES * k : LANES * (k + 1)] = jnp.concatenate(both, axis=0).astype(jnp.bfloat16)
        return carry

    lax.fori_loop(0, size_y // 2, columns, 0)

    @pl.when(plane == pl.num_programs(0) - 1)
    def _():
        count = flat.shape[1] * flat.shape[2]
        ahead_keys = [chosen(keys_ref[face : face + 1, :], rows) for face in range(4)]
        behind_keys = [chosen(keys_ref[3 + face : 4 + face, :], rows) for face in range(1, 4)]

        def tiles(t, carry):
            lanes = pl.ds(pl.multiple_of(2 * LANES * t, 2 * LANES), 2 * LANES)
            part = [flat[face, :, :, lanes].reshape(count, 2 * LANES) for face in range(4)]
            ahead = jnp.zeros((rows, 2 * LANES), jnp.float32)
            for face in range(4):
                ahead += jnp.dot(ahead_keys[face], part[face], preferred_element_type=jnp.float32)
            upper, lower = straightened(ahead[:, :LANES], ahead[:, LANES:])
            out_ref[:, pl.ds(pl.multiple_of(STEP * t, STEP), STEP), :] = upper.reshape(groups, STEP, LANES)
            out_ref[:, pl.ds(pl.multiple_of(STEP * (t + HALF // 2), STEP), STEP), :] = lower.reshape(groups, STEP, LANES)
            back = jnp.zeros((rows, 2 * LANES), jnp.float32)
            for face in range(1, 4):
                back += jnp.dot(behind_keys[face - 1], part[face], preferred_element_type=jnp.float32)
            for side in (0, 1):
                behind[:, pl.ds(pl.multiple_of(STEP * (2 * t + side), STEP), STEP), :] = (
                    back[:, LANES * side : LANES * (side + 1)].reshape(groups, STEP, LANES))
            return carry

        lax.fori_loop(0, HALF // 2, tiles, 0)

        def turn(g, carry):
            low = low_lanes(HALF)
            for p in range(STEP // 2):
                one, two = [block_of(behind.at[g], 2 * p + side, STEP) for side in (0, 1)]
                upper = jnp.where(low, one, swapped(two))
                lower = jnp.where(low, swapped(one), two)
                wide[p, :, :NODES] = jnp.concatenate([upper, lower], axis=0).T
            for p in range(STEP // 2):
                for side in (0, 1):
                    even = wide[p, pl.ds(NODES * side, HALF, stride=2), :]
                    odd = wide[p, pl.ds(NODES * side + 1, HALF, stride=2), :]
                    where = pl.ds(2 * p + side, HALF, stride=STEP)
                    out_ref[g, where, :] = out_ref[g, where, :] + jnp.where(low, even, swapped(odd))
            return carry

        lax.fori_loop(0, groups, turn, 0)


def interior(keys, diag, faces, natural, turned, shifted, sizes):
    size_x, size_y, depth = sizes
    pairs, block = depth // 2, diag.shape[-1]
    columns, groups = size_x * size_y, AGG_DEV * SLOTS // STEP
    by_plane = lambda shift: pl.BlockSpec((size_y, pairs // 2, LANES, LANES), lambda i: (jnp.maximum(i - shift, 0), 0, 0, 0))
    spot = pltpu.VMEM((2, 4, depth * HALF, LANES), jnp.float32)
    total = (groups, STEP * HALF, LANES)
    return pl.pallas_call(
        interior_kernel,
        grid=(size_x,),
        in_specs=[
            pl.BlockSpec(keys.shape, lambda i: (0, 0)),
            pl.BlockSpec((size_y, depth, block), lambda i: (i, 0, 0)),
            pl.BlockSpec((1, size_y, depth, block), lambda i: (0, jnp.maximum(i - 1, 0), 0, 0)),
            pl.BlockSpec((1, size_y, depth, block), lambda i: (1, i, 0, 0)),
            pl.BlockSpec((1, size_y, depth, block), lambda i: (2, i, 0, 0)),
            pl.BlockSpec((size_y, pairs, NODES, LANES), lambda i: (i, 0, 0, 0)),
            by_plane(0), by_plane(1), by_plane(0),
        ],
        out_specs=pl.BlockSpec(total, lambda i: (0, 0, 0)),
        out_shape=jax.ShapeDtypeStruct(total, jnp.float32),
        scratch_shapes=[
            spot, spot,
            pltpu.VMEM((4, columns // 2, 2 * depth, block), jnp.bfloat16),
            pltpu.VMEM(total, jnp.float32),
            pltpu.VMEM((STEP // 2, LANES, LANES), jnp.float32),
        ],
        compiler_params=pltpu.CompilerParams(vmem_limit_bytes=VMEM_LIMIT),
        cost_estimate=pl.CostEstimate(flops=columns * depth * 14 * NODES**3, bytes_accessed=columns * depth * 6 * block * 2, transcendentals=0),
        name="interior",
    )(keys, diag, faces, faces, faces, natural, turned, turned, shifted)


def border_kernel(capacity, owners, place_ref, keys_ref, got_x, got_y, got_z, back_z, tail_x, tail_y, tail_z, turned_x, turned_y,
                  natural_x, natural_y, first_z, last_z, total_ref, out_ref, terms, flat, sums, filled):
    size_y, depth = tail_x.shape[0], tail_x.shape[1]
    size_x = tail_y.shape[0]
    pairs = depth // 2
    groups = total_ref.shape[0]
    rows = groups * STEP
    places = out_ref.shape[0]
    quarter = STEP // 2

    def couple(left0, left1, head):
        product = jnp.dot(jnp.concatenate([left0, left1], axis=1), paired_weights(head), preferred_element_type=jnp.float32)
        return upright(product)

    def ahead(tail, head, turned, term):
        couples = [couple(tail[2 * p], tail[2 * p + 1], head[p]) for p in range(pairs)]
        for h in range(pairs // 2):
            four = two_pairs(turned[h], couples[2 * h], couples[2 * h + 1])
            for z in range(4):
                put(term, 4 * h + z, four[z])

    def back(natural, rim, term):
        for p in range(pairs):
            two = folded(across(natural[p], rim[p]))
            for side in (0, 1):
                put(term, 2 * p + side, two[side])

    for first, count, axis, tail, got, turned, natural in (
            (0, size_y, 0, tail_x, got_x, turned_x, natural_x),
            (size_y, size_x, 1, tail_y, got_y, turned_y.at[:, 0], natural_y.at[:, 0])):
        @pl.when(place_ref[axis] == 0)
        def _():
            for j in range(count):
                ahead(tail.at[j], got.at[j], turned.at[j], terms.at[first + j])

        @pl.when(place_ref[axis] != 0)
        def _():
            for j in range(count):
                back(natural.at[j], got.at[j], terms.at[first + j])

    base = size_x + size_y
    columns_z = got_z.shape[0] // quarter
    for t in range(got_z.shape[0]):
        sums_z = folded(across(last_z[t], couple(tail_z[2 * t], tail_z[2 * t + 1], got_z[t])))
        past = folded(across(first_z[t], back_z[t]))
        for side in (0, 1):
            put(terms.at[base + t // quarter], 2 * (t % quarter) + side, sums_z[side])
            put(terms.at[base + columns_z + t // quarter], 2 * (t % quarter) + side, past[side])

    def pack(g, carry):
        for k in range(HALF):
            both = [terms[2 * g + u, STEP * k : STEP * (k + 1), :] for u in range(2)]
            flat[g, :, LANES * k : LANES * (k + 1)] = jnp.concatenate(both, axis=0).astype(jnp.bfloat16)
        return carry

    lax.fori_loop(0, flat.shape[0], pack, 0)
    picks = chosen(keys_ref[...], rows)

    def tiles(t, carry):
        lanes = pl.ds(pl.multiple_of(2 * LANES * t, 2 * LANES), 2 * LANES)
        part = flat[:, :, lanes].reshape(flat.shape[0] * flat.shape[1], 2 * LANES)
        extra = jnp.dot(picks, part, preferred_element_type=jnp.float32)
        for where, value in zip((t, t + HALF // 2), straightened(extra[:, :LANES], extra[:, LANES:])):
            spot = pl.ds(pl.multiple_of(STEP * where, STEP), STEP)
            sums[:, spot, :] = total_ref[:, spot, :] + value.reshape(groups, STEP, LANES)
        return carry

    lax.fori_loop(0, HALF // 2, tiles, 0)

    for owner in range(places // capacity):
        filled[owner] = 0
    if places * SLOTS != rows:
        out_ref[...] = jnp.zeros_like(out_ref)
    for r in range(rows // SLOTS):
        owner = owners[r]
        spot = owner * capacity + filled[owner]
        filled[owner] = filled[owner] + 1
        for s in range(SLOTS):
            key = r * SLOTS + s
            out_ref[spot, HALF * s : HALF * (s + 1), :] = block_of(sums.at[key // STEP], key % STEP, STEP).astype(jnp.bfloat16)


def border(owners, place, keys, operands, turned, natural, ends, capacity, places, sizes):
    size_x, size_y, depth = sizes
    pairs, groups = depth // 2, AGG_DEV * SLOTS // STEP
    count = keys.shape[1]
    smem = pl.BlockSpec(memory_space=pltpu.SMEM)
    whole = pl.BlockSpec(memory_space=pltpu.VMEM)
    planes = lambda array: array.reshape((size_x, size_y) + array.shape[1:])
    return pl.pallas_call(
        functools.partial(border_kernel, capacity),
        grid=(1,),
        in_specs=[smem, smem, whole] + [whole] * len(operands) + [
            pl.BlockSpec((size_y, pairs // 2, LANES, LANES), lambda i: (size_x - 1, 0, 0, 0)),
            pl.BlockSpec((size_x, 1, pairs // 2, LANES, LANES), lambda i: (0, size_y - 1, 0, 0, 0)),
            pl.BlockSpec((size_y, pairs, NODES, LANES), lambda i: (0, 0, 0, 0)),
            pl.BlockSpec((size_x, 1, pairs, NODES, LANES), lambda i: (0, 0, 0, 0, 0)),
        ] + [whole] * len(ends),
        out_specs=whole,
        out_shape=jax.ShapeDtypeStruct((places, SLOTS * HALF, LANES), jnp.bfloat16),
        scratch_shapes=[
            pltpu.VMEM((count // STEP, STEP * HALF, LANES), jnp.float32),
            pltpu.VMEM((count // (2 * STEP), 2 * STEP, HALF * LANES), jnp.bfloat16),
            pltpu.VMEM((groups, STEP * HALF, LANES), jnp.float32),
            pltpu.SMEM((places // capacity,), jnp.int32),
        ],
        compiler_params=pltpu.CompilerParams(vmem_limit_bytes=VMEM_LIMIT),
        name="border",
    )(owners, place, keys, *operands, turned, planes(turned), natural, planes(natural), *ends)


def layout_kernel(source, rows_ref, out_ref, stage):
    group = pl.program_id(0)
    height = out_ref.shape[1]
    for s in range(SLOTS):
        for r in range(height):
            row = source[group * height + r]
            block = rows_ref[jnp.maximum(row, 0), HALF * s : HALF * (s + 1), :].astype(jnp.float32)
            stage[s, pl.ds(r, HALF, stride=height), :] = jnp.where(row >= 0, block, jnp.zeros_like(block))
        for k in range(HALF):
            out_ref[s, :, LANES * k : LANES * (k + 1)] = stage[s, height * k : height * (k + 1), :].astype(jnp.bfloat16)


def laid_out(source, rows, block):
    places, height = rows.shape[0], 8
    return pl.pallas_call(
        layout_kernel,
        grid=(places // height,),
        in_specs=[pl.BlockSpec(memory_space=pltpu.SMEM), pl.BlockSpec(rows.shape, lambda g: (0, 0, 0))],
        out_specs=pl.BlockSpec((SLOTS, height, block), lambda g: (0, g, 0)),
        out_shape=jax.ShapeDtypeStruct((SLOTS, places, block), jnp.bfloat16),
        scratch_shapes=[pltpu.VMEM((SLOTS, height * HALF, LANES), jnp.float32)],
        compiler_params=pltpu.CompilerParams(vmem_limit_bytes=VMEM_LIMIT),
        name="layout",
    )(source, rows)


def swap(block, axis):
    assert lax.axis_size(axis) == 2
    return lax.ppermute(block, axis, [(0, 1), (1, 0)])


def pair_keys(keys, place):
    def moved(values, axis):
        return jnp.pad(values, [(1, 0) if dim == axis else (0, 0) for dim in range(3)], constant_values=-1)

    own = [keys[0]]
    own += [moved(lax.slice_in_dim(keys[2 * axis + 2], 0, -1, axis=axis), axis) for axis in range(3)]
    own += [moved(lax.slice_in_dim(keys[2 * axis + 1], 1, None, axis=axis), axis) for axis in range(3)]
    inner = jnp.stack(own).reshape(7, -1)
    outer = jnp.concatenate([
        jnp.where(place[0] == 0, keys[2, -1], keys[1, 0]).reshape(1, -1),
        jnp.where(place[1] == 0, keys[4, :, -1], keys[3, :, 0]).reshape(1, -1),
        keys[6, :, :, -1].reshape(1, -1),
        keys[5, :, :, 0].reshape(1, -1),
    ], axis=1)
    return inner, outer


def shards(a_diag, a_face, prolong, aggregate, pair_slot, row_owner):
    size_x, size_y, size_z, block = a_diag.shape
    sizes = (size_x, size_y, size_z)
    columns = size_x * size_y
    depth = lax.axis_size("gz")
    capacity = max(2, (AGG_DEV + depth - 1) // depth)
    holding = capacity * depth
    diag = a_diag.reshape(columns, size_z, block)
    faces = a_face.reshape(3, columns, size_z, block)
    place = jnp.stack([lax.axis_index("gx"), lax.axis_index("gy")]).astype(jnp.int32)
    inner_keys, outer_keys = pair_keys(aggregate[None] * SLOTS + pair_slot, place)

    natural, turned, shifted, swap_x, swap_y, head_z, rim_z, last_z, tail_x, tail_y, tail_z = prepare(
        place, prolong.reshape(columns, size_z, block), faces, sizes)
    got_z = passed_along(head_z, "gz", -1)
    back_z = passed_along(rim_z, "gz", 1)
    got_y = swap(swap_y, "gy")
    got_x = swap(swap_x, "gx")
    total = interior(inner_keys, diag, faces, natural, turned, shifted, sizes)
    outgoing = border(
        row_owner, place, outer_keys, (got_x, got_y, got_z, back_z, tail_x, tail_y, tail_z), turned, natural,
        (head_z, last_z, total), capacity, holding, sizes)
    arrived = lax.all_to_all(outgoing, "gz", 0, 0, tiled=True)
    source = jnp.arange(holding, dtype=jnp.int32)
    if holding != AGG_DEV:
        owner_ids = jnp.arange(depth, dtype=jnp.int32)
        counts = jnp.sum((row_owner[:, None] == owner_ids[None, :]).astype(jnp.int32), axis=0)
        arrived_counts = lax.all_to_all(counts, "gz", 0, 0, tiled=True)
        present = source % capacity < jnp.repeat(arrived_counts, capacity)
        target = jnp.cumsum(present.astype(jnp.int32)) - 1
        match = (present[None, :] & (target[None, :] == source[:, None])).astype(jnp.int32)
        source = jnp.sum(match * (source[None, :] + 1), axis=1) - 1
    result = laid_out(source, arrived, block)
    return jnp.transpose(result, (1, 0, 2)).reshape(1, 1, 1, holding, SLOTS, block)


def solution(mesh):
    return jax.shard_map(
        shards,
        mesh=mesh,
        in_specs=(
            P("gx", "gy", "gz", None),
            P(None, "gx", "gy", "gz", None),
            P("gx", "gy", "gz", None),
            P("gx", "gy", "gz"),
            P(None, "gx", "gy", "gz"),
            P(("gx", "gy", "gz")),
        ),
        out_specs=P("gx", "gy", "gz", None, None, None),
        check_vma=False,
    )
```

```python
import functools

import jax
import jax.numpy as jnp
from jax import lax
from jax.experimental import pallas as pl
from jax.experimental.pallas import tpu as pltpu
from jax.sharding import PartitionSpec as P

NODES = 64
SLOTS = 7
AGG_DEV = 24
LANES = 128
HALF = NODES // 2
VMEM_LIMIT = 48 * 1024 * 1024
STEP = 8


def passed_along(block, axis, distance):
    devices = range(lax.axis_size(axis))
    route = [(i - distance, i) for i in devices if i - distance in devices]
    return lax.ppermute(block, axis, route)


def low_lanes(rows):
    return lax.broadcasted_iota(jnp.int32, (rows, LANES), 1) < NODES


def swapped(value):
    return pltpu.roll(value, NODES, 1)


def zero_one(mask):
    return mask.astype(jnp.float32).astype(jnp.bfloat16)


def grid_of(rows, cols):
    return lax.broadcasted_iota(jnp.int32, (rows, cols), 0), lax.broadcasted_iota(jnp.int32, (rows, cols), 1)


def to_blocks():
    row, col = grid_of(STEP * HALF, STEP * HALF)
    return zero_one(col == (row % HALF) * STEP + row // HALF)


def to_lines():
    row, col = grid_of(STEP * HALF, STEP * HALF)
    return zero_one(col == (row % STEP) * HALF + row // STEP)


def product(left, right):
    return jnp.dot(left, right, preferred_element_type=jnp.float32)


def across(left, right):
    return lax.dot_general(left, right, (((0,), (0,)), ((), ())), preferred_element_type=jnp.float32)


def tiled(column):
    tiles = [column[:, LANES * k : LANES * (k + 1)].astype(jnp.float32) for k in range(HALF)]
    return jnp.concatenate(tiles, axis=0).astype(jnp.bfloat16)


def blocks_of(move, first, second):
    rows = product(move, jnp.concatenate([first, second], axis=1))
    return [[rows[HALF * z : HALF * (z + 1), LANES * side : LANES * (side + 1)] for z in range(STEP)] for side in (0, 1)]


def lines_of(move, first, second):
    return product(move, jnp.concatenate([jnp.concatenate(first, axis=0), jnp.concatenate(second, axis=0)], axis=1))


def stacked_pair(first, second):
    low = low_lanes(HALF)
    even = jnp.where(low, first, swapped(second))
    odd = jnp.where(low, swapped(first), second)
    return jnp.concatenate([even, odd], axis=0).astype(jnp.bfloat16)


def in_order(pair):
    row, col = grid_of(NODES, NODES)
    return product(zero_one(row == 2 * (col % HALF) + col // HALF), pair).astype(jnp.bfloat16)


def paired_weights(pair):
    low = low_lanes(NODES)
    zero = jnp.zeros_like(pair)
    first = jnp.where(low, pair, zero)
    second = jnp.where(low, zero, pair)
    left = jnp.concatenate([first, zero, second, zero], axis=0)
    right = jnp.concatenate([zero, first, zero, second], axis=0)
    return jnp.concatenate([left, right], axis=1)


def upright(value):
    return jnp.concatenate([value[:, :LANES], value[:, LANES:]], axis=0).astype(jnp.bfloat16)


def folded(square):
    low = low_lanes(HALF)
    moved = swapped(jnp.where(low, square[HALF : 2 * HALF], square[2 * HALF : 3 * HALF]))
    return [jnp.where(low, square[:HALF], moved).astype(jnp.bfloat16), jnp.where(low, moved, square[3 * HALF :]).astype(jnp.bfloat16)]


def diagonal(square):
    return jnp.where(low_lanes(NODES), square[:NODES], square[NODES:]).astype(jnp.bfloat16)


def turned_pairs(first, second):
    row, col = grid_of(LANES, LANES)
    return across(jnp.concatenate([first, second], axis=0), zero_one(row == col)).astype(jnp.bfloat16)


def apart(first, second):
    zero = jnp.zeros_like(first)
    return jnp.concatenate([jnp.concatenate([first, zero], axis=1), jnp.concatenate([zero, second], axis=1)], axis=0)


def two_pairs(squares):
    return folded(squares[:, :LANES]) + folded(squares[:, LANES:])


def chosen(keys, rows):
    return zero_one(lax.broadcasted_iota(jnp.int32, (rows, keys.shape[1]), 0) == keys)


def straightened(first, second):
    low = low_lanes(first.shape[0])
    return jnp.where(low, first, swapped(second)), jnp.where(low, swapped(first), second)


def keys_along(keys_ref, number, width, target):
    _, size_x, size_y, depth = keys_ref.shape
    total = jnp.zeros((1, width), jnp.float32)
    z, lane_z = grid_of(depth, width)
    row, lane = grid_of(size_y, width)
    for i in range(size_x):
        reach_z, reach_y = target(i, row, z, lane, lane_z)
        if reach_z is None:
            continue
        keys = (keys_ref[number, i] + 1).astype(jnp.float32).astype(jnp.bfloat16)
        wide = product(keys, zero_one(reach_z))
        total += jnp.sum(jnp.where(reach_y, wide, 0.0), axis=0, keepdims=True)
    return total.astype(jnp.int32) - 1


def prepare_kernel(place_ref, p_ref, fx_ref, fy_ref, fz_ref, natural_ref, stacked_ref, moved_ref, turned_ref, shifted_ref,
                   swap_x_ref, swap_y_ref, head_z_ref, rim_z_ref, last_z_ref, tail_x_ref, tail_y_ref, tail_z_ref, move_ref, ends):
    plane = pl.program_id(0)
    size_y, depth = p_ref.shape[0], p_ref.shape[1]
    pairs = depth // 2

    @pl.when(plane == 0)
    def _():
        move_ref[...] = to_blocks()

    for t in range(size_y // 2):
        both = blocks_of(move_ref[...], tiled(p_ref[2 * t]), tiled(p_ref[2 * t + 1]))
        faces_z = jnp.concatenate([tiled(fz_ref[0, 2 * t]), tiled(fz_ref[0, 2 * t + 1])], axis=1)
        last = product(move_ref[HALF * (depth - 1) : HALF * depth, :], faces_z)
        for side in (0, 1):
            j, block = 2 * t + side, both[side]
            stacked = [stacked_pair(block[2 * p], block[2 * p + 1]) for p in range(pairs)]
            moved = [stacked_pair(block[(2 * p - 1) % depth], block[2 * p]) for p in range(pairs)]
            for p in range(pairs):
                stacked_ref[j, p] = stacked[p]
                moved_ref[j, p] = moved[p]
                natural_ref[j, p] = in_order(stacked[p])
            for h in range(pairs // 2):
                turned_ref[j, h] = turned_pairs(stacked[2 * h], stacked[2 * h + 1])
                shifted_ref[j, h] = turned_pairs(moved[2 * h], moved[2 * h + 1])
            tail_z_ref[j] = last[:, LANES * side : LANES * (side + 1)].astype(jnp.bfloat16)
        head_z_ref[t] = in_order(stacked_pair(both[0][0], both[1][0]))
        end = stacked_pair(both[0][depth - 1], both[1][depth - 1])
        last_z_ref[t] = end
        rim_z_ref[t] = diagonal(across(stacked_pair(last[:, :LANES], last[:, LANES:]), end))

    def faces(block, j, tails, rims):
        for z in range(depth):
            tails[z] = block[z].astype(jnp.bfloat16)
        for p in range(pairs):
            rims[p] = diagonal(across(stacked_pair(block[2 * p], block[2 * p + 1]), stacked_ref[j, p]))

    @pl.when(place_ref[1] == 0)
    def _():
        source = tiled(fy_ref[0, 0])
        faces(blocks_of(move_ref[...], source, source)[0], size_y - 1, tail_y_ref.at[0], swap_y_ref.at[0])

    @pl.when(place_ref[1] != 0)
    def _():
        swap_y_ref[0] = natural_ref[0]

    @pl.when((place_ref[0] == 0) & (plane == pl.num_programs(0) - 1))
    def _():
        for t in range(size_y // 2):
            both = blocks_of(move_ref[...], tiled(fx_ref[0, 2 * t]), tiled(fx_ref[0, 2 * t + 1]))
            for side in (0, 1):
                faces(both[side], 2 * t + side, tail_x_ref.at[2 * t + side], swap_x_ref.at[2 * t + side])

    @pl.when((place_ref[0] != 0) & (plane == 0))
    def _():
        swap_x_ref[...] = natural_ref[...]


def prepare(place, prolong, faces, sizes):
    size_x, size_y, depth = sizes
    pairs, block = depth // 2, prolong.shape[-1]
    columns, half = size_x * size_y, size_y // 2
    shape = lambda *dims: jax.ShapeDtypeStruct(dims, jnp.bfloat16)
    by_half = pl.BlockSpec((half, NODES, LANES), lambda i: (i, 0, 0))
    by_plane = pl.BlockSpec((size_y, pairs, NODES, LANES), lambda i: (i, 0, 0, 0))
    by_square = pl.BlockSpec((size_y, pairs // 2, LANES, LANES), lambda i: (i, 0, 0, 0))
    all_pairs, all_squares = shape(columns, pairs, NODES, LANES), shape(columns, pairs // 2, LANES, LANES)
    edge = shape(columns // 2, NODES, LANES)
    return pl.pallas_call(
        prepare_kernel,
        grid=(size_x,),
        in_specs=[
            pl.BlockSpec(memory_space=pltpu.SMEM),
            pl.BlockSpec((size_y, depth, block), lambda i: (i, 0, 0)),
            pl.BlockSpec((1, size_y, depth, block), lambda i: (0, size_x - 1, 0, 0)),
            pl.BlockSpec((1, 1, depth, block), lambda i: (1, i * size_y + size_y - 1, 0, 0)),
            pl.BlockSpec((1, size_y, depth, block), lambda i: (2, i, 0, 0)),
        ],
        out_specs=[
            by_plane, by_plane, by_plane, by_square, by_square,
            pl.BlockSpec((size_y, pairs, NODES, LANES), lambda i: (0, 0, 0, 0)),
            pl.BlockSpec((1, pairs, NODES, LANES), lambda i: (i, 0, 0, 0)),
            by_half, by_half, by_half,
            pl.BlockSpec((size_y, depth, HALF, LANES), lambda i: (0, 0, 0, 0)),
            pl.BlockSpec((1, depth, HALF, LANES), lambda i: (i, 0, 0, 0)),
            pl.BlockSpec((size_y, HALF, LANES), lambda i: (i, 0, 0)),
        ],
        out_shape=[
            all_pairs, all_pairs, all_pairs, all_squares, all_squares,
            shape(size_y, pairs, NODES, LANES), shape(size_x, pairs, NODES, LANES), edge, edge, edge,
            shape(size_y, depth, HALF, LANES), shape(size_x, depth, HALF, LANES), shape(columns, HALF, LANES),
        ],
        scratch_shapes=[
            pltpu.VMEM((STEP * HALF, STEP * HALF), jnp.bfloat16),
            pltpu.VMEM((3, size_y, HALF, LANES), jnp.float32),
        ],
        compiler_params=pltpu.CompilerParams(vmem_limit_bytes=VMEM_LIMIT),
        name="prepare",
    )(place, prolong, faces, faces, faces)


def interior_kernel(keys_ref, diag_ref, fx_ref, fy_ref, fz_ref, natural_ref, stacked_ref, under_ref, moved_ref,
                    turned_ref, below_ref, shifted_ref, out_ref, blocks_ref, lines_ref, flat):
    plane = pl.program_id(0)
    size_y, depth = diag_ref.shape[0], diag_ref.shape[1]
    pairs = depth // 2
    groups = out_ref.shape[0]
    rows = groups * STEP

    @pl.when(plane == 0)
    def _():
        blocks_ref[...] = to_blocks()
        lines_ref[...] = to_lines()

    def column(j):
        row_y = jnp.maximum(j - 1, 0)
        sources = [tiled(source) for source in (diag_ref[j], fx_ref[0, j], fy_ref[0, row_y], fz_ref[0, j])]
        block = blocks_of(blocks_ref[...], sources[0], sources[1]) + blocks_of(blocks_ref[...], sources[2], sources[3])
        couples = []
        for p in range(pairs):
            left = []
            for face in range(4):
                shift = 1 if face == 3 else 0
                sides = [block[face][(2 * p + side - shift) % depth].astype(jnp.bfloat16) for side in (0, 1)]
                left.append(jnp.concatenate(sides, axis=1))
            pair = product(jnp.concatenate(left, axis=0), paired_weights(natural_ref[j, p]))
            couples.append([upright(pair[HALF * face : HALF * (face + 1)]) for face in range(4)])
        terms = [[] for _ in range(7)]
        for h in range(pairs // 2):
            turned = (turned_ref[j, h], below_ref[j, h], turned_ref[row_y, h], shifted_ref[j, h])
            straight = ((stacked_ref, j), (under_ref, j), (stacked_ref, row_y), (moved_ref, j))
            for face in range(4):
                first, second = couples[2 * h][face], couples[2 * h + 1][face]
                terms[face] += two_pairs(product(turned[face], apart(first, second)))
                if face:
                    source, at = straight[face]
                    weights = apart(source[at, 2 * h], source[at, 2 * h + 1])
                    terms[3 + face] += two_pairs(across(jnp.concatenate([first, second], axis=0), weights))
        return terms

    def columns(step, carry):
        both = [column(2 * step + u) for u in range(2)]
        for number in range(7):
            lines = lines_of(lines_ref[...], both[0][number], both[1][number])
            for k in range(HALF):
                part = lines[STEP * k : STEP * (k + 1)]
                line = jnp.concatenate([part[:, :LANES], part[:, LANES:]], axis=0).astype(jnp.bfloat16)
                flat[number, plane * (size_y // 2) + step, :, LANES * k : LANES * (k + 1)] = line
        return carry

    lax.fori_loop(0, size_y // 2, columns, 0)

    @pl.when(plane == pl.num_programs(0) - 1)
    def _():
        count = flat.shape[1] * flat.shape[2]

        def keys_of(number, step, least):
            def target(i, row, z, lane, lane_z):
                if i < least[0] or i + step[0] >= keys_ref.shape[1]:
                    return None, None
                here = (lane // (depth * size_y) == i + step[0]) & (lane // depth % size_y == row + step[1]) & (row >= least[1])
                return (lane_z % depth == z + step[2]) & (z >= least[2]), here

            return chosen(keys_along(keys_ref, number, count, target), rows)

        none = (0, 0, 0)
        unit = ((1, 0, 0), (0, 1, 0), (0, 0, 1))
        picks = [keys_of(0, none, none)]
        picks += [keys_of(2 * axis + 2, unit[axis], none) for axis in range(3)]
        picks += [keys_of(2 * axis + 1, none, unit[axis]) for axis in range(3)]

        def tiles(t, carry):
            lanes = pl.ds(pl.multiple_of(2 * LANES * t, 2 * LANES), 2 * LANES)
            total = jnp.zeros((rows, 2 * LANES), jnp.float32)
            for number in range(7):
                total += product(picks[number], flat[number, :, :, lanes].reshape(count, 2 * LANES))
            upper, lower = straightened(total[:, :LANES], total[:, LANES:])
            out_ref[:, pl.ds(pl.multiple_of(STEP * t, STEP), STEP), :] = upper.reshape(groups, STEP, LANES)
            out_ref[:, pl.ds(pl.multiple_of(STEP * (t + HALF // 2), STEP), STEP), :] = lower.reshape(groups, STEP, LANES)
            return carry

        lax.fori_loop(0, HALF // 2, tiles, 0)


def interior(keys, diag, faces, natural, stacked, moved, turned, shifted, sizes):
    size_x, size_y, depth = sizes
    pairs, block = depth // 2, diag.shape[-1]
    columns, groups = size_x * size_y, AGG_DEV * SLOTS // STEP
    squares = lambda shift: pl.BlockSpec((size_y, pairs // 2, LANES, LANES), lambda i: (jnp.maximum(i - shift, 0), 0, 0, 0))
    planes = lambda shift: pl.BlockSpec((size_y, pairs, NODES, LANES), lambda i: (jnp.maximum(i - shift, 0), 0, 0, 0))
    total = (groups, STEP * HALF, LANES)
    move = pltpu.VMEM((STEP * HALF, STEP * HALF), jnp.bfloat16)
    return pl.pallas_call(
        interior_kernel,
        grid=(size_x,),
        in_specs=[
            pl.BlockSpec(keys.shape, lambda i: (0, 0, 0, 0)),
            pl.BlockSpec((size_y, depth, block), lambda i: (i, 0, 0)),
            pl.BlockSpec((1, size_y, depth, block), lambda i: (0, jnp.maximum(i - 1, 0), 0, 0)),
            pl.BlockSpec((1, size_y, depth, block), lambda i: (1, i, 0, 0)),
            pl.BlockSpec((1, size_y, depth, block), lambda i: (2, i, 0, 0)),
            planes(0), planes(0), planes(1), planes(0), squares(0), squares(1), squares(0),
        ],
        out_specs=pl.BlockSpec(total, lambda i: (0, 0, 0)),
        out_shape=jax.ShapeDtypeStruct(total, jnp.float32),
        scratch_shapes=[move, move, pltpu.VMEM((7, columns // 2, 2 * depth, block), jnp.bfloat16)],
        compiler_params=pltpu.CompilerParams(vmem_limit_bytes=VMEM_LIMIT),
        cost_estimate=pl.CostEstimate(flops=columns * depth * 14 * NODES**3, bytes_accessed=columns * depth * 6 * block * 2, transcendentals=0),
        name="interior",
    )(keys, diag, faces, faces, faces, natural, stacked, stacked, moved, turned, turned, shifted)


def border_kernel(capacity, owners, place_ref, keys_ref, got_x, got_y, got_z, back_z, tail_x, tail_y, tail_z, turned_x, turned_y,
                  natural_x, natural_y, first_z, last_z, total_ref, out_ref, terms, flat, sums, lane_keys, filled):
    size_y, depth = tail_x.shape[0], tail_x.shape[1]
    size_x = tail_y.shape[0]
    pairs = depth // 2
    groups = total_ref.shape[0]
    rows = groups * STEP
    places = out_ref.shape[0]
    quarter = STEP // 2
    width = lane_keys.shape[1]

    def couple(left0, left1, head):
        return upright(product(jnp.concatenate([left0, left1], axis=1), paired_weights(head)))

    def put(group, z, term):
        terms[group, HALF * z : HALF * (z + 1), :] = term

    def ahead(tail, head, turned, group):
        couples = [couple(tail[2 * p], tail[2 * p + 1], head[p]) for p in range(pairs)]
        for h in range(pairs // 2):
            four = two_pairs(product(turned[h], apart(couples[2 * h], couples[2 * h + 1])))
            for z in range(4):
                put(group, 4 * h + z, four[z])

    def back(natural, rim, group):
        for p in range(pairs):
            two = folded(across(natural[p], rim[p]))
            for side in (0, 1):
                put(group, 2 * p + side, two[side])

    def keys_x(number, at):
        def target(i, row, z, lane, lane_z):
            if i != at:
                return None, None
            return lane_z % depth == z, lane // depth == row

        return keys_along(keys_ref, number, width, target)

    def keys_y(number, at):
        def target(i, row, z, lane, lane_z):
            return lane_z % depth == z, (lane // depth == size_y + i) & (row == at)

        return keys_along(keys_ref, number, width, target)

    def keys_z(number, at, base):
        def target(i, row, z, lane, lane_z):
            return z == at, lane == base + size_y * i + row

        return keys_along(keys_ref, number, width, target)

    for first, count, axis, tail, got, turned, natural in (
            (0, size_y, 0, tail_x, got_x, turned_x, natural_x),
            (size_y, size_x, 1, tail_y, got_y, turned_y.at[:, 0], natural_y.at[:, 0])):
        @pl.when(place_ref[axis] == 0)
        def _():
            for j in range(count):
                ahead(tail.at[j], got.at[j], turned.at[j], first + j)
            lane_keys[axis : axis + 1, :] = keys_x(2, size_x - 1) if axis == 0 else keys_y(4, size_y - 1)

        @pl.when(place_ref[axis] != 0)
        def _():
            for j in range(count):
                back(natural.at[j], got.at[j], first + j)
            lane_keys[axis : axis + 1, :] = keys_x(1, 0) if axis == 0 else keys_y(3, 0)

    base = size_x + size_y
    columns_z = got_z.shape[0] // quarter
    for t in range(got_z.shape[0]):
        front = folded(across(last_z[t], couple(tail_z[2 * t], tail_z[2 * t + 1], got_z[t])))
        past = folded(across(first_z[t], back_z[t]))
        for side in (0, 1):
            put(base + t // quarter, 2 * (t % quarter) + side, front[side])
            put(base + columns_z + t // quarter, 2 * (t % quarter) + side, past[side])
    keys = jnp.maximum(lane_keys[0:1, :], lane_keys[1:2, :])
    keys = jnp.maximum(keys, keys_z(6, depth - 1, STEP * base))
    keys = jnp.maximum(keys, keys_z(5, 0, STEP * base + size_x * size_y))
    picks = chosen(keys, rows)

    lines_move = to_lines()
    for g in range(flat.shape[0]):
        lines = product(lines_move, jnp.concatenate([terms[2 * g], terms[2 * g + 1]], axis=1))
        for k in range(HALF):
            part = lines[STEP * k : STEP * (k + 1)]
            flat[g, :, LANES * k : LANES * (k + 1)] = jnp.concatenate([part[:, :LANES], part[:, LANES:]], axis=0).astype(jnp.bfloat16)

    def tiles(t, carry):
        lanes = pl.ds(pl.multiple_of(2 * LANES * t, 2 * LANES), 2 * LANES)
        extra = product(picks, flat[:, :, lanes].reshape(flat.shape[0] * flat.shape[1], 2 * LANES))
        for where, value in zip((t, t + HALF // 2), straightened(extra[:, :LANES], extra[:, LANES:])):
            spot = pl.ds(pl.multiple_of(STEP * where, STEP), STEP)
            sums[:, spot, :] = total_ref[:, spot, :] + value.reshape(groups, STEP, LANES)
        return carry

    lax.fori_loop(0, HALF // 2, tiles, 0)

    for owner in range(places // capacity):
        filled[owner] = 0
    if places * SLOTS != rows:
        out_ref[...] = jnp.zeros_like(out_ref)
    spots = []
    for r in range(rows // SLOTS):
        owner = owners[r]
        spots.append(owner * capacity + filled[owner])
        filled[owner] = filled[owner] + 1
    blocks_move = to_blocks()
    for g in range(0, groups, 2):
        other = min(g + 1, groups - 1)
        both = blocks_of(blocks_move, sums[g].astype(jnp.bfloat16), sums[other].astype(jnp.bfloat16))
        for side in range(other - g + 1):
            for z in range(STEP):
                key = STEP * (g + side) + z
                s = key % SLOTS
                out_ref[spots[key // SLOTS], HALF * s : HALF * (s + 1), :] = both[side][z].astype(jnp.bfloat16)


def border(owners, place, keys, operands, turned, natural, ends, capacity, places, sizes):
    size_x, size_y, depth = sizes
    pairs, groups = depth // 2, AGG_DEV * SLOTS // STEP
    count = STEP * (size_x + size_y) + 2 * size_x * size_y
    smem = pl.BlockSpec(memory_space=pltpu.SMEM)
    whole = pl.BlockSpec(memory_space=pltpu.VMEM)
    planes = lambda array: array.reshape((size_x, size_y) + array.shape[1:])
    return pl.pallas_call(
        functools.partial(border_kernel, capacity),
        grid=(1,),
        in_specs=[smem, smem, whole] + [whole] * len(operands) + [
            pl.BlockSpec((size_y, pairs // 2, LANES, LANES), lambda i: (size_x - 1, 0, 0, 0)),
            pl.BlockSpec((size_x, 1, pairs // 2, LANES, LANES), lambda i: (0, size_y - 1, 0, 0, 0)),
            pl.BlockSpec((size_y, pairs, NODES, LANES), lambda i: (0, 0, 0, 0)),
            pl.BlockSpec((size_x, 1, pairs, NODES, LANES), lambda i: (0, 0, 0, 0, 0)),
        ] + [whole] * len(ends),
        out_specs=whole,
        out_shape=jax.ShapeDtypeStruct((places, SLOTS * HALF, LANES), jnp.bfloat16),
        scratch_shapes=[
            pltpu.VMEM((count // STEP, STEP * HALF, LANES), jnp.bfloat16),
            pltpu.VMEM((count // (2 * STEP), 2 * STEP, HALF * LANES), jnp.bfloat16),
            pltpu.VMEM((groups, STEP * HALF, LANES), jnp.float32),
            pltpu.VMEM((2, count), jnp.int32),
            pltpu.SMEM((places // capacity,), jnp.int32),
        ],
        compiler_params=pltpu.CompilerParams(vmem_limit_bytes=VMEM_LIMIT),
        name="border",
    )(owners, place, keys, *operands, turned, planes(turned), natural, planes(natural), *ends)


def layout_kernel(source, rows_ref, out_ref):
    group = pl.program_id(0)
    move = to_lines()

    def blocks(s):
        found = []
        for r in range(STEP):
            row = source[group * STEP + r]
            block = rows_ref[jnp.maximum(row, 0), HALF * s : HALF * (s + 1), :]
            found.append(jnp.where(row >= 0, block, jnp.zeros_like(block)))
        return found

    for s in range(0, SLOTS, 2):
        other = min(s + 1, SLOTS - 1)
        lines = lines_of(move, blocks(s), blocks(other))
        for side in range(other - s + 1):
            for k in range(HALF):
                part = lines[STEP * k : STEP * (k + 1), LANES * side : LANES * (side + 1)]
                out_ref[s + side, :, LANES * k : LANES * (k + 1)] = part.astype(jnp.bfloat16)


def laid_out(source, rows, block):
    places = rows.shape[0]
    return pl.pallas_call(
        layout_kernel,
        grid=(places // STEP,),
        in_specs=[pl.BlockSpec(memory_space=pltpu.SMEM), pl.BlockSpec(rows.shape, lambda g: (0, 0, 0))],
        out_specs=pl.BlockSpec((SLOTS, STEP, block), lambda g: (0, g, 0)),
        out_shape=jax.ShapeDtypeStruct((SLOTS, places, block), jnp.bfloat16),
        compiler_params=pltpu.CompilerParams(vmem_limit_bytes=VMEM_LIMIT),
        name="layout",
    )(source, rows)


def swap(block, axis):
    assert lax.axis_size(axis) == 2
    return lax.ppermute(block, axis, [(0, 1), (1, 0)])


def shards(a_diag, a_face, prolong, aggregate, pair_slot, row_owner):
    size_x, size_y, size_z, block = a_diag.shape
    sizes = (size_x, size_y, size_z)
    columns = size_x * size_y
    depth = lax.axis_size("gz")
    capacity = max(2, (AGG_DEV + depth - 1) // depth)
    holding = capacity * depth
    diag = a_diag.reshape(columns, size_z, block)
    faces = a_face.reshape(3, columns, size_z, block)
    place = jnp.stack([lax.axis_index("gx"), lax.axis_index("gy")]).astype(jnp.int32)
    keys = aggregate[None] * SLOTS + pair_slot

    natural, stacked, moved, turned, shifted, swap_x, swap_y, head_z, rim_z, last_z, tail_x, tail_y, tail_z = prepare(
        place, prolong.reshape(columns, size_z, block), faces, sizes)
    got_z = passed_along(head_z, "gz", -1)
    back_z = passed_along(rim_z, "gz", 1)
    got_y = swap(swap_y, "gy")
    got_x = swap(swap_x, "gx")
    total = interior(keys, diag, faces, natural, stacked, moved, turned, shifted, sizes)
    outgoing = border(
        row_owner, place, keys, (got_x, got_y, got_z, back_z, tail_x, tail_y, tail_z), turned, natural,
        (head_z, last_z, total), capacity, holding, sizes)
    arrived = lax.all_to_all(outgoing, "gz", 0, 0, tiled=True)
    source = jnp.arange(holding, dtype=jnp.int32)
    if holding != AGG_DEV:
        owner_ids = jnp.arange(depth, dtype=jnp.int32)
        counts = jnp.sum((row_owner[:, None] == owner_ids[None, :]).astype(jnp.int32), axis=0)
        arrived_counts = lax.all_to_all(counts, "gz", 0, 0, tiled=True)
        present = source % capacity < jnp.repeat(arrived_counts, capacity)
        target = jnp.cumsum(present.astype(jnp.int32)) - 1
        match = (present[None, :] & (target[None, :] == source[:, None])).astype(jnp.int32)
        source = jnp.sum(match * (source[None, :] + 1), axis=1) - 1
    result = laid_out(source, arrived, block)
    return jnp.transpose(result, (1, 0, 2)).reshape(1, 1, 1, holding, SLOTS, block)


def solution(mesh):
    return jax.shard_map(
        shards,
        mesh=mesh,
        in_specs=(
            P("gx", "gy", "gz", None),
            P(None, "gx", "gy", "gz", None),
            P("gx", "gy", "gz", None),
            P("gx", "gy", "gz"),
            P(None, "gx", "gy", "gz"),
            P(("gx", "gy", "gz")),
        ),
        out_specs=P("gx", "gy", "gz", None, None, None),
        check_vma=False,
    )
```

```python
import functools

import jax
import jax.numpy as jnp
from jax import lax
from jax.experimental import pallas as pl
from jax.experimental.pallas import tpu as pltpu
from jax.sharding import PartitionSpec as P

NODES = 64
SLOTS = 7
AGG_DEV = 24
LANES = 128
HALF = NODES // 2
VMEM_LIMIT = 48 * 1024 * 1024
STEP = 8


def passed_along(block, axis, distance):
    devices = range(lax.axis_size(axis))
    route = [(i - distance, i) for i in devices if i - distance in devices]
    return lax.ppermute(block, axis, route)


def low_lanes(rows):
    return lax.broadcasted_iota(jnp.int32, (rows, LANES), 1) < NODES


def swapped(value):
    return pltpu.roll(value, NODES, 1)


def zero_one(mask):
    return mask.astype(jnp.float32).astype(jnp.bfloat16)


def product(left, right):
    return jnp.dot(left, right, preferred_element_type=jnp.float32)


def across(left, right):
    return lax.dot_general(left, right, (((0,), (0,)), ((), ())), preferred_element_type=jnp.float32)


def spread(column, stage):
    depth = column.shape[0]
    for k in range(column.shape[1] // LANES):
        stage[depth * k : depth * (k + 1), :] = column[:, LANES * k : LANES * (k + 1)].astype(jnp.float32)


def block_of(stage, z, depth):
    return stage[pl.ds(z, HALF, stride=depth), :]


def stacked_pair(first, second):
    low = low_lanes(HALF)
    even = jnp.where(low, first, swapped(second))
    odd = jnp.where(low, swapped(first), second)
    return jnp.concatenate([even, odd], axis=0).astype(jnp.bfloat16)


def in_order(pair):
    row = lax.broadcasted_iota(jnp.int32, (NODES, NODES), 0)
    col = lax.broadcasted_iota(jnp.int32, (NODES, NODES), 1)
    return product(zero_one(row == 2 * (col % HALF) + col // HALF), pair).astype(jnp.bfloat16)


def paired_weights(pair):
    low = low_lanes(NODES)
    zero = jnp.zeros_like(pair)
    first = jnp.where(low, pair, zero)
    second = jnp.where(low, zero, pair)
    left = jnp.concatenate([first, zero, second, zero], axis=0)
    right = jnp.concatenate([zero, first, zero, second], axis=0)
    return jnp.concatenate([left, right], axis=1)


def upright(value):
    return jnp.concatenate([value[:, :LANES], value[:, LANES:]], axis=0)


def folded(square):
    low = low_lanes(HALF)
    moved = swapped(jnp.where(low, square[HALF : 2 * HALF], square[2 * HALF : 3 * HALF]))
    return [jnp.where(low, square[:HALF], moved), jnp.where(low, moved, square[3 * HALF :])]


def straightened(even, odd):
    low = low_lanes(HALF // 2)
    return jnp.concatenate([jnp.where(low, even, swapped(odd)), jnp.where(low, swapped(even), odd)], axis=0)


def diagonal(square):
    return jnp.where(low_lanes(NODES), square[:NODES], square[NODES:]).astype(jnp.bfloat16)


def apart(first, second):
    zero = jnp.zeros_like(first)
    return jnp.concatenate([jnp.concatenate([first, zero], axis=1), jnp.concatenate([zero, second], axis=1)], axis=0)


def two_pairs(squares):
    return folded(squares[:, :LANES]) + folded(squares[:, LANES:])


def add_all(updates):
    olds = [total[key] for total, key, _ in updates]
    news = []
    for number, (total, key, value) in enumerate(updates):
        for other, other_key, other_value in updates[:number]:
            if other is total:
                value = value + jnp.where(key == other_key, other_value, jnp.zeros_like(other_value))
        news.append(olds[number] + value)
    for (total, key, _), new in zip(updates, news):
        total[key] = new


def prepare_kernel(place_ref, p_ref, fx_ref, fy_ref, fz_ref, natural_ref, turned_ref, swap_x_ref, swap_y_ref, head_z_ref, rim_z_ref,
                   last_z_ref, tail_x_ref, tail_y_ref, tail_z_ref, stages, stages_f, stacks, ends):
    plane = pl.program_id(0)
    size_y, depth = p_ref.shape[0], p_ref.shape[1]
    pairs = depth // 2

    for j in range(size_y):
        stage = stages.at[j]
        spread(p_ref[j], stage)
        block = [block_of(stage, z, depth) for z in range(depth)]
        stacked = [stacked_pair(block[2 * p], block[2 * p + 1]) for p in range(pairs)]
        for p in range(pairs):
            stacks[j, p] = stacked[p]
            natural_ref[j, p] = in_order(stacked[p])
        for h in range(pairs // 2):
            turned_ref[j, h] = jnp.concatenate([stacked[2 * h], stacked[2 * h + 1]], axis=0).T
        ends[0, j] = block[0]
        ends[1, j] = block[depth - 1]
        stage_f = stages_f.at[j]
        spread(fz_ref[0, j], stage_f)
        last = block_of(stage_f, depth - 1, depth)
        ends[2, j] = last
        tail_z_ref[j] = last.astype(jnp.bfloat16)

    for t in range(size_y // 2):
        first, last, face = [stacked_pair(ends[kind, 2 * t], ends[kind, 2 * t + 1]) for kind in range(3)]
        head_z_ref[t] = in_order(first)
        last_z_ref[t] = last
        rim_z_ref[t] = diagonal(across(face, last))

    def faces(source, stage, j, tails, rims):
        spread(source, stage)
        block = [block_of(stage, z, depth) for z in range(depth)]
        for z in range(depth):
            tails[z] = block[z].astype(jnp.bfloat16)
        for p in range(pairs):
            rims[p] = diagonal(across(stacked_pair(block[2 * p], block[2 * p + 1]), stacks[j, p]))

    @pl.when(place_ref[1] == 0)
    def _():
        faces(fy_ref[0, 0], stages_f.at[0], size_y - 1, tail_y_ref.at[0], swap_y_ref.at[0])

    @pl.when(place_ref[1] != 0)
    def _():
        swap_y_ref[0] = natural_ref[0]

    @pl.when((place_ref[0] == 0) & (plane == pl.num_programs(0) - 1))
    def _():
        for j in range(size_y):
            faces(fx_ref[0, j], stages_f.at[j], j, tail_x_ref.at[j], swap_x_ref.at[j])

    @pl.when((place_ref[0] != 0) & (plane == 0))
    def _():
        swap_x_ref[...] = natural_ref[...]


def prepare(place, prolong, faces, sizes):
    size_x, size_y, depth = sizes
    pairs, block = depth // 2, prolong.shape[-1]
    columns, half = size_x * size_y, size_y // 2
    shape = lambda *dims: jax.ShapeDtypeStruct(dims, jnp.bfloat16)
    by_half = pl.BlockSpec((half, NODES, LANES), lambda i: (i, 0, 0))
    edge = shape(columns // 2, NODES, LANES)
    stage = pltpu.VMEM((size_y, depth * HALF, LANES), jnp.float32)
    return pl.pallas_call(
        prepare_kernel,
        grid=(size_x,),
        in_specs=[
            pl.BlockSpec(memory_space=pltpu.SMEM),
            pl.BlockSpec((size_y, depth, block), lambda i: (i, 0, 0)),
            pl.BlockSpec((1, size_y, depth, block), lambda i: (0, size_x - 1, 0, 0)),
            pl.BlockSpec((1, 1, depth, block), lambda i: (1, i * size_y + size_y - 1, 0, 0)),
            pl.BlockSpec((1, size_y, depth, block), lambda i: (2, i, 0, 0)),
        ],
        out_specs=[
            pl.BlockSpec((size_y, pairs, NODES, LANES), lambda i: (i, 0, 0, 0)),
            pl.BlockSpec((size_y, pairs // 2, LANES, LANES), lambda i: (i, 0, 0, 0)),
            pl.BlockSpec((size_y, pairs, NODES, LANES), lambda i: (0, 0, 0, 0)),
            pl.BlockSpec((1, pairs, NODES, LANES), lambda i: (i, 0, 0, 0)),
            by_half, by_half, by_half,
            pl.BlockSpec((size_y, depth, HALF, LANES), lambda i: (0, 0, 0, 0)),
            pl.BlockSpec((1, depth, HALF, LANES), lambda i: (i, 0, 0, 0)),
            pl.BlockSpec((size_y, HALF, LANES), lambda i: (i, 0, 0)),
        ],
        out_shape=[
            shape(columns, pairs, NODES, LANES), shape(columns, pairs // 2, LANES, LANES),
            shape(size_y, pairs, NODES, LANES), shape(size_x, pairs, NODES, LANES), edge, edge, edge,
            shape(size_y, depth, HALF, LANES), shape(size_x, depth, HALF, LANES), shape(columns, HALF, LANES),
        ],
        scratch_shapes=[
            stage, stage,
            pltpu.VMEM((size_y, pairs, NODES, LANES), jnp.bfloat16),
            pltpu.VMEM((3, size_y, HALF, LANES), jnp.float32),
        ],
        compiler_params=pltpu.CompilerParams(vmem_limit_bytes=VMEM_LIMIT),
        name="prepare",
    )(place, prolong, faces, faces, faces)


def interior_kernel(keys, diag_ref, fx_ref, fy_ref, fz_ref, natural_ref, turned_ref, below_ref, out_ref,
                    stages, ahead_even, ahead_odd, behind_even, behind_odd, wide):
    plane = pl.program_id(0)
    size_y, depth = diag_ref.shape[0], diag_ref.shape[1]
    pairs = depth // 2
    spare = out_ref.shape[0]
    ahead, behind = (ahead_even, ahead_odd), (behind_even, behind_odd)
    row_x = jnp.maximum(plane - 1, 0)
    has_x = plane > 0

    @pl.when(plane == 0)
    def _():
        for total in ahead + behind:
            total[...] = jnp.zeros_like(total)

    def couplings(j, stage):
        row_y = jnp.maximum(j - 1, 0)
        for face, source in zip(range(4), (diag_ref[j], fx_ref[0, j], fy_ref[0, row_y], fz_ref[0, j])):
            spread(source, stage.at[face])
        couples = [[] for _ in range(4)]
        for p in range(pairs):
            left = []
            for face in range(4):
                shift = 1 if face == 3 else 0
                sides = [block_of(stage.at[face], (2 * p + side - shift) % depth, depth).astype(jnp.bfloat16) for side in (0, 1)]
                left.append(jnp.concatenate(sides, axis=1))
            pair = product(jnp.concatenate(left, axis=0), paired_weights(natural_ref[j, p]))
            for face in range(4):
                couple = upright(pair[HALF * face : HALF * (face + 1)])
                couples[face].append(swapped(couple) if face == 3 else couple.astype(jnp.bfloat16))
        low = low_lanes(NODES)
        along = couples[3]
        couples[3] = [jnp.where(low, along[p], along[min(p + 1, pairs - 1)]).astype(jnp.bfloat16) for p in range(pairs)]
        return couples

    def sums(j, couples):
        row_y = jnp.maximum(j - 1, 0)
        has_y = j > 0
        for h in range(pairs // 2):
            turned = (turned_ref[j, h], below_ref[j, h], turned_ref[row_y, h], turned_ref[j, h])
            for face in range(4):
                four = two_pairs(product(turned[face], apart(couples[face][2 * h], couples[face][2 * h + 1])))
                updates = []
                for number, term in enumerate(four):
                    z, side = 4 * h + number, number % 2
                    if face == 0:
                        updates.append((ahead[side], keys[0, plane, j, z], term))
                        continue
                    if face == 1:
                        here, there = keys[2, row_x, j, z], keys[1, plane, j, z]
                        here, there = jnp.where(has_x, here, spare), jnp.where(has_x, there, spare)
                    elif face == 2:
                        here, there = keys[4, plane, row_y, z], keys[3, plane, j, z]
                        here, there = jnp.where(has_y, here, spare), jnp.where(has_y, there, spare)
                    elif z + 1 < depth:
                        here, there = keys[6, plane, j, z], keys[5, plane, j, z + 1]
                    else:
                        continue
                    updates.append((ahead[side], here, term))
                    updates.append((behind[side], there, term))
                add_all(updates)

    def columns(step, carry):
        couples = [couplings(2 * step + u, stages.at[u]) for u in range(2)]
        for u in range(2):
            sums(2 * step + u, couples[u])
        return carry

    lax.fori_loop(0, size_y // 2, columns, 0)

    @pl.when(plane == pl.num_programs(0) - 1)
    def _():
        def finish(g, carry):
            low = low_lanes(HALF)
            for p in range(STEP // 2):
                one, two = [behind_even[STEP * g + 2 * p + side] + behind_odd[STEP * g + 2 * p + side] for side in (0, 1)]
                upper = jnp.where(low, one, swapped(two))
                lower = jnp.where(low, swapped(one), two)
                wide[p, :, :NODES] = jnp.concatenate([upper, lower], axis=0).T
            for p in range(STEP // 2):
                for side in (0, 1):
                    key = STEP * g + 2 * p + side
                    even, odd = [
                        ahead_even[key, pl.ds(first, HALF // 2, stride=2), :] + ahead_odd[key, pl.ds(first, HALF // 2, stride=2), :]
                        for first in (0, 1)]
                    turned = [wide[p, pl.ds(NODES * side + first, HALF, stride=2), :] for first in (0, 1)]
                    out_ref[key] = straightened(even, odd) + jnp.where(low, turned[0], swapped(turned[1]))
            return carry

        lax.fori_loop(0, spare // STEP, finish, 0)


def interior(keys, diag, faces, natural, turned, sizes):
    size_x, size_y, depth = sizes
    pairs, block = depth // 2, diag.shape[-1]
    columns, rows = size_x * size_y, AGG_DEV * SLOTS
    squares = lambda shift: pl.BlockSpec((size_y, pairs // 2, LANES, LANES), lambda i: (jnp.maximum(i - shift, 0), 0, 0, 0))
    total = pltpu.VMEM((rows + 1, HALF, LANES), jnp.float32)
    return pl.pallas_call(
        interior_kernel,
        grid=(size_x,),
        in_specs=[
            pl.BlockSpec(memory_space=pltpu.SMEM),
            pl.BlockSpec((size_y, depth, block), lambda i: (i, 0, 0)),
            pl.BlockSpec((1, size_y, depth, block), lambda i: (0, jnp.maximum(i - 1, 0), 0, 0)),
            pl.BlockSpec((1, size_y, depth, block), lambda i: (1, i, 0, 0)),
            pl.BlockSpec((1, size_y, depth, block), lambda i: (2, i, 0, 0)),
            pl.BlockSpec((size_y, pairs, NODES, LANES), lambda i: (i, 0, 0, 0)),
            squares(0), squares(1),
        ],
        out_specs=pl.BlockSpec((rows, HALF, LANES), lambda i: (0, 0, 0)),
        out_shape=jax.ShapeDtypeStruct((rows, HALF, LANES), jnp.float32),
        scratch_shapes=[
            pltpu.VMEM((2, 4, depth * HALF, LANES), jnp.float32), total, total, total, total,
            pltpu.VMEM((STEP // 2, LANES, LANES), jnp.float32),
        ],
        compiler_params=pltpu.CompilerParams(vmem_limit_bytes=VMEM_LIMIT),
        cost_estimate=pl.CostEstimate(flops=columns * depth * 14 * NODES**3, bytes_accessed=columns * depth * 6 * block * 2, transcendentals=0),
        name="interior",
    )(keys, diag, faces, faces, faces, natural, turned, turned)


def border_kernel(capacity, owners, place_ref, keys, got_x, got_y, got_z, back_z, tail_x, tail_y, tail_z, turned_x, turned_y,
                  natural_x, natural_y, first_z, last_z, total_ref, out_ref, even_total, odd_total, filled):
    size_y, depth = tail_x.shape[0], tail_x.shape[1]
    size_x = tail_y.shape[0]
    pairs = depth // 2
    rows = total_ref.shape[0]
    places = out_ref.shape[0]
    totals = (even_total, odd_total)

    for total in totals:
        total[...] = jnp.zeros_like(total)

    def couple(left0, left1, head):
        return upright(product(jnp.concatenate([left0, left1], axis=1), paired_weights(head))).astype(jnp.bfloat16)

    def ahead(tail, head, turned, key):
        couples = [couple(tail[2 * p], tail[2 * p + 1], head[p]) for p in range(pairs)]
        for h in range(pairs // 2):
            four = two_pairs(product(turned[h], apart(couples[2 * h], couples[2 * h + 1])))
            add_all([(totals[number % 2], key(4 * h + number), term) for number, term in enumerate(four)])

    def back(natural, rim, key):
        for h in range(pairs // 2):
            four = [term for p in (2 * h, 2 * h + 1) for term in folded(across(natural[p], rim[p]))]
            add_all([(totals[number % 2], key(4 * h + number), term) for number, term in enumerate(four)])

    @pl.when(place_ref[0] == 0)
    def _():
        for j in range(size_y):
            ahead(tail_x.at[j], got_x.at[j], turned_x.at[j], lambda z: keys[2, size_x - 1, j, z])

    @pl.when(place_ref[0] != 0)
    def _():
        for j in range(size_y):
            back(natural_x.at[j], got_x.at[j], lambda z: keys[1, 0, j, z])

    @pl.when(place_ref[1] == 0)
    def _():
        for i in range(size_x):
            ahead(tail_y.at[i], got_y.at[i], turned_y.at[i, 0], lambda z: keys[4, i, size_y - 1, z])

    @pl.when(place_ref[1] != 0)
    def _():
        for i in range(size_x):
            back(natural_y.at[i, 0], got_y.at[i], lambda z: keys[3, i, 0, z])

    for t in range(got_z.shape[0]):
        i, j = 2 * t // size_y, 2 * t % size_y
        front = folded(across(last_z[t], couple(tail_z[2 * t], tail_z[2 * t + 1], got_z[t])))
        past = folded(across(first_z[t], back_z[t]))
        add_all([(totals[side], keys[6, i, j + side, depth - 1], front[side]) for side in (0, 1)]
                + [(totals[side], keys[5, i, j + side, 0], past[side]) for side in (0, 1)])

    for owner in range(places // capacity):
        filled[owner] = 0
    if places * SLOTS != rows:
        out_ref[...] = jnp.zeros_like(out_ref)
    for r in range(rows // SLOTS):
        owner = owners[r]
        spot = owner * capacity + filled[owner]
        filled[owner] = filled[owner] + 1
        for s in range(SLOTS):
            key = r * SLOTS + s
            even, odd = [
                even_total[key, pl.ds(first, HALF // 2, stride=2), :] + odd_total[key, pl.ds(first, HALF // 2, stride=2), :]
                for first in (0, 1)]
            out_ref[spot, HALF * s : HALF * (s + 1), :] = (total_ref[key] + straightened(even, odd)).astype(jnp.bfloat16)


def border(owners, place, keys, operands, turned, natural, ends, capacity, places, sizes):
    size_x, size_y, depth = sizes
    pairs, rows = depth // 2, AGG_DEV * SLOTS
    smem = pl.BlockSpec(memory_space=pltpu.SMEM)
    whole = pl.BlockSpec(memory_space=pltpu.VMEM)
    planes = lambda array: array.reshape((size_x, size_y) + array.shape[1:])
    total = pltpu.VMEM((rows, HALF, LANES), jnp.float32)
    return pl.pallas_call(
        functools.partial(border_kernel, capacity),
        grid=(1,),
        in_specs=[smem, smem, smem] + [whole] * len(operands) + [
            pl.BlockSpec((size_y, pairs // 2, LANES, LANES), lambda i: (size_x - 1, 0, 0, 0)),
            pl.BlockSpec((size_x, 1, pairs // 2, LANES, LANES), lambda i: (0, size_y - 1, 0, 0, 0)),
            pl.BlockSpec((size_y, pairs, NODES, LANES), lambda i: (0, 0, 0, 0)),
            pl.BlockSpec((size_x, 1, pairs, NODES, LANES), lambda i: (0, 0, 0, 0, 0)),
        ] + [whole] * len(ends),
        out_specs=whole,
        out_shape=jax.ShapeDtypeStruct((places, SLOTS * HALF, LANES), jnp.bfloat16),
        scratch_shapes=[total, total, pltpu.SMEM((places // capacity,), jnp.int32)],
        compiler_params=pltpu.CompilerParams(vmem_limit_bytes=VMEM_LIMIT),
        name="border",
    )(owners, place, keys, *operands, turned, planes(turned), natural, planes(natural), *ends)


def layout_kernel(source, rows_ref, out_ref, stage):
    group = pl.program_id(0)
    height = out_ref.shape[1]
    for s in range(SLOTS):
        for r in range(height):
            row = source[group * height + r]
            block = rows_ref[jnp.maximum(row, 0), HALF * s : HALF * (s + 1), :].astype(jnp.float32)
            stage[s, pl.ds(r, HALF, stride=height), :] = jnp.where(row >= 0, block, jnp.zeros_like(block))
        for k in range(HALF):
            out_ref[s, :, LANES * k : LANES * (k + 1)] = stage[s, height * k : height * (k + 1), :].astype(jnp.bfloat16)


def laid_out(source, rows, block):
    places, height = rows.shape[0], 8
    return pl.pallas_call(
        layout_kernel,
        grid=(places // height,),
        in_specs=[pl.BlockSpec(memory_space=pltpu.SMEM), pl.BlockSpec(rows.shape, lambda g: (0, 0, 0))],
        out_specs=pl.BlockSpec((SLOTS, height, block), lambda g: (0, g, 0)),
        out_shape=jax.ShapeDtypeStruct((SLOTS, places, block), jnp.bfloat16),
        scratch_shapes=[pltpu.VMEM((SLOTS, height * HALF, LANES), jnp.float32)],
        compiler_params=pltpu.CompilerParams(vmem_limit_bytes=VMEM_LIMIT),
        name="layout",
    )(source, rows)


def swap(block, axis):
    assert lax.axis_size(axis) == 2
    return lax.ppermute(block, axis, [(0, 1), (1, 0)])


def shards(a_diag, a_face, prolong, aggregate, pair_slot, row_owner):
    size_x, size_y, size_z, block = a_diag.shape
    sizes = (size_x, size_y, size_z)
    columns = size_x * size_y
    depth = lax.axis_size("gz")
    capacity = max(2, (AGG_DEV + depth - 1) // depth)
    holding = capacity * depth
    diag = a_diag.reshape(columns, size_z, block)
    faces = a_face.reshape(3, columns, size_z, block)
    place = jnp.stack([lax.axis_index("gx"), lax.axis_index("gy")]).astype(jnp.int32)
    keys = aggregate[None] * SLOTS + pair_slot

    natural, turned, swap_x, swap_y, head_z, rim_z, last_z, tail_x, tail_y, tail_z = prepare(
        place, prolong.reshape(columns, size_z, block), faces, sizes)
    got_z = passed_along(head_z, "gz", -1)
    back_z = passed_along(rim_z, "gz", 1)
    got_y = swap(swap_y, "gy")
    got_x = swap(swap_x, "gx")
    total = interior(keys, diag, faces, natural, turned, sizes)
    outgoing = border(
        row_owner, place, keys, (got_x, got_y, got_z, back_z, tail_x, tail_y, tail_z), turned, natural,
        (head_z, last_z, total), capacity, holding, sizes)
    arrived = lax.all_to_all(outgoing, "gz", 0, 0, tiled=True)
    source = jnp.arange(holding, dtype=jnp.int32)
    if holding != AGG_DEV:
        owner_ids = jnp.arange(depth, dtype=jnp.int32)
        counts = jnp.sum((row_owner[:, None] == owner_ids[None, :]).astype(jnp.int32), axis=0)
        arrived_counts = lax.all_to_all(counts, "gz", 0, 0, tiled=True)
        present = source % capacity < jnp.repeat(arrived_counts, capacity)
        target = jnp.cumsum(present.astype(jnp.int32)) - 1
        match = (present[None, :] & (target[None, :] == source[:, None])).astype(jnp.int32)
        source = jnp.sum(match * (source[None, :] + 1), axis=1) - 1
    result = laid_out(source, arrived, block)
    return jnp.transpose(result, (1, 0, 2)).reshape(1, 1, 1, holding, SLOTS, block)


def solution(mesh):
    return jax.shard_map(
        shards,
        mesh=mesh,
        in_specs=(
            P("gx", "gy", "gz", None),
            P(None, "gx", "gy", "gz", None),
            P("gx", "gy", "gz", None),
            P("gx", "gy", "gz"),
            P(None, "gx", "gy", "gz"),
            P(("gx", "gy", "gz")),
        ),
        out_specs=P("gx", "gy", "gz", None, None, None),
        check_vma=False,
    )
```

```python
import functools

import jax
import jax.numpy as jnp
from jax import lax
from jax.experimental import pallas as pl
from jax.experimental.pallas import tpu as pltpu
from jax.sharding import PartitionSpec as P

NODES = 64
SLOTS = 7
AGG_DEV = 24
LANES = 128
HALF = NODES // 2
MIB = 1024 * 1024
STEP = 8


def passed_along(block, axis, distance):
    devices = range(lax.axis_size(axis))
    route = [(i - distance, i) for i in devices if i - distance in devices]
    return lax.ppermute(block, axis, route)


def low_lanes(rows):
    return lax.broadcasted_iota(jnp.int32, (rows, LANES), 1) < NODES


def swapped(value):
    return pltpu.roll(value, NODES, 1)


def zero_one(mask):
    return mask.astype(jnp.float32).astype(jnp.bfloat16)


def product(left, right):
    return jnp.dot(left, right, preferred_element_type=jnp.float32)


def across(left, right):
    return lax.dot_general(left, right, (((0,), (0,)), ((), ())), preferred_element_type=jnp.float32)


def spread(column, stage):
    depth = column.shape[0]
    for k in range(column.shape[1] // LANES):
        stage[depth * k : depth * (k + 1), :] = column[:, LANES * k : LANES * (k + 1)].astype(jnp.float32)


def block_of(stage, z, depth):
    return stage[pl.ds(z, HALF, stride=depth), :]


def stacked_pair(first, second):
    low = low_lanes(HALF)
    even = jnp.where(low, first, swapped(second))
    odd = jnp.where(low, swapped(first), second)
    return jnp.concatenate([even, odd], axis=0).astype(jnp.bfloat16)


def in_order(pair):
    row = lax.broadcasted_iota(jnp.int32, (NODES, NODES), 0)
    col = lax.broadcasted_iota(jnp.int32, (NODES, NODES), 1)
    return product(zero_one(row == 2 * (col % HALF) + col // HALF), pair).astype(jnp.bfloat16)


def paired_weights(pair):
    low = low_lanes(NODES)
    zero = jnp.zeros_like(pair)
    first = jnp.where(low, pair, zero)
    second = jnp.where(low, zero, pair)
    left = jnp.concatenate([first, zero, second, zero], axis=0)
    right = jnp.concatenate([zero, first, zero, second], axis=0)
    return jnp.concatenate([left, right], axis=1)


def upright(value):
    return jnp.concatenate([value[:, :LANES], value[:, LANES:]], axis=0)


def folded(square):
    low = low_lanes(HALF)
    moved = swapped(jnp.where(low, square[HALF : 2 * HALF], square[2 * HALF : 3 * HALF]))
    return [jnp.where(low, square[:HALF], moved), jnp.where(low, moved, square[3 * HALF :])]


def straightened(even, odd):
    low = low_lanes(HALF // 2)
    return jnp.concatenate([jnp.where(low, even, swapped(odd)), jnp.where(low, swapped(even), odd)], axis=0)


def diagonal(square):
    return jnp.where(low_lanes(NODES), square[:NODES], square[NODES:]).astype(jnp.bfloat16)


def apart(first, second):
    zero = jnp.zeros_like(first)
    return jnp.concatenate([jnp.concatenate([first, zero], axis=1), jnp.concatenate([zero, second], axis=1)], axis=0)


def two_pairs(squares):
    return folded(squares[:, :LANES]) + folded(squares[:, LANES:])


def add_all(updates):
    olds = [total[key] for total, key, _ in updates]
    news = []
    for number, (total, key, value) in enumerate(updates):
        for other, other_key, other_value in updates[:number]:
            if other is total:
                value = value + jnp.where(key == other_key, other_value, jnp.zeros_like(other_value))
        news.append(olds[number] + value)
    for (total, key, _), new in zip(updates, news):
        total[key] = new


def prepare_kernel(place_ref, p_ref, fx_ref, fy_ref, fz_ref, natural_ref, turned_ref, swap_x_ref, swap_y_ref, head_z_ref, rim_z_ref,
                   last_z_ref, tail_x_ref, tail_y_ref, tail_z_ref, stages, stages_f, stacks, ends):
    plane = pl.program_id(0)
    size_y, depth = p_ref.shape[0], p_ref.shape[1]
    pairs = depth // 2

    for j in range(size_y):
        stage = stages.at[j]
        spread(p_ref[j], stage)
        block = [block_of(stage, z, depth) for z in range(depth)]
        stacked = [stacked_pair(block[2 * p], block[2 * p + 1]) for p in range(pairs)]
        for p in range(pairs):
            stacks[j, p] = stacked[p]
            natural_ref[j, p] = in_order(stacked[p])
        for h in range(pairs // 2):
            turned_ref[j, h] = jnp.concatenate([stacked[2 * h], stacked[2 * h + 1]], axis=0).T
        ends[0, j] = block[0]
        ends[1, j] = block[depth - 1]
        stage_f = stages_f.at[j]
        spread(fz_ref[0, j], stage_f)
        last = block_of(stage_f, depth - 1, depth)
        ends[2, j] = last
        tail_z_ref[j] = last.astype(jnp.bfloat16)

    for t in range(size_y // 2):
        first, last, face = [stacked_pair(ends[kind, 2 * t], ends[kind, 2 * t + 1]) for kind in range(3)]
        head_z_ref[t] = in_order(first)
        last_z_ref[t] = last
        rim_z_ref[t] = diagonal(across(face, last))

    def faces(source, stage, j, tails, rims):
        spread(source, stage)
        block = [block_of(stage, z, depth) for z in range(depth)]
        for z in range(depth):
            tails[z] = block[z].astype(jnp.bfloat16)
        for p in range(pairs):
            rims[p] = diagonal(across(stacked_pair(block[2 * p], block[2 * p + 1]), stacks[j, p]))

    @pl.when(place_ref[1] == 0)
    def _():
        faces(fy_ref[0, 0], stages_f.at[0], size_y - 1, tail_y_ref.at[0], swap_y_ref.at[0])

    @pl.when(place_ref[1] != 0)
    def _():
        swap_y_ref[0] = natural_ref[0]

    @pl.when((place_ref[0] == 0) & (plane == pl.num_programs(0) - 1))
    def _():
        for j in range(size_y):
            faces(fx_ref[0, j], stages_f.at[j], j, tail_x_ref.at[j], swap_x_ref.at[j])

    @pl.when((place_ref[0] != 0) & (plane == 0))
    def _():
        swap_x_ref[...] = natural_ref[...]


def prepare(place, prolong, faces, sizes):
    size_x, size_y, depth = sizes
    pairs, block = depth // 2, prolong.shape[-1]
    columns, half = size_x * size_y, size_y // 2
    shape = lambda *dims: jax.ShapeDtypeStruct(dims, jnp.bfloat16)
    by_half = pl.BlockSpec((half, NODES, LANES), lambda i: (i, 0, 0))
    edge = shape(columns // 2, NODES, LANES)
    stage = pltpu.VMEM((size_y, depth * HALF, LANES), jnp.float32)
    return pl.pallas_call(
        prepare_kernel,
        grid=(size_x,),
        in_specs=[
            pl.BlockSpec(memory_space=pltpu.SMEM),
            pl.BlockSpec((size_y, depth, block), lambda i: (i, 0, 0)),
            pl.BlockSpec((1, size_y, depth, block), lambda i: (0, size_x - 1, 0, 0)),
            pl.BlockSpec((1, 1, depth, block), lambda i: (1, i * size_y + size_y - 1, 0, 0)),
            pl.BlockSpec((1, size_y, depth, block), lambda i: (2, i, 0, 0)),
        ],
        out_specs=[
            pl.BlockSpec((size_y, pairs, NODES, LANES), lambda i: (i, 0, 0, 0)),
            pl.BlockSpec((size_y, pairs // 2, LANES, LANES), lambda i: (i, 0, 0, 0)),
            pl.BlockSpec((size_y, pairs, NODES, LANES), lambda i: (0, 0, 0, 0)),
            pl.BlockSpec((1, pairs, NODES, LANES), lambda i: (i, 0, 0, 0)),
            by_half, by_half, by_half,
            pl.BlockSpec((size_y, depth, HALF, LANES), lambda i: (0, 0, 0, 0)),
            pl.BlockSpec((1, depth, HALF, LANES), lambda i: (i, 0, 0, 0)),
            pl.BlockSpec((size_y, HALF, LANES), lambda i: (i, 0, 0)),
        ],
        out_shape=[
            shape(columns, pairs, NODES, LANES), shape(columns, pairs // 2, LANES, LANES),
            shape(size_y, pairs, NODES, LANES), shape(size_x, pairs, NODES, LANES), edge, edge, edge,
            shape(size_y, depth, HALF, LANES), shape(size_x, depth, HALF, LANES), shape(columns, HALF, LANES),
        ],
        scratch_shapes=[
            stage, stage,
            pltpu.VMEM((size_y, pairs, NODES, LANES), jnp.bfloat16),
            pltpu.VMEM((3, size_y, HALF, LANES), jnp.float32),
        ],
        compiler_params=pltpu.CompilerParams(vmem_limit_bytes=48 * MIB),
        name="prepare",
    )(place, prolong, faces, faces, faces)


def interior_kernel(keys, diag_ref, fx_ref, fy_ref, fz_ref, natural_ref, turned_ref, below_ref, out_ref,
                    stages, ahead_even, ahead_odd, behind_even, behind_odd, wide):
    plane = pl.program_id(0)
    size_y, depth = diag_ref.shape[0], diag_ref.shape[1]
    pairs = depth // 2
    spare = out_ref.shape[0]
    ahead, behind = (ahead_even, ahead_odd), (behind_even, behind_odd)
    row_x = jnp.maximum(plane - 1, 0)
    has_x = plane > 0

    @pl.when(plane == 0)
    def _():
        for total in ahead + behind:
            total[...] = jnp.zeros_like(total)

    def couplings(j, stage):
        row_y = jnp.maximum(j - 1, 0)
        for face, source in zip(range(4), (diag_ref[j], fx_ref[0, j], fy_ref[0, row_y], fz_ref[0, j])):
            spread(source, stage.at[face])
        couples = [[] for _ in range(4)]
        for p in range(pairs):
            left = []
            for face in range(4):
                shift = 1 if face == 3 else 0
                sides = [block_of(stage.at[face], (2 * p + side - shift) % depth, depth).astype(jnp.bfloat16) for side in (0, 1)]
                left.append(jnp.concatenate(sides, axis=1))
            pair = product(jnp.concatenate(left, axis=0), paired_weights(natural_ref[j, p]))
            for face in range(4):
                couple = upright(pair[HALF * face : HALF * (face + 1)])
                couples[face].append(swapped(couple) if face == 3 else couple.astype(jnp.bfloat16))
        low = low_lanes(NODES)
        along = couples[3]
        couples[3] = [jnp.where(low, along[p], along[min(p + 1, pairs - 1)]).astype(jnp.bfloat16) for p in range(pairs)]
        return couples

    def sums(j, couples):
        row_y = jnp.maximum(j - 1, 0)
        has_y = j > 0
        for h in range(pairs // 2):
            turned = (turned_ref[j, h], below_ref[j, h], turned_ref[row_y, h], turned_ref[j, h])
            for face in range(4):
                four = two_pairs(product(turned[face], apart(couples[face][2 * h], couples[face][2 * h + 1])))
                updates = []
                for number, term in enumerate(four):
                    z, side = 4 * h + number, number % 2
                    if face == 0:
                        updates.append((ahead[side], keys[0, plane, j, z], term))
                        continue
                    if face == 1:
                        here, there = keys[2, row_x, j, z], keys[1, plane, j, z]
                        here, there = jnp.where(has_x, here, spare), jnp.where(has_x, there, spare)
                    elif face == 2:
                        here, there = keys[4, plane, row_y, z], keys[3, plane, j, z]
                        here, there = jnp.where(has_y, here, spare), jnp.where(has_y, there, spare)
                    elif z + 1 < depth:
                        here, there = keys[6, plane, j, z], keys[5, plane, j, z + 1]
                    else:
                        continue
                    updates.append((ahead[side], here, term))
                    updates.append((behind[side], there, term))
                add_all(updates)

    def columns(step, carry):
        couples = [couplings(2 * step + u, stages.at[u]) for u in range(2)]
        for u in range(2):
            sums(2 * step + u, couples[u])
        return carry

    lax.fori_loop(0, size_y // 2, columns, 0)

    @pl.when(plane == pl.num_programs(0) - 1)
    def _():
        def finish(g, carry):
            low = low_lanes(HALF)
            for p in range(STEP // 2):
                one, two = [behind_even[STEP * g + 2 * p + side] + behind_odd[STEP * g + 2 * p + side] for side in (0, 1)]
                upper = jnp.where(low, one, swapped(two))
                lower = jnp.where(low, swapped(one), two)
                wide[p, :, :NODES] = jnp.concatenate([upper, lower], axis=0).T
            for p in range(STEP // 2):
                for side in (0, 1):
                    key = STEP * g + 2 * p + side
                    even, odd = [
                        ahead_even[key, pl.ds(first, HALF // 2, stride=2), :] + ahead_odd[key, pl.ds(first, HALF // 2, stride=2), :]
                        for first in (0, 1)]
                    turned = [wide[p, pl.ds(NODES * side + first, HALF, stride=2), :] for first in (0, 1)]
                    out_ref[key] = straightened(even, odd) + jnp.where(low, turned[0], swapped(turned[1]))
            return carry

        lax.fori_loop(0, spare // STEP, finish, 0)


def interior(keys, diag, faces, natural, turned, sizes):
    size_x, size_y, depth = sizes
    pairs, block = depth // 2, diag.shape[-1]
    columns, rows = size_x * size_y, AGG_DEV * SLOTS
    squares = lambda shift: pl.BlockSpec((size_y, pairs // 2, LANES, LANES), lambda i: (jnp.maximum(i - shift, 0), 0, 0, 0))
    total = pltpu.VMEM((rows + 1, HALF, LANES), jnp.float32)
    return pl.pallas_call(
        interior_kernel,
        grid=(size_x,),
        in_specs=[
            pl.BlockSpec(memory_space=pltpu.SMEM),
            pl.BlockSpec((size_y, depth, block), lambda i: (i, 0, 0)),
            pl.BlockSpec((1, size_y, depth, block), lambda i: (0, jnp.maximum(i - 1, 0), 0, 0)),
            pl.BlockSpec((1, size_y, depth, block), lambda i: (1, i, 0, 0)),
            pl.BlockSpec((1, size_y, depth, block), lambda i: (2, i, 0, 0)),
            pl.BlockSpec((size_y, pairs, NODES, LANES), lambda i: (i, 0, 0, 0)),
            squares(0), squares(1),
        ],
        out_specs=pl.BlockSpec((rows, HALF, LANES), lambda i: (0, 0, 0)),
        out_shape=jax.ShapeDtypeStruct((rows, HALF, LANES), jnp.float32),
        scratch_shapes=[
            pltpu.VMEM((2, 4, depth * HALF, LANES), jnp.float32), total, total, total, total,
            pltpu.VMEM((STEP // 2, LANES, LANES), jnp.float32),
        ],
        compiler_params=pltpu.CompilerParams(vmem_limit_bytes=28 * MIB),
        cost_estimate=pl.CostEstimate(flops=columns * depth * 14 * NODES**3, bytes_accessed=columns * depth * 6 * block * 2, transcendentals=0),
        name="interior",
    )(keys, diag, faces, faces, faces, natural, turned, turned)


def border_kernel(capacity, owners, place_ref, keys, got_x, got_y, got_z, back_z, tail_x, tail_y, tail_z, turned_x, turned_y,
                  natural_x, natural_y, first_z, last_z, total_ref, out_ref, even_total, odd_total, filled):
    size_y, depth = tail_x.shape[0], tail_x.shape[1]
    size_x = tail_y.shape[0]
    pairs = depth // 2
    rows = total_ref.shape[0]
    places = out_ref.shape[0]
    totals = (even_total, odd_total)

    for total in totals:
        total[...] = jnp.zeros_like(total)

    def couple(left0, left1, head):
        return upright(product(jnp.concatenate([left0, left1], axis=1), paired_weights(head))).astype(jnp.bfloat16)

    def ahead(tail, head, turned, key):
        couples = [couple(tail[2 * p], tail[2 * p + 1], head[p]) for p in range(pairs)]
        for h in range(pairs // 2):
            four = two_pairs(product(turned[h], apart(couples[2 * h], couples[2 * h + 1])))
            add_all([(totals[number % 2], key(4 * h + number), term) for number, term in enumerate(four)])

    def back(natural, rim, key):
        for h in range(pairs // 2):
            four = [term for p in (2 * h, 2 * h + 1) for term in folded(across(natural[p], rim[p]))]
            add_all([(totals[number % 2], key(4 * h + number), term) for number, term in enumerate(four)])

    @pl.when(place_ref[0] == 0)
    def _():
        for j in range(size_y):
            ahead(tail_x.at[j], got_x.at[1, j], turned_x.at[j], lambda z: keys[2, size_x - 1, j, z])

    @pl.when(place_ref[0] != 0)
    def _():
        for j in range(size_y):
            back(natural_x.at[j], got_x.at[0, j], lambda z: keys[1, 0, j, z])

    @pl.when(place_ref[1] == 0)
    def _():
        for i in range(size_x):
            ahead(tail_y.at[i], got_y.at[1, i], turned_y.at[i, 0], lambda z: keys[4, i, size_y - 1, z])

    @pl.when(place_ref[1] != 0)
    def _():
        for i in range(size_x):
            back(natural_y.at[i, 0], got_y.at[0, i], lambda z: keys[3, i, 0, z])

    for t in range(got_z.shape[0]):
        i, j = 2 * t // size_y, 2 * t % size_y
        front = folded(across(last_z[t], couple(tail_z[2 * t], tail_z[2 * t + 1], got_z[t])))
        past = folded(across(first_z[t], back_z[t]))
        add_all([(totals[side], keys[6, i, j + side, depth - 1], front[side]) for side in (0, 1)]
                + [(totals[side], keys[5, i, j + side, 0], past[side]) for side in (0, 1)])

    for owner in range(places // capacity):
        filled[owner] = 0
    if places * SLOTS != rows:
        out_ref[...] = jnp.zeros_like(out_ref)
    for r in range(rows // SLOTS):
        owner = owners[r]
        spot = owner * capacity + filled[owner]
        filled[owner] = filled[owner] + 1
        for s in range(SLOTS):
            key = r * SLOTS + s
            even, odd = [
                even_total[key, pl.ds(first, HALF // 2, stride=2), :] + odd_total[key, pl.ds(first, HALF // 2, stride=2), :]
                for first in (0, 1)]
            out_ref[spot, HALF * s : HALF * (s + 1), :] = (total_ref[key] + straightened(even, odd)).astype(jnp.bfloat16)


def border(owners, place, keys, operands, turned, natural, ends, capacity, places, sizes):
    size_x, size_y, depth = sizes
    pairs, rows = depth // 2, AGG_DEV * SLOTS
    smem = pl.BlockSpec(memory_space=pltpu.SMEM)
    whole = pl.BlockSpec(memory_space=pltpu.VMEM)
    planes = lambda array: array.reshape((size_x, size_y) + array.shape[1:])
    total = pltpu.VMEM((rows, HALF, LANES), jnp.float32)
    return pl.pallas_call(
        functools.partial(border_kernel, capacity),
        grid=(1,),
        in_specs=[smem, smem, smem] + [whole] * len(operands) + [
            pl.BlockSpec((size_y, pairs // 2, LANES, LANES), lambda i: (size_x - 1, 0, 0, 0)),
            pl.BlockSpec((size_x, 1, pairs // 2, LANES, LANES), lambda i: (0, size_y - 1, 0, 0, 0)),
            pl.BlockSpec((size_y, pairs, NODES, LANES), lambda i: (0, 0, 0, 0)),
            pl.BlockSpec((size_x, 1, pairs, NODES, LANES), lambda i: (0, 0, 0, 0, 0)),
        ] + [whole] * len(ends),
        out_specs=whole,
        out_shape=jax.ShapeDtypeStruct((places, SLOTS * HALF, LANES), jnp.bfloat16),
        scratch_shapes=[total, total, pltpu.SMEM((places // capacity,), jnp.int32)],
        compiler_params=pltpu.CompilerParams(vmem_limit_bytes=18 * MIB),
        name="border",
    )(owners, place, keys, *operands, turned, planes(turned), natural, planes(natural), *ends)


def layout_kernel(source, rows_ref, out_ref, stage):
    group = pl.program_id(0)
    height = out_ref.shape[1]
    for s in range(SLOTS):
        for r in range(height):
            row = source[group * height + r]
            block = rows_ref[jnp.maximum(row, 0), HALF * s : HALF * (s + 1), :].astype(jnp.float32)
            stage[s, pl.ds(r, HALF, stride=height), :] = jnp.where(row >= 0, block, jnp.zeros_like(block))
        for k in range(HALF):
            out_ref[s, :, LANES * k : LANES * (k + 1)] = stage[s, height * k : height * (k + 1), :].astype(jnp.bfloat16)


def laid_out(source, rows, block):
    places, height = rows.shape[0], 8
    return pl.pallas_call(
        layout_kernel,
        grid=(places // height,),
        in_specs=[pl.BlockSpec(memory_space=pltpu.SMEM), pl.BlockSpec(rows.shape, lambda g: (0, 0, 0))],
        out_specs=pl.BlockSpec((SLOTS, height, block), lambda g: (0, g, 0)),
        out_shape=jax.ShapeDtypeStruct((SLOTS, places, block), jnp.bfloat16),
        scratch_shapes=[pltpu.VMEM((SLOTS, height * HALF, LANES), jnp.float32)],
        compiler_params=pltpu.CompilerParams(vmem_limit_bytes=10 * MIB),
        name="layout",
    )(source, rows)


def shared(block, axis):
    assert lax.axis_size(axis) == 2
    return lax.all_gather(block, axis, axis=0, tiled=False)


def shards(a_diag, a_face, prolong, aggregate, pair_slot, row_owner):
    size_x, size_y, size_z, block = a_diag.shape
    sizes = (size_x, size_y, size_z)
    columns = size_x * size_y
    depth = lax.axis_size("gz")
    capacity = max(2, (AGG_DEV + depth - 1) // depth)
    holding = capacity * depth
    diag = a_diag.reshape(columns, size_z, block)
    faces = a_face.reshape(3, columns, size_z, block)
    place = jnp.stack([lax.axis_index("gx"), lax.axis_index("gy")]).astype(jnp.int32)
    keys = aggregate[None] * SLOTS + pair_slot

    natural, turned, swap_x, swap_y, head_z, rim_z, last_z, tail_x, tail_y, tail_z = prepare(
        place, prolong.reshape(columns, size_z, block), faces, sizes)
    got_z = passed_along(head_z, "gz", -1)
    back_z = passed_along(rim_z, "gz", 1)
    got_y = shared(swap_y, "gy")
    got_x = shared(swap_x, "gx")
    total = interior(keys, diag, faces, natural, turned, sizes)
    outgoing = border(
        row_owner, place, keys, (got_x, got_y, got_z, back_z, tail_x, tail_y, tail_z), turned, natural,
        (head_z, last_z, total), capacity, holding, sizes)
    arrived = lax.all_to_all(outgoing, "gz", 0, 0, tiled=True)
    source = jnp.arange(holding, dtype=jnp.int32)
    if holding != AGG_DEV:
        owner_ids = jnp.arange(depth, dtype=jnp.int32)
        counts = jnp.sum((row_owner[:, None] == owner_ids[None, :]).astype(jnp.int32), axis=0)
        arrived_counts = lax.all_to_all(counts, "gz", 0, 0, tiled=True)
        present = source % capacity < jnp.repeat(arrived_counts, capacity)
        target = jnp.cumsum(present.astype(jnp.int32)) - 1
        match = (present[None, :] & (target[None, :] == source[:, None])).astype(jnp.int32)
        source = jnp.sum(match * (source[None, :] + 1), axis=1) - 1
    result = laid_out(source, arrived, block)
    return jnp.transpose(result, (1, 0, 2)).reshape(1, 1, 1, holding, SLOTS, block)


def solution(mesh):
    return jax.shard_map(
        shards,
        mesh=mesh,
        in_specs=(
            P("gx", "gy", "gz", None),
            P(None, "gx", "gy", "gz", None),
            P("gx", "gy", "gz", None),
            P("gx", "gy", "gz"),
            P(None, "gx", "gy", "gz"),
            P(("gx", "gy", "gz")),
        ),
        out_specs=P("gx", "gy", "gz", None, None, None),
        check_vma=False,
    )
```

```python
import functools

import jax
import jax.numpy as jnp
from jax import lax
from jax.experimental import pallas as pl
from jax.experimental.pallas import tpu as pltpu
from jax.sharding import PartitionSpec as P

NODES = 64
SLOTS = 7
AGG_DEV = 24
LANES = 128
HALF = NODES // 2
MIB = 1024 * 1024
STEP = 8


def passed_along(block, axis, distance):
    devices = range(lax.axis_size(axis))
    route = [(i - distance, i) for i in devices if i - distance in devices]
    return lax.ppermute(block, axis, route)


def low_lanes(rows):
    return lax.broadcasted_iota(jnp.int32, (rows, LANES), 1) < NODES


def swapped(value):
    return pltpu.roll(value, NODES, 1)


def zero_one(mask):
    return mask.astype(jnp.float32).astype(jnp.bfloat16)


def product(left, right):
    return jnp.dot(left, right, preferred_element_type=jnp.float32)


def across(left, right):
    return lax.dot_general(left, right, (((0,), (0,)), ((), ())), preferred_element_type=jnp.float32)


def spread(column, stage):
    depth = column.shape[0]
    for k in range(column.shape[1] // LANES):
        stage[depth * k : depth * (k + 1), :] = column[:, LANES * k : LANES * (k + 1)].astype(jnp.float32)


def block_of(stage, z, depth):
    return stage[pl.ds(z, HALF, stride=depth), :]


def stacked_pair(first, second):
    low = low_lanes(HALF)
    even = jnp.where(low, first, swapped(second))
    odd = jnp.where(low, swapped(first), second)
    return jnp.concatenate([even, odd], axis=0).astype(jnp.bfloat16)


def in_order(pair):
    row = lax.broadcasted_iota(jnp.int32, (NODES, NODES), 0)
    col = lax.broadcasted_iota(jnp.int32, (NODES, NODES), 1)
    return product(zero_one(row == 2 * (col % HALF) + col // HALF), pair).astype(jnp.bfloat16)


def paired_weights(pair):
    low = low_lanes(NODES)
    zero = jnp.zeros_like(pair)
    first = jnp.where(low, pair, zero)
    second = jnp.where(low, zero, pair)
    left = jnp.concatenate([first, zero, second, zero], axis=0)
    right = jnp.concatenate([zero, first, zero, second], axis=0)
    return jnp.concatenate([left, right], axis=1)


def upright(value):
    return jnp.concatenate([value[:, :LANES], value[:, LANES:]], axis=0)


def folded(square):
    low = low_lanes(HALF)
    moved = swapped(jnp.where(low, square[HALF : 2 * HALF], square[2 * HALF : 3 * HALF]))
    return [jnp.where(low, square[:HALF], moved), jnp.where(low, moved, square[3 * HALF :])]


def straightened(even, odd):
    low = low_lanes(HALF // 2)
    return jnp.concatenate([jnp.where(low, even, swapped(odd)), jnp.where(low, swapped(even), odd)], axis=0)


def diagonal(square):
    return jnp.where(low_lanes(NODES), square[:NODES], square[NODES:]).astype(jnp.bfloat16)


def apart(first, second):
    zero = jnp.zeros_like(first)
    return jnp.concatenate([jnp.concatenate([first, zero], axis=1), jnp.concatenate([zero, second], axis=1)], axis=0)


def two_pairs(squares):
    return folded(squares[:, :LANES]) + folded(squares[:, LANES:])


def add_all(updates):
    olds = [total[key] for total, key, _ in updates]
    news = []
    for number, (total, key, value) in enumerate(updates):
        for other, other_key, other_value in updates[:number]:
            if other is total:
                value = value + jnp.where(key == other_key, other_value, jnp.zeros_like(other_value))
        news.append(olds[number] + value)
    for (total, key, _), new in zip(updates, news):
        total[key] = new


def prepare_kernel(place_ref, p_ref, fx_ref, fy_ref, fz_ref, natural_ref, turned_ref, swap_x_ref, swap_y_ref, head_z_ref, rim_z_ref,
                   last_z_ref, tail_x_ref, tail_y_ref, tail_z_ref, stages, stages_f, stacks, ends):
    plane = pl.program_id(0)
    size_y, depth = p_ref.shape[0], p_ref.shape[1]
    pairs = depth // 2

    for j in range(size_y):
        stage = stages.at[j]
        spread(p_ref[j], stage)
        block = [block_of(stage, z, depth) for z in range(depth)]
        stacked = [stacked_pair(block[2 * p], block[2 * p + 1]) for p in range(pairs)]
        for p in range(pairs):
            stacks[j, p] = stacked[p]
            natural_ref[j, p] = in_order(stacked[p])
        for h in range(pairs // 2):
            turned_ref[j, h] = jnp.concatenate([stacked[2 * h], stacked[2 * h + 1]], axis=0).T
        ends[0, j] = block[0]
        ends[1, j] = block[depth - 1]
        stage_f = stages_f.at[j]
        spread(fz_ref[0, j], stage_f)
        last = block_of(stage_f, depth - 1, depth)
        ends[2, j] = last
        tail_z_ref[j] = last.astype(jnp.bfloat16)

    for t in range(size_y // 2):
        first, last, face = [stacked_pair(ends[kind, 2 * t], ends[kind, 2 * t + 1]) for kind in range(3)]
        head_z_ref[t] = in_order(first)
        last_z_ref[t] = last
        rim_z_ref[t] = diagonal(across(face, last))

    def faces(source, stage, j, tails, rims):
        spread(source, stage)
        block = [block_of(stage, z, depth) for z in range(depth)]
        for z in range(depth):
            tails[z] = block[z].astype(jnp.bfloat16)
        for p in range(pairs):
            rims[p] = diagonal(across(stacked_pair(block[2 * p], block[2 * p + 1]), stacks[j, p]))

    @pl.when(place_ref[1] == 0)
    def _():
        faces(fy_ref[0, 0], stages_f.at[0], size_y - 1, tail_y_ref.at[0], swap_y_ref.at[0])

    @pl.when(place_ref[1] != 0)
    def _():
        swap_y_ref[0] = natural_ref[0]

    @pl.when((place_ref[0] == 0) & (plane == pl.num_programs(0) - 1))
    def _():
        for j in range(size_y):
            faces(fx_ref[0, j], stages_f.at[j], j, tail_x_ref.at[j], swap_x_ref.at[j])

    @pl.when((place_ref[0] != 0) & (plane == 0))
    def _():
        swap_x_ref[...] = natural_ref[...]


def prepare(place, prolong, faces, sizes):
    size_x, size_y, depth = sizes
    pairs, block = depth // 2, prolong.shape[-1]
    columns, half = size_x * size_y, size_y // 2
    shape = lambda *dims: jax.ShapeDtypeStruct(dims, jnp.bfloat16)
    by_half = pl.BlockSpec((half, NODES, LANES), lambda i: (i, 0, 0))
    edge = shape(columns // 2, NODES, LANES)
    stage = pltpu.VMEM((size_y, depth * HALF, LANES), jnp.float32)
    return pl.pallas_call(
        prepare_kernel,
        grid=(size_x,),
        in_specs=[
            pl.BlockSpec(memory_space=pltpu.SMEM),
            pl.BlockSpec((size_y, depth, block), lambda i: (i, 0, 0)),
            pl.BlockSpec((1, size_y, depth, block), lambda i: (0, size_x - 1, 0, 0)),
            pl.BlockSpec((1, 1, depth, block), lambda i: (1, i * size_y + size_y - 1, 0, 0)),
            pl.BlockSpec((1, size_y, depth, block), lambda i: (2, i, 0, 0)),
        ],
        out_specs=[
            pl.BlockSpec((size_y, pairs, NODES, LANES), lambda i: (i, 0, 0, 0)),
            pl.BlockSpec((size_y, pairs // 2, LANES, LANES), lambda i: (i, 0, 0, 0)),
            pl.BlockSpec((size_y, pairs, NODES, LANES), lambda i: (0, 0, 0, 0)),
            pl.BlockSpec((1, pairs, NODES, LANES), lambda i: (i, 0, 0, 0)),
            by_half, by_half, by_half,
            pl.BlockSpec((size_y, depth, HALF, LANES), lambda i: (0, 0, 0, 0)),
            pl.BlockSpec((1, depth, HALF, LANES), lambda i: (i, 0, 0, 0)),
            pl.BlockSpec((size_y, HALF, LANES), lambda i: (i, 0, 0)),
        ],
        out_shape=[
            shape(columns, pairs, NODES, LANES), shape(columns, pairs // 2, LANES, LANES),
            shape(size_y, pairs, NODES, LANES), shape(size_x, pairs, NODES, LANES), edge, edge, edge,
            shape(size_y, depth, HALF, LANES), shape(size_x, depth, HALF, LANES), shape(columns, HALF, LANES),
        ],
        scratch_shapes=[
            stage, stage,
            pltpu.VMEM((size_y, pairs, NODES, LANES), jnp.bfloat16),
            pltpu.VMEM((3, size_y, HALF, LANES), jnp.float32),
        ],
        compiler_params=pltpu.CompilerParams(vmem_limit_bytes=48 * MIB),
        name="prepare",
    )(place, prolong, faces, faces, faces)


def interior_kernel(keys, diag_ref, fx_ref, fy_ref, fz_ref, natural_ref, turned_ref, below_ref, out_ref,
                    stages, ahead_even, ahead_odd, behind_even, behind_odd, wide):
    plane = pl.program_id(0)
    size_y, depth = diag_ref.shape[0], diag_ref.shape[1]
    pairs = depth // 2
    spare = out_ref.shape[0]
    ahead, behind = (ahead_even, ahead_odd), (behind_even, behind_odd)
    row_x = jnp.maximum(plane - 1, 0)
    has_x = plane > 0

    @pl.when(plane == 0)
    def _():
        for total in ahead + behind:
            total[...] = jnp.zeros_like(total)

    def couplings(j, stage):
        row_y = jnp.maximum(j - 1, 0)
        for face, source in zip(range(4), (diag_ref[j], fx_ref[0, j], fy_ref[0, row_y], fz_ref[0, j])):
            spread(source, stage.at[face])
        couples = [[] for _ in range(4)]
        for p in range(pairs):
            left = []
            for face in range(4):
                shift = 1 if face == 3 else 0
                sides = [block_of(stage.at[face], (2 * p + side - shift) % depth, depth).astype(jnp.bfloat16) for side in (0, 1)]
                left.append(jnp.concatenate(sides, axis=1))
            pair = product(jnp.concatenate(left, axis=0), paired_weights(natural_ref[j, p]))
            for face in range(4):
                couple = upright(pair[HALF * face : HALF * (face + 1)])
                couples[face].append(swapped(couple) if face == 3 else couple.astype(jnp.bfloat16))
        low = low_lanes(NODES)
        along = couples[3]
        couples[3] = [jnp.where(low, along[p], along[min(p + 1, pairs - 1)]).astype(jnp.bfloat16) for p in range(pairs)]
        return couples

    def sums(j, couples):
        row_y = jnp.maximum(j - 1, 0)
        has_y = j > 0
        batches = []
        for h in range(pairs // 2):
            turned = (turned_ref[j, h], below_ref[j, h], turned_ref[row_y, h], turned_ref[j, h])
            for face in range(4):
                four = two_pairs(product(turned[face], apart(couples[face][2 * h], couples[face][2 * h + 1])))
                updates = []
                for number, term in enumerate(four):
                    z, side = 4 * h + number, number % 2
                    if face == 0:
                        updates.append((ahead[side], keys[0, plane, j, z], term))
                        continue
                    if face == 1:
                        here, there = keys[2, row_x, j, z], keys[1, plane, j, z]
                        here, there = jnp.where(has_x, here, spare), jnp.where(has_x, there, spare)
                    elif face == 2:
                        here, there = keys[4, plane, row_y, z], keys[3, plane, j, z]
                        here, there = jnp.where(has_y, here, spare), jnp.where(has_y, there, spare)
                    elif z + 1 < depth:
                        here, there = keys[6, plane, j, z], keys[5, plane, j, z + 1]
                    else:
                        continue
                    updates.append((ahead[side], here, term))
                    updates.append((behind[side], there, term))
                batches.append(updates)
        return batches

    def columns(step, carry):
        couples = [couplings(2 * step + u, stages.at[u]) for u in range(2)]
        for updates in [updates for u in range(2) for updates in sums(2 * step + u, couples[u])]:
            add_all(updates)
        return carry

    lax.fori_loop(0, size_y // 2, columns, 0)

    @pl.when(plane == pl.num_programs(0) - 1)
    def _():
        def finish(g, carry):
            low = low_lanes(HALF)
            for p in range(STEP // 2):
                one, two = [behind_even[STEP * g + 2 * p + side] + behind_odd[STEP * g + 2 * p + side] for side in (0, 1)]
                upper = jnp.where(low, one, swapped(two))
                lower = jnp.where(low, swapped(one), two)
                wide[p, :, :NODES] = jnp.concatenate([upper, lower], axis=0).T
            for p in range(STEP // 2):
                for side in (0, 1):
                    key = STEP * g + 2 * p + side
                    even, odd = [
                        ahead_even[key, pl.ds(first, HALF // 2, stride=2), :] + ahead_odd[key, pl.ds(first, HALF // 2, stride=2), :]
                        for first in (0, 1)]
                    turned = [wide[p, pl.ds(NODES * side + first, HALF, stride=2), :] for first in (0, 1)]
                    out_ref[key] = straightened(even, odd) + jnp.where(low, turned[0], swapped(turned[1]))
            return carry

        lax.fori_loop(0, spare // STEP, finish, 0)


def interior(keys, diag, faces, natural, turned, sizes):
    size_x, size_y, depth = sizes
    pairs, block = depth // 2, diag.shape[-1]
    columns, rows = size_x * size_y, AGG_DEV * SLOTS
    squares = lambda shift: pl.BlockSpec((size_y, pairs // 2, LANES, LANES), lambda i: (jnp.maximum(i - shift, 0), 0, 0, 0))
    total = pltpu.VMEM((rows + 1, HALF, LANES), jnp.float32)
    return pl.pallas_call(
        interior_kernel,
        grid=(size_x,),
        in_specs=[
            pl.BlockSpec(memory_space=pltpu.SMEM),
            pl.BlockSpec((size_y, depth, block), lambda i: (i, 0, 0)),
            pl.BlockSpec((1, size_y, depth, block), lambda i: (0, jnp.maximum(i - 1, 0), 0, 0)),
            pl.BlockSpec((1, size_y, depth, block), lambda i: (1, i, 0, 0)),
            pl.BlockSpec((1, size_y, depth, block), lambda i: (2, i, 0, 0)),
            pl.BlockSpec((size_y, pairs, NODES, LANES), lambda i: (i, 0, 0, 0)),
            squares(0), squares(1),
        ],
        out_specs=pl.BlockSpec((rows, HALF, LANES), lambda i: (0, 0, 0)),
        out_shape=jax.ShapeDtypeStruct((rows, HALF, LANES), jnp.float32),
        scratch_shapes=[
            pltpu.VMEM((2, 4, depth * HALF, LANES), jnp.float32), total, total, total, total,
            pltpu.VMEM((STEP // 2, LANES, LANES), jnp.float32),
        ],
        compiler_params=pltpu.CompilerParams(vmem_limit_bytes=28 * MIB),
        cost_estimate=pl.CostEstimate(flops=columns * depth * 14 * NODES**3, bytes_accessed=columns * depth * 6 * block * 2, transcendentals=0),
        name="interior",
    )(keys, diag, faces, faces, faces, natural, turned, turned)


def border_kernel(capacity, owners, place_ref, keys, got_x, got_y, got_z, back_z, tail_x, tail_y, tail_z, turned_x, turned_y,
                  natural_x, natural_y, first_z, last_z, total_ref, out_ref, even_total, odd_total, filled):
    size_y, depth = tail_x.shape[0], tail_x.shape[1]
    size_x = tail_y.shape[0]
    pairs = depth // 2
    rows = total_ref.shape[0]
    places = out_ref.shape[0]
    totals = (even_total, odd_total)

    for total in totals:
        total[...] = jnp.zeros_like(total)

    def key_at(number, i, j, z):
        return keys[number, i, j, z]

    def couple(left0, left1, head):
        return upright(product(jnp.concatenate([left0, left1], axis=1), paired_weights(head))).astype(jnp.bfloat16)

    def ahead(tail, head, turned, key):
        couples = [couple(tail[2 * p], tail[2 * p + 1], head[p]) for p in range(pairs)]
        for h in range(pairs // 2):
            four = two_pairs(product(turned[h], apart(couples[2 * h], couples[2 * h + 1])))
            yield [(totals[number % 2], key(4 * h + number), term) for number, term in enumerate(four)]

    def back(natural, rim, key):
        for h in range(pairs // 2):
            four = [term for p in (2 * h, 2 * h + 1) for term in folded(across(natural[p], rim[p]))]
            yield [(totals[number % 2], key(4 * h + number), term) for number, term in enumerate(four)]

    def add_batches(batches):
        for updates in list(batches):
            add_all(updates)

    @pl.when(place_ref[0] == 0)
    def _():
        add_batches(
            batch for j in range(size_y)
            for batch in ahead(tail_x.at[j], got_x.at[j], turned_x.at[j], functools.partial(key_at, 2, size_x - 1, j)))

    @pl.when(place_ref[0] != 0)
    def _():
        add_batches(
            batch for j in range(size_y) for batch in back(natural_x.at[j], got_x.at[j], functools.partial(key_at, 1, 0, j)))

    @pl.when(place_ref[1] == 0)
    def _():
        add_batches(
            batch for i in range(size_x)
            for batch in ahead(tail_y.at[i], got_y.at[i], turned_y.at[i, 0], functools.partial(key_at, 4, i, size_y - 1)))

    @pl.when(place_ref[1] != 0)
    def _():
        add_batches(
            batch for i in range(size_x) for batch in back(natural_y.at[i, 0], got_y.at[i], functools.partial(key_at, 3, i, 0)))

    batches = []
    for t in range(got_z.shape[0]):
        i, j = 2 * t // size_y, 2 * t % size_y
        front = folded(across(last_z[t], couple(tail_z[2 * t], tail_z[2 * t + 1], got_z[t])))
        past = folded(across(first_z[t], back_z[t]))
        batches.append([(totals[side], keys[6, i, j + side, depth - 1], front[side]) for side in (0, 1)]
                       + [(totals[side], keys[5, i, j + side, 0], past[side]) for side in (0, 1)])
    add_batches(batches)

    for owner in range(places // capacity):
        filled[owner] = 0
    if places * SLOTS != rows:
        out_ref[...] = jnp.zeros_like(out_ref)
    for r in range(rows // SLOTS):
        owner = owners[r]
        spot = owner * capacity + filled[owner]
        filled[owner] = filled[owner] + 1
        for s in range(SLOTS):
            key = r * SLOTS + s
            even, odd = [
                even_total[key, pl.ds(first, HALF // 2, stride=2), :] + odd_total[key, pl.ds(first, HALF // 2, stride=2), :]
                for first in (0, 1)]
            out_ref[spot, HALF * s : HALF * (s + 1), :] = (total_ref[key] + straightened(even, odd)).astype(jnp.bfloat16)


def border(owners, place, keys, operands, turned, natural, ends, capacity, places, sizes):
    size_x, size_y, depth = sizes
    pairs, rows = depth // 2, AGG_DEV * SLOTS
    smem = pl.BlockSpec(memory_space=pltpu.SMEM)
    whole = pl.BlockSpec(memory_space=pltpu.VMEM)
    planes = lambda array: array.reshape((size_x, size_y) + array.shape[1:])
    total = pltpu.VMEM((rows, HALF, LANES), jnp.float32)
    return pl.pallas_call(
        functools.partial(border_kernel, capacity),
        grid=(1,),
        in_specs=[smem, smem, smem] + [whole] * len(operands) + [
            pl.BlockSpec((size_y, pairs // 2, LANES, LANES), lambda i: (size_x - 1, 0, 0, 0)),
            pl.BlockSpec((size_x, 1, pairs // 2, LANES, LANES), lambda i: (0, size_y - 1, 0, 0, 0)),
            pl.BlockSpec((size_y, pairs, NODES, LANES), lambda i: (0, 0, 0, 0)),
            pl.BlockSpec((size_x, 1, pairs, NODES, LANES), lambda i: (0, 0, 0, 0, 0)),
        ] + [whole] * len(ends),
        out_specs=whole,
        out_shape=jax.ShapeDtypeStruct((places, SLOTS * HALF, LANES), jnp.bfloat16),
        scratch_shapes=[total, total, pltpu.SMEM((places // capacity,), jnp.int32)],
        compiler_params=pltpu.CompilerParams(vmem_limit_bytes=18 * MIB),
        name="border",
    )(owners, place, keys, *operands, turned, planes(turned), natural, planes(natural), *ends)


def layout_kernel(source, rows_ref, out_ref, stage):
    group = pl.program_id(0)
    height = out_ref.shape[1]
    for s in range(SLOTS):
        for r in range(height):
            row = source[group * height + r]
            block = rows_ref[jnp.maximum(row, 0), HALF * s : HALF * (s + 1), :].astype(jnp.float32)
            stage[s, pl.ds(r, HALF, stride=height), :] = jnp.where(row >= 0, block, jnp.zeros_like(block))
        for k in range(HALF):
            out_ref[s, :, LANES * k : LANES * (k + 1)] = stage[s, height * k : height * (k + 1), :].astype(jnp.bfloat16)


def laid_out(source, rows, block):
    places, height = rows.shape[0], 8
    return pl.pallas_call(
        layout_kernel,
        grid=(places // height,),
        in_specs=[pl.BlockSpec(memory_space=pltpu.SMEM), pl.BlockSpec(rows.shape, lambda g: (0, 0, 0))],
        out_specs=pl.BlockSpec((SLOTS, height, block), lambda g: (0, g, 0)),
        out_shape=jax.ShapeDtypeStruct((SLOTS, places, block), jnp.bfloat16),
        scratch_shapes=[pltpu.VMEM((SLOTS, height * HALF, LANES), jnp.float32)],
        compiler_params=pltpu.CompilerParams(vmem_limit_bytes=10 * MIB),
        name="layout",
    )(source, rows)


def swap(block, axis):
    assert lax.axis_size(axis) == 2
    return lax.ppermute(block, axis, [(0, 1), (1, 0)])


def shards(a_diag, a_face, prolong, aggregate, pair_slot, row_owner):
    size_x, size_y, size_z, block = a_diag.shape
    sizes = (size_x, size_y, size_z)
    columns = size_x * size_y
    depth = lax.axis_size("gz")
    capacity = max(2, (AGG_DEV + depth - 1) // depth)
    holding = capacity * depth
    diag = a_diag.reshape(columns, size_z, block)
    faces = a_face.reshape(3, columns, size_z, block)
    place = jnp.stack([lax.axis_index("gx"), lax.axis_index("gy")]).astype(jnp.int32)
    keys = aggregate[None] * SLOTS + pair_slot

    natural, turned, swap_x, swap_y, head_z, rim_z, last_z, tail_x, tail_y, tail_z = prepare(
        place, prolong.reshape(columns, size_z, block), faces, sizes)
    got_z = passed_along(head_z, "gz", -1)
    back_z = passed_along(rim_z, "gz", 1)
    got_y = swap(swap_y, "gy")
    got_x = swap(swap_x, "gx")
    total = interior(keys, diag, faces, natural, turned, sizes)
    outgoing = border(
        row_owner, place, keys, (got_x, got_y, got_z, back_z, tail_x, tail_y, tail_z), turned, natural,
        (head_z, last_z, total), capacity, holding, sizes)
    arrived = lax.all_to_all(outgoing, "gz", 0, 0, tiled=True)
    source = jnp.arange(holding, dtype=jnp.int32)
    if holding != AGG_DEV:
        owner_ids = jnp.arange(depth, dtype=jnp.int32)
        counts = jnp.sum((row_owner[:, None] == owner_ids[None, :]).astype(jnp.int32), axis=0)
        arrived_counts = lax.all_to_all(counts, "gz", 0, 0, tiled=True)
        present = source % capacity < jnp.repeat(arrived_counts, capacity)
        target = jnp.cumsum(present.astype(jnp.int32)) - 1
        match = (present[None, :] & (target[None, :] == source[:, None])).astype(jnp.int32)
        source = jnp.sum(match * (source[None, :] + 1), axis=1) - 1
    result = laid_out(source, arrived, block)
    return jnp.transpose(result, (1, 0, 2)).reshape(1, 1, 1, holding, SLOTS, block)


def solution(mesh):
    return jax.shard_map(
        shards,
        mesh=mesh,
        in_specs=(
            P("gx", "gy", "gz", None),
            P(None, "gx", "gy", "gz", None),
            P("gx", "gy", "gz", None),
            P("gx", "gy", "gz"),
            P(None, "gx", "gy", "gz"),
            P(("gx", "gy", "gz")),
        ),
        out_specs=P("gx", "gy", "gz", None, None, None),
        check_vma=False,
    )
```

```python
import functools

import jax
import jax.numpy as jnp
from jax import lax
from jax.experimental import pallas as pl
from jax.experimental.pallas import tpu as pltpu
from jax.sharding import PartitionSpec as P

NODES = 64
SLOTS = 7
AGG_DEV = 24
LANES = 128
HALF = NODES // 2
MIB = 1024 * 1024
STEP = 8


def swapped_along(block, axis, first):
    pairs = [(i, i + 1) for i in range(first, lax.axis_size(axis) - 1, 2)]
    return lax.ppermute(block, axis, pairs + [(i + 1, i) for i, _ in pairs])


def low_lanes(rows):
    return lax.broadcasted_iota(jnp.int32, (rows, LANES), 1) < NODES


def swapped(value):
    return pltpu.roll(value, NODES, 1)


def zero_one(mask):
    return mask.astype(jnp.float32).astype(jnp.bfloat16)


def product(left, right):
    return jnp.dot(left, right, preferred_element_type=jnp.float32)


def across(left, right):
    return lax.dot_general(left, right, (((0,), (0,)), ((), ())), preferred_element_type=jnp.float32)


def spread(column, stage):
    depth = column.shape[0]
    for k in range(column.shape[1] // LANES):
        stage[depth * k : depth * (k + 1), :] = column[:, LANES * k : LANES * (k + 1)].astype(jnp.float32)


def block_of(stage, z, depth):
    return stage[pl.ds(z, HALF, stride=depth), :].astype(jnp.bfloat16)


def stacked_pair(first, second):
    low = low_lanes(HALF)
    even = jnp.where(low, first, swapped(second))
    odd = jnp.where(low, swapped(first), second)
    return jnp.concatenate([even, odd], axis=0)


def in_order(pair):
    row = lax.broadcasted_iota(jnp.int32, (NODES, NODES), 0)
    col = lax.broadcasted_iota(jnp.int32, (NODES, NODES), 1)
    return product(zero_one(row == 2 * (col % HALF) + col // HALF), pair).astype(jnp.bfloat16)


def four_weights(first, second):
    low = low_lanes(NODES)
    zero = jnp.zeros_like(first)
    left = [jnp.where(low, first, zero), jnp.where(low, zero, first), zero, zero]
    right = [zero, zero, jnp.where(low, second, zero), jnp.where(low, zero, second)]
    return jnp.concatenate([jnp.concatenate(left, axis=0), jnp.concatenate(right, axis=0)], axis=1)


def folded(square):
    low = low_lanes(HALF)
    moved = swapped(jnp.where(low, square[HALF : 2 * HALF], square[2 * HALF : 3 * HALF]))
    return [jnp.where(low, square[:HALF], moved), jnp.where(low, moved, square[3 * HALF :])]


def straightened(even, odd):
    low = low_lanes(HALF // 2)
    return jnp.concatenate([jnp.where(low, even, swapped(odd)), jnp.where(low, swapped(even), odd)], axis=0)


def diagonal(square):
    return jnp.where(low_lanes(NODES), square[:NODES], square[NODES:]).astype(jnp.bfloat16)


def apart(first, second):
    zero = jnp.zeros_like(first)
    return jnp.concatenate([jnp.concatenate([first, zero], axis=1), jnp.concatenate([zero, second], axis=1)], axis=0)


def two_pairs(squares):
    return folded(squares[:, :LANES]) + folded(squares[:, LANES:])


def add_all(updates):
    olds = [total[key] for total, key, _ in updates]
    news = []
    for number, (total, key, value) in enumerate(updates):
        for other, other_key, other_value in updates[:number]:
            if other is total:
                value = value + jnp.where(key == other_key, other_value, jnp.zeros_like(other_value))
        news.append(olds[number] + value)
    for (total, key, _), new in zip(updates, news):
        total[key] = new


def prepare_kernel(place_ref, p_ref, fx_ref, fy_ref, fz_ref, natural_ref, turned_ref, swap_x_ref, swap_y_ref, near_z_ref, far_z_ref,
                   first_z_ref, last_z_ref, tail_x_ref, tail_y_ref, tail_z_ref, stages, stages_f, stacks, ends):
    plane = pl.program_id(0)
    size_y, depth = p_ref.shape[0], p_ref.shape[1]
    pairs = depth // 2

    for j in range(size_y):
        stage = stages.at[j]
        spread(p_ref[j], stage)
        block = [block_of(stage, z, depth) for z in range(depth)]
        stacked = [stacked_pair(block[2 * p], block[2 * p + 1]) for p in range(pairs)]
        for p in range(pairs):
            stacks[j, p] = stacked[p]
            natural_ref[j, p] = in_order(stacked[p])
        for h in range(pairs // 2):
            turned_ref[j, h] = jnp.concatenate([stacked[2 * h], stacked[2 * h + 1]], axis=0).T
        ends[0, j] = block[0]
        ends[1, j] = block[depth - 1]
        stage_f = stages_f.at[j]
        spread(fz_ref[0, j], stage_f)
        last = block_of(stage_f, depth - 1, depth)
        ends[2, j] = last

    for t in range(size_y // 2):
        first, last, face = [stacked_pair(ends[kind, 2 * t], ends[kind, 2 * t + 1]) for kind in range(3)]
        head = in_order(first)
        rim = diagonal(across(face, last))
        first_z_ref[t] = head
        last_z_ref[t] = last
        tail_z_ref[t] = face
        near_z_ref[t] = jnp.where(place_ref[2] == 0, rim, head)
        far_z_ref[t] = jnp.where(place_ref[2] == 0, head, rim)

    def faces(source, stage, j, tails, rims):
        spread(source, stage)
        block = [block_of(stage, z, depth) for z in range(depth)]
        for p in range(pairs):
            tails[p] = stacked_pair(block[2 * p], block[2 * p + 1])
            rims[p] = diagonal(across(tails[p], stacks[j, p]))

    @pl.when(place_ref[1] == 0)
    def _():
        faces(fy_ref[0, 0], stages_f.at[0], size_y - 1, tail_y_ref.at[0], swap_y_ref.at[0])

    @pl.when(place_ref[1] != 0)
    def _():
        swap_y_ref[0] = natural_ref[0]

    @pl.when((place_ref[0] == 0) & (plane == pl.num_programs(0) - 1))
    def _():
        for j in range(size_y):
            faces(fx_ref[0, j], stages_f.at[j], j, tail_x_ref.at[j], swap_x_ref.at[j])

    @pl.when((place_ref[0] != 0) & (plane == 0))
    def _():
        swap_x_ref[...] = natural_ref[...]


def prepare(place, prolong, faces, sizes):
    size_x, size_y, depth = sizes
    pairs, block = depth // 2, prolong.shape[-1]
    columns, half = size_x * size_y, size_y // 2
    shape = lambda *dims: jax.ShapeDtypeStruct(dims, jnp.bfloat16)
    by_half = pl.BlockSpec((half, NODES, LANES), lambda i: (i, 0, 0))
    edge = shape(columns // 2, NODES, LANES)
    stage = pltpu.VMEM((size_y, depth * HALF, LANES), jnp.float32)
    return pl.pallas_call(
        prepare_kernel,
        grid=(size_x,),
        in_specs=[
            pl.BlockSpec(memory_space=pltpu.SMEM),
            pl.BlockSpec((size_y, depth, block), lambda i: (i, 0, 0)),
            pl.BlockSpec((1, size_y, depth, block), lambda i: (0, size_x - 1, 0, 0)),
            pl.BlockSpec((1, 1, depth, block), lambda i: (1, i * size_y + size_y - 1, 0, 0)),
            pl.BlockSpec((1, size_y, depth, block), lambda i: (2, i, 0, 0)),
        ],
        out_specs=[
            pl.BlockSpec((size_y, pairs, NODES, LANES), lambda i: (i, 0, 0, 0)),
            pl.BlockSpec((size_y, pairs // 2, LANES, LANES), lambda i: (i, 0, 0, 0)),
            pl.BlockSpec((size_y, pairs, NODES, LANES), lambda i: (0, 0, 0, 0)),
            pl.BlockSpec((1, pairs, NODES, LANES), lambda i: (i, 0, 0, 0)),
            by_half, by_half, by_half, by_half,
            pl.BlockSpec((size_y, pairs, NODES, LANES), lambda i: (0, 0, 0, 0)),
            pl.BlockSpec((1, pairs, NODES, LANES), lambda i: (i, 0, 0, 0)),
            by_half,
        ],
        out_shape=[
            shape(columns, pairs, NODES, LANES), shape(columns, pairs // 2, LANES, LANES),
            shape(size_y, pairs, NODES, LANES), shape(size_x, pairs, NODES, LANES), edge, edge, edge, edge,
            shape(size_y, pairs, NODES, LANES), shape(size_x, pairs, NODES, LANES), edge,
        ],
        scratch_shapes=[
            stage, stage,
            pltpu.VMEM((size_y, pairs, NODES, LANES), jnp.bfloat16),
            pltpu.VMEM((3, size_y, HALF, LANES), jnp.bfloat16),
        ],
        compiler_params=pltpu.CompilerParams(vmem_limit_bytes=48 * MIB),
        name="prepare",
    )(place, prolong, faces, faces, faces)


def interior_kernel(keys, diag_ref, fx_ref, fy_ref, fz_ref, natural_ref, turned_ref, below_ref, out_ref,
                    stages, ahead_even, ahead_odd, behind_even, behind_odd, wide):
    plane = pl.program_id(0)
    size_y, depth = diag_ref.shape[0], diag_ref.shape[1]
    pairs = depth // 2
    spare = out_ref.shape[0]
    ahead, behind = (ahead_even, ahead_odd), (behind_even, behind_odd)
    row_x = jnp.maximum(plane - 1, 0)
    has_x = plane > 0

    @pl.when(plane == 0)
    def _():
        for total in ahead + behind:
            total[...] = jnp.zeros_like(total)

    def couplings(j, stage):
        row_y = jnp.maximum(j - 1, 0)
        for face, source in zip(range(4), (diag_ref[j], fx_ref[0, j], fy_ref[0, row_y], fz_ref[0, j])):
            spread(source, stage.at[face])
        stacked = []
        for face in range(4):
            shift = 1 if face == 3 else 0
            block = [block_of(stage.at[face], z, depth) for z in range(depth)]
            stacked.append([stacked_pair(block[(2 * p - shift) % depth], block[2 * p + 1 - shift]) for p in range(pairs)])
        couples = [[] for _ in range(4)]
        for h in range(pairs // 2):
            left = [jnp.concatenate([stacked[face][2 * h], stacked[face][2 * h + 1]], axis=1) for face in range(4)]
            weights = four_weights(natural_ref[j, 2 * h], natural_ref[j, 2 * h + 1])
            four = product(jnp.concatenate(left, axis=0), weights).astype(jnp.bfloat16)
            for face in range(4):
                rows = four[NODES * face : NODES * (face + 1)]
                for couple in (rows[:, :LANES], rows[:, LANES:]):
                    couples[face].append(swapped(couple) if face == 3 else couple)
        low = low_lanes(NODES)
        along = couples[3]
        couples[3] = [jnp.where(low, along[p], along[min(p + 1, pairs - 1)]) for p in range(pairs)]
        return couples

    def sums(j, couples):
        row_y = jnp.maximum(j - 1, 0)
        has_y = j > 0
        batches = []
        for h in range(pairs // 2):
            turned = (turned_ref[j, h], below_ref[j, h], turned_ref[row_y, h], turned_ref[j, h])
            for face in range(4):
                four = two_pairs(product(turned[face], apart(couples[face][2 * h], couples[face][2 * h + 1])))
                updates = []
                for number, term in enumerate(four):
                    z, side = 4 * h + number, number % 2
                    if face == 0:
                        updates.append((ahead[side], keys[0, plane, j, z], term))
                        continue
                    if face == 1:
                        here, there = keys[2, row_x, j, z], keys[1, plane, j, z]
                        here, there = jnp.where(has_x, here, spare), jnp.where(has_x, there, spare)
                    elif face == 2:
                        here, there = keys[4, plane, row_y, z], keys[3, plane, j, z]
                        here, there = jnp.where(has_y, here, spare), jnp.where(has_y, there, spare)
                    elif z + 1 < depth:
                        here, there = keys[6, plane, j, z], keys[5, plane, j, z + 1]
                    else:
                        continue
                    updates.append((ahead[side], here, term))
                    updates.append((behind[side], there, term))
                batches.append(updates)
        return batches

    def columns(step, carry):
        couples = [couplings(2 * step + u, stages.at[u]) for u in range(2)]
        for updates in [updates for u in range(2) for updates in sums(2 * step + u, couples[u])]:
            add_all(updates)
        return carry

    lax.fori_loop(0, size_y // 2, columns, 0)

    @pl.when(plane == pl.num_programs(0) - 1)
    def _():
        def finish(g, carry):
            low = low_lanes(HALF)
            spots = [(p, [wide.shape[0] * 2 * g + 2 * p + side for side in (0, 1)]) for p in range(wide.shape[0])]
            for p, key in spots:
                one, two = [behind_even[key[side]] + behind_odd[key[side]] for side in (0, 1)]
                upper = jnp.where(low, one, swapped(two))
                lower = jnp.where(low, swapped(one), two)
                wide[p, :, :NODES] = jnp.concatenate([upper, lower], axis=0).T
            for p, key in spots:
                for side in (0, 1):
                    first = wide[p, NODES * side : NODES * side + HALF, :]
                    second = wide[p, NODES * side + HALF : NODES * (side + 1), :]
                    turned = jnp.where(low, first, swapped(second))
                    out_ref[key[side]] = (ahead_even[key[side]] + ahead_odd[key[side]]) + turned
            return carry

        lax.fori_loop(0, spare // (2 * wide.shape[0]), finish, 0)


def interior(keys, diag, faces, natural, turned, sizes):
    size_x, size_y, depth = sizes
    pairs, block = depth // 2, diag.shape[-1]
    columns, rows = size_x * size_y, AGG_DEV * SLOTS
    squares = lambda shift: pl.BlockSpec((size_y, pairs // 2, LANES, LANES), lambda i: (jnp.maximum(i - shift, 0), 0, 0, 0))
    total = pltpu.VMEM((rows + 1, HALF, LANES), jnp.float32)
    return pl.pallas_call(
        interior_kernel,
        grid=(size_x,),
        in_specs=[
            pl.BlockSpec(memory_space=pltpu.SMEM),
            pl.BlockSpec((size_y, depth, block), lambda i: (i, 0, 0)),
            pl.BlockSpec((1, size_y, depth, block), lambda i: (0, jnp.maximum(i - 1, 0), 0, 0)),
            pl.BlockSpec((1, size_y, depth, block), lambda i: (1, i, 0, 0)),
            pl.BlockSpec((1, size_y, depth, block), lambda i: (2, i, 0, 0)),
            pl.BlockSpec((size_y, pairs, NODES, LANES), lambda i: (i, 0, 0, 0)),
            squares(0), squares(1),
        ],
        out_specs=pl.BlockSpec((rows, HALF, LANES), lambda i: (0, 0, 0)),
        out_shape=jax.ShapeDtypeStruct((rows, HALF, LANES), jnp.float32),
        scratch_shapes=[
            pltpu.VMEM((2, 4, depth * HALF, LANES), jnp.float32), total, total, total, total,
            pltpu.VMEM((12, LANES, LANES), jnp.float32),
        ],
        compiler_params=pltpu.CompilerParams(vmem_limit_bytes=28 * MIB),
        cost_estimate=pl.CostEstimate(flops=columns * depth * 14 * NODES**3, bytes_accessed=columns * depth * 6 * block * 2, transcendentals=0),
        name="interior",
    )(keys, diag, faces, faces, faces, natural, turned, turned)


def border_kernel(capacity, owners, place_ref, keys, got_x, got_y, near_z, far_z, tail_x, tail_y, tail_z, turned_x, turned_y,
                  natural_x, natural_y, first_z, last_z, total_ref, out_ref, even_total, odd_total, filled):
    size_y, pairs = tail_x.shape[0], tail_x.shape[1]
    size_x, depth = tail_y.shape[0], 2 * pairs
    rows = total_ref.shape[0]
    places = out_ref.shape[0]
    totals = (even_total, odd_total)

    for total in totals:
        total[...] = jnp.zeros_like(total)

    def key_at(number, i, j, z):
        return keys[number, i, j, z]

    def couplings(tail, head):
        left = jnp.concatenate(tail, axis=1)
        four = product(left, four_weights(*head)).astype(jnp.bfloat16)
        return four[:, :LANES], four[:, LANES:]

    def ahead(tail, head, turned, key):
        for h in range(pairs // 2):
            couples = couplings([tail[2 * h], tail[2 * h + 1]], [head[2 * h], head[2 * h + 1]])
            four = two_pairs(product(turned[h], apart(*couples)))
            yield [(totals[number % 2], key(4 * h + number), term) for number, term in enumerate(four)]

    def back(natural, rim, key):
        for h in range(pairs // 2):
            four = [term for p in (2 * h, 2 * h + 1) for term in folded(across(natural[p], rim[p]))]
            yield [(totals[number % 2], key(4 * h + number), term) for number, term in enumerate(four)]

    def add_batches(batches):
        for updates in list(batches):
            add_all(updates)

    @pl.when(place_ref[0] == 0)
    def _():
        add_batches(
            batch for j in range(size_y)
            for batch in ahead(tail_x.at[j], got_x.at[j], turned_x.at[j], functools.partial(key_at, 2, size_x - 1, j)))

    @pl.when(place_ref[0] != 0)
    def _():
        add_batches(
            batch for j in range(size_y) for batch in back(natural_x.at[j], got_x.at[j], functools.partial(key_at, 1, 0, j)))

    @pl.when(place_ref[1] == 0)
    def _():
        add_batches(
            batch for i in range(size_x)
            for batch in ahead(tail_y.at[i], got_y.at[i], turned_y.at[i, 0], functools.partial(key_at, 4, i, size_y - 1)))

    @pl.when(place_ref[1] != 0)
    def _():
        add_batches(
            batch for i in range(size_x) for batch in back(natural_y.at[i, 0], got_y.at[i], functools.partial(key_at, 3, i, 0)))

    batches = []
    even = place_ref[2] == 0
    for t in range(0, near_z.shape[0], 2):
        heads = [jnp.where(even, near_z[u], far_z[u]) for u in (t, t + 1)]
        couples = couplings([tail_z[t], tail_z[t + 1]], heads)
        for u in (t, t + 1):
            i, j = 2 * u // size_y, 2 * u % size_y
            front = folded(across(last_z[u], couples[u - t]))
            past = folded(across(first_z[u], jnp.where(even, far_z[u], near_z[u])))
            batches.append([(totals[side], keys[6, i, j + side, depth - 1], front[side]) for side in (0, 1)]
                           + [(totals[side], keys[5, i, j + side, 0], past[side]) for side in (0, 1)])
    add_batches(batches)

    for owner in range(places // capacity):
        filled[owner] = 0
    if places * SLOTS != rows:
        out_ref[...] = jnp.zeros_like(out_ref)
    for r in range(rows // SLOTS):
        owner = owners[r]
        spot = owner * capacity + filled[owner]
        filled[owner] = filled[owner] + 1
        for s in range(SLOTS):
            key = r * SLOTS + s
            even, odd = [
                sum(total[key, pl.ds(first, HALF // 2, stride=2), :] for total in (total_ref,) + totals) for first in (0, 1)]
            out_ref[spot, HALF * s : HALF * (s + 1), :] = straightened(even, odd).astype(jnp.bfloat16)


def border(owners, place, keys, operands, turned, natural, ends, capacity, places, sizes):
    size_x, size_y, depth = sizes
    pairs, rows = depth // 2, AGG_DEV * SLOTS
    smem = pl.BlockSpec(memory_space=pltpu.SMEM)
    whole = pl.BlockSpec(memory_space=pltpu.VMEM)
    planes = lambda array: array.reshape((size_x, size_y) + array.shape[1:])
    total = pltpu.VMEM((rows, HALF, LANES), jnp.float32)
    return pl.pallas_call(
        functools.partial(border_kernel, capacity),
        grid=(1,),
        in_specs=[smem, smem, smem] + [whole] * len(operands) + [
            pl.BlockSpec((size_y, pairs // 2, LANES, LANES), lambda i: (size_x - 1, 0, 0, 0)),
            pl.BlockSpec((size_x, 1, pairs // 2, LANES, LANES), lambda i: (0, size_y - 1, 0, 0, 0)),
            pl.BlockSpec((size_y, pairs, NODES, LANES), lambda i: (0, 0, 0, 0)),
            pl.BlockSpec((size_x, 1, pairs, NODES, LANES), lambda i: (0, 0, 0, 0, 0)),
        ] + [whole] * len(ends),
        out_specs=whole,
        out_shape=jax.ShapeDtypeStruct((places, SLOTS * HALF, LANES), jnp.bfloat16),
        scratch_shapes=[total, total, pltpu.SMEM((places // capacity,), jnp.int32)],
        compiler_params=pltpu.CompilerParams(vmem_limit_bytes=18 * MIB),
        name="border",
    )(owners, place, keys, *operands, turned, planes(turned), natural, planes(natural), *ends)


def layout_kernel(source, rows_ref, out_ref, stage):
    group = pl.program_id(0)
    height = out_ref.shape[1]
    for s in range(SLOTS):
        for r in range(height):
            row = source[group * height + r]
            block = rows_ref[jnp.maximum(row, 0), HALF * s : HALF * (s + 1), :].astype(jnp.float32)
            stage[s, pl.ds(r, HALF, stride=height), :] = jnp.where(row >= 0, block, jnp.zeros_like(block))
        for k in range(HALF):
            out_ref[s, :, LANES * k : LANES * (k + 1)] = stage[s, height * k : height * (k + 1), :].astype(jnp.bfloat16)


def laid_out(source, rows, block):
    places, height = rows.shape[0], 8
    return pl.pallas_call(
        layout_kernel,
        grid=(places // height,),
        in_specs=[pl.BlockSpec(memory_space=pltpu.SMEM), pl.BlockSpec(rows.shape, lambda g: (0, 0, 0))],
        out_specs=pl.BlockSpec((SLOTS, height, block), lambda g: (0, g, 0)),
        out_shape=jax.ShapeDtypeStruct((SLOTS, places, block), jnp.bfloat16),
        scratch_shapes=[pltpu.VMEM((SLOTS, height * HALF, LANES), jnp.float32)],
        compiler_params=pltpu.CompilerParams(vmem_limit_bytes=10 * MIB),
        name="layout",
    )(source, rows)


def shards(a_diag, a_face, prolong, aggregate, pair_slot, row_owner):
    size_x, size_y, size_z, block = a_diag.shape
    sizes = (size_x, size_y, size_z)
    columns = size_x * size_y
    depth = lax.axis_size("gz")
    capacity = max(2, (AGG_DEV + depth - 1) // depth)
    holding = capacity * depth
    diag = a_diag.reshape(columns, size_z, block)
    faces = a_face.reshape(3, columns, size_z, block)
    assert lax.axis_size("gx") == 2 and lax.axis_size("gy") == 2
    place = jnp.stack([lax.axis_index("gx"), lax.axis_index("gy"), lax.axis_index("gz") % 2]).astype(jnp.int32)
    keys = aggregate[None] * SLOTS + pair_slot

    natural, turned, swap_x, swap_y, near_z, far_z, first_z, last_z, tail_x, tail_y, tail_z = prepare(
        place, prolong.reshape(columns, size_z, block), faces, sizes)
    near_z = swapped_along(near_z, "gz", 0)
    far_z = swapped_along(far_z, "gz", 1)
    got_y = swapped_along(swap_y, "gy", 0)
    got_x = swapped_along(swap_x, "gx", 0)
    total = interior(keys, diag, faces, natural, turned, sizes)
    outgoing = border(
        row_owner, place, keys, (got_x, got_y, near_z, far_z, tail_x, tail_y, tail_z), turned, natural,
        (first_z, last_z, total), capacity, holding, sizes)
    arrived = lax.all_to_all(outgoing, "gz", 0, 0, tiled=True)
    source = jnp.arange(holding, dtype=jnp.int32)
    if holding != AGG_DEV:
        owner_ids = jnp.arange(depth, dtype=jnp.int32)
        counts = jnp.sum((row_owner[:, None] == owner_ids[None, :]).astype(jnp.int32), axis=0)
        arrived_counts = lax.all_to_all(counts, "gz", 0, 0, tiled=True)
        present = source % capacity < jnp.repeat(arrived_counts, capacity)
        target = jnp.cumsum(present.astype(jnp.int32)) - 1
        match = (present[None, :] & (target[None, :] == source[:, None])).astype(jnp.int32)
        source = jnp.sum(match * (source[None, :] + 1), axis=1) - 1
    result = laid_out(source, arrived, block)
    return jnp.transpose(result, (1, 0, 2)).reshape(1, 1, 1, holding, SLOTS, block)


def solution(mesh):
    return jax.shard_map(
        shards,
        mesh=mesh,
        in_specs=(
            P("gx", "gy", "gz", None),
            P(None, "gx", "gy", "gz", None),
            P("gx", "gy", "gz", None),
            P("gx", "gy", "gz"),
            P(None, "gx", "gy", "gz"),
            P(("gx", "gy", "gz")),
        ),
        out_specs=P("gx", "gy", "gz", None, None, None),
        check_vma=False,
    )
```

```python
import functools

import jax
import jax.numpy as jnp
from jax import lax
from jax.experimental import pallas as pl
from jax.experimental.pallas import tpu as pltpu
from jax.sharding import PartitionSpec as P

NODES = 64
SLOTS = 7
AGG_DEV = 24
LANES = 128
HALF = NODES // 2
MIB = 1024 * 1024
STEP = 8


def swapped_along(block, axis, first):
    pairs = [(i, i + 1) for i in range(first, lax.axis_size(axis) - 1, 2)]
    return lax.ppermute(block, axis, pairs + [(i + 1, i) for i, _ in pairs])


def low_lanes(rows):
    return lax.broadcasted_iota(jnp.int32, (rows, LANES), 1) < NODES


def swapped(value):
    return pltpu.roll(value, NODES, 1)


def zero_one(mask):
    return mask.astype(jnp.float32).astype(jnp.bfloat16)


def product(left, right):
    return jnp.dot(left, right, preferred_element_type=jnp.float32)


def across(left, right):
    return lax.dot_general(left, right, (((0,), (0,)), ((), ())), preferred_element_type=jnp.float32)


def spread(column, stage):
    depth = column.shape[0]
    for k in range(column.shape[1] // LANES):
        stage[depth * k : depth * (k + 1), :] = column[:, LANES * k : LANES * (k + 1)].astype(jnp.float32)


def block_of(stage, z, depth):
    return stage[pl.ds(z, HALF, stride=depth), :].astype(jnp.bfloat16)


def stacked_pair(first, second):
    low = low_lanes(HALF)
    even = jnp.where(low, first, swapped(second))
    odd = jnp.where(low, swapped(first), second)
    return jnp.concatenate([even, odd], axis=0)


def in_order(pair):
    row = lax.broadcasted_iota(jnp.int32, (NODES, NODES), 0)
    col = lax.broadcasted_iota(jnp.int32, (NODES, NODES), 1)
    return product(zero_one(row == 2 * (col % HALF) + col // HALF), pair).astype(jnp.bfloat16)


def four_weights(first, second):
    low = low_lanes(NODES)
    zero = jnp.zeros_like(first)
    left = [jnp.where(low, first, zero), jnp.where(low, zero, first), zero, zero]
    right = [zero, zero, jnp.where(low, second, zero), jnp.where(low, zero, second)]
    return jnp.concatenate([jnp.concatenate(left, axis=0), jnp.concatenate(right, axis=0)], axis=1)


def four_turned(first, second):
    low = low_lanes(NODES)
    zero = jnp.zeros_like(first)
    left = [jnp.where(low, first, zero), zero, jnp.where(low, zero, first), zero]
    right = [zero, jnp.where(low, second, zero), zero, jnp.where(low, zero, second)]
    return jnp.concatenate([jnp.concatenate(left, axis=0), jnp.concatenate(right, axis=0)], axis=1)


def four_across(first, second):
    turned = jnp.concatenate([first, second], axis=0).T
    return jnp.concatenate([turned[:NODES], turned[NODES:]], axis=1)


def folded_pair(pair):
    low = low_lanes(HALF)
    upper, lower = pair[:HALF], pair[HALF:]
    return [jnp.where(low, upper, swapped(lower)), jnp.where(low, swapped(upper), lower)]


def folded(square):
    low = low_lanes(HALF)
    moved = swapped(jnp.where(low, square[HALF : 2 * HALF], square[2 * HALF : 3 * HALF]))
    return [jnp.where(low, square[:HALF], moved), jnp.where(low, moved, square[3 * HALF :])]


def straightened(even, odd):
    low = low_lanes(HALF // 2)
    return jnp.concatenate([jnp.where(low, even, swapped(odd)), jnp.where(low, swapped(even), odd)], axis=0)


def diagonal(square):
    return jnp.where(low_lanes(NODES), square[:NODES], square[NODES:]).astype(jnp.bfloat16)


def apart(first, second):
    zero = jnp.zeros_like(first)
    return jnp.concatenate([jnp.concatenate([first, zero], axis=1), jnp.concatenate([zero, second], axis=1)], axis=0)


def two_pairs(squares):
    return folded(squares[:, :LANES]) + folded(squares[:, LANES:])


def add_all(updates):
    olds = [total[key] for total, key, _ in updates]
    news = []
    for number, (total, key, value) in enumerate(updates):
        for other, other_key, other_value in updates[:number]:
            if other is total:
                value = value + jnp.where(key == other_key, other_value, jnp.zeros_like(other_value))
        news.append(olds[number] + value)
    for (total, key, _), new in zip(updates, news):
        total[key] = new


def prepare_kernel(place_ref, p_ref, fx_ref, fy_ref, fz_ref, natural_ref, stacked_ref, swap_x_ref, swap_y_ref, near_z_ref, far_z_ref,
                   first_z_ref, last_z_ref, tail_x_ref, tail_y_ref, tail_z_ref, turned_x_ref, turned_y_ref, stages, stages_f, ends):
    plane = pl.program_id(0)
    size_y, depth = p_ref.shape[0], p_ref.shape[1]
    pairs = depth // 2

    for j in range(size_y):
        stage = stages.at[j]
        spread(p_ref[j], stage)
        block = [block_of(stage, z, depth) for z in range(depth)]
        stacked = [stacked_pair(block[2 * p], block[2 * p + 1]) for p in range(pairs)]
        for p in range(pairs):
            stacked_ref[j, p] = stacked[p]
            natural_ref[j, p] = in_order(stacked[p])
        ends[0, j] = block[0]
        ends[1, j] = block[depth - 1]
        stage_f = stages_f.at[j]
        spread(fz_ref[0, j], stage_f)
        last = block_of(stage_f, depth - 1, depth)
        ends[2, j] = last

    for t in range(size_y // 2):
        first, last, face = [stacked_pair(ends[kind, 2 * t], ends[kind, 2 * t + 1]) for kind in range(3)]
        head = in_order(first)
        rim = diagonal(across(face, last))
        first_z_ref[t] = head
        last_z_ref[t] = last
        tail_z_ref[t] = face
        near_z_ref[t] = jnp.where(place_ref[2] == 0, rim, head)
        far_z_ref[t] = jnp.where(place_ref[2] == 0, head, rim)

    def faces(source, stage, j, tails, rims, turned):
        spread(source, stage)
        block = [block_of(stage, z, depth) for z in range(depth)]
        for p in range(pairs):
            tails[p] = stacked_pair(block[2 * p], block[2 * p + 1])
            rims[p] = diagonal(across(tails[p], stacked_ref[j, p]))
        for h in range(pairs // 2):
            turned[h] = jnp.concatenate([stacked_ref[j, 2 * h], stacked_ref[j, 2 * h + 1]], axis=0).T

    @pl.when(place_ref[1] == 0)
    def _():
        faces(fy_ref[0, 0], stages_f.at[0], size_y - 1, tail_y_ref.at[0], swap_y_ref.at[0], turned_y_ref.at[0])

    @pl.when(place_ref[1] != 0)
    def _():
        swap_y_ref[0] = natural_ref[0]

    @pl.when((place_ref[0] == 0) & (plane == pl.num_programs(0) - 1))
    def _():
        for j in range(size_y):
            faces(fx_ref[0, j], stages_f.at[j], j, tail_x_ref.at[j], swap_x_ref.at[j], turned_x_ref.at[j])

    @pl.when((place_ref[0] != 0) & (plane == 0))
    def _():
        swap_x_ref[...] = natural_ref[...]


def prepare(place, prolong, faces, sizes):
    size_x, size_y, depth = sizes
    pairs, block = depth // 2, prolong.shape[-1]
    columns, half = size_x * size_y, size_y // 2
    shape = lambda *dims: jax.ShapeDtypeStruct(dims, jnp.bfloat16)
    by_half = pl.BlockSpec((half, NODES, LANES), lambda i: (i, 0, 0))
    edge = shape(columns // 2, NODES, LANES)
    stage = pltpu.VMEM((size_y, depth * HALF, LANES), jnp.float32)
    return pl.pallas_call(
        prepare_kernel,
        grid=(size_x,),
        in_specs=[
            pl.BlockSpec(memory_space=pltpu.SMEM),
            pl.BlockSpec((size_y, depth, block), lambda i: (i, 0, 0)),
            pl.BlockSpec((1, size_y, depth, block), lambda i: (0, size_x - 1, 0, 0)),
            pl.BlockSpec((1, 1, depth, block), lambda i: (1, i * size_y + size_y - 1, 0, 0)),
            pl.BlockSpec((1, size_y, depth, block), lambda i: (2, i, 0, 0)),
        ],
        out_specs=[
            pl.BlockSpec((size_y, pairs, NODES, LANES), lambda i: (i, 0, 0, 0)),
            pl.BlockSpec((size_y, pairs, NODES, LANES), lambda i: (i, 0, 0, 0)),
            pl.BlockSpec((size_y, pairs, NODES, LANES), lambda i: (0, 0, 0, 0)),
            pl.BlockSpec((1, pairs, NODES, LANES), lambda i: (i, 0, 0, 0)),
            by_half, by_half, by_half, by_half,
            pl.BlockSpec((size_y, pairs, NODES, LANES), lambda i: (0, 0, 0, 0)),
            pl.BlockSpec((1, pairs, NODES, LANES), lambda i: (i, 0, 0, 0)),
            by_half,
            pl.BlockSpec((size_y, pairs // 2, LANES, LANES), lambda i: (0, 0, 0, 0)),
            pl.BlockSpec((1, pairs // 2, LANES, LANES), lambda i: (i, 0, 0, 0)),
        ],
        out_shape=[
            shape(columns, pairs, NODES, LANES), shape(columns, pairs, NODES, LANES),
            shape(size_y, pairs, NODES, LANES), shape(size_x, pairs, NODES, LANES), edge, edge, edge, edge,
            shape(size_y, pairs, NODES, LANES), shape(size_x, pairs, NODES, LANES), edge,
            shape(size_y, pairs // 2, LANES, LANES), shape(size_x, pairs // 2, LANES, LANES),
        ],
        scratch_shapes=[
            stage, stage,
            pltpu.VMEM((3, size_y, HALF, LANES), jnp.bfloat16),
        ],
        compiler_params=pltpu.CompilerParams(vmem_limit_bytes=48 * MIB),
        name="prepare",
    )(place, prolong, faces, faces, faces)


def interior_kernel(keys, diag_ref, face_ref, natural_ref, stacked_ref, out_ref,
                    stages, couples, ahead_even, ahead_odd, behind_even, behind_odd, wide):
    _, size_x, size_y, depth = keys.shape
    pairs = depth // 2
    spare = out_ref.shape[0]
    ahead, behind = (ahead_even, ahead_odd), (behind_even, behind_odd)

    for total in ahead + behind:
        total[...] = jnp.zeros_like(total)

    def couplings(column, stage):
        below_x = jnp.maximum(column - size_y, 0)
        below_y = jnp.maximum(column - 1, 0)
        places = (column, below_x, below_y, column)
        sources = (diag_ref[column], face_ref[0, below_x], face_ref[1, below_y], face_ref[2, column])
        stacked = []
        for face in range(4):
            spread(sources[face], stage.at[face])
            shift = 1 if face == 3 else 0
            block = [block_of(stage.at[face], z, depth) for z in range(depth)]
            stacked.append([stacked_pair(block[(2 * p - shift) % depth], block[2 * p + 1 - shift]) for p in range(pairs)])
        found = [[] for _ in range(4)]
        for h in range(pairs // 2):
            left = [jnp.concatenate([stacked[face][2 * h], stacked[face][2 * h + 1]], axis=1) for face in range(4)]
            weights = four_weights(natural_ref[column, 2 * h], natural_ref[column, 2 * h + 1])
            four = product(jnp.concatenate(left, axis=0), weights).astype(jnp.bfloat16)
            for face in range(4):
                rows = four[NODES * face : NODES * (face + 1)]
                for couple in (rows[:, :LANES], rows[:, LANES:]):
                    found[face].append(swapped(couple) if face == 3 else couple)
        low = low_lanes(NODES)
        along = found[3]
        found[3] = [jnp.where(low, along[p], along[min(p + 1, pairs - 1)]) for p in range(pairs)]
        for face in range(4):
            for h in range(pairs // 2):
                couples[places[face], h, face] = four_across(found[face][2 * h], found[face][2 * h + 1])

    def form(step, carry):
        for u in range(2):
            couplings(2 * step + u, stages.at[u])
        return carry

    lax.fori_loop(0, size_x * size_y // 2, form, 0)

    def sums(i, j):
        has_x, has_y = i + 1 < size_x, j + 1 < size_y
        next_x, next_y = jnp.minimum(i + 1, size_x - 1), jnp.minimum(j + 1, size_y - 1)
        batches = []
        for h in range(pairs // 2):
            column = i * size_y + j
            weights = four_turned(stacked_ref[column, 2 * h], stacked_ref[column, 2 * h + 1])
            terms = product(couples[column, h].reshape(4 * NODES, 4 * NODES), weights)
            for face in range(4):
                rows = terms[NODES * face : NODES * (face + 1)]
                four = folded_pair(rows[:, :LANES]) + folded_pair(rows[:, LANES:])
                updates = []
                for number, term in enumerate(four):
                    z, side = 4 * h + number, number % 2
                    if face == 0:
                        updates.append((ahead[side], keys[0, i, j, z], term))
                        continue
                    if face == 1:
                        here, there = keys[2, i, j, z], keys[1, next_x, j, z]
                        here, there = jnp.where(has_x, here, spare), jnp.where(has_x, there, spare)
                    elif face == 2:
                        here, there = keys[4, i, j, z], keys[3, i, next_y, z]
                        here, there = jnp.where(has_y, here, spare), jnp.where(has_y, there, spare)
                    elif z + 1 < depth:
                        here, there = keys[6, i, j, z], keys[5, i, j, z + 1]
                    else:
                        continue
                    updates.append((ahead[side], here, term))
                    updates.append((behind[side], there, term))
                batches.append(updates)
        return batches

    def add(step, carry):
        i, first = step // (size_y // 2), 2 * (step % (size_y // 2))
        for updates in [updates for u in range(2) for updates in sums(i, first + u)]:
            add_all(updates)
        return carry

    lax.fori_loop(0, size_x * size_y // 2, add, 0)

    def finish(g, carry):
        low = low_lanes(HALF)
        spots = [(p, [wide.shape[0] * 2 * g + 2 * p + side for side in (0, 1)]) for p in range(wide.shape[0])]
        for p, key in spots:
            one, two = [ahead_even[key[side]] + ahead_odd[key[side]] for side in (0, 1)]
            upper = jnp.where(low, one, swapped(two))
            lower = jnp.where(low, swapped(one), two)
            wide[p, :, :NODES] = jnp.concatenate([upper, lower], axis=0).T
        for p, key in spots:
            for side in (0, 1):
                first = wide[p, NODES * side : NODES * side + HALF, :]
                second = wide[p, NODES * side + HALF : NODES * (side + 1), :]
                turned = jnp.where(low, first, swapped(second))
                out_ref[key[side]] = (behind_even[key[side]] + behind_odd[key[side]]) + turned
        return carry

    lax.fori_loop(0, spare // (2 * wide.shape[0]), finish, 0)


def interior(keys, diag, faces, natural, stacked, sizes):
    size_x, size_y, depth = sizes
    pairs, block = depth // 2, diag.shape[-1]
    columns, rows = size_x * size_y, AGG_DEV * SLOTS
    total = pltpu.VMEM((rows + 1, HALF, LANES), jnp.float32)
    whole = pl.BlockSpec(memory_space=pltpu.VMEM)
    return pl.pallas_call(
        interior_kernel,
        in_specs=[pl.BlockSpec(memory_space=pltpu.SMEM), whole, whole, whole, whole],
        out_specs=whole,
        out_shape=jax.ShapeDtypeStruct((rows, HALF, LANES), jnp.float32),
        scratch_shapes=[
            pltpu.VMEM((2, 4, depth * HALF, LANES), jnp.float32),
            pltpu.VMEM((columns, pairs // 2, 4, NODES, 4 * NODES), jnp.bfloat16),
            total, total, total, total,
            pltpu.VMEM((12, LANES, LANES), jnp.float32),
        ],
        compiler_params=pltpu.CompilerParams(vmem_limit_bytes=28 * MIB),
        cost_estimate=pl.CostEstimate(flops=columns * depth * 14 * NODES**3, bytes_accessed=columns * depth * 6 * block * 2, transcendentals=0),
        name="interior",
    )(keys, diag, faces, natural, stacked)


def border_kernel(capacity, owners, place_ref, keys, got_x, got_y, near_z, far_z, tail_x, tail_y, tail_z, turned_x, turned_y,
                  natural_x, natural_y, first_z, last_z, start_ref, out_ref, total, filled):
    size_y, pairs = tail_x.shape[0], tail_x.shape[1]
    size_x, depth = tail_y.shape[0], 2 * pairs
    rows = start_ref.shape[0]
    places = out_ref.shape[0]

    def key_at(number, i, j, z):
        return keys[number, i, j, z]

    def couplings(tail, head):
        left = jnp.concatenate(tail, axis=1)
        four = product(left, four_weights(*head)).astype(jnp.bfloat16)
        return four[:, :LANES], four[:, LANES:]

    def ahead(tail, head, turned, key):
        for h in range(pairs // 2):
            couples = couplings([tail[2 * h], tail[2 * h + 1]], [head[2 * h], head[2 * h + 1]])
            four = two_pairs(product(turned[h], apart(*couples)))
            yield [(total, key(4 * h + number), term) for number, term in enumerate(four)]

    def back(natural, rim, key):
        for h in range(pairs // 2):
            four = [term for p in (2 * h, 2 * h + 1) for term in folded(across(natural[p], rim[p]))]
            yield [(total, key(4 * h + number), term) for number, term in enumerate(four)]

    def add_batches(batches):
        for updates in list(batches):
            add_all(updates)

    @pl.when(place_ref[0] == 0)
    def _():
        add_batches(
            batch for j in range(size_y)
            for batch in ahead(tail_x.at[j], got_x.at[j], turned_x.at[j], functools.partial(key_at, 2, size_x - 1, j)))

    @pl.when(place_ref[0] != 0)
    def _():
        add_batches(
            batch for j in range(size_y) for batch in back(natural_x.at[j], got_x.at[j], functools.partial(key_at, 1, 0, j)))

    @pl.when(place_ref[1] == 0)
    def _():
        add_batches(
            batch for i in range(size_x)
            for batch in ahead(tail_y.at[i], got_y.at[i], turned_y.at[i], functools.partial(key_at, 4, i, size_y - 1)))

    @pl.when(place_ref[1] != 0)
    def _():
        add_batches(
            batch for i in range(size_x) for batch in back(natural_y.at[i, 0], got_y.at[i], functools.partial(key_at, 3, i, 0)))

    batches = []
    even = place_ref[2] == 0
    for t in range(0, near_z.shape[0], 2):
        heads = [jnp.where(even, near_z[u], far_z[u]) for u in (t, t + 1)]
        couples = couplings([tail_z[t], tail_z[t + 1]], heads)
        for u in (t, t + 1):
            i, j = 2 * u // size_y, 2 * u % size_y
            front = folded(across(last_z[u], couples[u - t]))
            past = folded(across(first_z[u], jnp.where(even, far_z[u], near_z[u])))
            batches.append([(total, keys[6, i, j + side, depth - 1], front[side]) for side in (0, 1)]
                           + [(total, keys[5, i, j + side, 0], past[side]) for side in (0, 1)])
    add_batches(batches)

    for owner in range(places // capacity):
        filled[owner] = 0
    if places * SLOTS != rows:
        out_ref[...] = jnp.zeros_like(out_ref)
    for r in range(rows // SLOTS):
        owner = owners[r]
        spot = owner * capacity + filled[owner]
        filled[owner] = filled[owner] + 1
        for s in range(SLOTS):
            key = r * SLOTS + s
            even, odd = [total[key, pl.ds(first, HALF // 2, stride=2), :] for first in (0, 1)]
            out_ref[spot, HALF * s : HALF * (s + 1), :] = straightened(even, odd).astype(jnp.bfloat16)


def border(owners, place, keys, operands, natural, ends, total, capacity, places, sizes):
    size_x, size_y, depth = sizes
    pairs = depth // 2
    smem = pl.BlockSpec(memory_space=pltpu.SMEM)
    whole = pl.BlockSpec(memory_space=pltpu.VMEM)
    before = 3 + len(operands) + 2 + len(ends)
    return pl.pallas_call(
        functools.partial(border_kernel, capacity),
        grid=(1,),
        in_specs=[smem, smem, smem] + [whole] * len(operands) + [
            pl.BlockSpec((size_y, pairs, NODES, LANES), lambda i: (0, 0, 0, 0)),
            pl.BlockSpec((size_x, 1, pairs, NODES, LANES), lambda i: (0, 0, 0, 0, 0)),
        ] + [whole] * (len(ends) + 1),
        out_specs=[whole, whole],
        out_shape=[
            jax.ShapeDtypeStruct((places, SLOTS * HALF, LANES), jnp.bfloat16),
            jax.ShapeDtypeStruct(total.shape, total.dtype),
        ],
        input_output_aliases={before: 1},
        scratch_shapes=[pltpu.SMEM((places // capacity,), jnp.int32)],
        compiler_params=pltpu.CompilerParams(vmem_limit_bytes=18 * MIB),
        name="border",
    )(owners, place, keys, *operands, natural, natural.reshape((size_x, size_y) + natural.shape[1:]), *ends, total)[0]


def layout_kernel(*refs):
    source, (rows_ref, out_ref, stage) = refs[:-3], refs[-3:]
    group = pl.program_id(0)
    height = out_ref.shape[1]
    for s in range(SLOTS):
        for r in range(height):
            row = group * height + r
            if source:
                row = source[0][row]
            block = rows_ref[jnp.maximum(row, 0), HALF * s : HALF * (s + 1), :].astype(jnp.float32)
            if source:
                block = jnp.where(row >= 0, block, jnp.zeros_like(block))
            stage[s, pl.ds(r, HALF, stride=height), :] = block
        for k in range(HALF):
            out_ref[s, :, LANES * k : LANES * (k + 1)] = stage[s, height * k : height * (k + 1), :].astype(jnp.bfloat16)


def laid_out(source, rows, block):
    places, height = rows.shape[0], 8
    return pl.pallas_call(
        layout_kernel,
        grid=(places // height,),
        in_specs=[pl.BlockSpec(memory_space=pltpu.SMEM)] * len(source) + [pl.BlockSpec(memory_space=pltpu.VMEM)],
        out_specs=pl.BlockSpec((SLOTS, height, block), lambda g: (0, g, 0)),
        out_shape=jax.ShapeDtypeStruct((SLOTS, places, block), jnp.bfloat16),
        scratch_shapes=[pltpu.VMEM((SLOTS, height * HALF, LANES), jnp.float32)],
        compiler_params=pltpu.CompilerParams(vmem_limit_bytes=10 * MIB),
        name="layout",
    )(*source, rows)


def shards(a_diag, a_face, prolong, aggregate, pair_slot, row_owner):
    size_x, size_y, size_z, block = a_diag.shape
    sizes = (size_x, size_y, size_z)
    columns = size_x * size_y
    depth = lax.axis_size("gz")
    capacity = max(2, (AGG_DEV + depth - 1) // depth)
    holding = capacity * depth
    diag = a_diag.reshape(columns, size_z, block)
    faces = a_face.reshape(3, columns, size_z, block)
    assert lax.axis_size("gx") == 2 and lax.axis_size("gy") == 2
    place = jnp.stack([lax.axis_index("gx"), lax.axis_index("gy"), lax.axis_index("gz") % 2]).astype(jnp.int32)
    keys = aggregate[None] * SLOTS + pair_slot

    (natural, stacked, swap_x, swap_y, near_z, far_z, first_z, last_z, tail_x, tail_y, tail_z, turned_x, turned_y) = prepare(
        place, prolong.reshape(columns, size_z, block), faces, sizes)
    near_z = swapped_along(near_z, "gz", 0)
    far_z = swapped_along(far_z, "gz", 1)
    got_y = swapped_along(swap_y, "gy", 0)
    got_x = swapped_along(swap_x, "gx", 0)
    total = interior(keys, diag, faces, natural, stacked, sizes)
    outgoing = border(
        row_owner, place, keys, (got_x, got_y, near_z, far_z, tail_x, tail_y, tail_z, turned_x, turned_y), natural,
        (first_z, last_z), total, capacity, holding, sizes)
    arrived = lax.all_to_all(outgoing, "gz", 0, 0, tiled=True)
    sources = []
    if holding != AGG_DEV:
        source = jnp.arange(holding, dtype=jnp.int32)
        owner_ids = jnp.arange(depth, dtype=jnp.int32)
        counts = jnp.sum((row_owner[:, None] == owner_ids[None, :]).astype(jnp.int32), axis=0)
        arrived_counts = lax.all_to_all(counts, "gz", 0, 0, tiled=True)
        present = source % capacity < jnp.repeat(arrived_counts, capacity)
        target = jnp.cumsum(present.astype(jnp.int32)) - 1
        match = (present[None, :] & (target[None, :] == source[:, None])).astype(jnp.int32)
        sources = [jnp.sum(match * (source[None, :] + 1), axis=1) - 1]
    result = laid_out(sources, arrived, block)
    return jnp.transpose(result, (1, 0, 2)).reshape(1, 1, 1, holding, SLOTS, block)


def solution(mesh):
    return jax.shard_map(
        shards,
        mesh=mesh,
        in_specs=(
            P("gx", "gy", "gz", None),
            P(None, "gx", "gy", "gz", None),
            P("gx", "gy", "gz", None),
            P("gx", "gy", "gz"),
            P(None, "gx", "gy", "gz"),
            P(("gx", "gy", "gz")),
        ),
        out_specs=P("gx", "gy", "gz", None, None, None),
        check_vma=False,
    )
```

```python
import functools

import jax
import jax.numpy as jnp
from jax import lax
from jax.experimental import pallas as pl
from jax.experimental.pallas import tpu as pltpu
from jax.sharding import PartitionSpec as P

NODES = 64
SLOTS = 7
AGG_DEV = 24
LANES = 128
HALF = NODES // 2
MIB = 1024 * 1024
STEP = 8


def swapped_along(block, axis, first):
    pairs = [(i, i + 1) for i in range(first, lax.axis_size(axis) - 1, 2)]
    return lax.ppermute(block, axis, pairs + [(i + 1, i) for i, _ in pairs])


def low_lanes(rows):
    return lax.broadcasted_iota(jnp.int32, (rows, LANES), 1) < NODES


def swapped(value):
    return pltpu.roll(value, NODES, 1)


def zero_one(mask):
    return mask.astype(jnp.float32).astype(jnp.bfloat16)


def product(left, right):
    return jnp.dot(left, right, preferred_element_type=jnp.float32)


def across(left, right):
    return lax.dot_general(left, right, (((0,), (0,)), ((), ())), preferred_element_type=jnp.float32)


def spread(column, stage):
    depth = column.shape[0]
    for k in range(column.shape[1] // LANES):
        stage[depth * k : depth * (k + 1), :] = column[:, LANES * k : LANES * (k + 1)].astype(jnp.float32)


def block_of(stage, z, depth):
    return stage[pl.ds(z, HALF, stride=depth), :].astype(jnp.bfloat16)


def stacked_pair(first, second):
    low = low_lanes(HALF)
    even = jnp.where(low, first, swapped(second))
    odd = jnp.where(low, swapped(first), second)
    return jnp.concatenate([even, odd], axis=0)


def in_order(pair):
    row = lax.broadcasted_iota(jnp.int32, (NODES, NODES), 0)
    col = lax.broadcasted_iota(jnp.int32, (NODES, NODES), 1)
    return product(zero_one(row == 2 * (col % HALF) + col // HALF), pair).astype(jnp.bfloat16)


def four_weights(first, second):
    low = low_lanes(NODES)
    zero = jnp.zeros_like(first)
    left = [jnp.where(low, first, zero), jnp.where(low, zero, first), zero, zero]
    right = [zero, zero, jnp.where(low, second, zero), jnp.where(low, zero, second)]
    return jnp.concatenate([jnp.concatenate(left, axis=0), jnp.concatenate(right, axis=0)], axis=1)


def folded(square):
    low = low_lanes(HALF)
    moved = swapped(jnp.where(low, square[HALF : 2 * HALF], square[2 * HALF : 3 * HALF]))
    return [jnp.where(low, square[:HALF], moved), jnp.where(low, moved, square[3 * HALF :])]


def straightened(even, odd):
    low = low_lanes(HALF // 2)
    return jnp.concatenate([jnp.where(low, even, swapped(odd)), jnp.where(low, swapped(even), odd)], axis=0)


def diagonal(square):
    return jnp.where(low_lanes(NODES), square[:NODES], square[NODES:]).astype(jnp.bfloat16)


def apart(first, second):
    zero = jnp.zeros_like(first)
    return jnp.concatenate([jnp.concatenate([first, zero], axis=1), jnp.concatenate([zero, second], axis=1)], axis=0)


def two_pairs(squares):
    return folded(squares[:, :LANES]) + folded(squares[:, LANES:])


def add_all(updates):
    olds = [total[key] for total, key, _ in updates]
    news = []
    for number, (total, key, value) in enumerate(updates):
        for other, other_key, other_value in updates[:number]:
            if other is total:
                value = value + jnp.where(key == other_key, other_value, jnp.zeros_like(other_value))
        news.append(olds[number] + value)
    for (total, key, _), new in zip(updates, news):
        total[key] = new


def prepare_kernel(place_ref, p_ref, fx_ref, fy_ref, fz_ref, natural_ref, turned_ref, swap_x_ref, swap_y_ref, near_z_ref, far_z_ref,
                   first_z_ref, last_z_ref, tail_x_ref, tail_y_ref, tail_z_ref, stages, stages_f, stacks, ends):
    plane = pl.program_id(0)
    size_y, depth = p_ref.shape[0], p_ref.shape[1]
    pairs = depth // 2

    for j in range(size_y):
        stage = stages.at[j]
        spread(p_ref[j], stage)
        block = [block_of(stage, z, depth) for z in range(depth)]
        stacked = [stacked_pair(block[2 * p], block[2 * p + 1]) for p in range(pairs)]
        for p in range(pairs):
            stacks[j, p] = stacked[p]
            natural_ref[j, p] = in_order(stacked[p])
        for h in range(pairs // 2):
            turned_ref[j, h] = jnp.concatenate([stacked[2 * h], stacked[2 * h + 1]], axis=0).T
        ends[0, j] = block[0]
        ends[1, j] = block[depth - 1]
        stage_f = stages_f.at[j]
        spread(fz_ref[0, j], stage_f)
        last = block_of(stage_f, depth - 1, depth)
        ends[2, j] = last

    for t in range(size_y // 2):
        first, last, face = [stacked_pair(ends[kind, 2 * t], ends[kind, 2 * t + 1]) for kind in range(3)]
        head = in_order(first)
        rim = diagonal(across(face, last))
        first_z_ref[t] = head
        last_z_ref[t] = last
        tail_z_ref[t] = face
        near_z_ref[t] = jnp.where(place_ref[2] == 0, rim, head)
        far_z_ref[t] = jnp.where(place_ref[2] == 0, head, rim)

    def faces(source, stage, j, tails, rims):
        spread(source, stage)
        block = [block_of(stage, z, depth) for z in range(depth)]
        for p in range(pairs):
            tails[p] = stacked_pair(block[2 * p], block[2 * p + 1])
            rims[p] = diagonal(across(tails[p], stacks[j, p]))

    @pl.when(place_ref[1] == 0)
    def _():
        faces(fy_ref[0, 0], stages_f.at[0], size_y - 1, tail_y_ref.at[0], swap_y_ref.at[0])

    @pl.when(place_ref[1] != 0)
    def _():
        swap_y_ref[0] = natural_ref[0]

    @pl.when((place_ref[0] == 0) & (plane == pl.num_programs(0) - 1))
    def _():
        for j in range(size_y):
            faces(fx_ref[0, j], stages_f.at[j], j, tail_x_ref.at[j], swap_x_ref.at[j])

    @pl.when((place_ref[0] != 0) & (plane == 0))
    def _():
        swap_x_ref[...] = natural_ref[...]


def prepare(place, prolong, faces, sizes):
    size_x, size_y, depth = sizes
    pairs, block = depth // 2, prolong.shape[-1]
    columns, half = size_x * size_y, size_y // 2
    shape = lambda *dims: jax.ShapeDtypeStruct(dims, jnp.bfloat16)
    by_half = pl.BlockSpec((half, NODES, LANES), lambda i: (i, 0, 0))
    edge = shape(columns // 2, NODES, LANES)
    stage = pltpu.VMEM((size_y, depth * HALF, LANES), jnp.float32)
    return pl.pallas_call(
        prepare_kernel,
        grid=(size_x,),
        in_specs=[
            pl.BlockSpec(memory_space=pltpu.SMEM),
            pl.BlockSpec((size_y, depth, block), lambda i: (i, 0, 0)),
            pl.BlockSpec((1, size_y, depth, block), lambda i: (0, size_x - 1, 0, 0)),
            pl.BlockSpec((1, 1, depth, block), lambda i: (1, i * size_y + size_y - 1, 0, 0)),
            pl.BlockSpec((1, size_y, depth, block), lambda i: (2, i, 0, 0)),
        ],
        out_specs=[
            pl.BlockSpec((size_y, pairs, NODES, LANES), lambda i: (i, 0, 0, 0)),
            pl.BlockSpec((size_y, pairs // 2, LANES, LANES), lambda i: (i, 0, 0, 0)),
            pl.BlockSpec((size_y, pairs, NODES, LANES), lambda i: (0, 0, 0, 0)),
            pl.BlockSpec((1, pairs, NODES, LANES), lambda i: (i, 0, 0, 0)),
            by_half, by_half, by_half, by_half,
            pl.BlockSpec((size_y, pairs, NODES, LANES), lambda i: (0, 0, 0, 0)),
            pl.BlockSpec((1, pairs, NODES, LANES), lambda i: (i, 0, 0, 0)),
            by_half,
        ],
        out_shape=[
            shape(columns, pairs, NODES, LANES), shape(columns, pairs // 2, LANES, LANES),
            shape(size_y, pairs, NODES, LANES), shape(size_x, pairs, NODES, LANES), edge, edge, edge, edge,
            shape(size_y, pairs, NODES, LANES), shape(size_x, pairs, NODES, LANES), edge,
        ],
        scratch_shapes=[
            stage, stage,
            pltpu.VMEM((size_y, pairs, NODES, LANES), jnp.bfloat16),
            pltpu.VMEM((3, size_y, HALF, LANES), jnp.bfloat16),
        ],
        compiler_params=pltpu.CompilerParams(vmem_limit_bytes=48 * MIB),
        name="prepare",
    )(place, prolong, faces, faces, faces)


def interior_kernel(keys, diag_ref, face_ref, natural_ref, turned_ref, out_ref,
                    stages, ahead_even, ahead_odd, behind_even, behind_odd, wide):
    _, size_x, size_y, depth = keys.shape
    pairs = depth // 2
    spare = out_ref.shape[0]
    ahead, behind = (ahead_even, ahead_odd), (behind_even, behind_odd)

    for total in ahead + behind:
        total[...] = jnp.zeros_like(total)

    def couplings(i, j, stage):
        column = i * size_y + j
        sources = [diag_ref[column], face_ref[0, jnp.maximum(column - size_y, 0)], face_ref[1, column - 1] if j else None, face_ref[2, column]]
        stacked = {}
        for face, source in enumerate(sources):
            if source is None:
                continue
            spread(source, stage.at[face])
            shift = 1 if face == 3 else 0
            block = [block_of(stage.at[face], z, depth) for z in range(depth)]
            stacked[face] = [stacked_pair(block[(2 * p - shift) % depth], block[2 * p + 1 - shift]) for p in range(pairs)]
        couples = {face: [] for face in stacked}
        for h in range(pairs // 2):
            left = [jnp.concatenate([rows[2 * h], rows[2 * h + 1]], axis=1) for rows in stacked.values()]
            weights = four_weights(natural_ref[column, 2 * h], natural_ref[column, 2 * h + 1])
            four = product(jnp.concatenate(left, axis=0), weights).astype(jnp.bfloat16)
            for number, face in enumerate(stacked):
                rows = four[NODES * number : NODES * (number + 1)]
                for couple in (rows[:, :LANES], rows[:, LANES:]):
                    couples[face].append(swapped(couple) if face == 3 else couple)
        low = low_lanes(NODES)
        along = couples[3]
        couples[3] = [jnp.where(low, along[p], along[min(p + 1, pairs - 1)]) for p in range(pairs)]
        return couples

    def sums(i, j, couples):
        column = i * size_y + j
        has_x, row_x = i > 0, jnp.maximum(i - 1, 0)
        origin = {0: column, 1: jnp.maximum(column - size_y, 0), 2: column - 1, 3: column}
        batches = []
        for h in range(pairs // 2):
            for face, pair in couples.items():
                four = two_pairs(product(turned_ref[origin[face], h], apart(pair[2 * h], pair[2 * h + 1])))
                updates = []
                for number, term in enumerate(four):
                    z, side = 4 * h + number, number % 2
                    if face == 0:
                        updates.append((ahead[side], keys[0, i, j, z], term))
                        continue
                    if face == 1:
                        here, there = keys[2, row_x, j, z], keys[1, i, j, z]
                        here, there = jnp.where(has_x, here, spare), jnp.where(has_x, there, spare)
                    elif face == 2:
                        here, there = keys[4, i, j - 1, z], keys[3, i, j, z]
                    elif z + 1 < depth:
                        here, there = keys[6, i, j, z], keys[5, i, j, z + 1]
                    else:
                        continue
                    updates.append((ahead[side], here, term))
                    updates.append((behind[side], there, term))
                batches.append(updates)
        return batches

    def plane(i, carry):
        couples = [couplings(i, j, stages.at[j]) for j in range(size_y)]
        for updates in [updates for j in range(size_y) for updates in sums(i, j, couples[j])]:
            add_all(updates)
        return carry

    lax.fori_loop(0, size_x, plane, 0)

    def finish(g, carry):
        low = low_lanes(HALF)
        spots = [(p, [wide.shape[0] * 2 * g + 2 * p + side for side in (0, 1)]) for p in range(wide.shape[0])]
        for p, key in spots:
            one, two = [behind_even[key[side]] + behind_odd[key[side]] for side in (0, 1)]
            upper = jnp.where(low, one, swapped(two))
            lower = jnp.where(low, swapped(one), two)
            wide[p, :, :NODES] = jnp.concatenate([upper, lower], axis=0).T
        for p, key in spots:
            for side in (0, 1):
                first = wide[p, NODES * side : NODES * side + HALF, :]
                second = wide[p, NODES * side + HALF : NODES * (side + 1), :]
                turned = jnp.where(low, first, swapped(second))
                out_ref[key[side]] = (ahead_even[key[side]] + ahead_odd[key[side]]) + turned
        return carry

    lax.fori_loop(0, spare // (2 * wide.shape[0]), finish, 0)


def interior(keys, diag, faces, natural, turned, sizes):
    size_x, size_y, depth = sizes
    pairs, block = depth // 2, diag.shape[-1]
    columns, rows = size_x * size_y, AGG_DEV * SLOTS
    total = pltpu.VMEM((rows + 1, HALF, LANES), jnp.float32)
    whole = pl.BlockSpec(memory_space=pltpu.VMEM)
    return pl.pallas_call(
        interior_kernel,
        in_specs=[pl.BlockSpec(memory_space=pltpu.SMEM), whole, whole, whole, whole],
        out_specs=whole,
        out_shape=jax.ShapeDtypeStruct((rows, HALF, LANES), jnp.float32),
        scratch_shapes=[
            pltpu.VMEM((size_y, 4, depth * HALF, LANES), jnp.float32),
            total, total, total, total,
            pltpu.VMEM((12, LANES, LANES), jnp.float32),
        ],
        compiler_params=pltpu.CompilerParams(vmem_limit_bytes=28 * MIB),
        cost_estimate=pl.CostEstimate(flops=columns * depth * 14 * NODES**3, bytes_accessed=columns * depth * 6 * block * 2, transcendentals=0),
        name="interior",
    )(keys, diag, faces, natural, turned)


def border_kernel(capacity, owners, place_ref, keys, got_x, got_y, near_z, far_z, tail_x, tail_y, tail_z, turned_x, turned_y,
                  natural_x, natural_y, first_z, last_z, start_ref, out_ref, total, filled):
    size_y, pairs = tail_x.shape[0], tail_x.shape[1]
    size_x, depth = tail_y.shape[0], 2 * pairs
    rows = start_ref.shape[0]
    places = out_ref.shape[0]

    def key_at(number, i, j, z):
        return keys[number, i, j, z]

    def couplings(tail, head):
        left = jnp.concatenate(tail, axis=1)
        four = product(left, four_weights(*head)).astype(jnp.bfloat16)
        return four[:, :LANES], four[:, LANES:]

    def ahead(tail, head, turned, key):
        for h in range(pairs // 2):
            couples = couplings([tail[2 * h], tail[2 * h + 1]], [head[2 * h], head[2 * h + 1]])
            four = two_pairs(product(turned[h], apart(*couples)))
            yield [(total, key(4 * h + number), term) for number, term in enumerate(four)]

    def back(natural, rim, key):
        for h in range(pairs // 2):
            four = [term for p in (2 * h, 2 * h + 1) for term in folded(across(natural[p], rim[p]))]
            yield [(total, key(4 * h + number), term) for number, term in enumerate(four)]

    def add_batches(batches):
        for updates in list(batches):
            add_all(updates)

    @pl.when(place_ref[0] == 0)
    def _():
        add_batches(
            batch for j in range(size_y)
            for batch in ahead(tail_x.at[j], got_x.at[j], turned_x.at[j], functools.partial(key_at, 2, size_x - 1, j)))

    @pl.when(place_ref[0] != 0)
    def _():
        add_batches(
            batch for j in range(size_y) for batch in back(natural_x.at[j], got_x.at[j], functools.partial(key_at, 1, 0, j)))

    @pl.when(place_ref[1] == 0)
    def _():
        add_batches(
            batch for i in range(size_x)
            for batch in ahead(tail_y.at[i], got_y.at[i], turned_y.at[i, 0], functools.partial(key_at, 4, i, size_y - 1)))

    @pl.when(place_ref[1] != 0)
    def _():
        add_batches(
            batch for i in range(size_x) for batch in back(natural_y.at[i, 0], got_y.at[i], functools.partial(key_at, 3, i, 0)))

    batches = []
    even = place_ref[2] == 0
    for t in range(0, near_z.shape[0], 2):
        heads = [jnp.where(even, near_z[u], far_z[u]) for u in (t, t + 1)]
        couples = couplings([tail_z[t], tail_z[t + 1]], heads)
        for u in (t, t + 1):
            i, j = 2 * u // size_y, 2 * u % size_y
            front = folded(across(last_z[u], couples[u - t]))
            past = folded(across(first_z[u], jnp.where(even, far_z[u], near_z[u])))
            batches.append([(total, keys[6, i, j + side, depth - 1], front[side]) for side in (0, 1)]
                           + [(total, keys[5, i, j + side, 0], past[side]) for side in (0, 1)])
    add_batches(batches)

    for owner in range(places // capacity):
        filled[owner] = 0
    if places * SLOTS != rows:
        out_ref[...] = jnp.zeros_like(out_ref)
    for r in range(rows // SLOTS):
        owner = owners[r]
        spot = owner * capacity + filled[owner]
        filled[owner] = filled[owner] + 1
        for s in range(SLOTS):
            key = r * SLOTS + s
            even, odd = [total[key, pl.ds(first, HALF // 2, stride=2), :] for first in (0, 1)]
            out_ref[spot, HALF * s : HALF * (s + 1), :] = straightened(even, odd).astype(jnp.bfloat16)


def border(owners, place, keys, operands, turned, natural, ends, total, capacity, places, sizes):
    size_x, size_y, depth = sizes
    pairs = depth // 2
    smem = pl.BlockSpec(memory_space=pltpu.SMEM)
    whole = pl.BlockSpec(memory_space=pltpu.VMEM)
    planes = lambda array: array.reshape((size_x, size_y) + array.shape[1:])
    before = 3 + len(operands) + 4 + len(ends)
    return pl.pallas_call(
        functools.partial(border_kernel, capacity),
        grid=(1,),
        in_specs=[smem, smem, smem] + [whole] * len(operands) + [
            pl.BlockSpec((size_y, pairs // 2, LANES, LANES), lambda i: (size_x - 1, 0, 0, 0)),
            pl.BlockSpec((size_x, 1, pairs // 2, LANES, LANES), lambda i: (0, size_y - 1, 0, 0, 0)),
            pl.BlockSpec((size_y, pairs, NODES, LANES), lambda i: (0, 0, 0, 0)),
            pl.BlockSpec((size_x, 1, pairs, NODES, LANES), lambda i: (0, 0, 0, 0, 0)),
        ] + [whole] * (len(ends) + 1),
        out_specs=[whole, whole],
        out_shape=[
            jax.ShapeDtypeStruct((places, SLOTS * HALF, LANES), jnp.bfloat16),
            jax.ShapeDtypeStruct(total.shape, total.dtype),
        ],
        input_output_aliases={before: 1},
        scratch_shapes=[pltpu.SMEM((places // capacity,), jnp.int32)],
        compiler_params=pltpu.CompilerParams(vmem_limit_bytes=18 * MIB),
        name="border",
    )(owners, place, keys, *operands, turned, planes(turned), natural, planes(natural), *ends, total)[0]


def layout_kernel(*refs):
    source, (rows_ref, out_ref, stage) = refs[:-3], refs[-3:]
    group = pl.program_id(0)
    height = out_ref.shape[1]
    for s in range(SLOTS):
        for r in range(height):
            row = group * height + r
            if source:
                row = source[0][row]
            block = rows_ref[jnp.maximum(row, 0), HALF * s : HALF * (s + 1), :].astype(jnp.float32)
            if source:
                block = jnp.where(row >= 0, block, jnp.zeros_like(block))
            stage[s, pl.ds(r, HALF, stride=height), :] = block
        for k in range(HALF):
            out_ref[s, :, LANES * k : LANES * (k + 1)] = stage[s, height * k : height * (k + 1), :].astype(jnp.bfloat16)


def laid_out(source, rows, block):
    places, height = rows.shape[0], 8
    return pl.pallas_call(
        layout_kernel,
        grid=(places // height,),
        in_specs=[pl.BlockSpec(memory_space=pltpu.SMEM)] * len(source) + [pl.BlockSpec(memory_space=pltpu.VMEM)],
        out_specs=pl.BlockSpec((SLOTS, height, block), lambda g: (0, g, 0)),
        out_shape=jax.ShapeDtypeStruct((SLOTS, places, block), jnp.bfloat16),
        scratch_shapes=[pltpu.VMEM((SLOTS, height * HALF, LANES), jnp.float32)],
        compiler_params=pltpu.CompilerParams(vmem_limit_bytes=10 * MIB),
        name="layout",
    )(*source, rows)


def shards(a_diag, a_face, prolong, aggregate, pair_slot, row_owner):
    size_x, size_y, size_z, block = a_diag.shape
    sizes = (size_x, size_y, size_z)
    columns = size_x * size_y
    depth = lax.axis_size("gz")
    capacity = max(2, (AGG_DEV + depth - 1) // depth)
    holding = capacity * depth
    diag = a_diag.reshape(columns, size_z, block)
    faces = a_face.reshape(3, columns, size_z, block)
    assert lax.axis_size("gx") == 2 and lax.axis_size("gy") == 2
    place = jnp.stack([lax.axis_index("gx"), lax.axis_index("gy"), lax.axis_index("gz") % 2]).astype(jnp.int32)
    keys = aggregate[None] * SLOTS + pair_slot

    natural, turned, swap_x, swap_y, near_z, far_z, first_z, last_z, tail_x, tail_y, tail_z = prepare(
        place, prolong.reshape(columns, size_z, block), faces, sizes)
    near_z = swapped_along(near_z, "gz", 0)
    far_z = swapped_along(far_z, "gz", 1)
    got_y = swapped_along(swap_y, "gy", 0)
    got_x = swapped_along(swap_x, "gx", 0)
    total = interior(keys, diag, faces, natural, turned, sizes)
    outgoing = border(
        row_owner, place, keys, (got_x, got_y, near_z, far_z, tail_x, tail_y, tail_z), turned, natural,
        (first_z, last_z), total, capacity, holding, sizes)
    arrived = lax.all_to_all(outgoing, "gz", 0, 0, tiled=True)
    sources = []
    if holding != AGG_DEV:
        source = jnp.arange(holding, dtype=jnp.int32)
        owner_ids = jnp.arange(depth, dtype=jnp.int32)
        counts = jnp.sum((row_owner[:, None] == owner_ids[None, :]).astype(jnp.int32), axis=0)
        arrived_counts = lax.all_to_all(counts, "gz", 0, 0, tiled=True)
        present = source % capacity < jnp.repeat(arrived_counts, capacity)
        target = jnp.cumsum(present.astype(jnp.int32)) - 1
        match = (present[None, :] & (target[None, :] == source[:, None])).astype(jnp.int32)
        sources = [jnp.sum(match * (source[None, :] + 1), axis=1) - 1]
    result = laid_out(sources, arrived, block)
    return jnp.transpose(result, (1, 0, 2)).reshape(1, 1, 1, holding, SLOTS, block)


def solution(mesh):
    return jax.shard_map(
        shards,
        mesh=mesh,
        in_specs=(
            P("gx", "gy", "gz", None),
            P(None, "gx", "gy", "gz", None),
            P("gx", "gy", "gz", None),
            P("gx", "gy", "gz"),
            P(None, "gx", "gy", "gz"),
            P(("gx", "gy", "gz")),
        ),
        out_specs=P("gx", "gy", "gz", None, None, None),
        check_vma=False,
    )
```

```python
import functools

import jax
import jax.numpy as jnp
from jax import lax
from jax.experimental import pallas as pl
from jax.experimental.pallas import tpu as pltpu
from jax.sharding import PartitionSpec as P

NODES = 64
SLOTS = 7
AGG_DEV = 24
LANES = 128
HALF = NODES // 2
MIB = 1024 * 1024
STEP = 8


def swapped_along(block, axis, first):
    pairs = [(i, i + 1) for i in range(first, lax.axis_size(axis) - 1, 2)]
    return lax.ppermute(block, axis, pairs + [(i + 1, i) for i, _ in pairs])


def low_lanes(rows):
    return lax.broadcasted_iota(jnp.int32, (rows, LANES), 1) < NODES


def swapped(value):
    return pltpu.roll(value, NODES, 1)


def zero_one(mask):
    return mask.astype(jnp.float32).astype(jnp.bfloat16)


def product(left, right):
    return jnp.dot(left, right, preferred_element_type=jnp.float32)


def across(left, right):
    return lax.dot_general(left, right, (((0,), (0,)), ((), ())), preferred_element_type=jnp.float32)


def spread(column, stage):
    depth = column.shape[0]
    for k in range(column.shape[1] // LANES):
        stage[depth * k : depth * (k + 1), :] = column[:, LANES * k : LANES * (k + 1)].astype(jnp.float32)


def block_of(stage, z, depth):
    return stage[pl.ds(z, HALF, stride=depth), :].astype(jnp.bfloat16)


def stacked_pair(first, second):
    low = low_lanes(HALF)
    even = jnp.where(low, first, swapped(second))
    odd = jnp.where(low, swapped(first), second)
    return jnp.concatenate([even, odd], axis=0)


def in_order(pair):
    row = lax.broadcasted_iota(jnp.int32, (NODES, NODES), 0)
    col = lax.broadcasted_iota(jnp.int32, (NODES, NODES), 1)
    return product(zero_one(row == 2 * (col % HALF) + col // HALF), pair).astype(jnp.bfloat16)


def four_weights(first, second):
    low = low_lanes(NODES)
    zero = jnp.zeros_like(first)
    left = [jnp.where(low, first, zero), jnp.where(low, zero, first), zero, zero]
    right = [zero, zero, jnp.where(low, second, zero), jnp.where(low, zero, second)]
    return jnp.concatenate([jnp.concatenate(left, axis=0), jnp.concatenate(right, axis=0)], axis=1)


def folded(square):
    low = low_lanes(HALF)
    moved = swapped(jnp.where(low, square[HALF : 2 * HALF], square[2 * HALF : 3 * HALF]))
    return [jnp.where(low, square[:HALF], moved), jnp.where(low, moved, square[3 * HALF :])]


def straightened(even, odd):
    low = low_lanes(HALF // 2)
    return jnp.concatenate([jnp.where(low, even, swapped(odd)), jnp.where(low, swapped(even), odd)], axis=0)


def diagonal(square):
    return jnp.where(low_lanes(NODES), square[:NODES], square[NODES:]).astype(jnp.bfloat16)


def apart(first, second):
    zero = jnp.zeros_like(first)
    return jnp.concatenate([jnp.concatenate([first, zero], axis=1), jnp.concatenate([zero, second], axis=1)], axis=0)


def two_pairs(squares):
    return folded(squares[:, :LANES]) + folded(squares[:, LANES:])


def add_all(updates):
    olds = [total[key] for total, key, _ in updates]
    news = []
    for number, (total, key, value) in enumerate(updates):
        for other, other_key, other_value in updates[:number]:
            if other is total:
                value = value + jnp.where(key == other_key, other_value, jnp.zeros_like(other_value))
        news.append(olds[number] + value)
    for (total, key, _), new in zip(updates, news):
        total[key] = new


def prepare_kernel(place_ref, p_ref, fx_ref, fy_ref, fz_ref, natural_ref, turned_ref, swap_x_ref, swap_y_ref, near_z_ref, far_z_ref,
                   first_z_ref, last_z_ref, tail_x_ref, tail_y_ref, tail_z_ref, stages, stages_f, stacks, ends):
    plane = pl.program_id(0)
    size_y, depth = p_ref.shape[0], p_ref.shape[1]
    pairs = depth // 2

    for j in range(size_y):
        stage = stages.at[j]
        spread(p_ref[j], stage)
        block = [block_of(stage, z, depth) for z in range(depth)]
        stacked = [stacked_pair(block[2 * p], block[2 * p + 1]) for p in range(pairs)]
        for p in range(pairs):
            stacks[j, p] = stacked[p]
            natural_ref[j, p] = in_order(stacked[p])
        for h in range(pairs // 2):
            turned_ref[j, h] = jnp.concatenate([stacked[2 * h], stacked[2 * h + 1]], axis=0).T
        ends[0, j] = block[0]
        ends[1, j] = block[depth - 1]
        stage_f = stages_f.at[j]
        spread(fz_ref[0, j], stage_f)
        last = block_of(stage_f, depth - 1, depth)
        ends[2, j] = last

    for t in range(size_y // 2):
        first, last, face = [stacked_pair(ends[kind, 2 * t], ends[kind, 2 * t + 1]) for kind in range(3)]
        head = in_order(first)
        rim = diagonal(across(face, last))
        first_z_ref[t] = head
        last_z_ref[t] = last
        tail_z_ref[t] = face
        near_z_ref[t] = jnp.where(place_ref[2] % 2 == 0, rim, head)
        far_z_ref[t] = jnp.where(place_ref[2] % 2 == 0, head, rim)

    def faces(source, stage, j, tails, rims):
        spread(source, stage)
        block = [block_of(stage, z, depth) for z in range(depth)]
        for p in range(pairs):
            tails[p] = stacked_pair(block[2 * p], block[2 * p + 1])
            rims[p] = diagonal(across(tails[p], stacks[j, p]))

    @pl.when(place_ref[1] == 0)
    def _():
        faces(fy_ref[0, 0], stages_f.at[0], size_y - 1, tail_y_ref.at[0], swap_y_ref.at[0])

    @pl.when(place_ref[1] != 0)
    def _():
        swap_y_ref[0] = natural_ref[0]

    @pl.when((place_ref[0] == 0) & (plane == pl.num_programs(0) - 1))
    def _():
        for j in range(size_y):
            faces(fx_ref[0, j], stages_f.at[j], j, tail_x_ref.at[j], swap_x_ref.at[j])

    @pl.when((place_ref[0] != 0) & (plane == 0))
    def _():
        swap_x_ref[...] = natural_ref[...]


def prepare(place, prolong, faces, sizes):
    size_x, size_y, depth = sizes
    pairs, block = depth // 2, prolong.shape[-1]
    columns, half = size_x * size_y, size_y // 2
    shape = lambda *dims: jax.ShapeDtypeStruct(dims, jnp.bfloat16)
    by_half = pl.BlockSpec((half, NODES, LANES), lambda i: (i, 0, 0))
    edge = shape(columns // 2, NODES, LANES)
    stage = pltpu.VMEM((size_y, depth * HALF, LANES), jnp.float32)
    return pl.pallas_call(
        prepare_kernel,
        grid=(size_x,),
        in_specs=[
            pl.BlockSpec(memory_space=pltpu.SMEM),
            pl.BlockSpec((size_y, depth, block), lambda i: (i, 0, 0)),
            pl.BlockSpec((1, size_y, depth, block), lambda i: (0, size_x - 1, 0, 0)),
            pl.BlockSpec((1, 1, depth, block), lambda i: (1, i * size_y + size_y - 1, 0, 0)),
            pl.BlockSpec((1, size_y, depth, block), lambda i: (2, i, 0, 0)),
        ],
        out_specs=[
            pl.BlockSpec((size_y, pairs, NODES, LANES), lambda i: (i, 0, 0, 0)),
            pl.BlockSpec((size_y, pairs // 2, LANES, LANES), lambda i: (i, 0, 0, 0)),
            pl.BlockSpec((size_y, pairs, NODES, LANES), lambda i: (0, 0, 0, 0)),
            pl.BlockSpec((1, pairs, NODES, LANES), lambda i: (i, 0, 0, 0)),
            by_half, by_half, by_half, by_half,
            pl.BlockSpec((size_y, pairs, NODES, LANES), lambda i: (0, 0, 0, 0)),
            pl.BlockSpec((1, pairs, NODES, LANES), lambda i: (i, 0, 0, 0)),
            by_half,
        ],
        out_shape=[
            shape(columns, pairs, NODES, LANES), shape(columns, pairs // 2, LANES, LANES),
            shape(size_y, pairs, NODES, LANES), shape(size_x, pairs, NODES, LANES), edge, edge, edge, edge,
            shape(size_y, pairs, NODES, LANES), shape(size_x, pairs, NODES, LANES), edge,
        ],
        scratch_shapes=[
            stage, stage,
            pltpu.VMEM((size_y, pairs, NODES, LANES), jnp.bfloat16),
            pltpu.VMEM((3, size_y, HALF, LANES), jnp.bfloat16),
        ],
        compiler_params=pltpu.CompilerParams(vmem_limit_bytes=48 * MIB),
        name="prepare",
    )(place, prolong, faces, faces, faces)


def interior_kernel(keys, diag_ref, face_ref, natural_ref, turned_ref, out_ref,
                    stages, ahead_even, ahead_odd, behind_even, behind_odd, wide):
    _, size_x, size_y, depth = keys.shape
    pairs = depth // 2
    spare = out_ref.shape[0]
    ahead, behind = (ahead_even, ahead_odd), (behind_even, behind_odd)

    for total in ahead + behind:
        total[...] = jnp.zeros_like(total)

    def couplings(i, j, stage):
        column = i * size_y + j
        sources = [diag_ref[column], face_ref[0, jnp.maximum(column - size_y, 0)], face_ref[1, column - 1] if j else None, face_ref[2, column]]
        stacked = {}
        for face, source in enumerate(sources):
            if source is None:
                continue
            spread(source, stage.at[face])
            shift = 1 if face == 3 else 0
            block = [block_of(stage.at[face], z, depth) for z in range(depth)]
            stacked[face] = [stacked_pair(block[(2 * p - shift) % depth], block[2 * p + 1 - shift]) for p in range(pairs)]
        couples = {face: [] for face in stacked}
        for h in range(pairs // 2):
            left = [jnp.concatenate([rows[2 * h], rows[2 * h + 1]], axis=1) for rows in stacked.values()]
            weights = four_weights(natural_ref[column, 2 * h], natural_ref[column, 2 * h + 1])
            four = product(jnp.concatenate(left, axis=0), weights).astype(jnp.bfloat16)
            for number, face in enumerate(stacked):
                rows = four[NODES * number : NODES * (number + 1)]
                for couple in (rows[:, :LANES], rows[:, LANES:]):
                    couples[face].append(swapped(couple) if face == 3 else couple)
        low = low_lanes(NODES)
        along = couples[3]
        couples[3] = [jnp.where(low, along[p], along[min(p + 1, pairs - 1)]) for p in range(pairs)]
        return couples

    def sums(i, j, couples):
        column = i * size_y + j
        has_x, row_x = i > 0, jnp.maximum(i - 1, 0)
        origin = {0: column, 1: jnp.maximum(column - size_y, 0), 2: column - 1, 3: column}
        batches = []
        for h in range(pairs // 2):
            for face, pair in couples.items():
                four = two_pairs(product(turned_ref[origin[face], h], apart(pair[2 * h], pair[2 * h + 1])))
                updates = []
                for number, term in enumerate(four):
                    z, side = 4 * h + number, number % 2
                    if face == 0:
                        updates.append((ahead[side], keys[0, i, j, z], term))
                        continue
                    if face == 1:
                        here, there = keys[2, row_x, j, z], keys[1, i, j, z]
                        here, there = jnp.where(has_x, here, spare), jnp.where(has_x, there, spare)
                    elif face == 2:
                        here, there = keys[4, i, j - 1, z], keys[3, i, j, z]
                    elif z + 1 < depth:
                        here, there = keys[6, i, j, z], keys[5, i, j, z + 1]
                    else:
                        continue
                    updates.append((ahead[side], here, term))
                    updates.append((behind[side], there, term))
                batches.append(updates)
        return batches

    def plane(i, carry):
        couples = [couplings(i, j, stages.at[j]) for j in range(size_y)]
        for updates in [updates for j in range(size_y) for updates in sums(i, j, couples[j])]:
            add_all(updates)
        return carry

    lax.fori_loop(0, size_x, plane, 0)

    def finish(g, carry):
        low = low_lanes(HALF)
        spots = [(p, [wide.shape[0] * 2 * g + 2 * p + side for side in (0, 1)]) for p in range(wide.shape[0])]
        for p, key in spots:
            one, two = [behind_even[key[side]] + behind_odd[key[side]] for side in (0, 1)]
            upper = jnp.where(low, one, swapped(two))
            lower = jnp.where(low, swapped(one), two)
            wide[p, :, :NODES] = jnp.concatenate([upper, lower], axis=0).T
        for p, key in spots:
            for side in (0, 1):
                first = wide[p, NODES * side : NODES * side + HALF, :]
                second = wide[p, NODES * side + HALF : NODES * (side + 1), :]
                turned = jnp.where(low, first, swapped(second))
                out_ref[key[side]] = (ahead_even[key[side]] + ahead_odd[key[side]]) + turned
        return carry

    lax.fori_loop(0, spare // (2 * wide.shape[0]), finish, 0)


def interior(keys, diag, faces, natural, turned, sizes):
    size_x, size_y, depth = sizes
    pairs, block = depth // 2, diag.shape[-1]
    columns, rows = size_x * size_y, AGG_DEV * SLOTS
    total = pltpu.VMEM((rows + 1, HALF, LANES), jnp.float32)
    whole = pl.BlockSpec(memory_space=pltpu.VMEM)
    return pl.pallas_call(
        interior_kernel,
        in_specs=[pl.BlockSpec(memory_space=pltpu.SMEM), whole, whole, whole, whole],
        out_specs=whole,
        out_shape=jax.ShapeDtypeStruct((rows, HALF, LANES), jnp.float32),
        scratch_shapes=[
            pltpu.VMEM((size_y, 4, depth * HALF, LANES), jnp.float32),
            total, total, total, total,
            pltpu.VMEM((12, LANES, LANES), jnp.float32),
        ],
        compiler_params=pltpu.CompilerParams(vmem_limit_bytes=28 * MIB),
        cost_estimate=pl.CostEstimate(flops=columns * depth * 14 * NODES**3, bytes_accessed=columns * depth * 6 * block * 2, transcendentals=0),
        name="interior",
    )(keys, diag, faces, natural, turned)


def border_kernel(capacity, paired, owners, place_ref, keys, got_x, got_y, near_z, far_z, tail_x, tail_y, tail_z, turned_x, turned_y,
                  natural_x, natural_y, first_z, last_z, start_ref, *refs):
    out_refs, (total, filled, listed) = refs[:-3], refs[-3:]
    size_y, pairs = tail_x.shape[0], tail_x.shape[1]
    size_x, depth = tail_y.shape[0], 2 * pairs
    rows = start_ref.shape[0]

    def key_at(number, i, j, z):
        return keys[number, i, j, z]

    def couplings(tail, head):
        left = jnp.concatenate(tail, axis=1)
        four = product(left, four_weights(*head)).astype(jnp.bfloat16)
        return four[:, :LANES], four[:, LANES:]

    def ahead(tail, head, turned, key):
        for h in range(pairs // 2):
            couples = couplings([tail[2 * h], tail[2 * h + 1]], [head[2 * h], head[2 * h + 1]])
            four = two_pairs(product(turned[h], apart(*couples)))
            yield [(total, key(4 * h + number), term) for number, term in enumerate(four)]

    def back(natural, rim, key):
        for h in range(pairs // 2):
            four = [term for p in (2 * h, 2 * h + 1) for term in folded(across(natural[p], rim[p]))]
            yield [(total, key(4 * h + number), term) for number, term in enumerate(four)]

    def batches_x(first):
        for j in range(size_y):
            if first:
                yield from ahead(tail_x.at[j], got_x.at[j], turned_x.at[j], functools.partial(key_at, 2, size_x - 1, j))
            else:
                yield from back(natural_x.at[j], got_x.at[j], functools.partial(key_at, 1, 0, j))

    def batches_y(first):
        for i in range(size_x):
            if first:
                yield from ahead(tail_y.at[i], got_y.at[i], turned_y.at[i, 0], functools.partial(key_at, 4, i, size_y - 1))
            else:
                yield from back(natural_y.at[i, 0], got_y.at[i], functools.partial(key_at, 3, i, 0))

    def batches_z():
        even = place_ref[2] % 2 == 0
        for t in range(0, near_z.shape[0], 2):
            heads = [jnp.where(even, near_z[u], far_z[u]) for u in (t, t + 1)]
            couples = couplings([tail_z[t], tail_z[t + 1]], heads)
            for u in (t, t + 1):
                i, j = 2 * u // size_y, 2 * u % size_y
                front = folded(across(last_z[u], couples[u - t]))
                past = folded(across(first_z[u], jnp.where(even, far_z[u], near_z[u])))
                yield ([(total, keys[6, i, j + side, depth - 1], front[side]) for side in (0, 1)]
                       + [(total, keys[5, i, j + side, 0], past[side]) for side in (0, 1)])

    for first_x in (True, False):
        for first_y in (True, False):
            @pl.when(((place_ref[0] == 0) == first_x) & ((place_ref[1] == 0) == first_y))
            def _():
                batches = list(batches_x(first_x)) + list(batches_y(first_y)) + list(batches_z())
                for updates in batches:
                    add_all(updates)

    places = capacity * len(out_refs)
    full = places * SLOTS == rows
    for spot in range(places):
        listed[spot] = -1
    for owner in range(len(out_refs)):
        filled[owner] = 0
    for r in range(rows // SLOTS):
        owner = owners[r]
        listed[jnp.bitwise_xor(owner, place_ref[2] if paired else 0) * capacity + filled[owner]] = r
        filled[owner] = filled[owner] + 1
    for spot in range(places):
        row = listed[spot]
        for s in range(SLOTS):
            key = jnp.maximum(row, 0) * SLOTS + s
            even, odd = [total[key, pl.ds(first, HALF // 2, stride=2), :] for first in (0, 1)]
            block = straightened(even, odd)
            if not full:
                block = jnp.where(row >= 0, block, jnp.zeros_like(block))
            out_refs[spot // capacity][spot % capacity, HALF * s : HALF * (s + 1), :] = block.astype(jnp.bfloat16)


def border(owners, place, keys, operands, turned, natural, ends, total, capacity, devices, paired, sizes):
    size_x, size_y, depth = sizes
    pairs = depth // 2
    smem = pl.BlockSpec(memory_space=pltpu.SMEM)
    whole = pl.BlockSpec(memory_space=pltpu.VMEM)
    planes = lambda array: array.reshape((size_x, size_y) + array.shape[1:])
    before = 3 + len(operands) + 4 + len(ends)
    return pl.pallas_call(
        functools.partial(border_kernel, capacity, paired),
        grid=(1,),
        in_specs=[smem, smem, smem] + [whole] * len(operands) + [
            pl.BlockSpec((size_y, pairs // 2, LANES, LANES), lambda i: (size_x - 1, 0, 0, 0)),
            pl.BlockSpec((size_x, 1, pairs // 2, LANES, LANES), lambda i: (0, size_y - 1, 0, 0, 0)),
            pl.BlockSpec((size_y, pairs, NODES, LANES), lambda i: (0, 0, 0, 0)),
            pl.BlockSpec((size_x, 1, pairs, NODES, LANES), lambda i: (0, 0, 0, 0, 0)),
        ] + [whole] * (len(ends) + 1),
        out_specs=[whole] * (devices + 1),
        out_shape=[jax.ShapeDtypeStruct((capacity, SLOTS * HALF, LANES), jnp.bfloat16)] * devices
        + [jax.ShapeDtypeStruct(total.shape, total.dtype)],
        input_output_aliases={before: devices},
        scratch_shapes=[pltpu.SMEM((devices,), jnp.int32), pltpu.SMEM((capacity * devices,), jnp.int32)],
        compiler_params=pltpu.CompilerParams(vmem_limit_bytes=18 * MIB),
        name="border",
    )(owners, place, keys, *operands, turned, planes(turned), natural, planes(natural), *ends, total)[:devices]


def layout_kernel(source, rows_ref, out_ref, stage):
    group = pl.program_id(0)
    height = out_ref.shape[1]
    for s in range(SLOTS):
        for r in range(height):
            row = source[group * height + r]
            block = rows_ref[jnp.maximum(row, 0), HALF * s : HALF * (s + 1), :].astype(jnp.float32)
            stage[s, pl.ds(r, HALF, stride=height), :] = jnp.where(row >= 0, block, jnp.zeros_like(block))
        for k in range(HALF):
            out_ref[s, :, LANES * k : LANES * (k + 1)] = stage[s, height * k : height * (k + 1), :].astype(jnp.bfloat16)


def laid_out(source, rows, block):
    places, height = rows.shape[0], 8
    return pl.pallas_call(
        layout_kernel,
        grid=(places // height,),
        in_specs=[pl.BlockSpec(memory_space=pltpu.SMEM), pl.BlockSpec(memory_space=pltpu.VMEM)],
        out_specs=pl.BlockSpec((SLOTS, height, block), lambda g: (0, g, 0)),
        out_shape=jax.ShapeDtypeStruct((SLOTS, places, block), jnp.bfloat16),
        scratch_shapes=[pltpu.VMEM((SLOTS, height * HALF, LANES), jnp.float32)],
        compiler_params=pltpu.CompilerParams(vmem_limit_bytes=10 * MIB),
        name="layout",
    )(source, rows)


def placed_kernel(place_ref, *refs):
    parts, (out_ref, stage) = refs[:-2], refs[-2:]
    capacity, height = parts[0].shape[0], out_ref.shape[1]
    for number, rows_ref in enumerate(parts):
        first = jnp.bitwise_xor(place_ref[2], number) * capacity
        for q in range(capacity):
            for s in range(SLOTS):
                block = rows_ref[q, HALF * s : HALF * (s + 1), :].astype(jnp.float32)
                stage[s, pl.ds(first + q, HALF, stride=height), :] = block
    for s in range(SLOTS):
        for k in range(HALF):
            out_ref[s, :, LANES * k : LANES * (k + 1)] = stage[s, height * k : height * (k + 1), :].astype(jnp.bfloat16)


def placed(place, parts, block):
    places = parts[0].shape[0] * len(parts)
    whole = pl.BlockSpec(memory_space=pltpu.VMEM)
    return pl.pallas_call(
        placed_kernel,
        in_specs=[pl.BlockSpec(memory_space=pltpu.SMEM)] + [whole] * len(parts),
        out_specs=whole,
        out_shape=jax.ShapeDtypeStruct((SLOTS, places, block), jnp.bfloat16),
        scratch_shapes=[pltpu.VMEM((SLOTS, places * HALF, LANES), jnp.float32)],
        compiler_params=pltpu.CompilerParams(vmem_limit_bytes=16 * MIB),
        name="placed",
    )(place, *parts)


def shards(a_diag, a_face, prolong, aggregate, pair_slot, row_owner):
    size_x, size_y, size_z, block = a_diag.shape
    sizes = (size_x, size_y, size_z)
    columns = size_x * size_y
    depth = lax.axis_size("gz")
    capacity = max(2, (AGG_DEV + depth - 1) // depth)
    holding = capacity * depth
    diag = a_diag.reshape(columns, size_z, block)
    faces = a_face.reshape(3, columns, size_z, block)
    assert lax.axis_size("gx") == 2 and lax.axis_size("gy") == 2
    place = jnp.stack([lax.axis_index("gx"), lax.axis_index("gy"), lax.axis_index("gz")]).astype(jnp.int32)
    keys = aggregate[None] * SLOTS + pair_slot

    natural, turned, swap_x, swap_y, near_z, far_z, first_z, last_z, tail_x, tail_y, tail_z = prepare(
        place, prolong.reshape(columns, size_z, block), faces, sizes)
    near_z = swapped_along(near_z, "gz", 0)
    far_z = swapped_along(far_z, "gz", 1)
    got_y = swapped_along(swap_y, "gy", 0)
    got_x = swapped_along(swap_x, "gx", 0)
    total = interior(keys, diag, faces, natural, turned, sizes)
    paired = holding == AGG_DEV and depth & (depth - 1) == 0
    outgoing = border(
        row_owner, place, keys, (got_x, got_y, near_z, far_z, tail_x, tail_y, tail_z), turned, natural,
        (first_z, last_z), total, capacity, depth, paired, sizes)
    if paired:
        parts = list(outgoing)
        far_first = sorted(range(1, depth), key=lambda k: (k < depth // 2, k))
        for k in far_first:
            parts[k] = lax.ppermute(outgoing[k], "gz", [(i, i ^ k) for i in range(depth)])
        result = placed(place, parts, block)
    else:
        arrived = lax.all_to_all(jnp.concatenate(outgoing, axis=0), "gz", 0, 0, tiled=True)
        slots = jnp.arange(holding, dtype=jnp.int32)
        owner_ids = jnp.arange(depth, dtype=jnp.int32)
        counts = jnp.sum((row_owner[:, None] == owner_ids[None, :]).astype(jnp.int32), axis=0)
        arrived_counts = lax.all_to_all(counts, "gz", 0, 0, tiled=True)
        present = slots % capacity < jnp.repeat(arrived_counts, capacity)
        target = jnp.cumsum(present.astype(jnp.int32)) - 1
        match = (present[None, :] & (target[None, :] == slots[:, None])).astype(jnp.int32)
        result = laid_out(jnp.sum(match * (slots[None, :] + 1), axis=1) - 1, arrived, block)
    return jnp.transpose(result, (1, 0, 2)).reshape(1, 1, 1, holding, SLOTS, block)


def solution(mesh):
    return jax.shard_map(
        shards,
        mesh=mesh,
        in_specs=(
            P("gx", "gy", "gz", None),
            P(None, "gx", "gy", "gz", None),
            P("gx", "gy", "gz", None),
            P("gx", "gy", "gz"),
            P(None, "gx", "gy", "gz"),
            P(("gx", "gy", "gz")),
        ),
        out_specs=P("gx", "gy", "gz", None, None, None),
        check_vma=False,
    )
```

```python
import functools

import jax
import jax.numpy as jnp
from jax import lax
from jax.experimental import pallas as pl
from jax.experimental.pallas import tpu as pltpu
from jax.sharding import PartitionSpec as P

NODES = 64
SLOTS = 7
AGG_DEV = 24
LANES = 128
HALF = NODES // 2
MIB = 1024 * 1024
STEP = 8


def swapped_along(block, axis, first):
    pairs = [(i, i + 1) for i in range(first, lax.axis_size(axis) - 1, 2)]
    return lax.ppermute(block, axis, pairs + [(i + 1, i) for i, _ in pairs])


def low_lanes(rows):
    return lax.broadcasted_iota(jnp.int32, (rows, LANES), 1) < NODES


def swapped(value):
    return pltpu.roll(value, NODES, 1)


def zero_one(mask):
    return mask.astype(jnp.float32).astype(jnp.bfloat16)


def product(left, right):
    return jnp.dot(left, right, preferred_element_type=jnp.float32)


def across(left, right):
    return lax.dot_general(left, right, (((0,), (0,)), ((), ())), preferred_element_type=jnp.float32)


def spread(column, stage):
    depth = column.shape[0]
    for k in range(column.shape[1] // LANES):
        stage[depth * k : depth * (k + 1), :] = column[:, LANES * k : LANES * (k + 1)].astype(jnp.float32)


def block_of(stage, z, depth):
    return stage[pl.ds(z, HALF, stride=depth), :].astype(jnp.bfloat16)


def stacked_pair(first, second):
    low = low_lanes(HALF)
    even = jnp.where(low, first, swapped(second))
    odd = jnp.where(low, swapped(first), second)
    return jnp.concatenate([even, odd], axis=0)


def in_order(pairs):
    row = lax.broadcasted_iota(jnp.int32, (NODES, NODES), 0)
    col = lax.broadcasted_iota(jnp.int32, (NODES, NODES), 1)
    moved = product(zero_one(row == 2 * (col % HALF) + col // HALF), jnp.concatenate(pairs, axis=1)).astype(jnp.bfloat16)
    return [moved[:, LANES * p : LANES * (p + 1)] for p in range(len(pairs))]


def four_weights(first, second):
    low = low_lanes(NODES)
    zero = jnp.zeros_like(first)
    left = [jnp.where(low, first, zero), jnp.where(low, zero, first), zero, zero]
    right = [zero, zero, jnp.where(low, second, zero), jnp.where(low, zero, second)]
    return jnp.concatenate([jnp.concatenate(left, axis=0), jnp.concatenate(right, axis=0)], axis=1)


def folded(square):
    low = low_lanes(HALF)
    moved = swapped(jnp.where(low, square[HALF : 2 * HALF], square[2 * HALF : 3 * HALF]))
    return [jnp.where(low, square[:HALF], moved), jnp.where(low, moved, square[3 * HALF :])]


def straightened(even, odd):
    low = low_lanes(HALF // 2)
    return jnp.concatenate([jnp.where(low, even, swapped(odd)), jnp.where(low, swapped(even), odd)], axis=0)


def diagonal(square):
    return jnp.where(low_lanes(NODES), square[:NODES], square[NODES:]).astype(jnp.bfloat16)


def apart(first, second):
    zero = jnp.zeros_like(first)
    return jnp.concatenate([jnp.concatenate([first, zero], axis=1), jnp.concatenate([zero, second], axis=1)], axis=0)


def two_pairs(squares):
    return folded(squares[:, :LANES]) + folded(squares[:, LANES:])


def add_all(updates):
    olds = [total[key] for total, key, _ in updates]
    news = []
    for number, (total, key, value) in enumerate(updates):
        for other, other_key, other_value in updates[:number]:
            if other is total:
                value = value + jnp.where(key == other_key, other_value, jnp.zeros_like(other_value))
        news.append(olds[number] + value)
    for (total, key, _), new in zip(updates, news):
        total[key] = new


def prepare_kernel(place_ref, p_ref, fx_ref, fy_ref, fz_ref, natural_ref, turned_ref, swap_x_ref, swap_y_ref, near_z_ref, far_z_ref,
                   first_z_ref, last_z_ref, tail_x_ref, tail_y_ref, tail_z_ref, stages, stages_f, stacks, ends):
    plane = pl.program_id(0)
    size_y, depth = p_ref.shape[0], p_ref.shape[1]
    pairs = depth // 2

    for j in range(size_y):
        stage = stages.at[j]
        spread(p_ref[j], stage)
        block = [block_of(stage, z, depth) for z in range(depth)]
        stacked = [stacked_pair(block[2 * p], block[2 * p + 1]) for p in range(pairs)]
        natural = in_order(stacked)
        for p in range(pairs):
            stacks[j, p] = stacked[p]
            natural_ref[j, p] = natural[p]
        for h in range(pairs // 2):
            turned_ref[j, h] = jnp.concatenate([stacked[2 * h], stacked[2 * h + 1]], axis=0).T
        ends[0, j] = block[0]
        ends[1, j] = block[depth - 1]
        stage_f = stages_f.at[j]
        spread(fz_ref[0, j], stage_f)
        last = block_of(stage_f, depth - 1, depth)
        ends[2, j] = last

    heads = in_order([stacked_pair(ends[0, 2 * t], ends[0, 2 * t + 1]) for t in range(size_y // 2)])
    for t, head in enumerate(heads):
        last, face = [stacked_pair(ends[kind, 2 * t], ends[kind, 2 * t + 1]) for kind in (1, 2)]
        rim = diagonal(across(face, last))
        first_z_ref[t] = head
        last_z_ref[t] = last
        tail_z_ref[t] = face
        near_z_ref[t] = jnp.where(place_ref[2] % 2 == 0, rim, head)
        far_z_ref[t] = jnp.where(place_ref[2] % 2 == 0, head, rim)

    def faces(source, stage, j, tails, rims):
        spread(source, stage)
        block = [block_of(stage, z, depth) for z in range(depth)]
        for p in range(pairs):
            tails[p] = stacked_pair(block[2 * p], block[2 * p + 1])
            rims[p] = diagonal(across(tails[p], stacks[j, p]))

    @pl.when(place_ref[1] == 0)
    def _():
        faces(fy_ref[0, 0], stages_f.at[0], size_y - 1, tail_y_ref.at[0], swap_y_ref.at[0])

    @pl.when(place_ref[1] != 0)
    def _():
        swap_y_ref[0] = natural_ref[0]

    @pl.when((place_ref[0] == 0) & (plane == pl.num_programs(0) - 1))
    def _():
        for j in range(size_y):
            faces(fx_ref[0, j], stages_f.at[j], j, tail_x_ref.at[j], swap_x_ref.at[j])

    @pl.when((place_ref[0] != 0) & (plane == 0))
    def _():
        swap_x_ref[...] = natural_ref[...]


def prepare(place, prolong, faces, sizes):
    size_x, size_y, depth = sizes
    pairs, block = depth // 2, prolong.shape[-1]
    columns, half = size_x * size_y, size_y // 2
    shape = lambda *dims: jax.ShapeDtypeStruct(dims, jnp.bfloat16)
    by_half = pl.BlockSpec((half, NODES, LANES), lambda i: (i, 0, 0))
    edge = shape(columns // 2, NODES, LANES)
    stage = pltpu.VMEM((size_y, depth * HALF, LANES), jnp.float32)
    return pl.pallas_call(
        prepare_kernel,
        grid=(size_x,),
        in_specs=[
            pl.BlockSpec(memory_space=pltpu.SMEM),
            pl.BlockSpec((size_y, depth, block), lambda i: (i, 0, 0)),
            pl.BlockSpec((1, size_y, depth, block), lambda i: (0, size_x - 1, 0, 0)),
            pl.BlockSpec((1, 1, depth, block), lambda i: (1, i * size_y + size_y - 1, 0, 0)),
            pl.BlockSpec((1, size_y, depth, block), lambda i: (2, i, 0, 0)),
        ],
        out_specs=[
            pl.BlockSpec((size_y, pairs, NODES, LANES), lambda i: (i, 0, 0, 0)),
            pl.BlockSpec((size_y, pairs // 2, LANES, LANES), lambda i: (i, 0, 0, 0)),
            pl.BlockSpec((size_y, pairs, NODES, LANES), lambda i: (0, 0, 0, 0)),
            pl.BlockSpec((1, pairs, NODES, LANES), lambda i: (i, 0, 0, 0)),
            by_half, by_half, by_half, by_half,
            pl.BlockSpec((size_y, pairs, NODES, LANES), lambda i: (0, 0, 0, 0)),
            pl.BlockSpec((1, pairs, NODES, LANES), lambda i: (i, 0, 0, 0)),
            by_half,
        ],
        out_shape=[
            shape(columns, pairs, NODES, LANES), shape(columns, pairs // 2, LANES, LANES),
            shape(size_y, pairs, NODES, LANES), shape(size_x, pairs, NODES, LANES), edge, edge, edge, edge,
            shape(size_y, pairs, NODES, LANES), shape(size_x, pairs, NODES, LANES), edge,
        ],
        scratch_shapes=[
            stage, stage,
            pltpu.VMEM((size_y, pairs, NODES, LANES), jnp.bfloat16),
            pltpu.VMEM((3, size_y, HALF, LANES), jnp.bfloat16),
        ],
        compiler_params=pltpu.CompilerParams(vmem_limit_bytes=48 * MIB),
        name="prepare",
    )(place, prolong, faces, faces, faces)


def interior_kernel(keys, diag_ref, face_ref, natural_ref, turned_ref, out_ref,
                    stages, ahead_even, ahead_odd, behind_even, behind_odd, wide):
    _, size_x, size_y, depth = keys.shape
    pairs = depth // 2
    spare = out_ref.shape[0]
    ahead, behind = (ahead_even, ahead_odd), (behind_even, behind_odd)

    for total in ahead + behind:
        total[...] = jnp.zeros_like(total)

    def couplings(i, j, stage, has_x):
        column = i * size_y + j
        sources = [diag_ref[column], face_ref[0, column - size_y] if has_x else None, face_ref[1, column - 1] if j else None, face_ref[2, column]]
        stacked = {}
        for face, source in enumerate(sources):
            if source is None:
                continue
            spread(source, stage.at[face])
            shift = 1 if face == 3 else 0
            block = [block_of(stage.at[face], z, depth) for z in range(depth)]
            stacked[face] = [stacked_pair(block[(2 * p - shift) % depth], block[2 * p + 1 - shift]) for p in range(pairs)]
        couples = {face: [] for face in stacked}
        for h in range(pairs // 2):
            left = [jnp.concatenate([rows[2 * h], rows[2 * h + 1]], axis=1) for rows in stacked.values()]
            weights = four_weights(natural_ref[column, 2 * h], natural_ref[column, 2 * h + 1])
            four = product(jnp.concatenate(left, axis=0), weights).astype(jnp.bfloat16)
            for number, face in enumerate(stacked):
                rows = four[NODES * number : NODES * (number + 1)]
                for couple in (rows[:, :LANES], rows[:, LANES:]):
                    couples[face].append(swapped(couple) if face == 3 else couple)
        low = low_lanes(NODES)
        along = couples[3]
        couples[3] = [jnp.where(low, along[p], along[min(p + 1, pairs - 1)]) for p in range(pairs)]
        return couples

    def sums(i, j, couples):
        column = i * size_y + j
        origin = {0: column, 1: column - size_y, 2: column - 1, 3: column}
        batches = []
        for h in range(pairs // 2):
            for face, pair in couples.items():
                four = two_pairs(product(turned_ref[origin[face], h], apart(pair[2 * h], pair[2 * h + 1])))
                updates = []
                for number, term in enumerate(four):
                    z, side = 4 * h + number, number % 2
                    if face == 0:
                        updates.append((ahead[side], keys[0, i, j, z], term))
                        continue
                    if face == 1:
                        here, there = keys[2, i - 1, j, z], keys[1, i, j, z]
                    elif face == 2:
                        here, there = keys[4, i, j - 1, z], keys[3, i, j, z]
                    elif z + 1 < depth:
                        here, there = keys[6, i, j, z], keys[5, i, j, z + 1]
                    else:
                        continue
                    updates.append((ahead[side], here, term))
                    updates.append((behind[side], there, term))
                batches.append(updates)
        return batches

    def plane(i, carry, has_x=True):
        couples = [couplings(i, j, stages.at[j], has_x) for j in range(size_y)]
        for updates in [updates for j in range(size_y) for updates in sums(i, j, couples[j])]:
            add_all(updates)
        return carry

    plane(0, 0, has_x=False)
    lax.fori_loop(1, size_x, plane, 0)

    def finish(g, carry):
        low = low_lanes(HALF)
        spots = [(p, [wide.shape[0] * 2 * g + 2 * p + side for side in (0, 1)]) for p in range(wide.shape[0])]
        for p, key in spots:
            one, two = [behind_even[key[side]] + behind_odd[key[side]] for side in (0, 1)]
            upper = jnp.where(low, one, swapped(two))
            lower = jnp.where(low, swapped(one), two)
            wide[p, :, :NODES] = jnp.concatenate([upper, lower], axis=0).T
        for p, key in spots:
            for side in (0, 1):
                first = wide[p, NODES * side : NODES * side + HALF, :]
                second = wide[p, NODES * side + HALF : NODES * (side + 1), :]
                turned = jnp.where(low, first, swapped(second))
                out_ref[key[side]] = (ahead_even[key[side]] + ahead_odd[key[side]]) + turned
        return carry

    lax.fori_loop(0, spare // (2 * wide.shape[0]), finish, 0)


def interior(keys, diag, faces, natural, turned, sizes):
    size_x, size_y, depth = sizes
    pairs, block = depth // 2, diag.shape[-1]
    columns, rows = size_x * size_y, AGG_DEV * SLOTS
    total = pltpu.VMEM((rows, HALF, LANES), jnp.float32)
    whole = pl.BlockSpec(memory_space=pltpu.VMEM)
    return pl.pallas_call(
        interior_kernel,
        in_specs=[pl.BlockSpec(memory_space=pltpu.SMEM), whole, whole, whole, whole],
        out_specs=whole,
        out_shape=jax.ShapeDtypeStruct((rows, HALF, LANES), jnp.float32),
        scratch_shapes=[
            pltpu.VMEM((size_y, 4, depth * HALF, LANES), jnp.float32),
            total, total, total, total,
            pltpu.VMEM((12, LANES, LANES), jnp.float32),
        ],
        compiler_params=pltpu.CompilerParams(vmem_limit_bytes=28 * MIB),
        cost_estimate=pl.CostEstimate(flops=columns * depth * 14 * NODES**3, bytes_accessed=columns * depth * 6 * block * 2, transcendentals=0),
        name="interior",
    )(keys, diag, faces, natural, turned)


def border_kernel(capacity, paired, first_part, owners, place_ref, keys, got_x, got_y, near_z, far_z, tail_x, tail_y, tail_z, turned_x, turned_y,
                  natural_x, natural_y, first_z, last_z, start_ref, *refs):
    out_refs, (total, filled, listed) = refs[:-3], refs[-3:]
    size_y, pairs = tail_x.shape[0], tail_x.shape[1]
    size_x, depth = tail_y.shape[0], 2 * pairs
    rows = start_ref.shape[0]

    def key_at(number, i, j, z):
        return keys[number, i, j, z]

    def couplings(tail, head):
        left = jnp.concatenate(tail, axis=1)
        four = product(left, four_weights(*head)).astype(jnp.bfloat16)
        return four[:, :LANES], four[:, LANES:]

    def ahead(tail, head, turned, key):
        for h in range(pairs // 2):
            couples = couplings([tail[2 * h], tail[2 * h + 1]], [head[2 * h], head[2 * h + 1]])
            four = two_pairs(product(turned[h], apart(*couples)))
            yield [(total, key(4 * h + number), term) for number, term in enumerate(four)]

    def turned_terms(first, second, rims):
        return two_pairs(product(jnp.concatenate([first, second], axis=0).T, apart(*rims)))

    def back(natural, rim, key):
        for h in range(pairs // 2):
            four = turned_terms(natural[2 * h], natural[2 * h + 1], (rim[2 * h], rim[2 * h + 1]))
            yield [(total, key(4 * h + number), term) for number, term in enumerate(four)]

    def batches_x(first):
        for j in range(size_y):
            if first:
                yield from ahead(tail_x.at[j], got_x.at[j], turned_x.at[j], functools.partial(key_at, 2, size_x - 1, j))
            else:
                yield from back(natural_x.at[j], got_x.at[j], functools.partial(key_at, 1, 0, j))

    def batches_y(first):
        for i in range(size_x):
            if first:
                yield from ahead(tail_y.at[i], got_y.at[i], turned_y.at[i, 0], functools.partial(key_at, 4, i, size_y - 1))
            else:
                yield from back(natural_y.at[i, 0], got_y.at[i], functools.partial(key_at, 3, i, 0))

    def batches_z():
        even = place_ref[2] % 2 == 0
        for t in range(0, near_z.shape[0], 2):
            heads = [jnp.where(even, near_z[u], far_z[u]) for u in (t, t + 1)]
            couples = couplings([tail_z[t], tail_z[t + 1]], heads)
            front = turned_terms(last_z[t], last_z[t + 1], couples)
            past = turned_terms(first_z[t], first_z[t + 1], [jnp.where(even, far_z[u], near_z[u]) for u in (t, t + 1)])
            spots = [(2 * u // size_y, 2 * u % size_y + side) for u in (t, t + 1) for side in (0, 1)]
            yield [(total, keys[6, i, j, depth - 1], term) for (i, j), term in zip(spots, front)]
            yield [(total, keys[5, i, j, 0], term) for (i, j), term in zip(spots, past)]

    for first_x in (True, False):
        for first_y in (True, False):
            @pl.when(((place_ref[0] == 0) == first_x) & ((place_ref[1] == 0) == first_y))
            def _():
                batches = list(batches_x(first_x)) + list(batches_y(first_y)) + list(batches_z())
                for updates in batches:
                    add_all(updates)

    emit(capacity, paired, first_part, owners, place_ref, total, out_refs, filled, listed)


def emit(capacity, paired, first_part, owners, place_ref, total, out_refs, filled, listed):
    rows, devices = total.shape[0] // SLOTS, filled.shape[0]
    for spot in range(capacity * devices):
        listed[spot] = -1
    for owner in range(devices):
        filled[owner] = 0
    for r in range(rows):
        owner = owners[r]
        listed[jnp.bitwise_xor(owner, place_ref[2] if paired else 0) * capacity + filled[owner]] = r
        filled[owner] = filled[owner] + 1
    for part, out_ref in enumerate(out_refs):
        for q in range(capacity):
            row = listed[(first_part + part) * capacity + q]
            for s in range(SLOTS):
                key = jnp.maximum(row, 0) * SLOTS + s
                even, odd = [total[key, pl.ds(first, HALF // 2, stride=2), :] for first in (0, 1)]
                block = straightened(even, odd)
                if capacity * devices != rows:
                    block = jnp.where(row >= 0, block, jnp.zeros_like(block))
                out_ref[q, HALF * s : HALF * (s + 1), :] = block.astype(jnp.bfloat16)


def near_kernel(capacity, owners, place_ref, total, arrived, *refs):
    emit(capacity, True, 0, owners, place_ref, total, refs[:-2], *refs[-2:])


def near_parts(owners, place, total, arrived, capacity, count, devices):
    smem = pl.BlockSpec(memory_space=pltpu.SMEM)
    whole = pl.BlockSpec(memory_space=pltpu.VMEM)
    return pl.pallas_call(
        functools.partial(near_kernel, capacity),
        in_specs=[smem, smem, whole, pl.BlockSpec(memory_space=pl.ANY)],
        out_specs=[whole] * count,
        out_shape=[jax.ShapeDtypeStruct((capacity, SLOTS * HALF, LANES), jnp.bfloat16)] * count,
        scratch_shapes=[pltpu.SMEM((devices,), jnp.int32), pltpu.SMEM((capacity * devices,), jnp.int32)],
        compiler_params=pltpu.CompilerParams(vmem_limit_bytes=10 * MIB),
        name="near",
    )(owners, place, total, arrived)


def border(owners, place, keys, operands, turned, natural, ends, total, capacity, devices, paired, first_part, sizes):
    size_x, size_y, depth = sizes
    pairs = depth // 2
    smem = pl.BlockSpec(memory_space=pltpu.SMEM)
    whole = pl.BlockSpec(memory_space=pltpu.VMEM)
    planes = lambda array: array.reshape((size_x, size_y) + array.shape[1:])
    before = 3 + len(operands) + 4 + len(ends)
    count = devices - first_part
    return pl.pallas_call(
        functools.partial(border_kernel, capacity, paired, first_part),
        grid=(1,),
        in_specs=[smem, smem, smem] + [whole] * len(operands) + [
            pl.BlockSpec((size_y, pairs // 2, LANES, LANES), lambda i: (size_x - 1, 0, 0, 0)),
            pl.BlockSpec((size_x, 1, pairs // 2, LANES, LANES), lambda i: (0, size_y - 1, 0, 0, 0)),
            pl.BlockSpec((size_y, pairs, NODES, LANES), lambda i: (0, 0, 0, 0)),
            pl.BlockSpec((size_x, 1, pairs, NODES, LANES), lambda i: (0, 0, 0, 0, 0)),
        ] + [whole] * (len(ends) + 1),
        out_specs=[whole] * (count + 1),
        out_shape=[jax.ShapeDtypeStruct((capacity, SLOTS * HALF, LANES), jnp.bfloat16)] * count
        + [jax.ShapeDtypeStruct(total.shape, total.dtype)],
        input_output_aliases={before: count},
        scratch_shapes=[pltpu.SMEM((devices,), jnp.int32), pltpu.SMEM((capacity * devices,), jnp.int32)],
        compiler_params=pltpu.CompilerParams(vmem_limit_bytes=18 * MIB),
        name="border",
    )(owners, place, keys, *operands, turned, planes(turned), natural, planes(natural), *ends, total)


def layout_kernel(source, rows_ref, out_ref, stage):
    group = pl.program_id(0)
    height = out_ref.shape[1]
    for s in range(SLOTS):
        for r in range(height):
            row = source[group * height + r]
            block = rows_ref[jnp.maximum(row, 0), HALF * s : HALF * (s + 1), :].astype(jnp.float32)
            stage[s, pl.ds(r, HALF, stride=height), :] = jnp.where(row >= 0, block, jnp.zeros_like(block))
        for k in range(HALF):
            out_ref[s, :, LANES * k : LANES * (k + 1)] = stage[s, height * k : height * (k + 1), :].astype(jnp.bfloat16)


def laid_out(source, rows, block):
    places, height = rows.shape[0], 8
    return pl.pallas_call(
        layout_kernel,
        grid=(places // height,),
        in_specs=[pl.BlockSpec(memory_space=pltpu.SMEM), pl.BlockSpec(memory_space=pltpu.VMEM)],
        out_specs=pl.BlockSpec((SLOTS, height, block), lambda g: (0, g, 0)),
        out_shape=jax.ShapeDtypeStruct((SLOTS, places, block), jnp.bfloat16),
        scratch_shapes=[pltpu.VMEM((SLOTS, height * HALF, LANES), jnp.float32)],
        compiler_params=pltpu.CompilerParams(vmem_limit_bytes=10 * MIB),
        name="layout",
    )(source, rows)


def placed_kernel(place_ref, *refs):
    parts, (out_ref, stage) = refs[:-2], refs[-2:]
    capacity, height = parts[0].shape[0], out_ref.shape[1]
    for number, rows_ref in enumerate(parts):
        first = jnp.bitwise_xor(place_ref[2], number) * capacity
        for q in range(capacity):
            for s in range(SLOTS):
                block = rows_ref[q, HALF * s : HALF * (s + 1), :].astype(jnp.float32)
                stage[s, pl.ds(first + q, HALF, stride=height), :] = block
    for s in range(SLOTS):
        for k in range(HALF):
            out_ref[s, :, LANES * k : LANES * (k + 1)] = stage[s, height * k : height * (k + 1), :].astype(jnp.bfloat16)


def placed(place, parts, block):
    places = parts[0].shape[0] * len(parts)
    whole = pl.BlockSpec(memory_space=pltpu.VMEM)
    return pl.pallas_call(
        placed_kernel,
        in_specs=[pl.BlockSpec(memory_space=pltpu.SMEM)] + [whole] * len(parts),
        out_specs=whole,
        out_shape=jax.ShapeDtypeStruct((SLOTS, places, block), jnp.bfloat16),
        scratch_shapes=[pltpu.VMEM((SLOTS, places * HALF, LANES), jnp.float32)],
        compiler_params=pltpu.CompilerParams(vmem_limit_bytes=16 * MIB),
        name="placed",
    )(place, *parts)


def shards(a_diag, a_face, prolong, aggregate, pair_slot, row_owner):
    size_x, size_y, size_z, block = a_diag.shape
    sizes = (size_x, size_y, size_z)
    columns = size_x * size_y
    depth = lax.axis_size("gz")
    capacity = max(2, (AGG_DEV + depth - 1) // depth)
    holding = capacity * depth
    diag = a_diag.reshape(columns, size_z, block)
    faces = a_face.reshape(3, columns, size_z, block)
    assert lax.axis_size("gx") == 2 and lax.axis_size("gy") == 2
    place = jnp.stack([lax.axis_index("gx"), lax.axis_index("gy"), lax.axis_index("gz")]).astype(jnp.int32)
    keys = aggregate[None] * SLOTS + pair_slot

    natural, turned, swap_x, swap_y, near_z, far_z, first_z, last_z, tail_x, tail_y, tail_z = prepare(
        place, prolong.reshape(columns, size_z, block), faces, sizes)
    near_z = swapped_along(near_z, "gz", 0)
    far_z = swapped_along(far_z, "gz", 1)
    got_y = swapped_along(swap_y, "gy", 0)
    got_x = swapped_along(swap_x, "gx", 0)
    total = interior(keys, diag, faces, natural, turned, sizes)
    paired = holding == AGG_DEV and depth & (depth - 1) == 0
    first_part = depth // 2 if paired else 0
    *outgoing, total = border(
        row_owner, place, keys, (got_x, got_y, near_z, far_z, tail_x, tail_y, tail_z), turned, natural,
        (first_z, last_z), total, capacity, depth, paired, first_part, sizes)
    if paired:
        def swapped_with(part, k):
            return lax.ppermute(part, "gz", [(i, i ^ k) for i in range(depth)]) if k else part

        far = [swapped_with(part, first_part + k) for k, part in enumerate(outgoing)]
        near = [swapped_with(part, k) for k, part in enumerate(near_parts(row_owner, place, total, far[0], capacity, first_part, depth))]
        parts = near + far
        result = placed(place, parts, block)
    else:
        arrived = lax.all_to_all(jnp.concatenate(outgoing, axis=0), "gz", 0, 0, tiled=True)
        slots = jnp.arange(holding, dtype=jnp.int32)
        owner_ids = jnp.arange(depth, dtype=jnp.int32)
        counts = jnp.sum((row_owner[:, None] == owner_ids[None, :]).astype(jnp.int32), axis=0)
        arrived_counts = lax.all_to_all(counts, "gz", 0, 0, tiled=True)
        present = slots % capacity < jnp.repeat(arrived_counts, capacity)
        target = jnp.cumsum(present.astype(jnp.int32)) - 1
        match = (present[None, :] & (target[None, :] == slots[:, None])).astype(jnp.int32)
        result = laid_out(jnp.sum(match * (slots[None, :] + 1), axis=1) - 1, arrived, block)
    return jnp.transpose(result, (1, 0, 2)).reshape(1, 1, 1, holding, SLOTS, block)


def solution(mesh):
    return jax.shard_map(
        shards,
        mesh=mesh,
        in_specs=(
            P("gx", "gy", "gz", None),
            P(None, "gx", "gy", "gz", None),
            P("gx", "gy", "gz", None),
            P("gx", "gy", "gz"),
            P(None, "gx", "gy", "gz"),
            P(("gx", "gy", "gz")),
        ),
        out_specs=P("gx", "gy", "gz", None, None, None),
        check_vma=False,
    )
```

```python
import functools

import jax
import jax.numpy as jnp
from jax import lax
from jax.experimental import pallas as pl
from jax.experimental.pallas import tpu as pltpu
from jax.sharding import PartitionSpec as P

NODES = 64
SLOTS = 7
AGG_DEV = 24
LANES = 128
HALF = NODES // 2
MIB = 1024 * 1024
STEP = 8


def swapped_along(block, axis, first):
    pairs = [(i, i + 1) for i in range(first, lax.axis_size(axis) - 1, 2)]
    return lax.ppermute(block, axis, pairs + [(i + 1, i) for i, _ in pairs])


def low_lanes(rows):
    return lax.broadcasted_iota(jnp.int32, (rows, LANES), 1) < NODES


def swapped(value):
    return pltpu.roll(value, NODES, 1)


def zero_one(mask):
    return mask.astype(jnp.float32).astype(jnp.bfloat16)


def product(left, right):
    return jnp.dot(left, right, preferred_element_type=jnp.float32)


def across(left, right):
    return lax.dot_general(left, right, (((0,), (0,)), ((), ())), preferred_element_type=jnp.float32)


def spread(column, stage):
    depth = column.shape[0]
    for k in range(column.shape[1] // LANES):
        stage[depth * k : depth * (k + 1), :] = column[:, LANES * k : LANES * (k + 1)].astype(jnp.float32)


def block_of(stage, z, depth):
    return stage[pl.ds(z, HALF, stride=depth), :].astype(jnp.bfloat16)


def stacked_pair(first, second):
    low = low_lanes(HALF)
    even = jnp.where(low, first, swapped(second))
    odd = jnp.where(low, swapped(first), second)
    return jnp.concatenate([even, odd], axis=0)


def in_order(pairs):
    row = lax.broadcasted_iota(jnp.int32, (NODES, NODES), 0)
    col = lax.broadcasted_iota(jnp.int32, (NODES, NODES), 1)
    moved = product(zero_one(row == 2 * (col % HALF) + col // HALF), jnp.concatenate(pairs, axis=1)).astype(jnp.bfloat16)
    return [moved[:, LANES * p : LANES * (p + 1)] for p in range(len(pairs))]


def four_weights(first, second):
    low = low_lanes(NODES)
    zero = jnp.zeros_like(first)
    left = [jnp.where(low, first, zero), jnp.where(low, zero, first), zero, zero]
    right = [zero, zero, jnp.where(low, second, zero), jnp.where(low, zero, second)]
    return jnp.concatenate([jnp.concatenate(left, axis=0), jnp.concatenate(right, axis=0)], axis=1)


def folded(square):
    low = low_lanes(HALF)
    moved = swapped(jnp.where(low, square[HALF : 2 * HALF], square[2 * HALF : 3 * HALF]))
    return [jnp.where(low, square[:HALF], moved), jnp.where(low, moved, square[3 * HALF :])]


def straightened(even, odd):
    low = low_lanes(HALF // 2)
    return jnp.concatenate([jnp.where(low, even, swapped(odd)), jnp.where(low, swapped(even), odd)], axis=0)


def diagonal(square):
    return jnp.where(low_lanes(NODES), square[:NODES], square[NODES:]).astype(jnp.bfloat16)


def apart(first, second):
    zero = jnp.zeros_like(first)
    return jnp.concatenate([jnp.concatenate([first, zero], axis=1), jnp.concatenate([zero, second], axis=1)], axis=0)


def two_pairs(squares):
    return folded(squares[:, :LANES]) + folded(squares[:, LANES:])


def add_all(updates):
    olds = [total[key] for total, key, _ in updates]
    news = []
    for number, (total, key, value) in enumerate(updates):
        for other, other_key, other_value in updates[:number]:
            if other is total:
                value = value + jnp.where(key == other_key, other_value, jnp.zeros_like(other_value))
        news.append(olds[number] + value)
    for (total, key, _), new in zip(updates, news):
        total[key] = new


def prepare_kernel(place_ref, p_ref, fx_ref, fy_ref, fz_ref, natural_ref, turned_ref, swap_x_ref, swap_y_ref, near_z_ref, far_z_ref,
                   first_z_ref, last_z_ref, tail_x_ref, tail_y_ref, tail_z_ref, stages, stages_f, stacks, ends):
    plane = pl.program_id(0)
    size_y, depth = p_ref.shape[0], p_ref.shape[1]
    pairs = depth // 2

    for j in range(size_y):
        stage = stages.at[j]
        spread(p_ref[j], stage)
        block = [block_of(stage, z, depth) for z in range(depth)]
        stacked = [stacked_pair(block[2 * p], block[2 * p + 1]) for p in range(pairs)]
        natural = in_order(stacked)
        for p in range(pairs):
            stacks[j, p] = stacked[p]
            natural_ref[j, p] = natural[p]
        for h in range(pairs // 2):
            turned_ref[j, h] = jnp.concatenate([stacked[2 * h], stacked[2 * h + 1]], axis=0).T
        ends[0, j] = block[0]
        ends[1, j] = block[depth - 1]
        stage_f = stages_f.at[j]
        spread(fz_ref[0, j], stage_f)
        last = block_of(stage_f, depth - 1, depth)
        ends[2, j] = last

    heads = in_order([stacked_pair(ends[0, 2 * t], ends[0, 2 * t + 1]) for t in range(size_y // 2)])
    for t, head in enumerate(heads):
        last, face = [stacked_pair(ends[kind, 2 * t], ends[kind, 2 * t + 1]) for kind in (1, 2)]
        rim = diagonal(across(face, last))
        first_z_ref[t] = head
        last_z_ref[t] = last
        tail_z_ref[t] = face
        near_z_ref[t] = jnp.where(place_ref[2] % 2 == 0, rim, head)
        far_z_ref[t] = jnp.where(place_ref[2] % 2 == 0, head, rim)

    def faces(source, stage, j, tails, rims):
        spread(source, stage)
        block = [block_of(stage, z, depth) for z in range(depth)]
        for p in range(pairs):
            tails[p] = stacked_pair(block[2 * p], block[2 * p + 1])
            rims[p] = diagonal(across(tails[p], stacks[j, p]))

    @pl.when(place_ref[1] == 0)
    def _():
        faces(fy_ref[0, 0], stages_f.at[0], size_y - 1, tail_y_ref.at[0], swap_y_ref.at[0])

    @pl.when(place_ref[1] != 0)
    def _():
        swap_y_ref[0] = natural_ref[0]

    @pl.when((place_ref[0] == 0) & (plane == pl.num_programs(0) - 1))
    def _():
        for j in range(size_y):
            faces(fx_ref[0, j], stages_f.at[j], j, tail_x_ref.at[j], swap_x_ref.at[j])

    @pl.when((place_ref[0] != 0) & (plane == 0))
    def _():
        swap_x_ref[...] = natural_ref[...]


def prepare(place, prolong, faces, sizes):
    size_x, size_y, depth = sizes
    pairs, block = depth // 2, prolong.shape[-1]
    columns, half = size_x * size_y, size_y // 2
    shape = lambda *dims: jax.ShapeDtypeStruct(dims, jnp.bfloat16)
    by_half = pl.BlockSpec((half, NODES, LANES), lambda i: (i, 0, 0))
    edge = shape(columns // 2, NODES, LANES)
    stage = pltpu.VMEM((size_y, depth * HALF, LANES), jnp.float32)
    return pl.pallas_call(
        prepare_kernel,
        grid=(size_x,),
        in_specs=[
            pl.BlockSpec(memory_space=pltpu.SMEM),
            pl.BlockSpec((size_y, depth, block), lambda i: (i, 0, 0)),
            pl.BlockSpec((1, size_y, depth, block), lambda i: (0, size_x - 1, 0, 0)),
            pl.BlockSpec((1, 1, depth, block), lambda i: (1, i * size_y + size_y - 1, 0, 0)),
            pl.BlockSpec((1, size_y, depth, block), lambda i: (2, i, 0, 0)),
        ],
        out_specs=[
            pl.BlockSpec((size_y, pairs, NODES, LANES), lambda i: (i, 0, 0, 0)),
            pl.BlockSpec((size_y, pairs // 2, LANES, LANES), lambda i: (i, 0, 0, 0)),
            pl.BlockSpec((size_y, pairs, NODES, LANES), lambda i: (0, 0, 0, 0)),
            pl.BlockSpec((1, pairs, NODES, LANES), lambda i: (i, 0, 0, 0)),
            by_half, by_half, by_half, by_half,
            pl.BlockSpec((size_y, pairs, NODES, LANES), lambda i: (0, 0, 0, 0)),
            pl.BlockSpec((1, pairs, NODES, LANES), lambda i: (i, 0, 0, 0)),
            by_half,
        ],
        out_shape=[
            shape(columns, pairs, NODES, LANES), shape(columns, pairs // 2, LANES, LANES),
            shape(size_y, pairs, NODES, LANES), shape(size_x, pairs, NODES, LANES), edge, edge, edge, edge,
            shape(size_y, pairs, NODES, LANES), shape(size_x, pairs, NODES, LANES), edge,
        ],
        scratch_shapes=[
            stage, stage,
            pltpu.VMEM((size_y, pairs, NODES, LANES), jnp.bfloat16),
            pltpu.VMEM((3, size_y, HALF, LANES), jnp.bfloat16),
        ],
        compiler_params=pltpu.CompilerParams(vmem_limit_bytes=48 * MIB),
        name="prepare",
    )(place, prolong, faces, faces, faces)


def interior_kernel(keys, diag_ref, face_ref, natural_ref, turned_ref, out_ref,
                    stages, ahead_even, ahead_odd, behind_even, behind_odd, wide):
    _, size_x, size_y, depth = keys.shape
    pairs = depth // 2
    spare = out_ref.shape[0]
    ahead, behind = (ahead_even, ahead_odd), (behind_even, behind_odd)

    for total in ahead + behind:
        total[...] = jnp.zeros_like(total)

    def couplings(i, j, stage, has_x):
        column = i * size_y + j
        sources = [diag_ref[column], face_ref[0, column - size_y] if has_x else None, face_ref[1, column - 1] if j else None, face_ref[2, column]]
        stacked = {}
        for face, source in enumerate(sources):
            if source is None:
                continue
            spread(source, stage.at[face])
            shift = 1 if face == 3 else 0
            block = [block_of(stage.at[face], z, depth) for z in range(depth)]
            stacked[face] = [stacked_pair(block[(2 * p - shift) % depth], block[2 * p + 1 - shift]) for p in range(pairs)]
        couples = {face: [] for face in stacked}
        for h in range(pairs // 2):
            left = [jnp.concatenate([rows[2 * h], rows[2 * h + 1]], axis=1) for rows in stacked.values()]
            weights = four_weights(natural_ref[column, 2 * h], natural_ref[column, 2 * h + 1])
            four = product(jnp.concatenate(left, axis=0), weights).astype(jnp.bfloat16)
            for number, face in enumerate(stacked):
                rows = four[NODES * number : NODES * (number + 1)]
                for couple in (rows[:, :LANES], rows[:, LANES:]):
                    couples[face].append(swapped(couple) if face == 3 else couple)
        low = low_lanes(NODES)
        along = couples[3]
        couples[3] = [jnp.where(low, along[p], along[min(p + 1, pairs - 1)]) for p in range(pairs)]
        return couples

    def sums(i, j, couples):
        column = i * size_y + j
        origin = {0: column, 1: column - size_y, 2: column - 1, 3: column}
        batches = []
        for h in range(pairs // 2):
            for face, pair in couples.items():
                four = two_pairs(product(turned_ref[origin[face], h], apart(pair[2 * h], pair[2 * h + 1])))
                updates = []
                for number, term in enumerate(four):
                    z, side = 4 * h + number, number % 2
                    if face == 0:
                        updates.append((ahead[side], keys[0, i, j, z], term))
                        continue
                    if face == 1:
                        here, there = keys[2, i - 1, j, z], keys[1, i, j, z]
                    elif face == 2:
                        here, there = keys[4, i, j - 1, z], keys[3, i, j, z]
                    elif z + 1 < depth:
                        here, there = keys[6, i, j, z], keys[5, i, j, z + 1]
                    else:
                        continue
                    updates.append((ahead[side], here, term))
                    updates.append((behind[side], there, term))
                batches.append(updates)
        return batches

    def plane(i, carry, has_x=True):
        couples = [couplings(i, j, stages.at[j], has_x) for j in range(size_y)]
        for updates in [updates for j in range(size_y) for updates in sums(i, j, couples[j])]:
            add_all(updates)
        return carry

    plane(0, 0, has_x=False)
    lax.fori_loop(1, size_x, plane, 0)

    def finish(g, carry):
        low = low_lanes(HALF)
        spots = [(p, [wide.shape[0] * 2 * g + 2 * p + side for side in (0, 1)]) for p in range(wide.shape[0])]
        for p, key in spots:
            one, two = [behind_even[key[side]] + behind_odd[key[side]] for side in (0, 1)]
            upper = jnp.where(low, one, swapped(two))
            lower = jnp.where(low, swapped(one), two)
            wide[p, :, :NODES] = jnp.concatenate([upper, lower], axis=0).T
        for p, key in spots:
            for side in (0, 1):
                first = wide[p, NODES * side : NODES * side + HALF, :]
                second = wide[p, NODES * side + HALF : NODES * (side + 1), :]
                turned = jnp.where(low, first, swapped(second))
                out_ref[key[side]] = (ahead_even[key[side]] + ahead_odd[key[side]]) + turned
        return carry

    lax.fori_loop(0, spare // (2 * wide.shape[0]), finish, 0)


def interior(keys, diag, faces, natural, turned, sizes):
    size_x, size_y, depth = sizes
    pairs, block = depth // 2, diag.shape[-1]
    columns, rows = size_x * size_y, AGG_DEV * SLOTS
    total = pltpu.VMEM((rows, HALF, LANES), jnp.float32)
    whole = pl.BlockSpec(memory_space=pltpu.VMEM)
    return pl.pallas_call(
        interior_kernel,
        in_specs=[pl.BlockSpec(memory_space=pltpu.SMEM), whole, whole, whole, whole],
        out_specs=whole,
        out_shape=jax.ShapeDtypeStruct((rows, HALF, LANES), jnp.float32),
        scratch_shapes=[
            pltpu.VMEM((size_y, 4, depth * HALF, LANES), jnp.float32),
            total, total, total, total,
            pltpu.VMEM((12, LANES, LANES), jnp.float32),
        ],
        compiler_params=pltpu.CompilerParams(vmem_limit_bytes=28 * MIB),
        cost_estimate=pl.CostEstimate(flops=columns * depth * 14 * NODES**3, bytes_accessed=columns * depth * 6 * block * 2, transcendentals=0),
        name="interior",
    )(keys, diag, faces, natural, turned)


def border_kernel(capacity, paired, first_part, owners, place_ref, keys, got_x, got_y, near_z, far_z, tail_x, tail_y, tail_z, turned_x, turned_y,
                  natural_x, natural_y, first_z, last_z, start_ref, *refs):
    out_refs, (total, filled, listed) = refs[:-3], refs[-3:]
    size_y, pairs = tail_x.shape[0], tail_x.shape[1]
    size_x, depth = tail_y.shape[0], 2 * pairs
    rows = start_ref.shape[0]

    def key_at(number, i, j, z):
        return keys[number, i, j, z]

    def couplings(tail, head):
        left = jnp.concatenate(tail, axis=1)
        four = product(left, four_weights(*head)).astype(jnp.bfloat16)
        return four[:, :LANES], four[:, LANES:]

    def ahead(tail, head, turned, key):
        for h in range(pairs // 2):
            couples = couplings([tail[2 * h], tail[2 * h + 1]], [head[2 * h], head[2 * h + 1]])
            four = two_pairs(product(turned[h], apart(*couples)))
            yield [(total, key(4 * h + number), term) for number, term in enumerate(four)]

    def turned_terms(first, second, rims):
        return two_pairs(product(jnp.concatenate([first, second], axis=0).T, apart(*rims)))

    def back(natural, rim, key):
        for h in range(pairs // 2):
            four = turned_terms(natural[2 * h], natural[2 * h + 1], (rim[2 * h], rim[2 * h + 1]))
            yield [(total, key(4 * h + number), term) for number, term in enumerate(four)]

    def batches_x(first):
        for j in range(size_y):
            if first:
                yield from ahead(tail_x.at[j], got_x.at[j], turned_x.at[j], functools.partial(key_at, 2, size_x - 1, j))
            else:
                yield from back(natural_x.at[j], got_x.at[j], functools.partial(key_at, 1, 0, j))

    def batches_y(first):
        for i in range(size_x):
            if first:
                yield from ahead(tail_y.at[i], got_y.at[i], turned_y.at[i, 0], functools.partial(key_at, 4, i, size_y - 1))
            else:
                yield from back(natural_y.at[i, 0], got_y.at[i], functools.partial(key_at, 3, i, 0))

    def batches_z():
        even = place_ref[2] % 2 == 0
        for t in range(0, near_z.shape[0], 2):
            heads = [jnp.where(even, near_z[u], far_z[u]) for u in (t, t + 1)]
            couples = couplings([tail_z[t], tail_z[t + 1]], heads)
            front = turned_terms(last_z[t], last_z[t + 1], couples)
            past = turned_terms(first_z[t], first_z[t + 1], [jnp.where(even, far_z[u], near_z[u]) for u in (t, t + 1)])
            spots = [(2 * u // size_y, 2 * u % size_y + side) for u in (t, t + 1) for side in (0, 1)]
            yield [(total, keys[6, i, j, depth - 1], term) for (i, j), term in zip(spots, front)]
            yield [(total, keys[5, i, j, 0], term) for (i, j), term in zip(spots, past)]

    for first_x in (True, False):
        for first_y in (True, False):
            @pl.when(((place_ref[0] == 0) == first_x) & ((place_ref[1] == 0) == first_y))
            def _():
                batches = list(batches_x(first_x)) + list(batches_y(first_y)) + list(batches_z())
                for updates in batches:
                    add_all(updates)

    emit(capacity, paired, first_part, owners, place_ref, total, out_refs, filled, listed)


def emit(capacity, paired, first_part, owners, place_ref, total, out_refs, filled, listed):
    rows, devices = total.shape[0] // SLOTS, filled.shape[0]
    for spot in range(capacity * devices):
        listed[spot] = -1
    for owner in range(devices):
        filled[owner] = 0
    for r in range(rows):
        owner = owners[r]
        listed[jnp.bitwise_xor(owner, place_ref[2] if paired else 0) * capacity + filled[owner]] = r
        filled[owner] = filled[owner] + 1
    for part, out_ref in enumerate(out_refs):
        for q in range(capacity):
            row = listed[(first_part + part) * capacity + q]
            for s in range(SLOTS):
                key = jnp.maximum(row, 0) * SLOTS + s
                even, odd = [total[key, pl.ds(first, HALF // 2, stride=2), :] for first in (0, 1)]
                block = straightened(even, odd)
                if capacity * devices != rows:
                    block = jnp.where(row >= 0, block, jnp.zeros_like(block))
                out_ref[q, HALF * s : HALF * (s + 1), :] = block.astype(jnp.bfloat16)


def near_kernel(capacity, owners, place_ref, total, arrived, *refs):
    emit(capacity, True, 0, owners, place_ref, total, refs[:-2], *refs[-2:])


def near_parts(owners, place, total, arrived, capacity, count, devices):
    smem = pl.BlockSpec(memory_space=pltpu.SMEM)
    whole = pl.BlockSpec(memory_space=pltpu.VMEM)
    return pl.pallas_call(
        functools.partial(near_kernel, capacity),
        in_specs=[smem, smem, whole, pl.BlockSpec(memory_space=pl.ANY)],
        out_specs=[whole] * count,
        out_shape=[jax.ShapeDtypeStruct((capacity, SLOTS * HALF, LANES), jnp.bfloat16)] * count,
        scratch_shapes=[pltpu.SMEM((devices,), jnp.int32), pltpu.SMEM((capacity * devices,), jnp.int32)],
        compiler_params=pltpu.CompilerParams(vmem_limit_bytes=10 * MIB),
        name="near",
    )(owners, place, total, arrived)


def border(owners, place, keys, operands, turned, natural, ends, total, capacity, devices, paired, first_part, sizes):
    size_x, size_y, depth = sizes
    pairs = depth // 2
    smem = pl.BlockSpec(memory_space=pltpu.SMEM)
    whole = pl.BlockSpec(memory_space=pltpu.VMEM)
    planes = lambda array: array.reshape((size_x, size_y) + array.shape[1:])
    before = 3 + len(operands) + 4 + len(ends)
    count = devices - first_part
    return pl.pallas_call(
        functools.partial(border_kernel, capacity, paired, first_part),
        grid=(1,),
        in_specs=[smem, smem, smem] + [whole] * len(operands) + [
            pl.BlockSpec((size_y, pairs // 2, LANES, LANES), lambda i: (size_x - 1, 0, 0, 0)),
            pl.BlockSpec((size_x, 1, pairs // 2, LANES, LANES), lambda i: (0, size_y - 1, 0, 0, 0)),
            pl.BlockSpec((size_y, pairs, NODES, LANES), lambda i: (0, 0, 0, 0)),
            pl.BlockSpec((size_x, 1, pairs, NODES, LANES), lambda i: (0, 0, 0, 0, 0)),
        ] + [whole] * (len(ends) + 1),
        out_specs=[whole] * (count + 1),
        out_shape=[jax.ShapeDtypeStruct((capacity, SLOTS * HALF, LANES), jnp.bfloat16)] * count
        + [jax.ShapeDtypeStruct(total.shape, total.dtype)],
        input_output_aliases={before: count},
        scratch_shapes=[pltpu.SMEM((devices,), jnp.int32), pltpu.SMEM((capacity * devices,), jnp.int32)],
        compiler_params=pltpu.CompilerParams(vmem_limit_bytes=18 * MIB),
        name="border",
    )(owners, place, keys, *operands, turned, planes(turned), natural, planes(natural), *ends, total)


def layout_kernel(source, rows_ref, out_ref, stage):
    group = pl.program_id(0)
    height = out_ref.shape[1]
    for s in range(SLOTS):
        for r in range(height):
            row = source[group * height + r]
            block = rows_ref[jnp.maximum(row, 0), HALF * s : HALF * (s + 1), :].astype(jnp.float32)
            stage[s, pl.ds(r, HALF, stride=height), :] = jnp.where(row >= 0, block, jnp.zeros_like(block))
        for k in range(HALF):
            out_ref[s, :, LANES * k : LANES * (k + 1)] = stage[s, height * k : height * (k + 1), :].astype(jnp.bfloat16)


def laid_out(source, rows, block):
    places, height = rows.shape[0], 8
    return pl.pallas_call(
        layout_kernel,
        grid=(places // height,),
        in_specs=[pl.BlockSpec(memory_space=pltpu.SMEM), pl.BlockSpec(memory_space=pltpu.VMEM)],
        out_specs=pl.BlockSpec((SLOTS, height, block), lambda g: (0, g, 0)),
        out_shape=jax.ShapeDtypeStruct((SLOTS, places, block), jnp.bfloat16),
        scratch_shapes=[pltpu.VMEM((SLOTS, height * HALF, LANES), jnp.float32)],
        compiler_params=pltpu.CompilerParams(vmem_limit_bytes=10 * MIB),
        name="layout",
    )(source, rows)


def placed_kernel(place_ref, *refs):
    parts, (out_ref, stage, laid, done) = refs[:-4], refs[-4:]
    capacity, height = parts[0].shape[0], out_ref.shape[1]
    copies = [pltpu.make_async_copy(laid.at[s], out_ref.at[s], done.at[s]) for s in range(SLOTS)]
    for s in range(SLOTS):
        for number, rows_ref in enumerate(parts):
            first = jnp.bitwise_xor(place_ref[2], number) * capacity
            for q in range(capacity):
                block = rows_ref[q, HALF * s : HALF * (s + 1), :].astype(jnp.float32)
                stage[s, pl.ds(first + q, HALF, stride=height), :] = block
        for k in range(HALF):
            laid[s, :, LANES * k : LANES * (k + 1)] = stage[s, height * k : height * (k + 1), :].astype(jnp.bfloat16)
        copies[s].start()
    for copy in copies:
        copy.wait()


def placed(place, parts, block):
    places = parts[0].shape[0] * len(parts)
    whole = pl.BlockSpec(memory_space=pltpu.VMEM)
    return pl.pallas_call(
        placed_kernel,
        in_specs=[pl.BlockSpec(memory_space=pltpu.SMEM)] + [whole] * len(parts),
        out_specs=pl.BlockSpec(memory_space=pl.ANY),
        out_shape=jax.ShapeDtypeStruct((SLOTS, places, block), jnp.bfloat16),
        scratch_shapes=[
            pltpu.VMEM((SLOTS, places * HALF, LANES), jnp.float32),
            pltpu.VMEM((SLOTS, places, block), jnp.bfloat16),
            pltpu.SemaphoreType.DMA((SLOTS,)),
        ],
        compiler_params=pltpu.CompilerParams(vmem_limit_bytes=16 * MIB),
        name="placed",
    )(place, *parts)


def shards(a_diag, a_face, prolong, aggregate, pair_slot, row_owner):
    size_x, size_y, size_z, block = a_diag.shape
    sizes = (size_x, size_y, size_z)
    columns = size_x * size_y
    depth = lax.axis_size("gz")
    capacity = max(2, (AGG_DEV + depth - 1) // depth)
    holding = capacity * depth
    diag = a_diag.reshape(columns, size_z, block)
    faces = a_face.reshape(3, columns, size_z, block)
    assert lax.axis_size("gx") == 2 and lax.axis_size("gy") == 2
    place = jnp.stack([lax.axis_index("gx"), lax.axis_index("gy"), lax.axis_index("gz")]).astype(jnp.int32)
    keys = aggregate[None] * SLOTS + pair_slot

    natural, turned, swap_x, swap_y, near_z, far_z, first_z, last_z, tail_x, tail_y, tail_z = prepare(
        place, prolong.reshape(columns, size_z, block), faces, sizes)
    near_z = swapped_along(near_z, "gz", 0)
    far_z = swapped_along(far_z, "gz", 1)
    got_y = swapped_along(swap_y, "gy", 0)
    got_x = swapped_along(swap_x, "gx", 0)
    total = interior(keys, diag, faces, natural, turned, sizes)
    paired = holding == AGG_DEV and depth & (depth - 1) == 0
    first_part = depth // 2 if paired else 0
    *outgoing, total = border(
        row_owner, place, keys, (got_x, got_y, near_z, far_z, tail_x, tail_y, tail_z), turned, natural,
        (first_z, last_z), total, capacity, depth, paired, first_part, sizes)
    if paired:
        def swapped_with(part, k):
            return lax.ppermute(part, "gz", [(i, i ^ k) for i in range(depth)]) if k else part

        far = [swapped_with(part, first_part + k) for k, part in enumerate(outgoing)]
        gate = swapped_with(outgoing[-1][:1, :HALF], 1)
        near = [swapped_with(part, k) for k, part in enumerate(near_parts(row_owner, place, total, gate, capacity, first_part, depth))]
        parts = near + far
        result = placed(place, parts, block)
    else:
        arrived = lax.all_to_all(jnp.concatenate(outgoing, axis=0), "gz", 0, 0, tiled=True)
        slots = jnp.arange(holding, dtype=jnp.int32)
        owner_ids = jnp.arange(depth, dtype=jnp.int32)
        counts = jnp.sum((row_owner[:, None] == owner_ids[None, :]).astype(jnp.int32), axis=0)
        arrived_counts = lax.all_to_all(counts, "gz", 0, 0, tiled=True)
        present = slots % capacity < jnp.repeat(arrived_counts, capacity)
        target = jnp.cumsum(present.astype(jnp.int32)) - 1
        match = (present[None, :] & (target[None, :] == slots[:, None])).astype(jnp.int32)
        result = laid_out(jnp.sum(match * (slots[None, :] + 1), axis=1) - 1, arrived, block)
    return jnp.transpose(result, (1, 0, 2)).reshape(1, 1, 1, holding, SLOTS, block)


def solution(mesh):
    return jax.shard_map(
        shards,
        mesh=mesh,
        in_specs=(
            P("gx", "gy", "gz", None),
            P(None, "gx", "gy", "gz", None),
            P("gx", "gy", "gz", None),
            P("gx", "gy", "gz"),
            P(None, "gx", "gy", "gz"),
            P(("gx", "gy", "gz")),
        ),
        out_specs=P("gx", "gy", "gz", None, None, None),
        check_vma=False,
    )
```

```python
import functools

import jax
import jax.numpy as jnp
from jax import lax
from jax.experimental import pallas as pl
from jax.experimental.pallas import tpu as pltpu
from jax.sharding import PartitionSpec as P

NODES = 64
SLOTS = 7
AGG_DEV = 24
LANES = 128
HALF = NODES // 2
MIB = 1024 * 1024
STEP = 8


def swapped_along(block, axis, first):
    pairs = [(i, i + 1) for i in range(first, lax.axis_size(axis) - 1, 2)]
    return lax.ppermute(block, axis, pairs + [(i + 1, i) for i, _ in pairs])


def low_lanes(rows):
    return lax.broadcasted_iota(jnp.int32, (rows, LANES), 1) < NODES


def swapped(value):
    return pltpu.roll(value, NODES, 1)


def zero_one(mask):
    return mask.astype(jnp.float32).astype(jnp.bfloat16)


def product(left, right):
    return jnp.dot(left, right, preferred_element_type=jnp.float32)


def across(left, right):
    return lax.dot_general(left, right, (((0,), (0,)), ((), ())), preferred_element_type=jnp.float32)


def spread(column, stage):
    depth = column.shape[0]
    for k in range(column.shape[1] // LANES):
        stage[depth * k : depth * (k + 1), :] = column[:, LANES * k : LANES * (k + 1)].astype(jnp.float32)


def block_of(stage, z, depth):
    return stage[pl.ds(z, HALF, stride=depth), :].astype(jnp.bfloat16)


def stacked_pair(first, second):
    low = low_lanes(HALF)
    even = jnp.where(low, first, swapped(second))
    odd = jnp.where(low, swapped(first), second)
    return jnp.concatenate([even, odd], axis=0)


def in_order(pairs):
    row = lax.broadcasted_iota(jnp.int32, (NODES, NODES), 0)
    col = lax.broadcasted_iota(jnp.int32, (NODES, NODES), 1)
    moved = product(zero_one(row == 2 * (col % HALF) + col // HALF), jnp.concatenate(pairs, axis=1)).astype(jnp.bfloat16)
    return [moved[:, LANES * p : LANES * (p + 1)] for p in range(len(pairs))]


def four_weights(first, second):
    low = low_lanes(NODES)
    zero = jnp.zeros_like(first)
    left = [jnp.where(low, first, zero), jnp.where(low, zero, first), zero, zero]
    right = [zero, zero, jnp.where(low, second, zero), jnp.where(low, zero, second)]
    return jnp.concatenate([jnp.concatenate(left, axis=0), jnp.concatenate(right, axis=0)], axis=1)


def folded(square):
    low = low_lanes(HALF)
    moved = swapped(jnp.where(low, square[HALF : 2 * HALF], square[2 * HALF : 3 * HALF]))
    return [jnp.where(low, square[:HALF], moved), jnp.where(low, moved, square[3 * HALF :])]


def straightened(even, odd):
    low = low_lanes(HALF // 2)
    return jnp.concatenate([jnp.where(low, even, swapped(odd)), jnp.where(low, swapped(even), odd)], axis=0)


def diagonal(square):
    return jnp.where(low_lanes(NODES), square[:NODES], square[NODES:]).astype(jnp.bfloat16)


def apart(first, second):
    zero = jnp.zeros_like(first)
    return jnp.concatenate([jnp.concatenate([first, zero], axis=1), jnp.concatenate([zero, second], axis=1)], axis=0)


def two_pairs(squares):
    return folded(squares[:, :LANES]) + folded(squares[:, LANES:])


def add_all(updates):
    olds = [total[key] for total, key, _ in updates]
    news = []
    for number, (total, key, value) in enumerate(updates):
        for other, other_key, other_value in updates[:number]:
            if other is total:
                value = value + jnp.where(key == other_key, other_value, jnp.zeros_like(other_value))
        news.append(olds[number] + value)
    for (total, key, _), new in zip(updates, news):
        total[key] = new


def prepare_kernel(place_ref, p_ref, fx_ref, fy_ref, fz_ref, natural_ref, turned_ref, swap_x_ref, swap_y_ref, near_z_ref, far_z_ref,
                   first_z_ref, last_z_ref, tail_x_ref, tail_y_ref, tail_z_ref, stages, stages_f, stacks, ends):
    plane = pl.program_id(0)
    size_y, depth = p_ref.shape[0], p_ref.shape[1]
    pairs = depth // 2

    for j in range(size_y):
        stage = stages.at[j]
        spread(p_ref[j], stage)
        block = [block_of(stage, z, depth) for z in range(depth)]
        stacked = [stacked_pair(block[2 * p], block[2 * p + 1]) for p in range(pairs)]
        natural = in_order(stacked)
        for p in range(pairs):
            stacks[j, p] = stacked[p]
            natural_ref[j, p] = natural[p]
        for h in range(pairs // 2):
            turned_ref[j, h] = jnp.concatenate([stacked[2 * h], stacked[2 * h + 1]], axis=0).T
        ends[0, j] = block[0]
        ends[1, j] = block[depth - 1]
        stage_f = stages_f.at[j]
        spread(fz_ref[0, j], stage_f)
        last = block_of(stage_f, depth - 1, depth)
        ends[2, j] = last

    heads = in_order([stacked_pair(ends[0, 2 * t], ends[0, 2 * t + 1]) for t in range(size_y // 2)])
    for t, head in enumerate(heads):
        last, face = [stacked_pair(ends[kind, 2 * t], ends[kind, 2 * t + 1]) for kind in (1, 2)]
        rim = diagonal(across(face, last))
        first_z_ref[t] = head
        last_z_ref[t] = last
        tail_z_ref[t] = face
        near_z_ref[t] = jnp.where(place_ref[2] % 2 == 0, rim, head)
        far_z_ref[t] = jnp.where(place_ref[2] % 2 == 0, head, rim)

    def faces(source, stage, j, tails, rims):
        spread(source, stage)
        block = [block_of(stage, z, depth) for z in range(depth)]
        for p in range(pairs):
            tails[p] = stacked_pair(block[2 * p], block[2 * p + 1])
            rims[p] = diagonal(across(tails[p], stacks[j, p]))

    @pl.when(place_ref[1] == 0)
    def _():
        faces(fy_ref[0, 0], stages_f.at[0], size_y - 1, tail_y_ref.at[0], swap_y_ref.at[0])

    @pl.when(place_ref[1] != 0)
    def _():
        swap_y_ref[0] = natural_ref[0]

    @pl.when((place_ref[0] == 0) & (plane == pl.num_programs(0) - 1))
    def _():
        for j in range(size_y):
            faces(fx_ref[0, j], stages_f.at[j], j, tail_x_ref.at[j], swap_x_ref.at[j])

    @pl.when((place_ref[0] != 0) & (plane == 0))
    def _():
        swap_x_ref[...] = natural_ref[...]


def prepare(place, prolong, faces, sizes):
    size_x, size_y, depth = sizes
    pairs, block = depth // 2, prolong.shape[-1]
    columns, half = size_x * size_y, size_y // 2
    shape = lambda *dims: jax.ShapeDtypeStruct(dims, jnp.bfloat16)
    by_half = pl.BlockSpec((half, NODES, LANES), lambda i: (i, 0, 0))
    edge = shape(columns // 2, NODES, LANES)
    stage = pltpu.VMEM((size_y, depth * HALF, LANES), jnp.float32)
    return pl.pallas_call(
        prepare_kernel,
        grid=(size_x,),
        in_specs=[
            pl.BlockSpec(memory_space=pltpu.SMEM),
            pl.BlockSpec((size_y, depth, block), lambda i: (i, 0, 0)),
            pl.BlockSpec((1, size_y, depth, block), lambda i: (0, size_x - 1, 0, 0)),
            pl.BlockSpec((1, 1, depth, block), lambda i: (1, i * size_y + size_y - 1, 0, 0)),
            pl.BlockSpec((1, size_y, depth, block), lambda i: (2, i, 0, 0)),
        ],
        out_specs=[
            pl.BlockSpec((size_y, pairs, NODES, LANES), lambda i: (i, 0, 0, 0)),
            pl.BlockSpec((size_y, pairs // 2, LANES, LANES), lambda i: (i, 0, 0, 0)),
            pl.BlockSpec((size_y, pairs, NODES, LANES), lambda i: (0, 0, 0, 0)),
            pl.BlockSpec((1, pairs, NODES, LANES), lambda i: (i, 0, 0, 0)),
            by_half, by_half, by_half, by_half,
            pl.BlockSpec((size_y, pairs, NODES, LANES), lambda i: (0, 0, 0, 0)),
            pl.BlockSpec((1, pairs, NODES, LANES), lambda i: (i, 0, 0, 0)),
            by_half,
        ],
        out_shape=[
            shape(columns, pairs, NODES, LANES), shape(columns, pairs // 2, LANES, LANES),
            shape(size_y, pairs, NODES, LANES), shape(size_x, pairs, NODES, LANES), edge, edge, edge, edge,
            shape(size_y, pairs, NODES, LANES), shape(size_x, pairs, NODES, LANES), edge,
        ],
        scratch_shapes=[
            stage, stage,
            pltpu.VMEM((size_y, pairs, NODES, LANES), jnp.bfloat16),
            pltpu.VMEM((3, size_y, HALF, LANES), jnp.bfloat16),
        ],
        compiler_params=pltpu.CompilerParams(vmem_limit_bytes=48 * MIB),
        name="prepare",
    )(place, prolong, faces, faces, faces)


def interior_kernel(keys, diag_ref, face_ref, natural_ref, turned_ref, out_ref,
                    stages, ahead_even, ahead_odd, behind_even, behind_odd, wide):
    _, size_x, size_y, depth = keys.shape
    pairs = depth // 2
    spare = out_ref.shape[0]
    ahead, behind = (ahead_even, ahead_odd), (behind_even, behind_odd)

    for total in ahead + behind:
        total[...] = jnp.zeros_like(total)

    def couplings(i, j, stage, has_x):
        column = i * size_y + j
        sources = [diag_ref[column], face_ref[0, column - size_y] if has_x else None, face_ref[1, column - 1] if j else None, face_ref[2, column]]
        stacked = {}
        for face, source in enumerate(sources):
            if source is None:
                continue
            spread(source, stage.at[face])
            shift = 1 if face == 3 else 0
            block = [block_of(stage.at[face], z, depth) for z in range(depth)]
            stacked[face] = [stacked_pair(block[(2 * p - shift) % depth], block[2 * p + 1 - shift]) for p in range(pairs)]
        couples = {face: [] for face in stacked}
        for h in range(pairs // 2):
            left = [jnp.concatenate([rows[2 * h], rows[2 * h + 1]], axis=1) for rows in stacked.values()]
            weights = four_weights(natural_ref[column, 2 * h], natural_ref[column, 2 * h + 1])
            four = product(jnp.concatenate(left, axis=0), weights).astype(jnp.bfloat16)
            for number, face in enumerate(stacked):
                rows = four[NODES * number : NODES * (number + 1)]
                for couple in (rows[:, :LANES], rows[:, LANES:]):
                    couples[face].append(swapped(couple) if face == 3 else couple)
        low = low_lanes(NODES)
        along = couples[3]
        couples[3] = [jnp.where(low, along[p], along[min(p + 1, pairs - 1)]) for p in range(pairs)]
        return couples

    def sums(i, j, couples):
        column = i * size_y + j
        origin = {0: column, 1: column - size_y, 2: column - 1, 3: column}
        batches = []
        for h in range(pairs // 2):
            for face, pair in couples.items():
                four = two_pairs(product(turned_ref[origin[face], h], apart(pair[2 * h], pair[2 * h + 1])))
                updates = []
                for number, term in enumerate(four):
                    z, side = 4 * h + number, number % 2
                    if face == 0:
                        updates.append((ahead[side], keys[0, i, j, z], term))
                        continue
                    if face == 1:
                        here, there = keys[2, i - 1, j, z], keys[1, i, j, z]
                    elif face == 2:
                        here, there = keys[4, i, j - 1, z], keys[3, i, j, z]
                    elif z + 1 < depth:
                        here, there = keys[6, i, j, z], keys[5, i, j, z + 1]
                    else:
                        continue
                    updates.append((ahead[side], here, term))
                    updates.append((behind[side], there, term))
                batches.append(updates)
        return batches

    def plane(i, carry, has_x=True):
        couples = [couplings(i, j, stages.at[j], has_x) for j in range(size_y)]
        for updates in [updates for j in range(size_y) for updates in sums(i, j, couples[j])]:
            add_all(updates)
        return carry

    plane(0, 0, has_x=False)
    lax.fori_loop(1, size_x, plane, 0)

    def finish(g, carry):
        low = low_lanes(HALF)
        spots = [(p, [wide.shape[0] * 2 * g + 2 * p + side for side in (0, 1)]) for p in range(wide.shape[0])]
        for p, key in spots:
            one, two = [behind_even[key[side]] + behind_odd[key[side]] for side in (0, 1)]
            upper = jnp.where(low, one, swapped(two))
            lower = jnp.where(low, swapped(one), two)
            wide[p, :, :NODES] = jnp.concatenate([upper, lower], axis=0).T
        for p, key in spots:
            for side in (0, 1):
                first = wide[p, NODES * side : NODES * side + HALF, :]
                second = wide[p, NODES * side + HALF : NODES * (side + 1), :]
                turned = jnp.where(low, first, swapped(second))
                out_ref[key[side]] = (ahead_even[key[side]] + ahead_odd[key[side]]) + turned
        return carry

    lax.fori_loop(0, spare // (2 * wide.shape[0]), finish, 0)


def interior(keys, diag, faces, natural, turned, sizes):
    size_x, size_y, depth = sizes
    pairs, block = depth // 2, diag.shape[-1]
    columns, rows = size_x * size_y, AGG_DEV * SLOTS
    total = pltpu.VMEM((rows, HALF, LANES), jnp.float32)
    whole = pl.BlockSpec(memory_space=pltpu.VMEM)
    return pl.pallas_call(
        interior_kernel,
        in_specs=[pl.BlockSpec(memory_space=pltpu.SMEM), whole, whole, whole, whole],
        out_specs=whole,
        out_shape=jax.ShapeDtypeStruct((rows, HALF, LANES), jnp.float32),
        scratch_shapes=[
            pltpu.VMEM((size_y, 4, depth * HALF, LANES), jnp.float32),
            total, total, total, total,
            pltpu.VMEM((12, LANES, LANES), jnp.float32),
        ],
        compiler_params=pltpu.CompilerParams(vmem_limit_bytes=28 * MIB),
        cost_estimate=pl.CostEstimate(flops=columns * depth * 14 * NODES**3, bytes_accessed=columns * depth * 6 * block * 2, transcendentals=0),
        name="interior",
    )(keys, diag, faces, natural, turned)


def border_kernel(capacity, paired, first_part, owners, place_ref, keys, got_x, got_y, near_z, far_z, tail_x, tail_y, tail_z, turned_x, turned_y,
                  natural_x, natural_y, first_z, last_z, start_ref, *refs):
    out_refs, (total, filled, listed) = refs[:-3], refs[-3:]
    size_y, pairs = tail_x.shape[0], tail_x.shape[1]
    size_x, depth = tail_y.shape[0], 2 * pairs
    rows = start_ref.shape[0]

    def key_at(number, i, j, z):
        return keys[number, i, j, z]

    def couplings(tail, head):
        left = jnp.concatenate(tail, axis=1)
        four = product(left, four_weights(*head)).astype(jnp.bfloat16)
        return four[:, :LANES], four[:, LANES:]

    def ahead(tail, head, turned, key):
        for h in range(pairs // 2):
            couples = couplings([tail[2 * h], tail[2 * h + 1]], [head[2 * h], head[2 * h + 1]])
            four = two_pairs(product(turned[h], apart(*couples)))
            yield [(total, key(4 * h + number), term) for number, term in enumerate(four)]

    def turned_terms(first, second, rims):
        return two_pairs(product(jnp.concatenate([first, second], axis=0).T, apart(*rims)))

    def back(natural, rim, key):
        for h in range(pairs // 2):
            four = turned_terms(natural[2 * h], natural[2 * h + 1], (rim[2 * h], rim[2 * h + 1]))
            yield [(total, key(4 * h + number), term) for number, term in enumerate(four)]

    def batches_x(first):
        for j in range(size_y):
            if first:
                yield from ahead(tail_x.at[j], got_x.at[j], turned_x.at[j], functools.partial(key_at, 2, size_x - 1, j))
            else:
                yield from back(natural_x.at[j], got_x.at[j], functools.partial(key_at, 1, 0, j))

    def batches_y(first):
        for i in range(size_x):
            if first:
                yield from ahead(tail_y.at[i], got_y.at[i], turned_y.at[i, 0], functools.partial(key_at, 4, i, size_y - 1))
            else:
                yield from back(natural_y.at[i, 0], got_y.at[i], functools.partial(key_at, 3, i, 0))

    def batches_z():
        even = place_ref[2] % 2 == 0
        for t in range(0, near_z.shape[0], 2):
            heads = [jnp.where(even, near_z[u], far_z[u]) for u in (t, t + 1)]
            couples = couplings([tail_z[t], tail_z[t + 1]], heads)
            front = turned_terms(last_z[t], last_z[t + 1], couples)
            past = turned_terms(first_z[t], first_z[t + 1], [jnp.where(even, far_z[u], near_z[u]) for u in (t, t + 1)])
            spots = [(2 * u // size_y, 2 * u % size_y + side) for u in (t, t + 1) for side in (0, 1)]
            yield [(total, keys[6, i, j, depth - 1], term) for (i, j), term in zip(spots, front)]
            yield [(total, keys[5, i, j, 0], term) for (i, j), term in zip(spots, past)]

    for first_x in (True, False):
        for first_y in (True, False):
            @pl.when(((place_ref[0] == 0) == first_x) & ((place_ref[1] == 0) == first_y))
            def _():
                batches = list(batches_x(first_x)) + list(batches_y(first_y)) + list(batches_z())
                for updates in batches:
                    add_all(updates)

    list_rows(capacity, paired, owners, place_ref, rows // SLOTS, filled, listed)
    full = capacity * filled.shape[0] * SLOTS == rows
    for part, out_ref in enumerate(out_refs):
        for q in range(capacity):
            write_row(total, listed[(first_part + part) * capacity + q], full, out_ref, q)


def list_rows(capacity, paired, owners, place_ref, rows, filled, listed):
    devices = filled.shape[0]
    for spot in range(capacity * devices):
        listed[spot] = -1
    for owner in range(devices):
        filled[owner] = 0
    for r in range(rows):
        owner = owners[r]
        listed[jnp.bitwise_xor(owner, place_ref[2] if paired else 0) * capacity + filled[owner]] = r
        filled[owner] = filled[owner] + 1


def write_row(total, row, full, out_ref, spot):
    for s in range(SLOTS):
        key = jnp.maximum(row, 0) * SLOTS + s
        even, odd = [total[key, pl.ds(first, HALF // 2, stride=2), :] for first in (0, 1)]
        block = straightened(even, odd)
        if not full:
            block = jnp.where(row >= 0, block, jnp.zeros_like(block))
        out_ref[spot, HALF * s : HALF * (s + 1), :] = block.astype(jnp.bfloat16)


def near_kernel(capacity, owners, place_ref, total, arrived, out_ref, filled, listed):
    count = out_ref.shape[0] // capacity
    list_rows(capacity, True, owners, place_ref, total.shape[0] // SLOTS, filled, listed)
    for member in range(count):
        partner = jnp.bitwise_xor(member, place_ref[2] % count)
        for q in range(capacity):
            write_row(total, listed[partner * capacity + q], True, out_ref, member * capacity + q)


def near_parts(owners, place, total, arrived, capacity, count, devices):
    smem = pl.BlockSpec(memory_space=pltpu.SMEM)
    whole = pl.BlockSpec(memory_space=pltpu.VMEM)
    return pl.pallas_call(
        functools.partial(near_kernel, capacity),
        in_specs=[smem, smem, whole, pl.BlockSpec(memory_space=pl.ANY)],
        out_specs=whole,
        out_shape=jax.ShapeDtypeStruct((count * capacity, SLOTS * HALF, LANES), jnp.bfloat16),
        scratch_shapes=[pltpu.SMEM((devices,), jnp.int32), pltpu.SMEM((capacity * devices,), jnp.int32)],
        compiler_params=pltpu.CompilerParams(vmem_limit_bytes=10 * MIB),
        name="near",
    )(owners, place, total, arrived)


def border(owners, place, keys, operands, turned, natural, ends, total, capacity, devices, paired, first_part, sizes):
    size_x, size_y, depth = sizes
    pairs = depth // 2
    smem = pl.BlockSpec(memory_space=pltpu.SMEM)
    whole = pl.BlockSpec(memory_space=pltpu.VMEM)
    planes = lambda array: array.reshape((size_x, size_y) + array.shape[1:])
    before = 3 + len(operands) + 4 + len(ends)
    count = devices - first_part
    return pl.pallas_call(
        functools.partial(border_kernel, capacity, paired, first_part),
        grid=(1,),
        in_specs=[smem, smem, smem] + [whole] * len(operands) + [
            pl.BlockSpec((size_y, pairs // 2, LANES, LANES), lambda i: (size_x - 1, 0, 0, 0)),
            pl.BlockSpec((size_x, 1, pairs // 2, LANES, LANES), lambda i: (0, size_y - 1, 0, 0, 0)),
            pl.BlockSpec((size_y, pairs, NODES, LANES), lambda i: (0, 0, 0, 0)),
            pl.BlockSpec((size_x, 1, pairs, NODES, LANES), lambda i: (0, 0, 0, 0, 0)),
        ] + [whole] * (len(ends) + 1),
        out_specs=[whole] * (count + 1),
        out_shape=[jax.ShapeDtypeStruct((capacity, SLOTS * HALF, LANES), jnp.bfloat16)] * count
        + [jax.ShapeDtypeStruct(total.shape, total.dtype)],
        input_output_aliases={before: count},
        scratch_shapes=[pltpu.SMEM((devices,), jnp.int32), pltpu.SMEM((capacity * devices,), jnp.int32)],
        compiler_params=pltpu.CompilerParams(vmem_limit_bytes=18 * MIB),
        name="border",
    )(owners, place, keys, *operands, turned, planes(turned), natural, planes(natural), *ends, total)


def layout_kernel(source, rows_ref, out_ref, stage):
    group = pl.program_id(0)
    height = out_ref.shape[1]
    for s in range(SLOTS):
        for r in range(height):
            row = source[group * height + r]
            block = rows_ref[jnp.maximum(row, 0), HALF * s : HALF * (s + 1), :].astype(jnp.float32)
            stage[s, pl.ds(r, HALF, stride=height), :] = jnp.where(row >= 0, block, jnp.zeros_like(block))
        for k in range(HALF):
            out_ref[s, :, LANES * k : LANES * (k + 1)] = stage[s, height * k : height * (k + 1), :].astype(jnp.bfloat16)


def laid_out(source, rows, block):
    places, height = rows.shape[0], 8
    return pl.pallas_call(
        layout_kernel,
        grid=(places // height,),
        in_specs=[pl.BlockSpec(memory_space=pltpu.SMEM), pl.BlockSpec(memory_space=pltpu.VMEM)],
        out_specs=pl.BlockSpec((SLOTS, height, block), lambda g: (0, g, 0)),
        out_shape=jax.ShapeDtypeStruct((SLOTS, places, block), jnp.bfloat16),
        scratch_shapes=[pltpu.VMEM((SLOTS, height * HALF, LANES), jnp.float32)],
        compiler_params=pltpu.CompilerParams(vmem_limit_bytes=10 * MIB),
        name="layout",
    )(source, rows)


def placed_kernel(capacity, place_ref, near_ref, *refs):
    parts, (out_ref, stage, laid, done) = refs[:-4], refs[-4:]
    height, count = out_ref.shape[1], near_ref.shape[0]
    copies = [pltpu.make_async_copy(laid.at[s], out_ref.at[s], done.at[s]) for s in range(SLOTS)]
    rows = [(near_ref, row, place_ref[2] // len(parts) * count + row) for row in range(count)]
    for number, part in enumerate(parts):
        first = jnp.bitwise_xor(place_ref[2], len(parts) + number) * capacity
        rows += [(part, q, first + q) for q in range(capacity)]
    for s in range(SLOTS):
        for source, row, spot in rows:
            block = source[row, HALF * s : HALF * (s + 1), :].astype(jnp.float32)
            stage[s, pl.ds(spot, HALF, stride=height), :] = block
        for k in range(HALF):
            laid[s, :, LANES * k : LANES * (k + 1)] = stage[s, height * k : height * (k + 1), :].astype(jnp.bfloat16)
        copies[s].start()
    for copy in copies:
        copy.wait()


def placed(place, near, parts, block):
    capacity = parts[0].shape[0]
    places = near.shape[0] + capacity * len(parts)
    whole = pl.BlockSpec(memory_space=pltpu.VMEM)
    return pl.pallas_call(
        functools.partial(placed_kernel, capacity),
        in_specs=[pl.BlockSpec(memory_space=pltpu.SMEM)] + [whole] * (1 + len(parts)),
        out_specs=pl.BlockSpec(memory_space=pl.ANY),
        out_shape=jax.ShapeDtypeStruct((SLOTS, places, block), jnp.bfloat16),
        scratch_shapes=[
            pltpu.VMEM((SLOTS, places * HALF, LANES), jnp.float32),
            pltpu.VMEM((SLOTS, places, block), jnp.bfloat16),
            pltpu.SemaphoreType.DMA((SLOTS,)),
        ],
        compiler_params=pltpu.CompilerParams(vmem_limit_bytes=16 * MIB),
        name="placed",
    )(place, near, *parts)


def shards(a_diag, a_face, prolong, aggregate, pair_slot, row_owner):
    size_x, size_y, size_z, block = a_diag.shape
    sizes = (size_x, size_y, size_z)
    columns = size_x * size_y
    depth = lax.axis_size("gz")
    capacity = max(2, (AGG_DEV + depth - 1) // depth)
    holding = capacity * depth
    diag = a_diag.reshape(columns, size_z, block)
    faces = a_face.reshape(3, columns, size_z, block)
    assert lax.axis_size("gx") == 2 and lax.axis_size("gy") == 2
    place = jnp.stack([lax.axis_index("gx"), lax.axis_index("gy"), lax.axis_index("gz")]).astype(jnp.int32)
    keys = aggregate[None] * SLOTS + pair_slot

    natural, turned, swap_x, swap_y, near_z, far_z, first_z, last_z, tail_x, tail_y, tail_z = prepare(
        place, prolong.reshape(columns, size_z, block), faces, sizes)
    near_z = swapped_along(near_z, "gz", 0)
    far_z = swapped_along(far_z, "gz", 1)
    got_y = swapped_along(swap_y, "gy", 0)
    got_x = swapped_along(swap_x, "gx", 0)
    total = interior(keys, diag, faces, natural, turned, sizes)
    paired = holding == AGG_DEV and depth & (depth - 1) == 0
    first_part = depth // 2 if paired else 0
    *outgoing, total = border(
        row_owner, place, keys, (got_x, got_y, near_z, far_z, tail_x, tail_y, tail_z), turned, natural,
        (first_z, last_z), total, capacity, depth, paired, first_part, sizes)
    if paired:
        def swapped_with(part, k):
            return lax.ppermute(part, "gz", [(i, i ^ k) for i in range(depth)])

        far = [swapped_with(part, first_part + k) for k, part in enumerate(outgoing)]
        gate = swapped_with(outgoing[-1][:1, :HALF], 1)
        near = near_parts(row_owner, place, total, gate, capacity, first_part, depth)
        sides = [list(range(first, first + first_part)) for first in (0, first_part)]
        near = lax.all_to_all(near, "gz", 0, 0, tiled=True, axis_index_groups=sides)
        result = placed(place, near, far, block)
    else:
        arrived = lax.all_to_all(jnp.concatenate(outgoing, axis=0), "gz", 0, 0, tiled=True)
        slots = jnp.arange(holding, dtype=jnp.int32)
        owner_ids = jnp.arange(depth, dtype=jnp.int32)
        counts = jnp.sum((row_owner[:, None] == owner_ids[None, :]).astype(jnp.int32), axis=0)
        arrived_counts = lax.all_to_all(counts, "gz", 0, 0, tiled=True)
        present = slots % capacity < jnp.repeat(arrived_counts, capacity)
        target = jnp.cumsum(present.astype(jnp.int32)) - 1
        match = (present[None, :] & (target[None, :] == slots[:, None])).astype(jnp.int32)
        result = laid_out(jnp.sum(match * (slots[None, :] + 1), axis=1) - 1, arrived, block)
    return jnp.transpose(result, (1, 0, 2)).reshape(1, 1, 1, holding, SLOTS, block)


def solution(mesh):
    return jax.shard_map(
        shards,
        mesh=mesh,
        in_specs=(
            P("gx", "gy", "gz", None),
            P(None, "gx", "gy", "gz", None),
            P("gx", "gy", "gz", None),
            P("gx", "gy", "gz"),
            P(None, "gx", "gy", "gz"),
            P(("gx", "gy", "gz")),
        ),
        out_specs=P("gx", "gy", "gz", None, None, None),
        check_vma=False,
    )
```

```python
import functools

import jax
import jax.numpy as jnp
from jax import lax
from jax.experimental import pallas as pl
from jax.experimental.pallas import tpu as pltpu
from jax.sharding import PartitionSpec as P

NODES = 64
SLOTS = 7
AGG_DEV = 24
LANES = 128
HALF = NODES // 2
MIB = 1024 * 1024
STEP = 8


def swapped_along(block, axis, first):
    pairs = [(i, i + 1) for i in range(first, lax.axis_size(axis) - 1, 2)]
    return lax.ppermute(block, axis, pairs + [(i + 1, i) for i, _ in pairs])


def low_lanes(rows):
    return lax.broadcasted_iota(jnp.int32, (rows, LANES), 1) < NODES


def swapped(value):
    return pltpu.roll(value, NODES, 1)


def zero_one(mask):
    return mask.astype(jnp.float32).astype(jnp.bfloat16)


def product(left, right):
    return jnp.dot(left, right, preferred_element_type=jnp.float32)


def across(left, right):
    return lax.dot_general(left, right, (((0,), (0,)), ((), ())), preferred_element_type=jnp.float32)


def spread(column, stage):
    depth = column.shape[0]
    for k in range(column.shape[1] // LANES):
        stage[depth * k : depth * (k + 1), :] = column[:, LANES * k : LANES * (k + 1)].astype(jnp.float32)


def block_of(stage, z, depth):
    return stage[pl.ds(z, HALF, stride=depth), :].astype(jnp.bfloat16)


def stacked_pair(first, second):
    low = low_lanes(HALF)
    even = jnp.where(low, first, swapped(second))
    odd = jnp.where(low, swapped(first), second)
    return jnp.concatenate([even, odd], axis=0)


def in_order(pairs):
    row = lax.broadcasted_iota(jnp.int32, (NODES, NODES), 0)
    col = lax.broadcasted_iota(jnp.int32, (NODES, NODES), 1)
    moved = product(zero_one(row == 2 * (col % HALF) + col // HALF), jnp.concatenate(pairs, axis=1)).astype(jnp.bfloat16)
    return [moved[:, LANES * p : LANES * (p + 1)] for p in range(len(pairs))]


def four_weights(first, second):
    low = low_lanes(NODES)
    zero = jnp.zeros_like(first)
    left = [jnp.where(low, first, zero), jnp.where(low, zero, first), zero, zero]
    right = [zero, zero, jnp.where(low, second, zero), jnp.where(low, zero, second)]
    return jnp.concatenate([jnp.concatenate(left, axis=0), jnp.concatenate(right, axis=0)], axis=1)


def folded(square):
    low = low_lanes(HALF)
    moved = swapped(jnp.where(low, square[HALF : 2 * HALF], square[2 * HALF : 3 * HALF]))
    return [jnp.where(low, square[:HALF], moved), jnp.where(low, moved, square[3 * HALF :])]


def straightened(even, odd):
    low = low_lanes(HALF // 2)
    return jnp.concatenate([jnp.where(low, even, swapped(odd)), jnp.where(low, swapped(even), odd)], axis=0)


def diagonal(square):
    return jnp.where(low_lanes(NODES), square[:NODES], square[NODES:]).astype(jnp.bfloat16)


def apart(first, second):
    zero = jnp.zeros_like(first)
    return jnp.concatenate([jnp.concatenate([first, zero], axis=1), jnp.concatenate([zero, second], axis=1)], axis=0)


def two_pairs(squares):
    return folded(squares[:, :LANES]) + folded(squares[:, LANES:])


def add_all(updates):
    olds = [total[key] for total, key, _ in updates]
    news = []
    for number, (total, key, value) in enumerate(updates):
        for other, other_key, other_value in updates[:number]:
            if other is total:
                value = value + jnp.where(key == other_key, other_value, jnp.zeros_like(other_value))
        news.append(olds[number] + value)
    for (total, key, _), new in zip(updates, news):
        total[key] = new


def prepare_kernel(place_ref, p_ref, fx_ref, fy_ref, fz_ref, natural_ref, turned_ref, swap_x_ref, swap_y_ref, near_z_ref, far_z_ref,
                   first_z_ref, last_z_ref, tail_x_ref, tail_y_ref, tail_z_ref, stages, stages_f, stacks, ends):
    plane = pl.program_id(0)
    size_y, depth = p_ref.shape[0], p_ref.shape[1]
    pairs = depth // 2

    for j in range(size_y):
        stage = stages.at[j]
        spread(p_ref[j], stage)
        block = [block_of(stage, z, depth) for z in range(depth)]
        stacked = [stacked_pair(block[2 * p], block[2 * p + 1]) for p in range(pairs)]
        natural = in_order(stacked)
        for p in range(pairs):
            stacks[j, p] = stacked[p]
            natural_ref[j, p] = natural[p]
        for h in range(pairs // 2):
            turned_ref[j, h] = jnp.concatenate([stacked[2 * h], stacked[2 * h + 1]], axis=0).T
        ends[0, j] = block[0]
        ends[1, j] = block[depth - 1]
        stage_f = stages_f.at[j]
        spread(fz_ref[0, j], stage_f)
        last = block_of(stage_f, depth - 1, depth)
        ends[2, j] = last

    heads = in_order([stacked_pair(ends[0, 2 * t], ends[0, 2 * t + 1]) for t in range(size_y // 2)])
    for t, head in enumerate(heads):
        last, face = [stacked_pair(ends[kind, 2 * t], ends[kind, 2 * t + 1]) for kind in (1, 2)]
        rim = diagonal(across(face, last))
        first_z_ref[t] = head
        last_z_ref[t] = last
        tail_z_ref[t] = face
        near_z_ref[t] = jnp.where(place_ref[2] % 2 == 0, rim, head)
        far_z_ref[t] = jnp.where(place_ref[2] % 2 == 0, head, rim)

    def faces(source, stage, j, tails, rims):
        spread(source, stage)
        block = [block_of(stage, z, depth) for z in range(depth)]
        for p in range(pairs):
            tails[p] = stacked_pair(block[2 * p], block[2 * p + 1])
            rims[p] = diagonal(across(tails[p], stacks[j, p]))

    @pl.when(place_ref[1] == 0)
    def _():
        faces(fy_ref[0, 0], stages_f.at[0], size_y - 1, tail_y_ref.at[0], swap_y_ref.at[0])

    @pl.when(place_ref[1] != 0)
    def _():
        swap_y_ref[0] = natural_ref[0]

    @pl.when((place_ref[0] == 0) & (plane == pl.num_programs(0) - 1))
    def _():
        for j in range(size_y):
            faces(fx_ref[0, j], stages_f.at[j], j, tail_x_ref.at[j], swap_x_ref.at[j])

    @pl.when((place_ref[0] != 0) & (plane == 0))
    def _():
        swap_x_ref[...] = natural_ref[...]


def prepare(place, prolong, faces, sizes):
    size_x, size_y, depth = sizes
    pairs, block = depth // 2, prolong.shape[-1]
    columns, half = size_x * size_y, size_y // 2
    shape = lambda *dims: jax.ShapeDtypeStruct(dims, jnp.bfloat16)
    by_half = pl.BlockSpec((half, NODES, LANES), lambda i: (i, 0, 0))
    edge = shape(columns // 2, NODES, LANES)
    stage = pltpu.VMEM((size_y, depth * HALF, LANES), jnp.float32)
    return pl.pallas_call(
        prepare_kernel,
        grid=(size_x,),
        in_specs=[
            pl.BlockSpec(memory_space=pltpu.SMEM),
            pl.BlockSpec((size_y, depth, block), lambda i: (i, 0, 0)),
            pl.BlockSpec((1, size_y, depth, block), lambda i: (0, size_x - 1, 0, 0)),
            pl.BlockSpec((1, 1, depth, block), lambda i: (1, i * size_y + size_y - 1, 0, 0)),
            pl.BlockSpec((1, size_y, depth, block), lambda i: (2, i, 0, 0)),
        ],
        out_specs=[
            pl.BlockSpec((size_y, pairs, NODES, LANES), lambda i: (i, 0, 0, 0)),
            pl.BlockSpec((size_y, pairs // 2, LANES, LANES), lambda i: (i, 0, 0, 0)),
            pl.BlockSpec((size_y, pairs, NODES, LANES), lambda i: (0, 0, 0, 0)),
            pl.BlockSpec((1, pairs, NODES, LANES), lambda i: (i, 0, 0, 0)),
            by_half, by_half, by_half, by_half,
            pl.BlockSpec((size_y, pairs, NODES, LANES), lambda i: (0, 0, 0, 0)),
            pl.BlockSpec((1, pairs, NODES, LANES), lambda i: (i, 0, 0, 0)),
            by_half,
        ],
        out_shape=[
            shape(columns, pairs, NODES, LANES), shape(columns, pairs // 2, LANES, LANES),
            shape(size_y, pairs, NODES, LANES), shape(size_x, pairs, NODES, LANES), edge, edge, edge, edge,
            shape(size_y, pairs, NODES, LANES), shape(size_x, pairs, NODES, LANES), edge,
        ],
        scratch_shapes=[
            stage, stage,
            pltpu.VMEM((size_y, pairs, NODES, LANES), jnp.bfloat16),
            pltpu.VMEM((3, size_y, HALF, LANES), jnp.bfloat16),
        ],
        compiler_params=pltpu.CompilerParams(vmem_limit_bytes=48 * MIB),
        name="prepare",
    )(place, prolong, faces, faces, faces)


def interior_kernel(keys, diag_ref, face_ref, natural_ref, turned_ref, out_ref,
                    stages, ahead_even, ahead_odd, behind_even, behind_odd, wide):
    _, size_x, size_y, depth = keys.shape
    pairs = depth // 2
    spare = out_ref.shape[0]
    ahead, behind = (ahead_even, ahead_odd), (behind_even, behind_odd)

    for total in ahead + behind:
        total[...] = jnp.zeros_like(total)

    def couplings(i, j, stage, has_x):
        column = i * size_y + j
        sources = [diag_ref[column], face_ref[0, column - size_y] if has_x else None, face_ref[1, column - 1] if j else None, face_ref[2, column]]
        stacked = {}
        for face, source in enumerate(sources):
            if source is None:
                continue
            spread(source, stage.at[face])
            shift = 1 if face == 3 else 0
            block = [block_of(stage.at[face], z, depth) for z in range(depth)]
            stacked[face] = [stacked_pair(block[(2 * p - shift) % depth], block[2 * p + 1 - shift]) for p in range(pairs)]
        couples = {face: [] for face in stacked}
        for h in range(pairs // 2):
            left = [jnp.concatenate([rows[2 * h], rows[2 * h + 1]], axis=1) for rows in stacked.values()]
            weights = four_weights(natural_ref[column, 2 * h], natural_ref[column, 2 * h + 1])
            four = product(jnp.concatenate(left, axis=0), weights).astype(jnp.bfloat16)
            for number, face in enumerate(stacked):
                rows = four[NODES * number : NODES * (number + 1)]
                for couple in (rows[:, :LANES], rows[:, LANES:]):
                    couples[face].append(swapped(couple) if face == 3 else couple)
        low = low_lanes(NODES)
        along = couples[3]
        couples[3] = [jnp.where(low, along[p], along[min(p + 1, pairs - 1)]) for p in range(pairs)]
        return couples

    def sums(i, j, couples):
        column = i * size_y + j
        origin = {0: column, 1: column - size_y, 2: column - 1, 3: column}
        batches = []
        for h in range(pairs // 2):
            for face, pair in couples.items():
                four = two_pairs(product(turned_ref[origin[face], h], apart(pair[2 * h], pair[2 * h + 1])))
                updates = []
                for number, term in enumerate(four):
                    z, side = 4 * h + number, number % 2
                    if face == 0:
                        updates.append((ahead[side], keys[0, i, j, z], term))
                        continue
                    if face == 1:
                        here, there = keys[2, i - 1, j, z], keys[1, i, j, z]
                    elif face == 2:
                        here, there = keys[4, i, j - 1, z], keys[3, i, j, z]
                    elif z + 1 < depth:
                        here, there = keys[6, i, j, z], keys[5, i, j, z + 1]
                    else:
                        continue
                    updates.append((ahead[side], here, term))
                    updates.append((behind[side], there, term))
                batches.append(updates)
        return batches

    def plane(i, carry, has_x=True):
        couples = [couplings(i, j, stages.at[j], has_x) for j in range(size_y)]
        for updates in [updates for j in range(size_y) for updates in sums(i, j, couples[j])]:
            add_all(updates)
        return carry

    plane(0, 0, has_x=False)
    lax.fori_loop(1, size_x, plane, 0)

    def finish(g, carry):
        low = low_lanes(HALF)
        spots = [(p, [wide.shape[0] * 2 * g + 2 * p + side for side in (0, 1)]) for p in range(wide.shape[0])]
        for p, key in spots:
            one, two = [behind_even[key[side]] + behind_odd[key[side]] for side in (0, 1)]
            upper = jnp.where(low, one, swapped(two))
            lower = jnp.where(low, swapped(one), two)
            wide[p, :, :NODES] = jnp.concatenate([upper, lower], axis=0).T
        for p, key in spots:
            for side in (0, 1):
                first = wide[p, NODES * side : NODES * side + HALF, :]
                second = wide[p, NODES * side + HALF : NODES * (side + 1), :]
                turned = jnp.where(low, first, swapped(second))
                out_ref[key[side]] = (ahead_even[key[side]] + ahead_odd[key[side]]) + turned
        return carry

    lax.fori_loop(0, spare // (2 * wide.shape[0]), finish, 0)


def interior(keys, diag, faces, natural, turned, sizes):
    size_x, size_y, depth = sizes
    pairs, block = depth // 2, diag.shape[-1]
    columns, rows = size_x * size_y, AGG_DEV * SLOTS
    total = pltpu.VMEM((rows, HALF, LANES), jnp.float32)
    whole = pl.BlockSpec(memory_space=pltpu.VMEM)
    return pl.pallas_call(
        interior_kernel,
        in_specs=[pl.BlockSpec(memory_space=pltpu.SMEM), whole, whole, whole, whole],
        out_specs=whole,
        out_shape=jax.ShapeDtypeStruct((rows, HALF, LANES), jnp.float32),
        scratch_shapes=[
            pltpu.VMEM((size_y, 4, depth * HALF, LANES), jnp.float32),
            total, total, total, total,
            pltpu.VMEM((12, LANES, LANES), jnp.float32),
        ],
        compiler_params=pltpu.CompilerParams(vmem_limit_bytes=28 * MIB),
        cost_estimate=pl.CostEstimate(flops=columns * depth * 14 * NODES**3, bytes_accessed=columns * depth * 6 * block * 2, transcendentals=0),
        name="interior",
    )(keys, diag, faces, natural, turned)


def border_kernel(capacity, paired, first_part, owners, place_ref, keys, got_x, got_y, near_z, far_z, tail_x, tail_y, tail_z, turned_x, turned_y,
                  natural_x, natural_y, first_z, last_z, start_ref, *refs):
    out_refs, (total, filled, listed) = refs[:-3], refs[-3:]
    size_y, pairs = tail_x.shape[0], tail_x.shape[1]
    size_x, depth = tail_y.shape[0], 2 * pairs
    rows = start_ref.shape[0]

    def key_at(number, i, j, z):
        return keys[number, i, j, z]

    def couplings(tail, head):
        left = jnp.concatenate(tail, axis=1)
        four = product(left, four_weights(*head)).astype(jnp.bfloat16)
        return four[:, :LANES], four[:, LANES:]

    def ahead(tail, head, turned, key):
        for h in range(pairs // 2):
            couples = couplings([tail[2 * h], tail[2 * h + 1]], [head[2 * h], head[2 * h + 1]])
            four = two_pairs(product(turned[h], apart(*couples)))
            yield [(total, key(4 * h + number), term) for number, term in enumerate(four)]

    def turned_terms(first, second, rims):
        return two_pairs(product(jnp.concatenate([first, second], axis=0).T, apart(*rims)))

    def back(natural, rim, key):
        for h in range(pairs // 2):
            four = turned_terms(natural[2 * h], natural[2 * h + 1], (rim[2 * h], rim[2 * h + 1]))
            yield [(total, key(4 * h + number), term) for number, term in enumerate(four)]

    def batches_x(first):
        for j in range(size_y):
            if first:
                yield from ahead(tail_x.at[j], got_x.at[j], turned_x.at[j], functools.partial(key_at, 2, size_x - 1, j))
            else:
                yield from back(natural_x.at[j], got_x.at[j], functools.partial(key_at, 1, 0, j))

    def batches_y(first):
        for i in range(size_x):
            if first:
                yield from ahead(tail_y.at[i], got_y.at[i], turned_y.at[i, 0], functools.partial(key_at, 4, i, size_y - 1))
            else:
                yield from back(natural_y.at[i, 0], got_y.at[i], functools.partial(key_at, 3, i, 0))

    def batches_z():
        even = place_ref[2] % 2 == 0
        for t in range(0, near_z.shape[0], 2):
            heads = [jnp.where(even, near_z[u], far_z[u]) for u in (t, t + 1)]
            couples = couplings([tail_z[t], tail_z[t + 1]], heads)
            front = turned_terms(last_z[t], last_z[t + 1], couples)
            past = turned_terms(first_z[t], first_z[t + 1], [jnp.where(even, far_z[u], near_z[u]) for u in (t, t + 1)])
            spots = [(2 * u // size_y, 2 * u % size_y + side) for u in (t, t + 1) for side in (0, 1)]
            yield [(total, keys[6, i, j, depth - 1], term) for (i, j), term in zip(spots, front)]
            yield [(total, keys[5, i, j, 0], term) for (i, j), term in zip(spots, past)]

    for first_x in (True, False):
        for first_y in (True, False):
            @pl.when(((place_ref[0] == 0) == first_x) & ((place_ref[1] == 0) == first_y))
            def _():
                batches = list(batches_x(first_x)) + list(batches_y(first_y)) + list(batches_z())
                for updates in batches:
                    add_all(updates)

    list_rows(capacity, paired, owners, place_ref, rows // SLOTS, filled, listed)
    full = capacity * filled.shape[0] * SLOTS == rows
    far_refs = out_refs[1:] if first_part else out_refs
    for part, out_ref in enumerate(far_refs):
        for q in range(capacity):
            write_row(total, listed[(first_part + part) * capacity + q], full, out_ref, q)
    for member in range(first_part):
        partner = jnp.bitwise_xor(member, place_ref[2] % first_part)
        for q in range(capacity):
            write_row(total, listed[partner * capacity + q], full, out_refs[0], member * capacity + q)


def list_rows(capacity, paired, owners, place_ref, rows, filled, listed):
    devices = filled.shape[0]
    for spot in range(capacity * devices):
        listed[spot] = -1
    for owner in range(devices):
        filled[owner] = 0
    for r in range(rows):
        owner = owners[r]
        listed[jnp.bitwise_xor(owner, place_ref[2] if paired else 0) * capacity + filled[owner]] = r
        filled[owner] = filled[owner] + 1


def write_row(total, row, full, out_ref, spot):
    for s in range(SLOTS):
        key = jnp.maximum(row, 0) * SLOTS + s
        even, odd = [total[key, pl.ds(first, HALF // 2, stride=2), :] for first in (0, 1)]
        block = straightened(even, odd)
        if not full:
            block = jnp.where(row >= 0, block, jnp.zeros_like(block))
        out_ref[spot, HALF * s : HALF * (s + 1), :] = block.astype(jnp.bfloat16)


def border(owners, place, keys, operands, turned, natural, ends, total, capacity, devices, paired, first_part, sizes):
    size_x, size_y, depth = sizes
    pairs = depth // 2
    smem = pl.BlockSpec(memory_space=pltpu.SMEM)
    whole = pl.BlockSpec(memory_space=pltpu.VMEM)
    planes = lambda array: array.reshape((size_x, size_y) + array.shape[1:])
    before = 3 + len(operands) + 4 + len(ends)
    heights = ([first_part * capacity] if first_part else []) + [capacity] * (devices - first_part)
    count = len(heights)
    return pl.pallas_call(
        functools.partial(border_kernel, capacity, paired, first_part),
        grid=(1,),
        in_specs=[smem, smem, smem] + [whole] * len(operands) + [
            pl.BlockSpec((size_y, pairs // 2, LANES, LANES), lambda i: (size_x - 1, 0, 0, 0)),
            pl.BlockSpec((size_x, 1, pairs // 2, LANES, LANES), lambda i: (0, size_y - 1, 0, 0, 0)),
            pl.BlockSpec((size_y, pairs, NODES, LANES), lambda i: (0, 0, 0, 0)),
            pl.BlockSpec((size_x, 1, pairs, NODES, LANES), lambda i: (0, 0, 0, 0, 0)),
        ] + [whole] * (len(ends) + 1),
        out_specs=[whole] * (count + 1),
        out_shape=[jax.ShapeDtypeStruct((height, SLOTS * HALF, LANES), jnp.bfloat16) for height in heights]
        + [jax.ShapeDtypeStruct(total.shape, total.dtype)],
        input_output_aliases={before: count},
        scratch_shapes=[pltpu.SMEM((devices,), jnp.int32), pltpu.SMEM((capacity * devices,), jnp.int32)],
        compiler_params=pltpu.CompilerParams(vmem_limit_bytes=18 * MIB),
        name="border",
    )(owners, place, keys, *operands, turned, planes(turned), natural, planes(natural), *ends, total)


def layout_kernel(source, rows_ref, out_ref, stage):
    group = pl.program_id(0)
    height = out_ref.shape[1]
    for s in range(SLOTS):
        for r in range(height):
            row = source[group * height + r]
            block = rows_ref[jnp.maximum(row, 0), HALF * s : HALF * (s + 1), :].astype(jnp.float32)
            stage[s, pl.ds(r, HALF, stride=height), :] = jnp.where(row >= 0, block, jnp.zeros_like(block))
        for k in range(HALF):
            out_ref[s, :, LANES * k : LANES * (k + 1)] = stage[s, height * k : height * (k + 1), :].astype(jnp.bfloat16)


def laid_out(source, rows, block):
    places, height = rows.shape[0], 8
    return pl.pallas_call(
        layout_kernel,
        grid=(places // height,),
        in_specs=[pl.BlockSpec(memory_space=pltpu.SMEM), pl.BlockSpec(memory_space=pltpu.VMEM)],
        out_specs=pl.BlockSpec((SLOTS, height, block), lambda g: (0, g, 0)),
        out_shape=jax.ShapeDtypeStruct((SLOTS, places, block), jnp.bfloat16),
        scratch_shapes=[pltpu.VMEM((SLOTS, height * HALF, LANES), jnp.float32)],
        compiler_params=pltpu.CompilerParams(vmem_limit_bytes=10 * MIB),
        name="layout",
    )(source, rows)


def placed_kernel(capacity, place_ref, near_ref, *refs):
    parts, (out_ref, stage, laid, done) = refs[:-4], refs[-4:]
    height, count = out_ref.shape[1], near_ref.shape[0]
    copies = [pltpu.make_async_copy(laid.at[s], out_ref.at[s], done.at[s]) for s in range(SLOTS)]
    rows = [(near_ref, row, place_ref[2] // len(parts) * count + row) for row in range(count)]
    for number, part in enumerate(parts):
        first = jnp.bitwise_xor(place_ref[2], len(parts) + number) * capacity
        rows += [(part, q, first + q) for q in range(capacity)]
    for s in range(SLOTS):
        for source, row, spot in rows:
            block = source[row, HALF * s : HALF * (s + 1), :].astype(jnp.float32)
            stage[s, pl.ds(spot, HALF, stride=height), :] = block
        for k in range(HALF):
            laid[s, :, LANES * k : LANES * (k + 1)] = stage[s, height * k : height * (k + 1), :].astype(jnp.bfloat16)
        copies[s].start()
    for copy in copies:
        copy.wait()


def placed(place, near, parts, block):
    capacity = parts[0].shape[0]
    places = near.shape[0] + capacity * len(parts)
    whole = pl.BlockSpec(memory_space=pltpu.VMEM)
    return pl.pallas_call(
        functools.partial(placed_kernel, capacity),
        in_specs=[pl.BlockSpec(memory_space=pltpu.SMEM)] + [whole] * (1 + len(parts)),
        out_specs=pl.BlockSpec(memory_space=pl.ANY),
        out_shape=jax.ShapeDtypeStruct((SLOTS, places, block), jnp.bfloat16),
        scratch_shapes=[
            pltpu.VMEM((SLOTS, places * HALF, LANES), jnp.float32),
            pltpu.VMEM((SLOTS, places, block), jnp.bfloat16),
            pltpu.SemaphoreType.DMA((SLOTS,)),
        ],
        compiler_params=pltpu.CompilerParams(vmem_limit_bytes=16 * MIB),
        name="placed",
    )(place, near, *parts)


def shards(a_diag, a_face, prolong, aggregate, pair_slot, row_owner):
    size_x, size_y, size_z, block = a_diag.shape
    sizes = (size_x, size_y, size_z)
    columns = size_x * size_y
    depth = lax.axis_size("gz")
    capacity = max(2, (AGG_DEV + depth - 1) // depth)
    holding = capacity * depth
    diag = a_diag.reshape(columns, size_z, block)
    faces = a_face.reshape(3, columns, size_z, block)
    assert lax.axis_size("gx") == 2 and lax.axis_size("gy") == 2
    place = jnp.stack([lax.axis_index("gx"), lax.axis_index("gy"), lax.axis_index("gz")]).astype(jnp.int32)
    keys = aggregate[None] * SLOTS + pair_slot

    natural, turned, swap_x, swap_y, near_z, far_z, first_z, last_z, tail_x, tail_y, tail_z = prepare(
        place, prolong.reshape(columns, size_z, block), faces, sizes)
    near_z = swapped_along(near_z, "gz", 0)
    far_z = swapped_along(far_z, "gz", 1)
    got_y = swapped_along(swap_y, "gy", 0)
    got_x = swapped_along(swap_x, "gx", 0)
    total = interior(keys, diag, faces, natural, turned, sizes)
    paired = holding == AGG_DEV and depth & (depth - 1) == 0
    first_part = depth // 2 if paired else 0
    *outgoing, _ = border(
        row_owner, place, keys, (got_x, got_y, near_z, far_z, tail_x, tail_y, tail_z), turned, natural,
        (first_z, last_z), total, capacity, depth, paired, first_part, sizes)
    if paired:
        def swapped_with(part, k):
            return lax.ppermute(part, "gz", [(i, i ^ k) for i in range(depth)])

        near, *far = outgoing
        far = [swapped_with(part, first_part + k) for k, part in enumerate(far)]
        sides = [list(range(first, first + first_part)) for first in (0, first_part)]
        near = lax.all_to_all(near, "gz", 0, 0, tiled=True, axis_index_groups=sides)
        result = placed(place, near, far, block)
    else:
        arrived = lax.all_to_all(jnp.concatenate(outgoing, axis=0), "gz", 0, 0, tiled=True)
        slots = jnp.arange(holding, dtype=jnp.int32)
        owner_ids = jnp.arange(depth, dtype=jnp.int32)
        counts = jnp.sum((row_owner[:, None] == owner_ids[None, :]).astype(jnp.int32), axis=0)
        arrived_counts = lax.all_to_all(counts, "gz", 0, 0, tiled=True)
        present = slots % capacity < jnp.repeat(arrived_counts, capacity)
        target = jnp.cumsum(present.astype(jnp.int32)) - 1
        match = (present[None, :] & (target[None, :] == slots[:, None])).astype(jnp.int32)
        result = laid_out(jnp.sum(match * (slots[None, :] + 1), axis=1) - 1, arrived, block)
    return jnp.transpose(result, (1, 0, 2)).reshape(1, 1, 1, holding, SLOTS, block)


def solution(mesh):
    return jax.shard_map(
        shards,
        mesh=mesh,
        in_specs=(
            P("gx", "gy", "gz", None),
            P(None, "gx", "gy", "gz", None),
            P("gx", "gy", "gz", None),
            P("gx", "gy", "gz"),
            P(None, "gx", "gy", "gz"),
            P(("gx", "gy", "gz")),
        ),
        out_specs=P("gx", "gy", "gz", None, None, None),
        check_vma=False,
    )
```

```python
import functools

import jax
import jax.numpy as jnp
from jax import lax
from jax.experimental import pallas as pl
from jax.experimental.pallas import tpu as pltpu
from jax.sharding import PartitionSpec as P

NODES = 64
SLOTS = 7
AGG_DEV = 24
LANES = 128
HALF = NODES // 2
MIB = 1024 * 1024
STEP = 8


def swapped_along(block, axis, first):
    pairs = [(i, i + 1) for i in range(first, lax.axis_size(axis) - 1, 2)]
    return lax.ppermute(block, axis, pairs + [(i + 1, i) for i, _ in pairs])


def low_lanes(rows):
    return lax.broadcasted_iota(jnp.int32, (rows, LANES), 1) < NODES


def swapped(value):
    return pltpu.roll(value, NODES, 1)


def zero_one(mask):
    return mask.astype(jnp.float32).astype(jnp.bfloat16)


def product(left, right):
    return jnp.dot(left, right, preferred_element_type=jnp.float32)


def across(left, right):
    return lax.dot_general(left, right, (((0,), (0,)), ((), ())), preferred_element_type=jnp.float32)


def spread(column, stage):
    depth = column.shape[0]
    for k in range(column.shape[1] // LANES):
        stage[depth * k : depth * (k + 1), :] = column[:, LANES * k : LANES * (k + 1)].astype(jnp.float32)


def block_of(stage, z, depth):
    return stage[pl.ds(z, HALF, stride=depth), :].astype(jnp.bfloat16)


def stacked_pair(first, second):
    low = low_lanes(HALF)
    even = jnp.where(low, first, swapped(second))
    odd = jnp.where(low, swapped(first), second)
    return jnp.concatenate([even, odd], axis=0)


def in_order(pairs):
    row = lax.broadcasted_iota(jnp.int32, (NODES, NODES), 0)
    col = lax.broadcasted_iota(jnp.int32, (NODES, NODES), 1)
    moved = product(zero_one(row == 2 * (col % HALF) + col // HALF), jnp.concatenate(pairs, axis=1)).astype(jnp.bfloat16)
    return [moved[:, LANES * p : LANES * (p + 1)] for p in range(len(pairs))]


def four_weights(first, second):
    low = low_lanes(NODES)
    zero = jnp.zeros_like(first)
    left = [jnp.where(low, first, zero), jnp.where(low, zero, first), zero, zero]
    right = [zero, zero, jnp.where(low, second, zero), jnp.where(low, zero, second)]
    return jnp.concatenate([jnp.concatenate(left, axis=0), jnp.concatenate(right, axis=0)], axis=1)


def folded(square):
    low = low_lanes(HALF)
    moved = swapped(jnp.where(low, square[HALF : 2 * HALF], square[2 * HALF : 3 * HALF]))
    return [jnp.where(low, square[:HALF], moved), jnp.where(low, moved, square[3 * HALF :])]


def straightened(even, odd):
    low = low_lanes(HALF // 2)
    return jnp.concatenate([jnp.where(low, even, swapped(odd)), jnp.where(low, swapped(even), odd)], axis=0)


def diagonal(square):
    return jnp.where(low_lanes(NODES), square[:NODES], square[NODES:]).astype(jnp.bfloat16)


def apart(first, second):
    zero = jnp.zeros_like(first)
    return jnp.concatenate([jnp.concatenate([first, zero], axis=1), jnp.concatenate([zero, second], axis=1)], axis=0)


def two_pairs(squares):
    return folded(squares[:, :LANES]) + folded(squares[:, LANES:])


def add_all(updates):
    olds = [total[key] for total, key, _ in updates]
    news = []
    for number, (total, key, value) in enumerate(updates):
        for other, other_key, other_value in updates[:number]:
            if other is total:
                value = value + jnp.where(key == other_key, other_value, jnp.zeros_like(other_value))
        news.append(olds[number] + value)
    for (total, key, _), new in zip(updates, news):
        total[key] = new


def prepare_kernel(place_ref, p_ref, fx_ref, fy_ref, fz_ref, natural_ref, turned_ref, swap_x_ref, swap_y_ref, near_z_ref, far_z_ref,
                   first_z_ref, last_z_ref, tail_x_ref, tail_y_ref, tail_z_ref, stages, stages_f, stacks, ends):
    plane = pl.program_id(0)
    size_y, depth = p_ref.shape[0], p_ref.shape[1]
    pairs = depth // 2

    for j in range(size_y):
        stage = stages.at[j]
        spread(p_ref[j], stage)
        block = [block_of(stage, z, depth) for z in range(depth)]
        stacked = [stacked_pair(block[2 * p], block[2 * p + 1]) for p in range(pairs)]
        natural = in_order(stacked)
        for p in range(pairs):
            stacks[j, p] = stacked[p]
            natural_ref[j, p] = natural[p]
        for h in range(pairs // 2):
            turned_ref[j, h] = jnp.concatenate([stacked[2 * h], stacked[2 * h + 1]], axis=0).T
        ends[0, j] = block[0]
        ends[1, j] = block[depth - 1]
        stage_f = stages_f.at[j]
        spread(fz_ref[0, j], stage_f)
        last = block_of(stage_f, depth - 1, depth)
        ends[2, j] = last

    heads = in_order([stacked_pair(ends[0, 2 * t], ends[0, 2 * t + 1]) for t in range(size_y // 2)])
    for t, head in enumerate(heads):
        last, face = [stacked_pair(ends[kind, 2 * t], ends[kind, 2 * t + 1]) for kind in (1, 2)]
        rim = diagonal(across(face, last))
        first_z_ref[t] = head
        last_z_ref[t] = last
        tail_z_ref[t] = face
        near_z_ref[t] = jnp.where(place_ref[2] % 2 == 0, rim, head)
        far_z_ref[t] = jnp.where(place_ref[2] % 2 == 0, head, rim)

    def faces(source, stage, j, tails, rims):
        spread(source, stage)
        block = [block_of(stage, z, depth) for z in range(depth)]
        for p in range(pairs):
            tails[p] = stacked_pair(block[2 * p], block[2 * p + 1])
            rims[p] = diagonal(across(tails[p], stacks[j, p]))

    @pl.when(place_ref[1] == 0)
    def _():
        faces(fy_ref[0, 0], stages_f.at[0], size_y - 1, tail_y_ref.at[0], swap_y_ref.at[0])

    @pl.when(place_ref[1] != 0)
    def _():
        swap_y_ref[0] = natural_ref[0]

    @pl.when((place_ref[0] == 0) & (plane == pl.num_programs(0) - 1))
    def _():
        for j in range(size_y):
            faces(fx_ref[0, j], stages_f.at[j], j, tail_x_ref.at[j], swap_x_ref.at[j])

    @pl.when((place_ref[0] != 0) & (plane == 0))
    def _():
        swap_x_ref[...] = natural_ref[...]


def prepare(place, prolong, faces, sizes):
    size_x, size_y, depth = sizes
    pairs, block = depth // 2, prolong.shape[-1]
    columns, half = size_x * size_y, size_y // 2
    shape = lambda *dims: jax.ShapeDtypeStruct(dims, jnp.bfloat16)
    by_half = pl.BlockSpec((half, NODES, LANES), lambda i: (i, 0, 0))
    edge = shape(columns // 2, NODES, LANES)
    stage = pltpu.VMEM((size_y, depth * HALF, LANES), jnp.float32)
    return pl.pallas_call(
        prepare_kernel,
        grid=(size_x,),
        in_specs=[
            pl.BlockSpec(memory_space=pltpu.SMEM),
            pl.BlockSpec((size_y, depth, block), lambda i: (i, 0, 0)),
            pl.BlockSpec((1, size_y, depth, block), lambda i: (0, size_x - 1, 0, 0)),
            pl.BlockSpec((1, 1, depth, block), lambda i: (1, i * size_y + size_y - 1, 0, 0)),
            pl.BlockSpec((1, size_y, depth, block), lambda i: (2, i, 0, 0)),
        ],
        out_specs=[
            pl.BlockSpec((size_y, pairs, NODES, LANES), lambda i: (i, 0, 0, 0)),
            pl.BlockSpec((size_y, pairs // 2, LANES, LANES), lambda i: (i, 0, 0, 0)),
            pl.BlockSpec((size_y, pairs, NODES, LANES), lambda i: (0, 0, 0, 0)),
            pl.BlockSpec((1, pairs, NODES, LANES), lambda i: (i, 0, 0, 0)),
            by_half, by_half, by_half, by_half,
            pl.BlockSpec((size_y, pairs, NODES, LANES), lambda i: (0, 0, 0, 0)),
            pl.BlockSpec((1, pairs, NODES, LANES), lambda i: (i, 0, 0, 0)),
            by_half,
        ],
        out_shape=[
            shape(columns, pairs, NODES, LANES), shape(columns, pairs // 2, LANES, LANES),
            shape(size_y, pairs, NODES, LANES), shape(size_x, pairs, NODES, LANES), edge, edge, edge, edge,
            shape(size_y, pairs, NODES, LANES), shape(size_x, pairs, NODES, LANES), edge,
        ],
        scratch_shapes=[
            stage, stage,
            pltpu.VMEM((size_y, pairs, NODES, LANES), jnp.bfloat16),
            pltpu.VMEM((3, size_y, HALF, LANES), jnp.bfloat16),
        ],
        compiler_params=pltpu.CompilerParams(vmem_limit_bytes=48 * MIB),
        name="prepare",
    )(place, prolong, faces, faces, faces)


def interior_kernel(keys, diag_ref, face_ref, natural_ref, turned_ref, out_ref,
                    stages, ahead_even, ahead_odd, behind_even, behind_odd, wide):
    _, size_x, size_y, depth = keys.shape
    pairs = depth // 2
    spare = out_ref.shape[0]
    ahead, behind = (ahead_even, ahead_odd), (behind_even, behind_odd)

    for total in ahead + behind:
        total[...] = jnp.zeros_like(total)

    def couplings(i, j, stage, has_x):
        column = i * size_y + j
        sources = [diag_ref[column], face_ref[0, column - size_y] if has_x else None, face_ref[1, column - 1] if j else None, face_ref[2, column]]
        stacked = {}
        for face, source in enumerate(sources):
            if source is None:
                continue
            spread(source, stage.at[face])
            shift = 1 if face == 3 else 0
            block = [block_of(stage.at[face], z, depth) for z in range(depth)]
            stacked[face] = [stacked_pair(block[(2 * p - shift) % depth], block[2 * p + 1 - shift]) for p in range(pairs)]
        couples = {face: [] for face in stacked}
        for h in range(pairs // 2):
            left = [jnp.concatenate([rows[2 * h], rows[2 * h + 1]], axis=1) for rows in stacked.values()]
            weights = four_weights(natural_ref[column, 2 * h], natural_ref[column, 2 * h + 1])
            four = product(jnp.concatenate(left, axis=0), weights).astype(jnp.bfloat16)
            for number, face in enumerate(stacked):
                rows = four[NODES * number : NODES * (number + 1)]
                for couple in (rows[:, :LANES], rows[:, LANES:]):
                    couples[face].append(swapped(couple) if face == 3 else couple)
        low = low_lanes(NODES)
        along = couples[3]
        couples[3] = [jnp.where(low, along[p], along[min(p + 1, pairs - 1)]) for p in range(pairs)]
        return couples

    def sums(i, j, couples):
        column = i * size_y + j
        origin = {0: column, 1: column - size_y, 2: column - 1, 3: column}
        batches = []
        for h in range(pairs // 2):
            for face, pair in couples.items():
                four = two_pairs(product(turned_ref[origin[face], h], apart(pair[2 * h], pair[2 * h + 1])))
                updates = []
                for number, term in enumerate(four):
                    z, side = 4 * h + number, number % 2
                    if face == 0:
                        updates.append((ahead[side], keys[0, i, j, z], term))
                        continue
                    if face == 1:
                        here, there = keys[2, i - 1, j, z], keys[1, i, j, z]
                    elif face == 2:
                        here, there = keys[4, i, j - 1, z], keys[3, i, j, z]
                    elif z + 1 < depth:
                        here, there = keys[6, i, j, z], keys[5, i, j, z + 1]
                    else:
                        continue
                    updates.append((ahead[side], here, term))
                    updates.append((behind[side], there, term))
                batches.append(updates)
        return batches

    def plane(i, carry, has_x=True):
        couples = [couplings(i, j, stages.at[j], has_x) for j in range(size_y)]
        for updates in [updates for j in range(size_y) for updates in sums(i, j, couples[j])]:
            add_all(updates)
        return carry

    plane(0, 0, has_x=False)
    lax.fori_loop(1, size_x, plane, 0)

    def finish(g, carry):
        low = low_lanes(HALF)
        spots = [(p, [wide.shape[0] * 2 * g + 2 * p + side for side in (0, 1)]) for p in range(wide.shape[0])]
        for p, key in spots:
            one, two = [behind_even[key[side]] + behind_odd[key[side]] for side in (0, 1)]
            upper = jnp.where(low, one, swapped(two))
            lower = jnp.where(low, swapped(one), two)
            wide[p, :, :NODES] = jnp.concatenate([upper, lower], axis=0).T
        for p, key in spots:
            for side in (0, 1):
                first = wide[p, NODES * side : NODES * side + HALF, :]
                second = wide[p, NODES * side + HALF : NODES * (side + 1), :]
                turned = jnp.where(low, first, swapped(second))
                out_ref[key[side]] = (ahead_even[key[side]] + ahead_odd[key[side]]) + turned
        return carry

    lax.fori_loop(0, spare // (2 * wide.shape[0]), finish, 0)


def interior(keys, diag, faces, natural, turned, sizes):
    size_x, size_y, depth = sizes
    pairs, block = depth // 2, diag.shape[-1]
    columns, rows = size_x * size_y, AGG_DEV * SLOTS
    total = pltpu.VMEM((rows, HALF, LANES), jnp.float32)
    whole = pl.BlockSpec(memory_space=pltpu.VMEM)
    return pl.pallas_call(
        interior_kernel,
        in_specs=[pl.BlockSpec(memory_space=pltpu.SMEM), whole, whole, whole, whole],
        out_specs=whole,
        out_shape=jax.ShapeDtypeStruct((rows, HALF, LANES), jnp.float32),
        scratch_shapes=[
            pltpu.VMEM((size_y, 4, depth * HALF, LANES), jnp.float32),
            total, total, total, total,
            pltpu.VMEM((28, LANES, LANES), jnp.float32),
        ],
        compiler_params=pltpu.CompilerParams(vmem_limit_bytes=28 * MIB),
        cost_estimate=pl.CostEstimate(flops=columns * depth * 14 * NODES**3, bytes_accessed=columns * depth * 6 * block * 2, transcendentals=0),
        name="interior",
    )(keys, diag, faces, natural, turned)


def border_kernel(capacity, paired, first_part, owners, place_ref, keys, got_x, got_y, near_z, far_z, tail_x, tail_y, tail_z, turned_x, turned_y,
                  natural_x, natural_y, first_z, last_z, start_ref, *refs):
    out_refs, (total, filled, listed) = refs[:-3], refs[-3:]
    size_y, pairs = tail_x.shape[0], tail_x.shape[1]
    size_x, depth = tail_y.shape[0], 2 * pairs
    rows = start_ref.shape[0]

    def key_at(number, i, j, z):
        return keys[number, i, j, z]

    def couplings(tail, head):
        left = jnp.concatenate(tail, axis=1)
        four = product(left, four_weights(*head)).astype(jnp.bfloat16)
        return four[:, :LANES], four[:, LANES:]

    def ahead(tail, head, turned, key):
        for h in range(pairs // 2):
            couples = couplings([tail[2 * h], tail[2 * h + 1]], [head[2 * h], head[2 * h + 1]])
            four = two_pairs(product(turned[h], apart(*couples)))
            yield [(total, key(4 * h + number), term) for number, term in enumerate(four)]

    def turned_terms(first, second, rims):
        return two_pairs(product(jnp.concatenate([first, second], axis=0).T, apart(*rims)))

    def back(natural, rim, key):
        for h in range(pairs // 2):
            four = turned_terms(natural[2 * h], natural[2 * h + 1], (rim[2 * h], rim[2 * h + 1]))
            yield [(total, key(4 * h + number), term) for number, term in enumerate(four)]

    def batches_x(first):
        for j in range(size_y):
            if first:
                yield from ahead(tail_x.at[j], got_x.at[j], turned_x.at[j], functools.partial(key_at, 2, size_x - 1, j))
            else:
                yield from back(natural_x.at[j], got_x.at[j], functools.partial(key_at, 1, 0, j))

    def batches_y(first):
        for i in range(size_x):
            if first:
                yield from ahead(tail_y.at[i], got_y.at[i], turned_y.at[i, 0], functools.partial(key_at, 4, i, size_y - 1))
            else:
                yield from back(natural_y.at[i, 0], got_y.at[i], functools.partial(key_at, 3, i, 0))

    def batches_z():
        even = place_ref[2] % 2 == 0
        for t in range(0, near_z.shape[0], 2):
            heads = [jnp.where(even, near_z[u], far_z[u]) for u in (t, t + 1)]
            couples = couplings([tail_z[t], tail_z[t + 1]], heads)
            front = turned_terms(last_z[t], last_z[t + 1], couples)
            past = turned_terms(first_z[t], first_z[t + 1], [jnp.where(even, far_z[u], near_z[u]) for u in (t, t + 1)])
            spots = [(2 * u // size_y, 2 * u % size_y + side) for u in (t, t + 1) for side in (0, 1)]
            yield [(total, keys[6, i, j, depth - 1], term) for (i, j), term in zip(spots, front)]
            yield [(total, keys[5, i, j, 0], term) for (i, j), term in zip(spots, past)]

    for first_x in (True, False):
        for first_y in (True, False):
            @pl.when(((place_ref[0] == 0) == first_x) & ((place_ref[1] == 0) == first_y))
            def _():
                batches = list(batches_x(first_x)) + list(batches_y(first_y)) + list(batches_z())
                for updates in batches:
                    add_all(updates)

    emit(capacity, paired, first_part, owners, place_ref, total, out_refs, filled, listed)


def emit(capacity, paired, first_part, owners, place_ref, total, out_refs, filled, listed):
    rows, devices = total.shape[0] // SLOTS, filled.shape[0]
    for spot in range(capacity * devices):
        listed[spot] = -1
    for owner in range(devices):
        filled[owner] = 0
    for r in range(rows):
        owner = owners[r]
        listed[jnp.bitwise_xor(owner, place_ref[2] if paired else 0) * capacity + filled[owner]] = r
        filled[owner] = filled[owner] + 1
    for part, out_ref in enumerate(out_refs):
        for q in range(capacity):
            row = listed[(first_part + part) * capacity + q]
            for s in range(SLOTS):
                key = jnp.maximum(row, 0) * SLOTS + s
                even, odd = [total[key, pl.ds(first, HALF // 2, stride=2), :] for first in (0, 1)]
                block = straightened(even, odd)
                if capacity * devices != rows:
                    block = jnp.where(row >= 0, block, jnp.zeros_like(block))
                out_ref[q, HALF * s : HALF * (s + 1), :] = block.astype(jnp.bfloat16)


def near_kernel(capacity, owners, place_ref, total, arrived, *refs):
    emit(capacity, True, 0, owners, place_ref, total, refs[:-2], *refs[-2:])


def near_parts(owners, place, total, arrived, capacity, count, devices):
    smem = pl.BlockSpec(memory_space=pltpu.SMEM)
    whole = pl.BlockSpec(memory_space=pltpu.VMEM)
    return pl.pallas_call(
        functools.partial(near_kernel, capacity),
        in_specs=[smem, smem, whole, pl.BlockSpec(memory_space=pl.ANY)],
        out_specs=[whole] * count,
        out_shape=[jax.ShapeDtypeStruct((capacity, SLOTS * HALF, LANES), jnp.bfloat16)] * count,
        scratch_shapes=[pltpu.SMEM((devices,), jnp.int32), pltpu.SMEM((capacity * devices,), jnp.int32)],
        compiler_params=pltpu.CompilerParams(vmem_limit_bytes=10 * MIB),
        name="near",
    )(owners, place, total, arrived)


def border(owners, place, keys, operands, turned, natural, ends, total, capacity, devices, paired, first_part, sizes):
    size_x, size_y, depth = sizes
    pairs = depth // 2
    smem = pl.BlockSpec(memory_space=pltpu.SMEM)
    whole = pl.BlockSpec(memory_space=pltpu.VMEM)
    planes = lambda array: array.reshape((size_x, size_y) + array.shape[1:])
    before = 3 + len(operands) + 4 + len(ends)
    count = devices - first_part
    return pl.pallas_call(
        functools.partial(border_kernel, capacity, paired, first_part),
        grid=(1,),
        in_specs=[smem, smem, smem] + [whole] * len(operands) + [
            pl.BlockSpec((size_y, pairs // 2, LANES, LANES), lambda i: (size_x - 1, 0, 0, 0)),
            pl.BlockSpec((size_x, 1, pairs // 2, LANES, LANES), lambda i: (0, size_y - 1, 0, 0, 0)),
            pl.BlockSpec((size_y, pairs, NODES, LANES), lambda i: (0, 0, 0, 0)),
            pl.BlockSpec((size_x, 1, pairs, NODES, LANES), lambda i: (0, 0, 0, 0, 0)),
        ] + [whole] * (len(ends) + 1),
        out_specs=[whole] * (count + 1),
        out_shape=[jax.ShapeDtypeStruct((capacity, SLOTS * HALF, LANES), jnp.bfloat16)] * count
        + [jax.ShapeDtypeStruct(total.shape, total.dtype)],
        input_output_aliases={before: count},
        scratch_shapes=[pltpu.SMEM((devices,), jnp.int32), pltpu.SMEM((capacity * devices,), jnp.int32)],
        compiler_params=pltpu.CompilerParams(vmem_limit_bytes=18 * MIB),
        name="border",
    )(owners, place, keys, *operands, turned, planes(turned), natural, planes(natural), *ends, total)


def layout_kernel(source, rows_ref, out_ref, stage):
    group = pl.program_id(0)
    height = out_ref.shape[1]
    for s in range(SLOTS):
        for r in range(height):
            row = source[group * height + r]
            block = rows_ref[jnp.maximum(row, 0), HALF * s : HALF * (s + 1), :].astype(jnp.float32)
            stage[s, pl.ds(r, HALF, stride=height), :] = jnp.where(row >= 0, block, jnp.zeros_like(block))
        for k in range(HALF):
            out_ref[s, :, LANES * k : LANES * (k + 1)] = stage[s, height * k : height * (k + 1), :].astype(jnp.bfloat16)


def laid_out(source, rows, block):
    places, height = rows.shape[0], 8
    return pl.pallas_call(
        layout_kernel,
        grid=(places // height,),
        in_specs=[pl.BlockSpec(memory_space=pltpu.SMEM), pl.BlockSpec(memory_space=pltpu.VMEM)],
        out_specs=pl.BlockSpec((SLOTS, height, block), lambda g: (0, g, 0)),
        out_shape=jax.ShapeDtypeStruct((SLOTS, places, block), jnp.bfloat16),
        scratch_shapes=[pltpu.VMEM((SLOTS, height * HALF, LANES), jnp.float32)],
        compiler_params=pltpu.CompilerParams(vmem_limit_bytes=10 * MIB),
        name="layout",
    )(source, rows)


def placed_kernel(place_ref, *refs):
    parts, (out_ref, stage, laid, done) = refs[:-4], refs[-4:]
    capacity, height = parts[0].shape[0], out_ref.shape[1]
    copies = [pltpu.make_async_copy(laid.at[s], out_ref.at[s], done.at[s]) for s in range(SLOTS)]
    for s in range(SLOTS):
        for number, rows_ref in enumerate(parts):
            first = jnp.bitwise_xor(place_ref[2], number) * capacity
            for q in range(capacity):
                block = rows_ref[q, HALF * s : HALF * (s + 1), :].astype(jnp.float32)
                stage[s, pl.ds(first + q, HALF, stride=height), :] = block
        for k in range(HALF):
            laid[s, :, LANES * k : LANES * (k + 1)] = stage[s, height * k : height * (k + 1), :].astype(jnp.bfloat16)
        copies[s].start()
    for copy in copies:
        copy.wait()


def placed(place, parts, block):
    places = parts[0].shape[0] * len(parts)
    whole = pl.BlockSpec(memory_space=pltpu.VMEM)
    return pl.pallas_call(
        placed_kernel,
        in_specs=[pl.BlockSpec(memory_space=pltpu.SMEM)] + [whole] * len(parts),
        out_specs=pl.BlockSpec(memory_space=pl.ANY),
        out_shape=jax.ShapeDtypeStruct((SLOTS, places, block), jnp.bfloat16),
        scratch_shapes=[
            pltpu.VMEM((SLOTS, places * HALF, LANES), jnp.float32),
            pltpu.VMEM((SLOTS, places, block), jnp.bfloat16),
            pltpu.SemaphoreType.DMA((SLOTS,)),
        ],
        compiler_params=pltpu.CompilerParams(vmem_limit_bytes=16 * MIB),
        name="placed",
    )(place, *parts)


def shards(a_diag, a_face, prolong, aggregate, pair_slot, row_owner):
    size_x, size_y, size_z, block = a_diag.shape
    sizes = (size_x, size_y, size_z)
    columns = size_x * size_y
    depth = lax.axis_size("gz")
    capacity = max(2, (AGG_DEV + depth - 1) // depth)
    holding = capacity * depth
    diag = a_diag.reshape(columns, size_z, block)
    faces = a_face.reshape(3, columns, size_z, block)
    assert lax.axis_size("gx") == 2 and lax.axis_size("gy") == 2
    place = jnp.stack([lax.axis_index("gx"), lax.axis_index("gy"), lax.axis_index("gz")]).astype(jnp.int32)
    keys = aggregate[None] * SLOTS + pair_slot

    natural, turned, swap_x, swap_y, near_z, far_z, first_z, last_z, tail_x, tail_y, tail_z = prepare(
        place, prolong.reshape(columns, size_z, block), faces, sizes)
    near_z = swapped_along(near_z, "gz", 0)
    far_z = swapped_along(far_z, "gz", 1)
    got_y = swapped_along(swap_y, "gy", 0)
    got_x = swapped_along(swap_x, "gx", 0)
    total = interior(keys, diag, faces, natural, turned, sizes)
    paired = holding == AGG_DEV and depth & (depth - 1) == 0
    first_part = depth // 2 if paired else 0
    *outgoing, total = border(
        row_owner, place, keys, (got_x, got_y, near_z, far_z, tail_x, tail_y, tail_z), turned, natural,
        (first_z, last_z), total, capacity, depth, paired, first_part, sizes)
    if paired:
        def swapped_with(part, k):
            return lax.ppermute(part, "gz", [(i, i ^ k) for i in range(depth)]) if k else part

        far = [swapped_with(part, first_part + k) for k, part in enumerate(outgoing)]
        gate = swapped_with(outgoing[-1][:1, :HALF], 1)
        near = [swapped_with(part, k) for k, part in enumerate(near_parts(row_owner, place, total, gate, capacity, first_part, depth))]
        parts = near + far
        result = placed(place, parts, block)
    else:
        arrived = lax.all_to_all(jnp.concatenate(outgoing, axis=0), "gz", 0, 0, tiled=True)
        slots = jnp.arange(holding, dtype=jnp.int32)
        owner_ids = jnp.arange(depth, dtype=jnp.int32)
        counts = jnp.sum((row_owner[:, None] == owner_ids[None, :]).astype(jnp.int32), axis=0)
        arrived_counts = lax.all_to_all(counts, "gz", 0, 0, tiled=True)
        present = slots % capacity < jnp.repeat(arrived_counts, capacity)
        target = jnp.cumsum(present.astype(jnp.int32)) - 1
        match = (present[None, :] & (target[None, :] == slots[:, None])).astype(jnp.int32)
        result = laid_out(jnp.sum(match * (slots[None, :] + 1), axis=1) - 1, arrived, block)
    return jnp.transpose(result, (1, 0, 2)).reshape(1, 1, 1, holding, SLOTS, block)


def solution(mesh):
    return jax.shard_map(
        shards,
        mesh=mesh,
        in_specs=(
            P("gx", "gy", "gz", None),
            P(None, "gx", "gy", "gz", None),
            P("gx", "gy", "gz", None),
            P("gx", "gy", "gz"),
            P(None, "gx", "gy", "gz"),
            P(("gx", "gy", "gz")),
        ),
        out_specs=P("gx", "gy", "gz", None, None, None),
        check_vma=False,
    )
```
